32 devices in a mesh: dp: 16 (over z, y, core), mp: 2 (over x).
Axes of the slice: x: 2, y: 2, z: 4, core: 2. Of those that a mesh axis runs over, the one named last changes fastest.
Arguments:
- block_input: bfloat16 [16384, 1024], P(('dp', 'mp')), may hold values from -6 to 6
- seq_lengths: int32 [16], replicated, may hold values from 576 to 1024, as said below
- seq_owner: int32 [16], replicated, may hold values from 0 to 15, as said below
- mix_gain: float32 [1024], replicated, may hold values from 0.5 to 1.5
- query_weight: bfloat16 [1024, 512], P('dp', 'mp'), may hold values from -0.1875 to 0.1875
- key_weight: bfloat16 [1024, 512], P('dp', 'mp'), may hold values from -0.1875 to 0.1875
- value_weight: bfloat16 [1024, 1024], P('dp', 'mp'), may hold values from -0.1875 to 0.1875
- gate_weight: bfloat16 [1024, 1024], P('dp', 'mp'), may hold values from -0.1875 to 0.1875
- decay_weight: bfloat16 [1024, 4], replicated, may hold values from -0.1875 to 0.1875
- beta_weight: bfloat16 [1024, 4], replicated, may hold values from -0.1875 to 0.1875
- query_filter: float32 [4, 512], replicated, may hold values from -3 to 3
- key_filter: float32 [4, 512], replicated, may hold values from -3 to 3
- value_filter: float32 [4, 1024], replicated, may hold values from -3 to 3
- decay_log: float32 [4], replicated, may hold values from -4 to 0
- decay_bias: float32 [4], replicated, may hold values from -5 to -1
- head_gain: float32 [256], replicated, may hold values from 0.5 to 1.5
- out_weight: bfloat16 [1024, 1024], P('mp', 'dp'), may hold values from -0.1875 to 0.1875
- ffn_gain: float32 [1024], replicated, may hold values from 0.5 to 1.5
- ffn_gate: bfloat16 [1024, 2816], P('dp', 'mp'), may hold values from -0.1875 to 0.1875
- ffn_up: bfloat16 [1024, 2816], P('dp', 'mp'), may hold values from -0.1875 to 0.1875
- ffn_down: bfloat16 [2816, 1024], P('mp', 'dp'), may hold values from -0.109375 to 0.109375
- cotangent: bfloat16 [16384, 1024], P(('dp', 'mp')), may hold values from -6 to 6
Outputs:
- block_output: bfloat16 [16384, 1024], P(('dp', 'mp'))
- input_grad: float32 [16384, 1024], P(('dp', 'mp'))
- mix_gain_grad: float32 [1024], replicated
- query_weight_grad: float32 [1024, 512], P('dp', 'mp')
- key_weight_grad: float32 [1024, 512], P('dp', 'mp')
- value_weight_grad: float32 [1024, 1024], P('dp', 'mp')
- gate_weight_grad: float32 [1024, 1024], P('dp', 'mp')
- decay_weight_grad: float32 [1024, 4], replicated
- beta_weight_grad: float32 [1024, 4], replicated
- query_filter_grad: float32 [4, 512], replicated
- key_filter_grad: float32 [4, 512], replicated
- value_filter_grad: float32 [4, 1024], replicated
- decay_log_grad: float32 [4], replicated
- decay_bias_grad: float32 [4], replicated
- head_gain_grad: float32 [256], replicated
- out_weight_grad: float32 [1024, 1024], P('mp', 'dp')
- ffn_gain_grad: float32 [1024], replicated
- ffn_gate_grad: float32 [1024, 2816], P('dp', 'mp')
- ffn_up_grad: float32 [1024, 2816], P('dp', 'mp')
- ffn_down_grad: float32 [2816, 1024], P('mp', 'dp')
The draws below stay inside these ranges and needn't reach their ends.
Inputs may be any that keep to these rules, and one draw needn't show every extreme that they name: `seq_lengths`: each entry is a multiple of 64 from 576 to 1024; the entries that one index of dp holds sum to at most 1024, and some index's sum equals it. `seq_owner`: every index of dp holds exactly one entry.
All inputs are finite; a program needn't handle non-finite values.
Results may differ from the reference program's by a relative error of at most 0.023.
Values may be sent and summed in bfloat16 or wider, within the bound.
No kernel may reach another device: no remote copies, remote signals or barrier semaphores. Data moves between devices by JAX's collectives and lax.ppermute only.
A program may use at most 256 MiB of HBM per device.

```python
import math
from functools import partial
import jax
import jax.numpy as jnp
from jax import lax

D = 1024
HEADS = 4
DK = 128
DV = 256
FF = 2816
KW = 4
SPAN = 64
TOK_DEV = 1024
SEQ_MIN = 576
SLOTS = 1
SEQS = 16
TOKENS = 16384
HK = 512
HV = 1024
N_DP = 16


def dealing(key):
    base_key = jax.random.fold_in(key, 11)
    count_key, full_key, extra_key, lucky_key, shuffle_key = jax.random.split(base_key, 5)
    span_rows = TOK_DEV // SPAN
    least_spans = SEQ_MIN // SPAN
    devices = jnp.arange(N_DP, dtype=jnp.int32)
    counts = jax.random.randint(count_key, (N_DP,), 1, SLOTS + 1)
    full_device = jax.random.randint(full_key, (), 0, N_DP)
    counts = jnp.where(devices == full_device, 1, counts)
    spare_spans = span_rows - counts * least_spans
    extra_spans = jax.random.randint(extra_key, (N_DP,), 0, spare_spans + 1)
    extra_spans = jnp.where(devices == full_device, spare_spans, extra_spans)
    lucky_slot = jax.random.randint(lucky_key, (N_DP,), 0, counts)
    slot_index = jnp.arange(SLOTS, dtype=jnp.int32)[None, :]
    lengths = jnp.where(slot_index < counts[:, None], least_spans + jnp.where(slot_index == lucky_slot[:, None], extra_spans[:, None], 0), 0) * SPAN
    owners = jnp.broadcast_to(devices[:, None], (N_DP, SLOTS))
    shuffle = jax.random.permutation(shuffle_key, N_DP * SLOTS)
    shuffled_lengths = jnp.zeros((SEQS,), jnp.int32).at[shuffle].set(lengths.reshape(-1).astype(jnp.int32))
    shuffled_owners = jnp.zeros((SEQS,), jnp.int32).at[shuffle].set(owners.reshape(-1).astype(jnp.int32))
    return (shuffled_lengths, shuffled_owners)


def draw_seq_lengths(key, part):
    return dealing(key)[0]


def draw_seq_owner(key, part):
    return dealing(key)[1]


def block_levels(rng, dims, pieces, low, top_value):
    factor_of = 1.0
    for axis_at, parts in pieces:
        steps = jax.random.uniform(jax.random.fold_in(jax.random.fold_in(rng, 6), axis_at), (parts,), jnp.float32, low / len(pieces), top_value / len(pieces))
        factor_of = factor_of * jnp.repeat(jnp.exp(steps), dims[axis_at] // parts).reshape((-1,) + (1,) * (len(dims) - 1 - axis_at))
    return factor_of


def normal_values(own_key, extent, width, bound, shards=(), kind=jnp.bfloat16):
    gain = block_levels(own_key, extent, shards, -0.22, 0.18) if shards else 1.0
    result = jax.random.normal(own_key, extent, jnp.float32) * width * gain
    return jnp.minimum(jnp.maximum(result, -bound), bound).astype(kind)


def setup_inputs(seed: int = 0) -> dict:
    splits = jax.random.split(jax.random.key(seed), 23)
    block_input = normal_values(splits[0], (TOKENS, D), 1.0, 6.0, ((0, 32),))
    seq_lengths = draw_seq_lengths(jax.random.fold_in(splits[22], 71), 0)
    seq_owner = draw_seq_owner(jax.random.fold_in(splits[22], 71), 0)
    mix_gain = jnp.clip(1.0 + 0.1 * jax.random.normal(splits[3], (D,), jnp.float32), 0.5, 1.5)
    query_weight = normal_values(splits[4], (D, HK), D ** -0.5, 0.1875, ((0, 16), (1, 2)))
    key_weight = normal_values(splits[5], (D, HK), D ** -0.5, 0.1875, ((0, 16), (1, 2)))
    value_weight = normal_values(splits[6], (D, HV), D ** -0.5, 0.1875, ((0, 16), (1, 2)))
    gate_weight = normal_values(splits[7], (D, HV), D ** -0.5, 0.1875, ((0, 16), (1, 2)))
    decay_weight = normal_values(splits[8], (D, HEADS), D ** -0.5, 0.1875)
    beta_weight = normal_values(splits[9], (D, HEADS), D ** -0.5, 0.1875)
    query_filter = normal_values(splits[10], (KW, HK), KW ** -0.5, 3.0, (), jnp.float32)
    key_filter = normal_values(splits[11], (KW, HK), KW ** -0.5, 3.0, (), jnp.float32)
    value_filter = normal_values(splits[12], (KW, HV), KW ** -0.5, 3.0, (), jnp.float32)
    decay_log = jnp.clip(jax.random.uniform(splits[13], (HEADS,), jnp.float32, -4.0, 0.0), -4.0, 0.0)
    decay_bias = jnp.clip(jax.random.uniform(splits[14], (HEADS,), jnp.float32, -5.0, -1.0), -5.0, -1.0)
    head_gain = jnp.clip(1.0 + 0.1 * jax.random.normal(splits[15], (DV,), jnp.float32), 0.5, 1.5)
    out_weight = normal_values(splits[16], (HV, D), HV ** -0.5, 0.1875, ((0, 2), (1, 16)))
    ffn_gain = jnp.clip(1.0 + 0.1 * jax.random.normal(splits[17], (D,), jnp.float32), 0.5, 1.5)
    ffn_gate = normal_values(splits[18], (D, FF), D ** -0.5, 0.1875, ((0, 16), (1, 2)))
    ffn_up = normal_values(splits[19], (D, FF), D ** -0.5, 0.1875, ((0, 16), (1, 2)))
    ffn_down = normal_values(splits[20], (FF, D), FF ** -0.5, 0.109375, ((0, 2), (1, 16)))
    cotangent = normal_values(splits[21], (TOKENS, D), 1.0, 6.0, ((0, 32),))
    return {"block_input": block_input, "seq_lengths": seq_lengths, "seq_owner": seq_owner, "mix_gain": mix_gain, "query_weight": query_weight, "key_weight": key_weight, "value_weight": value_weight, "gate_weight": gate_weight, "decay_weight": decay_weight, "beta_weight": beta_weight, "query_filter": query_filter, "key_filter": key_filter, "value_filter": value_filter, "decay_log": decay_log, "decay_bias": decay_bias, "head_gain": head_gain, "out_weight": out_weight, "ffn_gain": ffn_gain, "ffn_gate": ffn_gate, "ffn_up": ffn_up, "ffn_down": ffn_down, "cotangent": cotangent}


EPS = 1e-06
PRECISE = lax.Precision.HIGHEST

def layout(seq_lengths, seq_owner, device, row_count):
    owned = seq_owner == device
    own_lengths = jnp.where(owned, seq_lengths, 0)
    offsets = jnp.cumsum(own_lengths) - own_lengths
    loaded = jnp.sum(own_lengths)
    span_starts = jnp.arange(row_count // SPAN, dtype=jnp.int32) * SPAN
    begins = jnp.any((offsets[None, :] == span_starts[:, None]) & (own_lengths[None, :] > 0), axis=1)
    resets = begins | (span_starts == loaded)
    within = jnp.arange(SPAN, dtype=jnp.int32)
    keep_masks = jnp.stack([jnp.logical_not(resets[:, None] & (within[None, :] < offset)).reshape(row_count) for offset in range(KW)]).astype(jnp.float32)
    valid_rows = (jnp.arange(row_count, dtype=jnp.int32) < loaded).astype(jnp.float32)
    return (keep_masks, resets, valid_rows)

def head_dot_product(formula, left, right):
    return jnp.einsum(formula, left, right, precision=PRECISE)

def across_rows(left, right):
    return lax.dot_general(left, right, (((0,), (0,)), ((), ())), preferred_element_type=jnp.float32)

def against(left, right):
    return lax.dot_general(left, right, (((1,), (1,)), ((), ())), preferred_element_type=jnp.float32)

def rms_forward(values):
    inv_rms = lax.rsqrt(lax.optimization_barrier(jnp.mean(values * values, -1, keepdims=True)) + EPS)
    return (values * inv_rms, inv_rms)

def rms_backward(upstream, normed, inv_rms):
    return inv_rms * (upstream - normed * lax.optimization_barrier(jnp.mean(upstream * normed, -1, keepdims=True)))

def causal_conv(signal, filters, keep_masks):
    summed = signal * filters[0]
    for offset in range(1, KW):
        delayed = jnp.concatenate([jnp.zeros((offset, signal.shape[1]), jnp.float32), signal[:-offset]], axis=0)
        summed = summed + delayed * filters[offset] * keep_masks[offset][:, None]
    return summed

def unit_norm(vectors):
    return vectors * lax.rsqrt(lax.optimization_barrier(jnp.sum(vectors * vectors, -1, keepdims=True)) + EPS)

def delta_rule(queries, keys_unit, values_in, decays, betas, resets):
    row_count, heads_local = decays.shape
    blocks = row_count // SPAN

    def blocked(tensor):
        return jnp.swapaxes(tensor.reshape((blocks, SPAN) + tensor.shape[1:]), 1, 2)
    query_blocks = blocked(queries)
    key_blocks = blocked(keys_unit)
    value_blocks = blocked(values_in)
    beta_blocks = blocked(betas)
    cumulative = jnp.cumsum(blocked(decays), axis=-1)
    gap_matrix = cumulative[..., :, None] - cumulative[..., None, :]
    lower_mask = jnp.tril(jnp.ones((SPAN, SPAN), jnp.float32))
    strict = lower_mask - jnp.eye(SPAN, dtype=jnp.float32)
    factor = jnp.exp(gap_matrix * lower_mask) * lower_mask
    key_gram = head_dot_product('bhik,bhjk->bhij', key_blocks, key_blocks)
    query_key = head_dot_product('bhik,bhjk->bhij', query_blocks, key_blocks)
    coupling = beta_blocks[..., :, None] * factor * strict * key_gram
    inverse = jnp.eye(SPAN, dtype=jnp.float32) - coupling
    powered = coupling
    for round_index in range(SPAN.bit_length() - 2):
        powered = head_dot_product('bhij,bhjk->bhik', powered, powered)
        inverse = inverse + head_dot_product('bhij,bhjk->bhik', inverse, powered)
    growth = jnp.exp(cumulative)
    span_end = cumulative[..., -1:]
    value_part = head_dot_product('bhij,bhjv->bhiv', inverse, beta_blocks[..., None] * value_blocks)
    key_part = head_dot_product('bhij,bhjk->bhik', inverse, (beta_blocks * growth)[..., None] * key_blocks)
    query_grown = growth[..., None] * query_blocks
    key_tail = jnp.exp(span_end - cumulative)[..., None] * key_blocks
    tail_decay = jnp.exp(span_end)
    mixing_all = factor * query_key

    def advance(state, inputs):
        restart, projected_value, projected_key, query_gathered_rows, key_at_step, tail_decay_cumulative, token_mixer_output = inputs
        starting_state = jnp.where(restart, jnp.zeros_like(state), state)
        written_value_rows = projected_value - head_dot_product('dqw,dwy->dqy', projected_key, starting_state)
        block_result_output = head_dot_product('dqw,dwy->dqy', query_gathered_rows, starting_state) + head_dot_product('mgy,myt->mgt', token_mixer_output, written_value_rows)
        state_after_update = tail_decay_cumulative[:, :, None] * starting_state + head_dot_product('gny,gnr->gyr', key_at_step, written_value_rows)
        return (state_after_update, block_result_output)
    initial = jnp.zeros((heads_local, DK, DV), jnp.float32)
    final_state, outputs = lax.scan(advance, initial, (resets, value_part, key_part, query_grown, key_tail, tail_decay, mixing_all))
    return jnp.swapaxes(outputs, 1, 2).reshape(row_count, heads_local, DV)

def packed_mixer(projections, smalls, keep_masks, resets):
    proj_q, proj_k, proj_v, proj_gate, proj_decay, proj_beta = projections
    query_filter, key_filter, value_filter, decay_log, decay_bias, head_gain = smalls
    row_count = proj_q.shape[0]
    heads_local = decay_log.shape[0]
    queries = unit_norm(jax.nn.silu(causal_conv(proj_q, query_filter, keep_masks)).reshape(row_count, heads_local, DK)) * (1.0 / math.sqrt(DK))
    keys_unit = unit_norm(jax.nn.silu(causal_conv(proj_k, key_filter, keep_masks)).reshape(row_count, heads_local, DK))
    values_in = jax.nn.silu(causal_conv(proj_v, value_filter, keep_masks)).reshape(row_count, heads_local, DV)
    betas = jax.nn.sigmoid(proj_beta)
    decays = -jnp.exp(decay_log) * jax.nn.softplus(proj_decay + decay_bias)
    outputs = delta_rule(queries, keys_unit, values_in, decays, betas, resets)
    normed = outputs * lax.rsqrt(lax.optimization_barrier(jnp.mean(outputs * outputs, -1, keepdims=True)) + EPS)
    gated = normed * head_gain * jax.nn.silu(proj_gate.reshape(row_count, heads_local, DV))
    return gated.reshape(row_count, heads_local * DV)

def block_pass(inputs_rows, cotangent_rows, keep_masks, resets, valid_rows, mix_gain, query_weight, key_weight, value_weight, gate_weight, decay_weight, beta_weight, query_filter, key_filter, value_filter, decay_log, decay_bias, head_gain, out_weight, ffn_gain, ffn_gate, ffn_up, ffn_down):
    inputs_f = inputs_rows.astype(jnp.float32)
    valid_col = valid_rows[:, None]
    normed1, inv_rms1 = rms_forward(inputs_f)
    mixed_in = (normed1 * mix_gain).astype(jnp.bfloat16)
    proj_weights = (query_weight, key_weight, value_weight, gate_weight, decay_weight, beta_weight)
    projections = tuple((jnp.dot(mixed_in, weight_mat, preferred_element_type=jnp.float32) for weight_mat in proj_weights))
    smalls = (query_filter, key_filter, value_filter, decay_log, decay_bias, head_gain)
    gated, pullback = jax.vjp(partial(packed_mixer, keep_masks=keep_masks, resets=resets), projections, smalls)
    gated_b = gated.astype(jnp.bfloat16)
    resid = inputs_f + valid_col * jnp.dot(gated_b, out_weight, preferred_element_type=jnp.float32)
    normed2, inv_rms2 = rms_forward(resid)
    ffn_in = (normed2 * ffn_gain).astype(jnp.bfloat16)
    gate_pre = jnp.dot(ffn_in, ffn_gate, preferred_element_type=jnp.float32)
    up_pre = jnp.dot(ffn_in, ffn_up, preferred_element_type=jnp.float32)
    sigmoid_gate = jax.nn.sigmoid(gate_pre)
    activated = gate_pre * sigmoid_gate
    hidden = (activated * up_pre).astype(jnp.bfloat16)
    block_output = (resid + valid_col * jnp.dot(hidden, ffn_down, preferred_element_type=jnp.float32)).astype(jnp.bfloat16)
    cot_masked = cotangent_rows * valid_col.astype(jnp.bfloat16)
    down_grad = across_rows(hidden, cot_masked)
    hidden_grad = against(cot_masked, ffn_down)
    gate_grad_pre = (hidden_grad * up_pre * sigmoid_gate * (1.0 + gate_pre * (1.0 - sigmoid_gate))).astype(jnp.bfloat16)
    up_grad_pre = (hidden_grad * activated).astype(jnp.bfloat16)
    ffn_gate_grad = across_rows(ffn_in, gate_grad_pre)
    ffn_up_grad = across_rows(ffn_in, up_grad_pre)
    ffn_in_grad = against(gate_grad_pre, ffn_gate) + against(up_grad_pre, ffn_up)
    ffn_gain_grad = lax.optimization_barrier(jnp.sum(ffn_in_grad * normed2, 0))
    resid_grad = cotangent_rows.astype(jnp.float32) + rms_backward(ffn_in_grad * ffn_gain, normed2, inv_rms2)
    mix_cot = (resid_grad * valid_col).astype(jnp.bfloat16)
    out_grad = across_rows(gated_b, mix_cot)
    gated_grad = against(mix_cot, out_weight)
    proj_grads, small_grads = pullback(gated_grad)
    proj_grads_b = tuple((grad_piece.astype(jnp.bfloat16) for grad_piece in proj_grads))
    weight_grads = tuple((across_rows(mixed_in, grad_piece) for grad_piece in proj_grads_b))
    mix_in_grad = jnp.zeros_like(inputs_f)
    for grad_piece, weight_mat in zip(proj_grads_b, proj_weights):
        mix_in_grad = mix_in_grad + against(grad_piece, weight_mat)
    mix_gain_grad = lax.optimization_barrier(jnp.sum(mix_in_grad * normed1, 0))
    input_grad = resid_grad + rms_backward(mix_in_grad * mix_gain, normed1, inv_rms1)
    grads = (mix_gain_grad, weight_grads[0], weight_grads[1], weight_grads[2], weight_grads[3], weight_grads[4], weight_grads[5], small_grads[0], small_grads[1], small_grads[2], small_grads[3], small_grads[4], small_grads[5], out_grad, ffn_gain_grad, ffn_gate_grad, ffn_up_grad, down_grad)
    return (block_output, input_grad, grads)

def reference(block_input, seq_lengths, seq_owner, mix_gain, query_weight, key_weight, value_weight, gate_weight, decay_weight, beta_weight, query_filter, key_filter, value_filter, decay_log, decay_bias, head_gain, out_weight, ffn_gain, ffn_gate, ffn_up, ffn_down, cotangent):
    stacked_in = block_input.reshape(N_DP, TOK_DEV, D)
    stacked_cot = cotangent.reshape(N_DP, TOK_DEV, D)
    params = (mix_gain, query_weight, key_weight, value_weight, gate_weight, decay_weight, beta_weight, query_filter, key_filter, value_filter, decay_log, decay_bias, head_gain, out_weight, ffn_gain, ffn_gate, ffn_up, ffn_down)

    def visit(carry, items):
        device, inputs_rows, cot_rows = items
        keep_masks, resets, valid_rows = layout(seq_lengths, seq_owner, device, TOK_DEV)
        block_output, input_grad, grads = block_pass(inputs_rows, cot_rows, keep_masks, resets, valid_rows, *params)
        return (tuple((held + fresh for held, fresh in zip(carry, grads))), (block_output, input_grad))
    initial = tuple((jnp.zeros(parameter.shape, jnp.float32) for parameter in params))
    totals, results = lax.scan(visit, initial, (jnp.arange(N_DP, dtype=jnp.int32), stacked_in, stacked_cot))
    outputs = results[0].reshape(TOKENS, D)
    input_grads = results[1].reshape(TOKENS, D)
    return (outputs, input_grads, totals[0], totals[1], totals[2], totals[3], totals[4], totals[5], totals[6], totals[7], totals[8], totals[9], totals[10], totals[11], totals[12], totals[13], totals[14], totals[15], totals[16], totals[17])
```

```python
from functools import partial
import math

import jax
import jax.numpy as jnp
from jax import lax
from jax.sharding import PartitionSpec as P

DK = 128
DV = 256
KW = 4
SPAN = 64


EPS = 1e-06
PRECISE = lax.Precision.HIGHEST


def layout(seq_lengths, seq_owner, device, row_count):
    owned = seq_owner == device
    own_lengths = jnp.where(owned, seq_lengths, 0)
    offsets = jnp.cumsum(own_lengths) - own_lengths
    loaded = jnp.sum(own_lengths)
    span_starts = jnp.arange(row_count // SPAN, dtype=jnp.int32) * SPAN
    begins = jnp.any(
        (offsets[None, :] == span_starts[:, None]) & (own_lengths[None, :] > 0), axis=1
    )
    resets = begins | (span_starts == loaded)
    within = jnp.arange(SPAN, dtype=jnp.int32)
    keep_masks = jnp.stack(
        [
            jnp.logical_not(resets[:, None] & (within[None, :] < offset)).reshape(row_count)
            for offset in range(KW)
        ]
    ).astype(jnp.float32)
    valid_rows = (jnp.arange(row_count, dtype=jnp.int32) < loaded).astype(jnp.float32)
    return (keep_masks, resets, valid_rows)


def head_dot_product(formula, left, right):
    return jnp.einsum(formula, left, right, precision=PRECISE)


def across_rows(left, right):
    return lax.dot_general(
        left, right, (((0,), (0,)), ((), ())), preferred_element_type=jnp.float32
    )


def against(left, right):
    return lax.dot_general(
        left, right, (((1,), (1,)), ((), ())), preferred_element_type=jnp.float32
    )


def rms_forward(values):
    inv_rms = lax.rsqrt(jnp.mean(values * values, -1, keepdims=True) + EPS)
    return (values * inv_rms, inv_rms)


def rms_backward(upstream, normed, inv_rms):
    return inv_rms * (upstream - normed * jnp.mean(upstream * normed, -1, keepdims=True))


def causal_conv(signal, filters, keep_masks):
    summed = signal * filters[0]
    for offset in range(1, KW):
        delayed = jnp.concatenate(
            [jnp.zeros((offset, signal.shape[1]), jnp.float32), signal[:-offset]], axis=0
        )
        summed = summed + delayed * filters[offset] * keep_masks[offset][:, None]
    return summed


def unit_norm(vectors):
    return vectors * lax.rsqrt(jnp.sum(vectors * vectors, -1, keepdims=True) + EPS)


def delta_rule(queries, keys_unit, values_in, decays, betas, resets):
    row_count, heads_local = decays.shape
    blocks = row_count // SPAN

    def blocked(tensor):
        return jnp.swapaxes(tensor.reshape((blocks, SPAN) + tensor.shape[1:]), 1, 2)

    query_blocks = blocked(queries)
    key_blocks = blocked(keys_unit)
    value_blocks = blocked(values_in)
    beta_blocks = blocked(betas)
    cumulative = jnp.cumsum(blocked(decays), axis=-1)
    gap_matrix = cumulative[..., :, None] - cumulative[..., None, :]
    lower_mask = jnp.tril(jnp.ones((SPAN, SPAN), jnp.float32))
    strict = lower_mask - jnp.eye(SPAN, dtype=jnp.float32)
    factor = jnp.exp(gap_matrix * lower_mask) * lower_mask
    key_gram = head_dot_product("bhik,bhjk->bhij", key_blocks, key_blocks)
    query_key = head_dot_product("bhik,bhjk->bhij", query_blocks, key_blocks)
    coupling = beta_blocks[..., :, None] * factor * strict * key_gram
    inverse = jnp.eye(SPAN, dtype=jnp.float32) - coupling
    powered = coupling
    for round_index in range(SPAN.bit_length() - 2):
        powered = head_dot_product("bhij,bhjk->bhik", powered, powered)
        inverse = inverse + head_dot_product("bhij,bhjk->bhik", inverse, powered)
    growth = jnp.exp(cumulative)
    span_end = cumulative[..., -1:]
    value_part = head_dot_product("bhij,bhjv->bhiv", inverse, beta_blocks[..., None] * value_blocks)
    key_part = head_dot_product(
        "bhij,bhjk->bhik", inverse, (beta_blocks * growth)[..., None] * key_blocks
    )
    query_grown = growth[..., None] * query_blocks
    key_tail = jnp.exp(span_end - cumulative)[..., None] * key_blocks
    tail_decay = jnp.exp(span_end)
    mixing_all = factor * query_key

    def advance(state, inputs):
        (
            restart,
            projected_value,
            projected_key,
            query_gathered_rows,
            key_at_step,
            tail_decay_cumulative,
            token_mixer_output,
        ) = inputs
        starting_state = jnp.where(restart, jnp.zeros_like(state), state)
        written_value_rows = projected_value - head_dot_product(
            "dqw,dwy->dqy", projected_key, starting_state
        )
        block_result_output = head_dot_product(
            "dqw,dwy->dqy", query_gathered_rows, starting_state
        ) + head_dot_product("mgy,myt->mgt", token_mixer_output, written_value_rows)
        state_after_update = tail_decay_cumulative[:, :, None] * starting_state + head_dot_product(
            "gny,gnr->gyr", key_at_step, written_value_rows
        )
        return (state_after_update, block_result_output)

    initial = jnp.zeros((heads_local, DK, DV), jnp.float32)
    final_state, outputs = lax.scan(
        advance,
        initial,
        (resets, value_part, key_part, query_grown, key_tail, tail_decay, mixing_all),
    )
    return jnp.swapaxes(outputs, 1, 2).reshape(row_count, heads_local, DV)


def packed_mixer(projections, smalls, keep_masks, resets):
    proj_q, proj_k, proj_v, proj_gate, proj_decay, proj_beta = projections
    query_filter, key_filter, value_filter, decay_log, decay_bias, head_gain = smalls
    row_count = proj_q.shape[0]
    heads_local = decay_log.shape[0]
    queries = unit_norm(
        jax.nn.silu(causal_conv(proj_q, query_filter, keep_masks)).reshape(
            row_count, heads_local, DK
        )
    ) * (1.0 / math.sqrt(DK))
    keys_unit = unit_norm(
        jax.nn.silu(causal_conv(proj_k, key_filter, keep_masks)).reshape(row_count, heads_local, DK)
    )
    values_in = jax.nn.silu(causal_conv(proj_v, value_filter, keep_masks)).reshape(
        row_count, heads_local, DV
    )
    betas = jax.nn.sigmoid(proj_beta)
    decays = -jnp.exp(decay_log) * jax.nn.softplus(proj_decay + decay_bias)
    outputs = delta_rule(queries, keys_unit, values_in, decays, betas, resets)
    normed = outputs * lax.rsqrt(jnp.mean(outputs * outputs, -1, keepdims=True) + EPS)
    gated = normed * head_gain * jax.nn.silu(proj_gate.reshape(row_count, heads_local, DV))
    return gated.reshape(row_count, heads_local * DV)


def swap_halves(array):
    return lax.ppermute(array, "mp", [(0, 1), (1, 0)])


def dp_total(array):
    count = lax.axis_size("dp")
    step = 1
    while step < count:
        array = array + lax.ppermute(array, "dp", [(i, i ^ step) for i in range(count)])
        step *= 2
    return array


def in_order(own, other, model_index, axis):
    first = jnp.where(model_index == 0, own, other)
    second = jnp.where(model_index == 0, other, own)
    return jnp.concatenate([first, second], axis=axis)


def on_device(
    block_input,
    seq_lengths,
    seq_owner,
    mix_gain,
    query_weight,
    key_weight,
    value_weight,
    gate_weight,
    decay_weight,
    beta_weight,
    query_filter,
    key_filter,
    value_filter,
    decay_log,
    decay_bias,
    head_gain,
    out_weight,
    ffn_gain,
    ffn_gate,
    ffn_up,
    ffn_down,
    cotangent,
):
    bf16 = jnp.bfloat16
    f32 = jnp.float32
    local_rows, width = block_input.shape
    dp_index = lax.axis_index("dp")
    model_count = lax.axis_size("mp")
    model_index = lax.axis_index("mp")
    row_count = local_rows * model_count
    keep_masks, resets, valid_rows = layout(seq_lengths, seq_owner, dp_index, row_count)
    valid_all = valid_rows[:, None]
    heads_local = decay_log.shape[0] // model_count
    qk_cols = heads_local * DK
    v_cols = heads_local * DV
    ff_cols = ffn_gate.shape[1]
    shard_rows = query_weight.shape[0]
    proj_cols = 2 * qk_cols + 2 * v_cols

    def own_columns(array, col_count):
        return lax.dynamic_slice_in_dim(array, model_index * col_count, col_count, array.ndim - 1)

    def own_shard(array):
        return lax.dynamic_slice_in_dim(array, dp_index * shard_rows, shard_rows, 0)

    small_weight = jnp.concatenate(
        [own_columns(decay_weight, heads_local), own_columns(beta_weight, heads_local)], axis=1
    )
    small_weight = jnp.pad(small_weight, ((0, 0), (0, 128 - 2 * heads_local)))
    shard_mix = jnp.concatenate(
        [query_weight, key_weight, value_weight, gate_weight, own_shard(small_weight)], axis=1
    )
    mix_weight = lax.all_gather(shard_mix, "dp", axis=0, tiled=True)
    input_other = swap_halves(block_input)
    out_rows = out_weight.T
    out_other = swap_halves(out_rows)
    shard_rest = jnp.concatenate([out_rows, out_other, ffn_gate, ffn_up, ffn_down.T], axis=1)
    rest_weight = lax.all_gather(shard_rest, "dp", axis=0, tiled=True)
    out_both = rest_weight[:, : 2 * v_cols]
    ffn_in_weight = rest_weight[:, 2 * v_cols : 2 * v_cols + 2 * ff_cols]
    down_weight = rest_weight[:, 2 * v_cols + 2 * ff_cols :]
    cot_other = swap_halves(cotangent)

    smalls = (
        own_columns(query_filter, qk_cols),
        own_columns(key_filter, qk_cols),
        own_columns(value_filter, v_cols),
        own_columns(decay_log, heads_local),
        own_columns(decay_bias, heads_local),
        head_gain,
    )
    inputs_f = in_order(block_input, input_other, model_index, 0).astype(f32)
    cot_all = in_order(cotangent, cot_other, model_index, 0)
    normed1, inv_rms1 = rms_forward(inputs_f)
    mixed_in = (normed1 * mix_gain).astype(bf16)
    proj = jnp.dot(mixed_in, mix_weight, preferred_element_type=f32)
    cuts = (qk_cols, 2 * qk_cols, 2 * qk_cols + v_cols, proj_cols, proj_cols + heads_local)

    def split(array):
        return (
            array[:, : cuts[0]],
            array[:, cuts[0] : cuts[1]],
            array[:, cuts[1] : cuts[2]],
            array[:, cuts[2] : cuts[3]],
            array[:, cuts[3] : cuts[4]],
            array[:, cuts[4] : cuts[4] + heads_local],
        )

    gated, pullback = jax.vjp(
        partial(packed_mixer, keep_masks=keep_masks, resets=resets), split(proj), smalls
    )
    gated_b = gated.astype(bf16)
    gated_both = jnp.concatenate([gated_b, swap_halves(gated_b)], axis=1)
    resid = inputs_f + valid_all * against(gated_both, out_both)
    normed2, inv_rms2 = rms_forward(resid)
    ffn_in = (normed2 * ffn_gain).astype(bf16)
    pre = jnp.dot(ffn_in, ffn_in_weight, preferred_element_type=f32)
    gate_pre, up_pre = pre[:, :ff_cols], pre[:, ff_cols:]
    sigmoid_gate = jax.nn.sigmoid(gate_pre)
    activated = gate_pre * sigmoid_gate
    hidden = (activated * up_pre).astype(bf16)
    cot_masked = cot_all * valid_all.astype(bf16)
    hidden_grad = jnp.dot(cot_masked, down_weight, preferred_element_type=f32)
    gate_grad_pre = (
        hidden_grad * up_pre * sigmoid_gate * (1.0 + gate_pre * (1.0 - sigmoid_gate))
    ).astype(bf16)
    up_grad_pre = (hidden_grad * activated).astype(bf16)
    pre_grad = jnp.concatenate([gate_grad_pre, up_grad_pre], axis=1)
    ffn_in_part = against(pre_grad, ffn_in_weight)
    ffn_in_sent = ffn_in_part.astype(bf16)
    ffn_in_grad = ffn_in_sent.astype(f32) + swap_halves(ffn_in_sent).astype(f32)

    def own_half(array):
        return lax.dynamic_slice_in_dim(array, model_index * local_rows, local_rows, 0)

    def other_half(array):
        return lax.dynamic_slice_in_dim(array, (1 - model_index) * local_rows, local_rows, 0)

    ffn_part = against(hidden, down_weight)
    ffn_sum = own_half(ffn_part) + swap_halves(other_half(ffn_part).astype(bf16)).astype(f32)
    block_output = (own_half(resid) + own_half(valid_all) * ffn_sum).astype(bf16)
    rest_grads = jnp.concatenate(
        [across_rows(ffn_in, pre_grad).astype(bf16), across_rows(cot_masked, hidden).astype(bf16)],
        axis=1,
    )
    ffn_shard = lax.psum_scatter(rest_grads, "dp", scatter_dimension=0, tiled=True)
    ffn_gain_part = jnp.sum(ffn_in_part * normed2, 0)
    resid_grad = cot_all.astype(f32) + rms_backward(ffn_in_grad * ffn_gain, normed2, inv_rms2)
    mix_cot = (resid_grad * valid_all).astype(bf16)
    gated_grad = jnp.dot(mix_cot, out_both[:, :v_cols], preferred_element_type=f32)
    proj_grads, small_grads = pullback(gated_grad)
    pad = jnp.zeros((row_count, 128 - 2 * heads_local), f32)
    proj_grad = jnp.concatenate(list(proj_grads) + [pad], axis=1).astype(bf16)
    mix_grads = jnp.concatenate(
        [
            across_rows(mixed_in, proj_grad[:, :proj_cols]).astype(bf16),
            across_rows(mix_cot, gated_b).astype(bf16),
        ],
        axis=1,
    )
    mix_shard = lax.psum_scatter(mix_grads, "dp", scatter_dimension=0, tiled=True)
    rate_grads = across_rows(proj_grad[:, proj_cols:], mixed_in)[: 2 * heads_local]
    mix_in_part = against(proj_grad, mix_weight)
    mix_in_sum = own_half(mix_in_part) + swap_halves(
        other_half(mix_in_part).astype(bf16)
    ).astype(f32)
    mix_gain_part = jnp.sum(mix_in_part * normed1, 0)
    input_grad = own_half(resid_grad) + rms_backward(
        mix_in_sum * mix_gain, own_half(normed1), own_half(inv_rms1)
    )
    common = jnp.concatenate(
        [mix_gain_part, ffn_gain_part, small_grads[5], jnp.zeros((width - DV,), f32)]
    ).reshape(3, width)
    tail_row = jnp.concatenate(
        [small_grads[3], small_grads[4], jnp.zeros((width - 2 * heads_local,), f32)]
    )
    split_rows = jnp.concatenate(
        [
            rate_grads,
            small_grads[0].reshape(-1, width),
            small_grads[1].reshape(-1, width),
            small_grads[2].reshape(-1, width),
            tail_row[None],
        ],
        axis=0,
    )
    totals = dp_total(jnp.concatenate([common, split_rows], axis=0))
    totals_other = swap_halves(totals)
    common = totals[:3] + totals_other[:3]
    lower = jnp.where(model_index == 0, totals, totals_other)[3:]
    upper = jnp.where(model_index == 0, totals_other, totals)[3:]

    def joined(start, rows, cols):
        return jnp.concatenate(
            [
                lower[start : start + rows].reshape(-1, cols),
                upper[start : start + rows].reshape(-1, cols),
            ],
            axis=1,
        )

    q_rows = KW * qk_cols // width
    v_rows = KW * v_cols // width
    at_q = 2 * heads_local
    at_k = at_q + q_rows
    at_v = at_k + q_rows
    at_tail = at_v + v_rows

    def rate_weight_grad(start):
        return jnp.concatenate(
            [lower[start : start + heads_local], upper[start : start + heads_local]], axis=0
        ).T

    def rate_grad(start):
        return jnp.concatenate(
            [
                lower[at_tail, start : start + heads_local],
                upper[at_tail, start : start + heads_local],
            ]
        )

    mix_shard = mix_shard.astype(f32)
    ffn_shard = ffn_shard.astype(f32)
    return (
        block_output,
        input_grad,
        common[0],
        mix_shard[:, : cuts[0]],
        mix_shard[:, cuts[0] : cuts[1]],
        mix_shard[:, cuts[1] : cuts[2]],
        mix_shard[:, cuts[2] : cuts[3]],
        rate_weight_grad(0),
        rate_weight_grad(heads_local),
        joined(at_q, q_rows, qk_cols),
        joined(at_k, q_rows, qk_cols),
        joined(at_v, v_rows, v_cols),
        rate_grad(0),
        rate_grad(heads_local),
        common[2, :DV],
        mix_shard[:, proj_cols:].T,
        common[1],
        ffn_shard[:, :ff_cols],
        ffn_shard[:, ff_cols : 2 * ff_cols],
        ffn_shard[:, 2 * ff_cols :].T,
    )


def solution(mesh):
    in_specs = (
        P(("dp", "mp"), None),
        P(),
        P(),
        P(),
        P("dp", "mp"),
        P("dp", "mp"),
        P("dp", "mp"),
        P("dp", "mp"),
        P(),
        P(),
        P(),
        P(),
        P(),
        P(),
        P(),
        P(),
        P("mp", "dp"),
        P(),
        P("dp", "mp"),
        P("dp", "mp"),
        P("mp", "dp"),
        P(("dp", "mp"), None),
    )
    out_specs = (
        P(("dp", "mp"), None),
        P(("dp", "mp"), None),
        P(),
        P("dp", "mp"),
        P("dp", "mp"),
        P("dp", "mp"),
        P("dp", "mp"),
        P(),
        P(),
        P(),
        P(),
        P(),
        P(),
        P(),
        P(),
        P("mp", "dp"),
        P(),
        P("dp", "mp"),
        P("dp", "mp"),
        P("mp", "dp"),
    )
    return jax.shard_map(
        on_device, mesh=mesh, in_specs=in_specs, out_specs=out_specs, check_vma=False
    )
```

```python
from functools import partial
import math

import jax
import jax.numpy as jnp
from jax import lax
from jax.experimental import pallas as pl
from jax.experimental.pallas import tpu as pltpu
from jax.sharding import PartitionSpec as P

DK = 128
DV = 256
KW = 4
SPAN = 64


EPS = 1e-06


def layout(seq_lengths, seq_owner, device, row_count):
    owned = seq_owner == device
    own_lengths = jnp.where(owned, seq_lengths, 0)
    offsets = jnp.cumsum(own_lengths) - own_lengths
    loaded = jnp.sum(own_lengths)
    span_starts = jnp.arange(row_count // SPAN, dtype=jnp.int32) * SPAN
    begins = jnp.any(
        (offsets[None, :] == span_starts[:, None]) & (own_lengths[None, :] > 0), axis=1
    )
    resets = begins | (span_starts == loaded)
    within = jnp.arange(SPAN, dtype=jnp.int32)
    keep_masks = jnp.stack(
        [
            jnp.logical_not(resets[:, None] & (within[None, :] < offset)).reshape(row_count)
            for offset in range(KW)
        ]
    ).astype(jnp.float32)
    valid_rows = (jnp.arange(row_count, dtype=jnp.int32) < loaded).astype(jnp.float32)
    return (keep_masks, resets, valid_rows)


def across_rows(left, right):
    return lax.dot_general(
        left, right, (((0,), (0,)), ((), ())), preferred_element_type=jnp.float32
    )


def against(left, right):
    return lax.dot_general(
        left, right, (((1,), (1,)), ((), ())), preferred_element_type=jnp.float32
    )


def rms_forward(values):
    inv_rms = lax.rsqrt(jnp.mean(values * values, -1, keepdims=True) + EPS)
    return (values * inv_rms, inv_rms)


def rms_backward(upstream, normed, inv_rms):
    return inv_rms * (upstream - normed * jnp.mean(upstream * normed, -1, keepdims=True))


ROWS = 128
NN = ((1,), (0,))
NT = ((1,), (1,))
TN = ((0,), (0,))
FINE_GRAM = False
FINE_INVERSE = True
FINE_APPLY = False
FINE_STATE = False
FINE_BACK = False


def dot(left, right, dims):
    return lax.dot_general(left, right, (dims, ((), ())), preferred_element_type=jnp.float32)


def high_low(values):
    high = values.astype(jnp.bfloat16)
    return high, (values - high.astype(jnp.float32)).astype(jnp.bfloat16)


def product(left, right, dims, fine=False):
    if not fine:
        return dot(left.astype(jnp.bfloat16), right.astype(jnp.bfloat16), dims)
    left_high, left_low = high_low(left)
    right_high, right_low = high_low(right)
    return dot(left_high, right_high, dims) + (
        dot(left_high, right_low, dims) + dot(left_low, right_high, dims)
    )


def summed_by(mask, values, dims=NN):
    high, low = high_low(values)
    return dot(mask, high, dims) + dot(mask, low, dims)


def chunk_masks(resets_ref, chunk):
    first = 1.0 - resets_ref[2 * chunk].astype(jnp.float32)
    second = 1.0 - resets_ref[2 * chunk + 1].astype(jnp.float32)
    row = lax.broadcasted_iota(jnp.int32, (ROWS, ROWS), 0)
    col = lax.broadcasted_iota(jnp.int32, (ROWS, ROWS), 1)
    late = row >= SPAN
    reached = jnp.where(late, first * second, first)
    reaching = jnp.where(late, 1.0, second)
    joined = jnp.where(late & (col < SPAN), second, 1.0)
    return row, col, reached, reaching, joined, first * second


def unit_lower_inverse(coupling, row, col):
    eye = jnp.where(row == col, 1.0, 0.0)
    base = 16
    near = jnp.where((row // base) == (col // base), coupling, 0.0)
    inverse = eye - near
    powered = near
    size = 2
    while size < base:
        powered = product(powered, powered, NN, FINE_INVERSE)
        inverse = inverse + product(inverse, powered, NN, FINE_INVERSE)
        size *= 2
    while base < ROWS:
        wide = 2 * base
        link = jnp.where(
            ((row // wide) == (col // wide)) & ((row // base) != (col // base)), coupling, 0.0
        )
        inverse = inverse - product(
            inverse, product(link, inverse, NN, FINE_INVERSE), NN, FINE_INVERSE
        )
        base = wide
    return inverse


def sigmoid(values):
    return 1.0 / (1.0 + jnp.exp(-values))


def lane_sum(values):
    return jnp.sum(values, -1, keepdims=True)


def forward_kernel(
    heads,
    resets_ref,
    proj_ref,
    keep_ref,
    filter_ref,
    rates_ref,
    gain_ref,
    gated_ref,
    conv_ref,
    mixed_ref,
    state_ref,
    inverse_ref,
    parts_ref,
    written_ref,
    factor_ref,
    grams_ref,
    rows_buf,
    state_buf,
):
    chunk = pl.program_id(0)
    qk = heads * DK
    conv_cols = 2 * qk + heads * DV
    proj_cols = conv_cols + heads * DV

    @pl.when(chunk == 0)
    def _():
        rows_buf[0:8, :] = jnp.zeros((8, conv_cols), jnp.float32)
        state_buf[...] = jnp.zeros_like(state_buf)

    rows_buf[8 : 8 + ROWS, :] = proj_ref[:, :conv_cols]
    conv = rows_buf[8 : 8 + ROWS, :] * filter_ref[0:1, :]
    for offset in range(1, KW):
        conv = conv + rows_buf[8 - offset : 8 - offset + ROWS, :] * (
            filter_ref[offset : offset + 1, :] * keep_ref[:, offset : offset + 1]
        )
    rows_buf[0:8, :] = rows_buf[ROWS : ROWS + 8, :]
    conv_ref[...] = conv

    row, col, reached, reaching, joined, passed = chunk_masks(resets_ref, chunk)
    lower = jnp.where(row >= col, 1.0, 0.0)
    lower_b = lower.astype(jnp.bfloat16)
    rate = proj_ref[:, proj_cols : proj_cols + 128]
    shifted = rate + rates_ref[0:1, :]
    decay_all = rates_ref[1:2, :] * (
        jnp.maximum(shifted, 0.0) + jnp.log1p(jnp.exp(-jnp.abs(shifted)))
    )
    beta_all = sigmoid(rate)
    for head in range(heads):
        decay = jnp.broadcast_to(decay_all[:, head : head + 1], (ROWS, ROWS))
        beta = beta_all[:, heads + head : heads + head + 1]
        sums = summed_by(
            lower_b, jnp.concatenate([jnp.where(row > col, decay, 0.0), decay], axis=1)
        )
        factor = jnp.exp(sums[:, :ROWS]) * (lower * joined)
        total = sums[:, ROWS:]
        total_end = total[ROWS - 1 : ROWS, :]
        grown = jnp.exp(total) * reached
        tail = jnp.exp(total_end - total) * reaching
        end_decay = jnp.exp(total_end[:, :1]) * passed

        conv_q = conv[:, head * DK : (head + 1) * DK]
        conv_k = conv[:, qk + head * DK : qk + (head + 1) * DK]
        conv_v = conv[:, 2 * qk + head * DV : 2 * qk + (head + 1) * DV]
        query = conv_q * sigmoid(conv_q)
        query = query * (lax.rsqrt(lane_sum(query * query) + EPS) * (1.0 / math.sqrt(DK)))
        key = conv_k * sigmoid(conv_k)
        key = key * lax.rsqrt(lane_sum(key * key) + EPS)
        value = conv_v * sigmoid(conv_v)

        grams = product(jnp.concatenate([key, query], axis=0), key, NT, FINE_GRAM)
        coupling = jnp.where(row > col, factor * grams[:ROWS] * beta, 0.0)
        inverse = unit_lower_inverse(coupling, row, col)
        parts = product(
            inverse,
            jnp.concatenate([beta * value, (beta * grown) * key], axis=1),
            NN,
            FINE_APPLY,
        )
        state = state_buf[head]
        from_state = product(
            jnp.concatenate([parts[:, DV:], grown * query], axis=0), state, NN, FINE_STATE
        )
        written = parts[:, :DV] - from_state[:ROWS]
        mixed = from_state[ROWS:] + product(factor * grams[ROWS:], written, NN, FINE_STATE)
        state_buf[head] = end_decay * state + product(tail * key, written, TN, FINE_STATE)

        gate = proj_ref[:, conv_cols + head * DV : conv_cols + (head + 1) * DV]
        normed = mixed * lax.rsqrt(lane_sum(mixed * mixed) * (1.0 / DV) + EPS)
        gated_ref[:, head * DV : (head + 1) * DV] = (
            normed * gain_ref[...] * (gate * sigmoid(gate))
        ).astype(jnp.bfloat16)
        mixed_ref[:, head * DV : (head + 1) * DV] = mixed
        state_ref[0, head] = state
        inverse_ref[0, head] = inverse
        parts_ref[0, head] = parts
        written_ref[0, head] = written
        factor_ref[0, head] = factor
        grams_ref[0, head] = grams


def backward_kernel(
    heads,
    chunks,
    resets_ref,
    upstream_ref,
    proj_ref,
    keep_ref,
    filter_ref,
    rates_ref,
    gain_ref,
    conv_ref,
    mixed_ref,
    state_ref,
    inverse_ref,
    parts_ref,
    written_ref,
    factor_ref,
    grams_ref,
    dproj_ref,
    dfilter_ref,
    dsmall_ref,
    rows_buf,
    dstate_buf,
):
    step = pl.program_id(0)
    chunk = chunks - 1 - step
    qk = heads * DK
    conv_cols = 2 * qk + heads * DV
    proj_cols = conv_cols + heads * DV

    @pl.when(step == 0)
    def _():
        rows_buf[ROWS : ROWS + 8, :] = jnp.zeros((8, conv_cols), jnp.float32)
        dstate_buf[...] = jnp.zeros_like(dstate_buf)
        dfilter_ref[...] = jnp.zeros_like(dfilter_ref)
        dsmall_ref[...] = jnp.zeros_like(dsmall_ref)

    row, col, reached, reaching, joined, passed = chunk_masks(resets_ref, chunk)
    lower = jnp.where(row >= col, 1.0, 0.0)
    lower_b = lower.astype(jnp.bfloat16)
    upper_b = jnp.where(row <= col, 1.0, 0.0).astype(jnp.bfloat16)
    rate = proj_ref[:, proj_cols : proj_cols + 128]
    shifted = rate + rates_ref[0:1, :]
    decay_all = rates_ref[1:2, :] * (
        jnp.maximum(shifted, 0.0) + jnp.log1p(jnp.exp(-jnp.abs(shifted)))
    )
    slope_all = rates_ref[1:2, :] * sigmoid(shifted)
    beta_all = sigmoid(rate)
    drate = jnp.zeros((ROWS, 128), jnp.float32)
    dsums = jnp.zeros((ROWS, 128), jnp.float32)
    lane = lax.broadcasted_iota(jnp.int32, (ROWS, 128), 1)
    dgain = jnp.zeros((1, DV), jnp.float32)
    for head in range(heads):
        decay = jnp.broadcast_to(decay_all[:, head : head + 1], (ROWS, ROWS))
        beta = beta_all[:, heads + head : heads + head + 1]
        total = summed_by(lower_b, decay)
        total_end = total[ROWS - 1 : ROWS, :]
        grown = jnp.exp(total) * reached
        tail = jnp.exp(total_end - total) * reaching
        end_decay = jnp.exp(total_end[:, :1]) * passed

        v_at = slice(head * DV, (head + 1) * DV)
        gate_at = slice(conv_cols + head * DV, conv_cols + (head + 1) * DV)
        q_at = slice(head * DK, (head + 1) * DK)
        k_at = slice(qk + head * DK, qk + (head + 1) * DK)
        value_at = slice(2 * qk + head * DV, 2 * qk + (head + 1) * DV)
        conv_q = conv_ref[:, q_at]
        conv_k = conv_ref[:, k_at]
        conv_v = conv_ref[:, value_at]
        sig_q = sigmoid(conv_q)
        sig_k = sigmoid(conv_k)
        sig_v = sigmoid(conv_v)
        query = conv_q * sig_q
        inv_q = lax.rsqrt(lane_sum(query * query) + EPS)
        query = query * (inv_q * (1.0 / math.sqrt(DK)))
        key = conv_k * sig_k
        inv_k = lax.rsqrt(lane_sum(key * key) + EPS)
        key = key * inv_k
        value = conv_v * sig_v

        mixed = mixed_ref[:, v_at]
        inv_o = lax.rsqrt(lane_sum(mixed * mixed) * (1.0 / DV) + EPS)
        normed = mixed * inv_o
        gate = proj_ref[:, gate_at]
        sig_g = sigmoid(gate)
        upstream = upstream_ref[:, v_at]
        up_normed = upstream * normed
        dgain = dgain + jnp.sum(up_normed * (gate * sig_g), 0, keepdims=True)
        dproj_ref[:, gate_at] = (
            up_normed * gain_ref[...] * (sig_g * (1.0 + gate * (1.0 - sig_g)))
        ).astype(jnp.bfloat16)
        dnormed = upstream * gain_ref[...] * (gate * sig_g)
        dmixed = inv_o * (dnormed - normed * (lane_sum(dnormed * normed) * (1.0 / DV)))

        state = state_ref[0, head]
        dstate = dstate_buf[head]
        inverse = inverse_ref[0, head]
        parts = parts_ref[0, head]
        written = written_ref[0, head]
        factor = factor_ref[0, head]
        key_gram = grams_ref[0, head, :ROWS]
        query_key = grams_ref[0, head, ROWS:]
        mixing = factor * query_key
        query_grown = grown * query
        key_tail = tail * key

        dwritten = product(mixing, dmixed, TN, FINE_BACK) + product(
            key_tail, dstate, NN, FINE_BACK
        )
        stacked = jnp.concatenate([dmixed, -dwritten], axis=0)
        through = product(stacked, state, NT, FINE_BACK)
        dquery_grown = through[:ROWS]
        dprojected_key = through[ROWS:]
        dmixing = product(dmixed, written, NT, FINE_BACK)
        dkey_tail = product(written, dstate, NT, FINE_BACK)
        end_grad = end_decay * lane_sum(jnp.sum(state * dstate, 0, keepdims=True))
        dstate_buf[head] = end_decay * dstate + product(
            jnp.concatenate([query_grown, parts[:, DV:]], axis=0), stacked, TN, FINE_BACK
        )
        solved = product(
            inverse, jnp.concatenate([dwritten, dprojected_key], axis=1), TN, FINE_BACK
        )
        dcoupling = product(solved, parts, NT, FINE_BACK)
        dcoupling = jnp.where(row > col, -dcoupling * factor, 0.0)
        dcoupling_gram = dcoupling * key_gram
        dbeta = lane_sum(dcoupling_gram)
        dgap = beta * dcoupling_gram + dmixing * mixing
        dgrams = jnp.concatenate([beta * dcoupling, dmixing * factor], axis=0)
        by_key = product(dgrams, key, NN, FINE_BACK)
        dkey = by_key[:ROWS] + product(
            dgrams, jnp.concatenate([key, query], axis=0), TN, FINE_BACK
        )
        dquery = by_key[ROWS:] + grown * dquery_grown
        dvalue_scaled = solved[:, :DV]
        dkey_scaled = solved[:, DV:]
        scaled_rows = lane_sum(dkey_scaled * (grown * key))
        dbeta = dbeta + lane_sum(dvalue_scaled * value) + scaled_rows
        tail_rows = lane_sum(dkey_tail * key_tail)
        dkey = dkey + tail * dkey_tail + (beta * grown) * dkey_scaled
        dtotal = lane_sum(dquery_grown * query_grown) + beta * scaled_rows - tail_rows
        sums = summed_by(
            upper_b, jnp.concatenate([dgap, jnp.broadcast_to(dtotal, (ROWS, ROWS))], axis=1)
        )
        ddecay = (
            lane_sum(jnp.where(col < row, sums[:, :ROWS], 0.0))
            + sums[:, ROWS : ROWS + 1]
            + (end_grad + jnp.sum(tail_rows, 0, keepdims=True))
        )
        dshifted = ddecay * slope_all[:, head : head + 1]
        drate = drate + jnp.where(lane == head, dshifted, 0.0)
        drate = drate + jnp.where(lane == heads + head, dbeta * (beta * (1.0 - beta)), 0.0)
        dsums = dsums + jnp.where(lane == head, ddecay * decay, 0.0)
        dsums = dsums + jnp.where(lane == heads + head, dshifted, 0.0)

        unit = query * math.sqrt(DK)
        dunit = dquery * (1.0 / math.sqrt(DK))
        dsilu = inv_q * (dunit - unit * lane_sum(dunit * unit))
        rows_buf[0:ROWS, q_at] = dsilu * (sig_q * (1.0 + conv_q * (1.0 - sig_q)))
        dsilu = inv_k * (dkey - key * lane_sum(dkey * key))
        rows_buf[0:ROWS, k_at] = dsilu * (sig_k * (1.0 + conv_k * (1.0 - sig_k)))
        rows_buf[0:ROWS, value_at] = (beta * dvalue_scaled) * (
            sig_v * (1.0 + conv_v * (1.0 - sig_v))
        )

    signal = proj_ref[:, :conv_cols]
    shifted_grad = rows_buf[0:ROWS, :]
    dsignal = shifted_grad * filter_ref[0:1, :]
    dfilter_ref[0:1, :] += jnp.sum(signal * shifted_grad, 0, keepdims=True)
    for offset in range(1, KW):
        shifted_grad = (
            rows_buf[offset : offset + ROWS, :] * keep_ref[:, KW + offset : KW + offset + 1]
        )
        dsignal = dsignal + shifted_grad * filter_ref[offset : offset + 1, :]
        dfilter_ref[offset : offset + 1, :] += jnp.sum(signal * shifted_grad, 0, keepdims=True)
    rows_buf[ROWS : ROWS + 8, :] = rows_buf[0:8, :]
    dproj_ref[:, :conv_cols] = dsignal.astype(jnp.bfloat16)
    dproj_ref[:, proj_cols : proj_cols + 128] = drate.astype(jnp.bfloat16)
    dsmall_ref[0:1, :] += dgain
    dsmall_ref[1:2, 0:128] += jnp.sum(dsums, 0, keepdims=True)


def mixer_forward(resets, proj, keep, filters, rates, head_gain, heads):
    row_count, proj_width = proj.shape
    chunks = row_count // ROWS
    conv_cols = 2 * heads * DK + heads * DV
    f32 = jnp.float32

    def rows_of(cols, dtype=f32):
        return jax.ShapeDtypeStruct((row_count, cols), dtype)

    def saved(rows, cols):
        return jax.ShapeDtypeStruct((chunks, heads, rows, cols), f32)

    def row_block(cols):
        return pl.BlockSpec((ROWS, cols), lambda c, r: (c, 0))

    def saved_block(rows, cols):
        return pl.BlockSpec((1, heads, rows, cols), lambda c, r: (c, 0, 0, 0))

    def whole(array):
        return pl.BlockSpec(array.shape, lambda c, r: (0, 0))

    return pl.pallas_call(
        partial(forward_kernel, heads),
        grid_spec=pltpu.PrefetchScalarGridSpec(
            num_scalar_prefetch=1,
            grid=(chunks,),
            in_specs=[
                row_block(proj_width),
                row_block(keep.shape[1]),
                whole(filters),
                whole(rates),
                whole(head_gain),
            ],
            out_specs=[
                row_block(heads * DV),
                row_block(conv_cols),
                row_block(heads * DV),
                saved_block(DK, DV),
                saved_block(ROWS, ROWS),
                saved_block(ROWS, DV + DK),
                saved_block(ROWS, DV),
                saved_block(ROWS, ROWS),
                saved_block(2 * ROWS, ROWS),
            ],
            scratch_shapes=[
                pltpu.VMEM((ROWS + 8, conv_cols), f32),
                pltpu.VMEM((heads, DK, DV), f32),
            ],
        ),
        out_shape=[
            rows_of(heads * DV, jnp.bfloat16),
            rows_of(conv_cols),
            rows_of(heads * DV),
            saved(DK, DV),
            saved(ROWS, ROWS),
            saved(ROWS, DV + DK),
            saved(ROWS, DV),
            saved(ROWS, ROWS),
            saved(2 * ROWS, ROWS),
        ],
        compiler_params=pltpu.CompilerParams(vmem_limit_bytes=40 << 20),
        name="mixer_forward",
    )(resets, proj, keep, filters, rates, head_gain)


def mixer_backward(resets, upstream, proj, keep, filters, rates, head_gain, saved, heads):
    row_count, proj_width = proj.shape
    chunks = row_count // ROWS
    conv_cols = 2 * heads * DK + heads * DV
    f32 = jnp.float32

    def row_block(array):
        return pl.BlockSpec((ROWS, array.shape[1]), lambda c, r: (chunks - 1 - c, 0))

    def saved_block(array):
        return pl.BlockSpec((1,) + array.shape[1:], lambda c, r: (chunks - 1 - c, 0, 0, 0))

    def whole(array):
        return pl.BlockSpec(array.shape, lambda c, r: (0, 0))

    dproj = jax.ShapeDtypeStruct((row_count, proj_width), jnp.bfloat16)
    dfilter = jax.ShapeDtypeStruct((8, conv_cols), f32)
    dsmall = jax.ShapeDtypeStruct((8, DV), f32)
    return pl.pallas_call(
        partial(backward_kernel, heads, chunks),
        grid_spec=pltpu.PrefetchScalarGridSpec(
            num_scalar_prefetch=1,
            grid=(chunks,),
            in_specs=[row_block(upstream), row_block(proj), row_block(keep)]
            + [whole(filters), whole(rates), whole(head_gain)]
            + [row_block(saved[0]), row_block(saved[1])]
            + [saved_block(array) for array in saved[2:]],
            out_specs=[row_block(dproj), whole(dfilter), whole(dsmall)],
            scratch_shapes=[
                pltpu.VMEM((ROWS + 8, conv_cols), f32),
                pltpu.VMEM((heads, DK, DV), f32),
            ],
        ),
        out_shape=[dproj, dfilter, dsmall],
        compiler_params=pltpu.CompilerParams(vmem_limit_bytes=40 << 20),
        name="mixer_backward",
    )(resets, upstream, proj, keep, filters, rates, head_gain, *saved)


def swap_halves(array):
    return lax.ppermute(array, "mp", [(0, 1), (1, 0)])


def dp_total(array):
    count = lax.axis_size("dp")
    step = 1
    while step < count:
        array = array + lax.ppermute(array, "dp", [(i, i ^ step) for i in range(count)])
        step *= 2
    return array


def in_order(own, other, model_index, axis):
    first = jnp.where(model_index == 0, own, other)
    second = jnp.where(model_index == 0, other, own)
    return jnp.concatenate([first, second], axis=axis)


def on_device(
    block_input,
    seq_lengths,
    seq_owner,
    mix_gain,
    query_weight,
    key_weight,
    value_weight,
    gate_weight,
    decay_weight,
    beta_weight,
    query_filter,
    key_filter,
    value_filter,
    decay_log,
    decay_bias,
    head_gain,
    out_weight,
    ffn_gain,
    ffn_gate,
    ffn_up,
    ffn_down,
    cotangent,
):
    bf16 = jnp.bfloat16
    f32 = jnp.float32
    local_rows, width = block_input.shape
    dp_index = lax.axis_index("dp")
    model_count = lax.axis_size("mp")
    model_index = lax.axis_index("mp")
    row_count = local_rows * model_count
    keep_masks, resets, valid_rows = layout(seq_lengths, seq_owner, dp_index, row_count)
    valid_all = valid_rows[:, None]
    heads_local = decay_log.shape[0] // model_count
    qk_cols = heads_local * DK
    v_cols = heads_local * DV
    ff_cols = ffn_gate.shape[1]
    shard_rows = query_weight.shape[0]
    proj_cols = 2 * qk_cols + 2 * v_cols

    def own_columns(array, col_count):
        return lax.dynamic_slice_in_dim(array, model_index * col_count, col_count, array.ndim - 1)

    def own_shard(array):
        return lax.dynamic_slice_in_dim(array, dp_index * shard_rows, shard_rows, 0)

    small_weight = jnp.concatenate(
        [own_columns(decay_weight, heads_local), own_columns(beta_weight, heads_local)], axis=1
    )
    small_weight = jnp.pad(small_weight, ((0, 0), (0, 128 - 2 * heads_local)))
    shard_mix = jnp.concatenate(
        [query_weight, key_weight, value_weight, gate_weight, own_shard(small_weight)], axis=1
    )
    mix_weight = lax.all_gather(shard_mix, "dp", axis=0, tiled=True)
    input_other = swap_halves(block_input)
    out_rows = out_weight.T
    out_other = swap_halves(out_rows)
    shard_rest = jnp.concatenate([out_rows, out_other, ffn_gate, ffn_up, ffn_down.T], axis=1)
    rest_weight = lax.all_gather(shard_rest, "dp", axis=0, tiled=True)
    out_both = rest_weight[:, : 2 * v_cols]
    ffn_in_weight = rest_weight[:, 2 * v_cols : 2 * v_cols + 2 * ff_cols]
    down_weight = rest_weight[:, 2 * v_cols + 2 * ff_cols :]
    cot_other = swap_halves(cotangent)

    filters = jnp.concatenate(
        [
            own_columns(query_filter, qk_cols),
            own_columns(key_filter, qk_cols),
            own_columns(value_filter, v_cols),
        ],
        axis=1,
    )
    filters = jnp.pad(filters, ((0, 8 - KW), (0, 0)))
    rates = jnp.stack(
        [own_columns(decay_bias, heads_local), -jnp.exp(own_columns(decay_log, heads_local))]
    )
    rates = jnp.pad(rates, ((0, 6), (0, 128 - heads_local)))
    gain_row = head_gain[None]
    restarts = resets.astype(jnp.int32)
    later_masks = [
        jnp.concatenate([keep_masks[offset, offset:], jnp.ones((offset,), f32)])
        for offset in range(KW)
    ]
    keep_cols = jnp.stack([keep_masks[offset] for offset in range(KW)] + later_masks, axis=1)
    inputs_f = in_order(block_input, input_other, model_index, 0).astype(f32)
    cot_all = in_order(cotangent, cot_other, model_index, 0)
    normed1, inv_rms1 = rms_forward(inputs_f)
    mixed_in = (normed1 * mix_gain).astype(bf16)
    proj = jnp.dot(mixed_in, mix_weight, preferred_element_type=f32)
    cuts = (qk_cols, 2 * qk_cols, 2 * qk_cols + v_cols, proj_cols)
    gated_b, *saved = mixer_forward(
        restarts, proj, keep_cols, filters, rates, gain_row, heads_local
    )
    gated_both = jnp.concatenate([gated_b, swap_halves(gated_b)], axis=1)
    resid = inputs_f + valid_all * against(gated_both, out_both)
    normed2, inv_rms2 = rms_forward(resid)
    ffn_in = (normed2 * ffn_gain).astype(bf16)
    pre = jnp.dot(ffn_in, ffn_in_weight, preferred_element_type=f32)
    gate_pre, up_pre = pre[:, :ff_cols], pre[:, ff_cols:]
    sigmoid_gate = jax.nn.sigmoid(gate_pre)
    activated = gate_pre * sigmoid_gate
    hidden = (activated * up_pre).astype(bf16)
    cot_masked = cot_all * valid_all.astype(bf16)
    hidden_grad = jnp.dot(cot_masked, down_weight, preferred_element_type=f32)
    gate_grad_pre = (
        hidden_grad * up_pre * sigmoid_gate * (1.0 + gate_pre * (1.0 - sigmoid_gate))
    ).astype(bf16)
    up_grad_pre = (hidden_grad * activated).astype(bf16)
    pre_grad = jnp.concatenate([gate_grad_pre, up_grad_pre], axis=1)
    ffn_in_part = against(pre_grad, ffn_in_weight)
    ffn_in_sent = ffn_in_part.astype(bf16)
    ffn_in_grad = ffn_in_sent.astype(f32) + swap_halves(ffn_in_sent).astype(f32)

    def own_half(array):
        return lax.dynamic_slice_in_dim(array, model_index * local_rows, local_rows, 0)

    def other_half(array):
        return lax.dynamic_slice_in_dim(array, (1 - model_index) * local_rows, local_rows, 0)

    ffn_part = against(hidden, down_weight)
    ffn_sum = own_half(ffn_part) + swap_halves(other_half(ffn_part).astype(bf16)).astype(f32)
    block_output = (own_half(resid) + own_half(valid_all) * ffn_sum).astype(bf16)
    rest_grads = jnp.concatenate(
        [across_rows(ffn_in, pre_grad).astype(bf16), across_rows(cot_masked, hidden).astype(bf16)],
        axis=1,
    )
    ffn_shard = lax.psum_scatter(rest_grads, "dp", scatter_dimension=0, tiled=True)
    ffn_gain_part = jnp.sum(ffn_in_part * normed2, 0)
    resid_grad = cot_all.astype(f32) + rms_backward(ffn_in_grad * ffn_gain, normed2, inv_rms2)
    mix_cot = (resid_grad * valid_all).astype(bf16)
    gated_grad = jnp.dot(mix_cot, out_both[:, :v_cols], preferred_element_type=f32)
    proj_grad, filter_grads, small_grads = mixer_backward(
        restarts, gated_grad, proj, keep_cols, filters, rates, gain_row, saved, heads_local
    )
    mix_grads = jnp.concatenate(
        [
            across_rows(mixed_in, proj_grad[:, :proj_cols]).astype(bf16),
            across_rows(mix_cot, gated_b).astype(bf16),
        ],
        axis=1,
    )
    mix_shard = lax.psum_scatter(mix_grads, "dp", scatter_dimension=0, tiled=True)
    rate_grads = across_rows(proj_grad[:, proj_cols:], mixed_in)[: 2 * heads_local]
    mix_in_part = against(proj_grad, mix_weight)
    mix_in_sum = own_half(mix_in_part) + swap_halves(
        other_half(mix_in_part).astype(bf16)
    ).astype(f32)
    mix_gain_part = jnp.sum(mix_in_part * normed1, 0)
    input_grad = own_half(resid_grad) + rms_backward(
        mix_in_sum * mix_gain, own_half(normed1), own_half(inv_rms1)
    )
    common = jnp.concatenate(
        [mix_gain_part, ffn_gain_part, small_grads[0], jnp.zeros((width - DV,), f32)]
    ).reshape(3, width)
    tail_row = jnp.concatenate(
        [small_grads[1, : 2 * heads_local], jnp.zeros((width - 2 * heads_local,), f32)]
    )
    split_rows = jnp.concatenate(
        [
            rate_grads,
            filter_grads[:KW, : cuts[0]].reshape(-1, width),
            filter_grads[:KW, cuts[0] : cuts[1]].reshape(-1, width),
            filter_grads[:KW, cuts[1] : cuts[2]].reshape(-1, width),
            tail_row[None],
        ],
        axis=0,
    )
    totals = dp_total(jnp.concatenate([common, split_rows], axis=0))
    totals_other = swap_halves(totals)
    common = totals[:3] + totals_other[:3]
    lower = jnp.where(model_index == 0, totals, totals_other)[3:]
    upper = jnp.where(model_index == 0, totals_other, totals)[3:]

    def joined(start, rows, cols):
        return jnp.concatenate(
            [
                lower[start : start + rows].reshape(-1, cols),
                upper[start : start + rows].reshape(-1, cols),
            ],
            axis=1,
        )

    q_rows = KW * qk_cols // width
    v_rows = KW * v_cols // width
    at_q = 2 * heads_local
    at_k = at_q + q_rows
    at_v = at_k + q_rows
    at_tail = at_v + v_rows

    def rate_weight_grad(start):
        return jnp.concatenate(
            [lower[start : start + heads_local], upper[start : start + heads_local]], axis=0
        ).T

    def rate_grad(start):
        return jnp.concatenate(
            [
                lower[at_tail, start : start + heads_local],
                upper[at_tail, start : start + heads_local],
            ]
        )

    mix_shard = mix_shard.astype(f32)
    ffn_shard = ffn_shard.astype(f32)
    return (
        block_output,
        input_grad,
        common[0],
        mix_shard[:, : cuts[0]],
        mix_shard[:, cuts[0] : cuts[1]],
        mix_shard[:, cuts[1] : cuts[2]],
        mix_shard[:, cuts[2] : cuts[3]],
        rate_weight_grad(0),
        rate_weight_grad(heads_local),
        joined(at_q, q_rows, qk_cols),
        joined(at_k, q_rows, qk_cols),
        joined(at_v, v_rows, v_cols),
        rate_grad(0),
        rate_grad(heads_local),
        common[2, :DV],
        mix_shard[:, proj_cols:].T,
        common[1],
        ffn_shard[:, :ff_cols],
        ffn_shard[:, ff_cols : 2 * ff_cols],
        ffn_shard[:, 2 * ff_cols :].T,
    )


def solution(mesh):
    in_specs = (
        P(("dp", "mp"), None),
        P(),
        P(),
        P(),
        P("dp", "mp"),
        P("dp", "mp"),
        P("dp", "mp"),
        P("dp", "mp"),
        P(),
        P(),
        P(),
        P(),
        P(),
        P(),
        P(),
        P(),
        P("mp", "dp"),
        P(),
        P("dp", "mp"),
        P("dp", "mp"),
        P("mp", "dp"),
        P(("dp", "mp"), None),
    )
    out_specs = (
        P(("dp", "mp"), None),
        P(("dp", "mp"), None),
        P(),
        P("dp", "mp"),
        P("dp", "mp"),
        P("dp", "mp"),
        P("dp", "mp"),
        P(),
        P(),
        P(),
        P(),
        P(),
        P(),
        P(),
        P(),
        P("mp", "dp"),
        P(),
        P("dp", "mp"),
        P("dp", "mp"),
        P("mp", "dp"),
    )
    return jax.shard_map(
        on_device, mesh=mesh, in_specs=in_specs, out_specs=out_specs, check_vma=False
    )
```

```python
from functools import partial
import math

import jax
import jax.numpy as jnp
from jax import lax
from jax.experimental import pallas as pl
from jax.experimental.pallas import tpu as pltpu
from jax.sharding import PartitionSpec as P

DK = 128
DV = 256
KW = 4
SPAN = 64


EPS = 1e-06


def layout(seq_lengths, seq_owner, device, row_count):
    owned = seq_owner == device
    own_lengths = jnp.where(owned, seq_lengths, 0)
    offsets = jnp.cumsum(own_lengths) - own_lengths
    loaded = jnp.sum(own_lengths)
    span_starts = jnp.arange(row_count // SPAN, dtype=jnp.int32) * SPAN
    begins = jnp.any(
        (offsets[None, :] == span_starts[:, None]) & (own_lengths[None, :] > 0), axis=1
    )
    resets = begins | (span_starts == loaded)
    within = jnp.arange(SPAN, dtype=jnp.int32)
    keep_masks = jnp.stack(
        [
            jnp.logical_not(resets[:, None] & (within[None, :] < offset)).reshape(row_count)
            for offset in range(KW)
        ]
    ).astype(jnp.float32)
    valid_rows = (jnp.arange(row_count, dtype=jnp.int32) < loaded).astype(jnp.float32)
    return (keep_masks, resets, valid_rows)


def across_rows(left, right):
    return lax.dot_general(
        left, right, (((0,), (0,)), ((), ())), preferred_element_type=jnp.float32
    )


def against(left, right):
    return lax.dot_general(
        left, right, (((1,), (1,)), ((), ())), preferred_element_type=jnp.float32
    )


def rms_forward(values):
    inv_rms = lax.rsqrt(jnp.mean(values * values, -1, keepdims=True) + EPS)
    return (values * inv_rms, inv_rms)


def rms_backward(upstream, normed, inv_rms):
    return inv_rms * (upstream - normed * jnp.mean(upstream * normed, -1, keepdims=True))


ROWS = 128
NN = ((1,), (0,))
NT = ((1,), (1,))
TN = ((0,), (0,))
FINE_GRAM = False
FINE_INVERSE = True
FINE_MERGE = True
SUBS = 2
FINE_APPLY = False
FINE_STATE = False
FINE_BACK = False


def dot(left, right, dims):
    return lax.dot_general(left, right, (dims, ((), ())), preferred_element_type=jnp.float32)


def high_low(values):
    high = values.astype(jnp.bfloat16)
    return high, (values - high.astype(jnp.float32)).astype(jnp.bfloat16)


def product(left, right, dims, fine=False):
    if not fine:
        return dot(left.astype(jnp.bfloat16), right.astype(jnp.bfloat16), dims)
    left_high, left_low = high_low(left)
    right_high, right_low = high_low(right)
    return dot(left_high, right_high, dims) + (
        dot(left_high, right_low, dims) + dot(left_low, right_high, dims)
    )


def summed_by(mask, values, dims=NN):
    high, low = high_low(values)
    return dot(mask, high, dims) + dot(mask, low, dims)


def chunk_masks(resets_ref, chunk):
    first = 1.0 - resets_ref[2 * chunk].astype(jnp.float32)
    second = 1.0 - resets_ref[2 * chunk + 1].astype(jnp.float32)
    row = lax.broadcasted_iota(jnp.int32, (ROWS, ROWS), 0)
    col = lax.broadcasted_iota(jnp.int32, (ROWS, ROWS), 1)
    late = row >= SPAN
    reached = jnp.where(late, first * second, first)
    reaching = jnp.where(late, 1.0, second)
    joined = jnp.where(late & (col < SPAN), second, 1.0)
    return row, col, reached, reaching, joined, first * second


def unit_lower_inverses(couplings, row, col):
    eye = jnp.where(row == col, 1.0, 0.0)
    base = 16
    near = (row // base) == (col // base)
    powered = [jnp.where(near, coupling, 0.0) for coupling in couplings]
    inverses = [eye - power for power in powered]
    size = 2
    while size < base:
        powered = [product(power, power, NN, FINE_INVERSE) for power in powered]
        inverses = [
            inverse + product(inverse, power, NN, FINE_INVERSE)
            for inverse, power in zip(inverses, powered)
        ]
        size *= 2
    while base < ROWS:
        wide = 2 * base
        linked = ((row // wide) == (col // wide)) & ((row // base) != (col // base))
        steps = [
            product(jnp.where(linked, coupling, 0.0), inverse, NN, FINE_MERGE)
            for coupling, inverse in zip(couplings, inverses)
        ]
        inverses = [
            inverse - product(inverse, step, NN, FINE_MERGE)
            for inverse, step in zip(inverses, steps)
        ]
        base = wide
    return inverses


def sigmoid(values):
    return 1.0 / (1.0 + jnp.exp(-values))


def lane_sum(values):
    return jnp.sum(values, -1, keepdims=True)


def forward_kernel(
    heads,
    resets_ref,
    proj_ref,
    keep_ref,
    filter_ref,
    rates_ref,
    gain_ref,
    gated_ref,
    conv_ref,
    mixed_ref,
    state_ref,
    inverse_ref,
    parts_ref,
    written_ref,
    factor_ref,
    grams_ref,
    rows_buf,
    state_buf,
):
    step = pl.program_id(0)
    qk = heads * DK
    conv_cols = 2 * qk + heads * DV
    proj_cols = conv_cols + heads * DV
    rows = SUBS * ROWS

    @pl.when(step == 0)
    def _():
        rows_buf[0:8, :] = jnp.zeros((8, conv_cols), jnp.float32)
        state_buf[...] = jnp.zeros_like(state_buf)

    rows_buf[8 : 8 + rows, :] = proj_ref[:, :conv_cols]
    conv = rows_buf[8 : 8 + rows, :] * filter_ref[0:1, :]
    for offset in range(1, KW):
        conv = conv + rows_buf[8 - offset : 8 - offset + rows, :] * (
            filter_ref[offset : offset + 1, :] * keep_ref[:, offset : offset + 1]
        )
    rows_buf[0:8, :] = rows_buf[rows : rows + 8, :]
    conv_ref[...] = conv

    rate = proj_ref[:, proj_cols : proj_cols + 128]
    shifted = rate + rates_ref[0:1, :]
    decay_all = rates_ref[1:2, :] * (
        jnp.maximum(shifted, 0.0) + jnp.log1p(jnp.exp(-jnp.abs(shifted)))
    )
    beta_all = sigmoid(rate)
    units = [(sub, head) for sub in range(SUBS) for head in range(heads)]
    prepared = []
    for sub, head in units:
        row, col, reached, reaching, joined, passed = chunk_masks(resets_ref, step * SUBS + sub)
        lower = jnp.where(row >= col, 1.0, 0.0)
        at = slice(sub * ROWS, (sub + 1) * ROWS)
        decay = jnp.broadcast_to(decay_all[at, head : head + 1], (ROWS, ROWS))
        beta = beta_all[at, heads + head : heads + head + 1]
        sums = summed_by(
            lower.astype(jnp.bfloat16),
            jnp.concatenate([jnp.where(row > col, decay, 0.0), decay], axis=1),
        )
        factor = jnp.exp(sums[:, :ROWS]) * (lower * joined)
        total = sums[:, ROWS:]
        total_end = total[ROWS - 1 : ROWS, :]
        grown = jnp.exp(total) * reached
        tail = jnp.exp(total_end - total) * reaching
        end_decay = jnp.exp(total_end[:, :1]) * passed

        conv_q = conv[at, head * DK : (head + 1) * DK]
        conv_k = conv[at, qk + head * DK : qk + (head + 1) * DK]
        conv_v = conv[at, 2 * qk + head * DV : 2 * qk + (head + 1) * DV]
        query = conv_q * sigmoid(conv_q)
        query = query * (lax.rsqrt(lane_sum(query * query) + EPS) * (1.0 / math.sqrt(DK)))
        key = conv_k * sigmoid(conv_k)
        key = key * lax.rsqrt(lane_sum(key * key) + EPS)
        value = conv_v * sigmoid(conv_v)

        grams = product(jnp.concatenate([key, query], axis=0), key, NT, FINE_GRAM)
        coupling = jnp.where(row > col, factor * grams[:ROWS] * beta, 0.0)
        scaled = jnp.concatenate([beta * value, (beta * grown) * key], axis=1)
        factor_ref[sub, head] = factor
        grams_ref[sub, head] = grams
        prepared.append(
            (coupling, scaled, grown * query, factor * grams[ROWS:], tail * key, end_decay)
        )
    row = lax.broadcasted_iota(jnp.int32, (ROWS, ROWS), 0)
    col = lax.broadcasted_iota(jnp.int32, (ROWS, ROWS), 1)
    inverses = unit_lower_inverses([entry[0] for entry in prepared], row, col)
    for (sub, head), inverse, entry in zip(units, inverses, prepared):
        _, scaled, query_grown, mixing, key_tail, end_decay = entry
        at = slice(sub * ROWS, (sub + 1) * ROWS)
        parts = product(inverse, scaled, NN, FINE_APPLY)
        state = state_buf[head]
        from_state = product(
            jnp.concatenate([parts[:, DV:], query_grown], axis=0), state, NN, FINE_STATE
        )
        written = parts[:, :DV] - from_state[:ROWS]
        mixed = from_state[ROWS:] + product(mixing, written, NN, FINE_STATE)
        state_buf[head] = end_decay * state + product(key_tail, written, TN, FINE_STATE)

        gate = proj_ref[at, conv_cols + head * DV : conv_cols + (head + 1) * DV]
        normed = mixed * lax.rsqrt(lane_sum(mixed * mixed) * (1.0 / DV) + EPS)
        gated_ref[at, head * DV : (head + 1) * DV] = (
            normed * gain_ref[...] * (gate * sigmoid(gate))
        ).astype(jnp.bfloat16)
        mixed_ref[at, head * DV : (head + 1) * DV] = mixed
        state_ref[sub, head] = state
        inverse_ref[sub, head] = inverse
        parts_ref[sub, head] = parts
        written_ref[sub, head] = written


def backward_kernel(
    heads,
    chunks,
    resets_ref,
    upstream_ref,
    proj_ref,
    keep_ref,
    filter_ref,
    rates_ref,
    gain_ref,
    conv_ref,
    mixed_ref,
    state_ref,
    inverse_ref,
    parts_ref,
    written_ref,
    factor_ref,
    grams_ref,
    dproj_ref,
    dfilter_ref,
    dsmall_ref,
    rows_buf,
    dstate_buf,
):
    step = pl.program_id(0)
    chunk = chunks - 1 - step
    qk = heads * DK
    conv_cols = 2 * qk + heads * DV
    proj_cols = conv_cols + heads * DV

    @pl.when(step == 0)
    def _():
        rows_buf[ROWS : ROWS + 8, :] = jnp.zeros((8, conv_cols), jnp.float32)
        dstate_buf[...] = jnp.zeros_like(dstate_buf)
        dfilter_ref[...] = jnp.zeros_like(dfilter_ref)
        dsmall_ref[...] = jnp.zeros_like(dsmall_ref)

    row, col, reached, reaching, joined, passed = chunk_masks(resets_ref, chunk)
    lower = jnp.where(row >= col, 1.0, 0.0)
    lower_b = lower.astype(jnp.bfloat16)
    upper_b = jnp.where(row <= col, 1.0, 0.0).astype(jnp.bfloat16)
    rate = proj_ref[:, proj_cols : proj_cols + 128]
    shifted = rate + rates_ref[0:1, :]
    decay_all = rates_ref[1:2, :] * (
        jnp.maximum(shifted, 0.0) + jnp.log1p(jnp.exp(-jnp.abs(shifted)))
    )
    slope_all = rates_ref[1:2, :] * sigmoid(shifted)
    beta_all = sigmoid(rate)
    drate = jnp.zeros((ROWS, 128), jnp.float32)
    dsums = jnp.zeros((ROWS, 128), jnp.float32)
    lane = lax.broadcasted_iota(jnp.int32, (ROWS, 128), 1)
    dgain = jnp.zeros((1, DV), jnp.float32)
    for head in range(heads):
        decay = jnp.broadcast_to(decay_all[:, head : head + 1], (ROWS, ROWS))
        beta = beta_all[:, heads + head : heads + head + 1]
        total = summed_by(lower_b, decay)
        total_end = total[ROWS - 1 : ROWS, :]
        grown = jnp.exp(total) * reached
        tail = jnp.exp(total_end - total) * reaching
        end_decay = jnp.exp(total_end[:, :1]) * passed

        v_at = slice(head * DV, (head + 1) * DV)
        gate_at = slice(conv_cols + head * DV, conv_cols + (head + 1) * DV)
        q_at = slice(head * DK, (head + 1) * DK)
        k_at = slice(qk + head * DK, qk + (head + 1) * DK)
        value_at = slice(2 * qk + head * DV, 2 * qk + (head + 1) * DV)
        conv_q = conv_ref[:, q_at]
        conv_k = conv_ref[:, k_at]
        conv_v = conv_ref[:, value_at]
        sig_q = sigmoid(conv_q)
        sig_k = sigmoid(conv_k)
        sig_v = sigmoid(conv_v)
        query = conv_q * sig_q
        inv_q = lax.rsqrt(lane_sum(query * query) + EPS)
        query = query * (inv_q * (1.0 / math.sqrt(DK)))
        key = conv_k * sig_k
        inv_k = lax.rsqrt(lane_sum(key * key) + EPS)
        key = key * inv_k
        value = conv_v * sig_v

        mixed = mixed_ref[:, v_at]
        inv_o = lax.rsqrt(lane_sum(mixed * mixed) * (1.0 / DV) + EPS)
        normed = mixed * inv_o
        gate = proj_ref[:, gate_at]
        sig_g = sigmoid(gate)
        upstream = upstream_ref[:, v_at]
        up_normed = upstream * normed
        dgain = dgain + jnp.sum(up_normed * (gate * sig_g), 0, keepdims=True)
        dproj_ref[:, gate_at] = (
            up_normed * gain_ref[...] * (sig_g * (1.0 + gate * (1.0 - sig_g)))
        ).astype(jnp.bfloat16)
        dnormed = upstream * gain_ref[...] * (gate * sig_g)
        dmixed = inv_o * (dnormed - normed * (lane_sum(dnormed * normed) * (1.0 / DV)))

        state = state_ref[0, head]
        dstate = dstate_buf[head]
        inverse = inverse_ref[0, head]
        parts = parts_ref[0, head]
        written = written_ref[0, head]
        factor = factor_ref[0, head]
        key_gram = grams_ref[0, head, :ROWS]
        query_key = grams_ref[0, head, ROWS:]
        mixing = factor * query_key
        query_grown = grown * query
        key_tail = tail * key

        dwritten = product(mixing, dmixed, TN, FINE_BACK) + product(
            key_tail, dstate, NN, FINE_BACK
        )
        stacked = jnp.concatenate([dmixed, -dwritten], axis=0)
        through = product(stacked, state, NT, FINE_BACK)
        dquery_grown = through[:ROWS]
        dprojected_key = through[ROWS:]
        dmixing = product(dmixed, written, NT, FINE_BACK)
        dkey_tail = product(written, dstate, NT, FINE_BACK)
        end_grad = end_decay * lane_sum(jnp.sum(state * dstate, 0, keepdims=True))
        dstate_buf[head] = end_decay * dstate + product(
            jnp.concatenate([query_grown, parts[:, DV:]], axis=0), stacked, TN, FINE_BACK
        )
        solved = product(
            inverse, jnp.concatenate([dwritten, dprojected_key], axis=1), TN, FINE_BACK
        )
        dcoupling = product(solved, parts, NT, FINE_BACK)
        dcoupling = jnp.where(row > col, -dcoupling * factor, 0.0)
        dcoupling_gram = dcoupling * key_gram
        dbeta = lane_sum(dcoupling_gram)
        dgap = beta * dcoupling_gram + dmixing * mixing
        dgrams = jnp.concatenate([beta * dcoupling, dmixing * factor], axis=0)
        by_key = product(dgrams, key, NN, FINE_BACK)
        dkey = by_key[:ROWS] + product(
            dgrams, jnp.concatenate([key, query], axis=0), TN, FINE_BACK
        )
        dquery = by_key[ROWS:] + grown * dquery_grown
        dvalue_scaled = solved[:, :DV]
        dkey_scaled = solved[:, DV:]
        scaled_rows = lane_sum(dkey_scaled * (grown * key))
        dbeta = dbeta + lane_sum(dvalue_scaled * value) + scaled_rows
        tail_rows = lane_sum(dkey_tail * key_tail)
        dkey = dkey + tail * dkey_tail + (beta * grown) * dkey_scaled
        dtotal = lane_sum(dquery_grown * query_grown) + beta * scaled_rows - tail_rows
        sums = summed_by(
            upper_b, jnp.concatenate([dgap, jnp.broadcast_to(dtotal, (ROWS, ROWS))], axis=1)
        )
        ddecay = (
            lane_sum(jnp.where(col < row, sums[:, :ROWS], 0.0))
            + sums[:, ROWS : ROWS + 1]
            + (end_grad + jnp.sum(tail_rows, 0, keepdims=True))
        )
        dshifted = ddecay * slope_all[:, head : head + 1]
        drate = drate + jnp.where(lane == head, dshifted, 0.0)
        drate = drate + jnp.where(lane == heads + head, dbeta * (beta * (1.0 - beta)), 0.0)
        dsums = dsums + jnp.where(lane == head, ddecay * decay, 0.0)
        dsums = dsums + jnp.where(lane == heads + head, dshifted, 0.0)

        unit = query * math.sqrt(DK)
        dunit = dquery * (1.0 / math.sqrt(DK))
        dsilu = inv_q * (dunit - unit * lane_sum(dunit * unit))
        rows_buf[0:ROWS, q_at] = dsilu * (sig_q * (1.0 + conv_q * (1.0 - sig_q)))
        dsilu = inv_k * (dkey - key * lane_sum(dkey * key))
        rows_buf[0:ROWS, k_at] = dsilu * (sig_k * (1.0 + conv_k * (1.0 - sig_k)))
        rows_buf[0:ROWS, value_at] = (beta * dvalue_scaled) * (
            sig_v * (1.0 + conv_v * (1.0 - sig_v))
        )

    signal = proj_ref[:, :conv_cols]
    shifted_grad = rows_buf[0:ROWS, :]
    dsignal = shifted_grad * filter_ref[0:1, :]
    dfilter_ref[0:1, :] += jnp.sum(signal * shifted_grad, 0, keepdims=True)
    for offset in range(1, KW):
        shifted_grad = (
            rows_buf[offset : offset + ROWS, :] * keep_ref[:, KW + offset : KW + offset + 1]
        )
        dsignal = dsignal + shifted_grad * filter_ref[offset : offset + 1, :]
        dfilter_ref[offset : offset + 1, :] += jnp.sum(signal * shifted_grad, 0, keepdims=True)
    rows_buf[ROWS : ROWS + 8, :] = rows_buf[0:8, :]
    dproj_ref[:, :conv_cols] = dsignal.astype(jnp.bfloat16)
    dproj_ref[:, proj_cols : proj_cols + 128] = drate.astype(jnp.bfloat16)
    dsmall_ref[0:1, :] += dgain
    dsmall_ref[1:2, 0:128] += jnp.sum(dsums, 0, keepdims=True)


def mixer_forward(resets, proj, keep, filters, rates, head_gain, heads):
    row_count, proj_width = proj.shape
    chunks = row_count // ROWS
    conv_cols = 2 * heads * DK + heads * DV
    f32 = jnp.float32

    def rows_of(cols, dtype=f32):
        return jax.ShapeDtypeStruct((row_count, cols), dtype)

    def saved(rows, cols):
        return jax.ShapeDtypeStruct((chunks, heads, rows, cols), f32)

    def row_block(cols):
        return pl.BlockSpec((SUBS * ROWS, cols), lambda c, r: (c, 0))

    def saved_block(rows, cols):
        return pl.BlockSpec((SUBS, heads, rows, cols), lambda c, r: (c, 0, 0, 0))

    def whole(array):
        return pl.BlockSpec(array.shape, lambda c, r: (0, 0))

    return pl.pallas_call(
        partial(forward_kernel, heads),
        grid_spec=pltpu.PrefetchScalarGridSpec(
            num_scalar_prefetch=1,
            grid=(chunks // SUBS,),
            in_specs=[
                row_block(proj_width),
                row_block(keep.shape[1]),
                whole(filters),
                whole(rates),
                whole(head_gain),
            ],
            out_specs=[
                row_block(heads * DV),
                row_block(conv_cols),
                row_block(heads * DV),
                saved_block(DK, DV),
                saved_block(ROWS, ROWS),
                saved_block(ROWS, DV + DK),
                saved_block(ROWS, DV),
                saved_block(ROWS, ROWS),
                saved_block(2 * ROWS, ROWS),
            ],
            scratch_shapes=[
                pltpu.VMEM((SUBS * ROWS + 8, conv_cols), f32),
                pltpu.VMEM((heads, DK, DV), f32),
            ],
        ),
        out_shape=[
            rows_of(heads * DV, jnp.bfloat16),
            rows_of(conv_cols),
            rows_of(heads * DV),
            saved(DK, DV),
            saved(ROWS, ROWS),
            saved(ROWS, DV + DK),
            saved(ROWS, DV),
            saved(ROWS, ROWS),
            saved(2 * ROWS, ROWS),
        ],
        compiler_params=pltpu.CompilerParams(vmem_limit_bytes=40 << 20),
        name="mixer_forward",
    )(resets, proj, keep, filters, rates, head_gain)


def mixer_backward(resets, upstream, proj, keep, filters, rates, head_gain, saved, heads):
    row_count, proj_width = proj.shape
    chunks = row_count // ROWS
    conv_cols = 2 * heads * DK + heads * DV
    f32 = jnp.float32

    def row_block(array):
        return pl.BlockSpec((ROWS, array.shape[1]), lambda c, r: (chunks - 1 - c, 0))

    def saved_block(array):
        return pl.BlockSpec((1,) + array.shape[1:], lambda c, r: (chunks - 1 - c, 0, 0, 0))

    def whole(array):
        return pl.BlockSpec(array.shape, lambda c, r: (0, 0))

    dproj = jax.ShapeDtypeStruct((row_count, proj_width), jnp.bfloat16)
    dfilter = jax.ShapeDtypeStruct((8, conv_cols), f32)
    dsmall = jax.ShapeDtypeStruct((8, DV), f32)
    return pl.pallas_call(
        partial(backward_kernel, heads, chunks),
        grid_spec=pltpu.PrefetchScalarGridSpec(
            num_scalar_prefetch=1,
            grid=(chunks,),
            in_specs=[row_block(upstream), row_block(proj), row_block(keep)]
            + [whole(filters), whole(rates), whole(head_gain)]
            + [row_block(saved[0]), row_block(saved[1])]
            + [saved_block(array) for array in saved[2:]],
            out_specs=[row_block(dproj), whole(dfilter), whole(dsmall)],
            scratch_shapes=[
                pltpu.VMEM((ROWS + 8, conv_cols), f32),
                pltpu.VMEM((heads, DK, DV), f32),
            ],
        ),
        out_shape=[dproj, dfilter, dsmall],
        compiler_params=pltpu.CompilerParams(vmem_limit_bytes=40 << 20),
        name="mixer_backward",
    )(resets, upstream, proj, keep, filters, rates, head_gain, *saved)


def swap_halves(array):
    return lax.ppermute(array, "mp", [(0, 1), (1, 0)])


def dp_total(array):
    count = lax.axis_size("dp")
    step = 1
    while step < count:
        array = array + lax.ppermute(array, "dp", [(i, i ^ step) for i in range(count)])
        step *= 2
    return array


def dp_swap(array, bit):
    count = lax.axis_size("dp")
    return lax.ppermute(array, "dp", [(i, i ^ bit) for i in range(count)])


def dp_gather(shard, cuts):
    index = lax.axis_index("dp")
    bits = [1 << i for i in reversed(range((lax.axis_size("dp") - 1).bit_length()))]
    pieces = [shard[None, :, start:stop] for start, stop in cuts]
    for bit in bits:
        others = [dp_swap(piece, bit) for piece in pieces]
        upper = (index & bit) != 0
        pieces = [
            jnp.stack(
                [jnp.where(upper, other, piece), jnp.where(upper, piece, other)], axis=1
            ).reshape((-1,) + piece.shape[1:])
            for piece, other in zip(pieces, others)
        ]
    return [piece.reshape(-1, piece.shape[-1]) for piece in pieces]


def dp_scatter(pieces):
    index = lax.axis_index("dp")
    count = lax.axis_size("dp")
    pieces = [piece.reshape(count, -1, piece.shape[-1]) for piece in pieces]
    bit = 1
    while bit < count:
        side = (index & bit) // bit
        pairs = [piece.reshape((-1, 2) + piece.shape[1:]) for piece in pieces]
        others = [
            dp_swap(
                lax.dynamic_index_in_dim(pair, 1 - side, 1, False).astype(jnp.bfloat16), bit
            )
            for pair in pairs
        ]
        pieces = [
            lax.dynamic_index_in_dim(pair, side, 1, False) + other.astype(jnp.float32)
            for pair, other in zip(pairs, others)
        ]
        bit *= 2
    return [piece[0] for piece in pieces]


def in_order(own, other, model_index, axis):
    first = jnp.where(model_index == 0, own, other)
    second = jnp.where(model_index == 0, other, own)
    return jnp.concatenate([first, second], axis=axis)


def on_device(
    block_input,
    seq_lengths,
    seq_owner,
    mix_gain,
    query_weight,
    key_weight,
    value_weight,
    gate_weight,
    decay_weight,
    beta_weight,
    query_filter,
    key_filter,
    value_filter,
    decay_log,
    decay_bias,
    head_gain,
    out_weight,
    ffn_gain,
    ffn_gate,
    ffn_up,
    ffn_down,
    cotangent,
):
    bf16 = jnp.bfloat16
    f32 = jnp.float32
    local_rows, width = block_input.shape
    dp_index = lax.axis_index("dp")
    model_count = lax.axis_size("mp")
    model_index = lax.axis_index("mp")
    row_count = local_rows * model_count
    keep_masks, resets, valid_rows = layout(seq_lengths, seq_owner, dp_index, row_count)
    valid_all = valid_rows[:, None]
    heads_local = decay_log.shape[0] // model_count
    qk_cols = heads_local * DK
    v_cols = heads_local * DV
    ff_cols = ffn_gate.shape[1]
    shard_rows = query_weight.shape[0]
    proj_cols = 2 * qk_cols + 2 * v_cols

    def own_columns(array, col_count):
        return lax.dynamic_slice_in_dim(array, model_index * col_count, col_count, array.ndim - 1)

    def own_shard(array):
        return lax.dynamic_slice_in_dim(array, dp_index * shard_rows, shard_rows, 0)

    small_weight = jnp.concatenate(
        [own_columns(decay_weight, heads_local), own_columns(beta_weight, heads_local)], axis=1
    )
    small_weight = jnp.pad(small_weight, ((0, 0), (0, 128 - 2 * heads_local)))
    shard_mix = jnp.concatenate(
        [query_weight, key_weight, value_weight, gate_weight, own_shard(small_weight)], axis=1
    )
    half = proj_cols // 256 * 128
    mix_weight = jnp.concatenate(
        dp_gather(shard_mix, ((0, half), (half, shard_mix.shape[1]))), axis=1
    )
    input_other = swap_halves(block_input)
    out_rows = out_weight.T
    out_other = swap_halves(out_rows)
    shard_rest = jnp.concatenate([out_rows, out_other, ffn_gate, ffn_up, ffn_down.T], axis=1)
    rest_weight = lax.all_gather(shard_rest, "dp", axis=0, tiled=True)
    out_both = rest_weight[:, : 2 * v_cols]
    ffn_in_weight = rest_weight[:, 2 * v_cols : 2 * v_cols + 2 * ff_cols]
    down_weight = rest_weight[:, 2 * v_cols + 2 * ff_cols :]
    cot_other = swap_halves(cotangent)

    filters = jnp.concatenate(
        [
            own_columns(query_filter, qk_cols),
            own_columns(key_filter, qk_cols),
            own_columns(value_filter, v_cols),
        ],
        axis=1,
    )
    filters = jnp.pad(filters, ((0, 8 - KW), (0, 0)))
    rates = jnp.stack(
        [own_columns(decay_bias, heads_local), -jnp.exp(own_columns(decay_log, heads_local))]
    )
    rates = jnp.pad(rates, ((0, 6), (0, 128 - heads_local)))
    gain_row = head_gain[None]
    restarts = resets.astype(jnp.int32)
    later_masks = [
        jnp.concatenate([keep_masks[offset, offset:], jnp.ones((offset,), f32)])
        for offset in range(KW)
    ]
    keep_cols = jnp.stack([keep_masks[offset] for offset in range(KW)] + later_masks, axis=1)
    inputs_f = in_order(block_input, input_other, model_index, 0).astype(f32)
    cot_all = in_order(cotangent, cot_other, model_index, 0)
    normed1, inv_rms1 = rms_forward(inputs_f)
    mixed_in = (normed1 * mix_gain).astype(bf16)
    proj = jnp.dot(mixed_in, mix_weight, preferred_element_type=f32)
    cuts = (qk_cols, 2 * qk_cols, 2 * qk_cols + v_cols, proj_cols)
    gated_b, *saved = mixer_forward(
        restarts, proj, keep_cols, filters, rates, gain_row, heads_local
    )
    gated_both = jnp.concatenate([gated_b, swap_halves(gated_b)], axis=1)
    resid = inputs_f + valid_all * against(gated_both, out_both)
    normed2, inv_rms2 = rms_forward(resid)
    ffn_in = (normed2 * ffn_gain).astype(bf16)
    pre = jnp.dot(ffn_in, ffn_in_weight, preferred_element_type=f32)
    gate_pre, up_pre = pre[:, :ff_cols], pre[:, ff_cols:]
    sigmoid_gate = jax.nn.sigmoid(gate_pre)
    activated = gate_pre * sigmoid_gate
    hidden = (activated * up_pre).astype(bf16)
    cot_masked = cot_all * valid_all.astype(bf16)
    hidden_grad = jnp.dot(cot_masked, down_weight, preferred_element_type=f32)
    gate_grad_pre = (
        hidden_grad * up_pre * sigmoid_gate * (1.0 + gate_pre * (1.0 - sigmoid_gate))
    ).astype(bf16)
    up_grad_pre = (hidden_grad * activated).astype(bf16)
    pre_grad = jnp.concatenate([gate_grad_pre, up_grad_pre], axis=1)
    ffn_in_part = against(pre_grad, ffn_in_weight)
    ffn_in_sent = ffn_in_part.astype(bf16)
    rest_grads = jnp.concatenate(
        [across_rows(ffn_in, pre_grad).astype(bf16), across_rows(cot_masked, hidden).astype(bf16)],
        axis=1,
    )
    ffn_shard = lax.psum_scatter(rest_grads, "dp", scatter_dimension=0, tiled=True)
    ffn_in_got, _ = lax.optimization_barrier((swap_halves(ffn_in_sent), rest_grads))
    ffn_in_grad = ffn_in_sent.astype(f32) + ffn_in_got.astype(f32)

    def own_half(array):
        return lax.dynamic_slice_in_dim(array, model_index * local_rows, local_rows, 0)

    def other_half(array):
        return lax.dynamic_slice_in_dim(array, (1 - model_index) * local_rows, local_rows, 0)

    ffn_part = against(hidden, down_weight)
    ffn_sent, _ = lax.optimization_barrier((other_half(ffn_part).astype(bf16), ffn_in_got))
    ffn_sum = own_half(ffn_part) + swap_halves(ffn_sent).astype(f32)
    block_output = (own_half(resid) + own_half(valid_all) * ffn_sum).astype(bf16)
    ffn_gain_part = jnp.sum(ffn_in_part * normed2, 0)
    resid_grad = cot_all.astype(f32) + rms_backward(ffn_in_grad * ffn_gain, normed2, inv_rms2)
    mix_cot = (resid_grad * valid_all).astype(bf16)
    gated_grad = jnp.dot(mix_cot, out_both[:, :v_cols], preferred_element_type=f32)
    proj_grad, filter_grads, small_grads = mixer_backward(
        restarts, gated_grad, proj, keep_cols, filters, rates, gain_row, saved, heads_local
    )
    split_at = cuts[1]
    mix_shards = dp_scatter(
        [
            jnp.concatenate(
                [across_rows(mix_cot, gated_b), across_rows(mixed_in, proj_grad[:, :split_at])],
                axis=1,
            ),
            across_rows(mixed_in, proj_grad[:, split_at:proj_cols]),
        ]
    )
    rate_grads = across_rows(proj_grad[:, proj_cols:], mixed_in)[: 2 * heads_local]
    mix_in_part = against(proj_grad, mix_weight)
    mix_in_sum = own_half(mix_in_part) + swap_halves(
        other_half(mix_in_part).astype(bf16)
    ).astype(f32)
    mix_gain_part = jnp.sum(mix_in_part * normed1, 0)
    input_grad = own_half(resid_grad) + rms_backward(
        mix_in_sum * mix_gain, own_half(normed1), own_half(inv_rms1)
    )
    common = jnp.concatenate(
        [mix_gain_part, ffn_gain_part, small_grads[0], jnp.zeros((width - DV,), f32)]
    ).reshape(3, width)
    tail_row = jnp.concatenate(
        [small_grads[1, : 2 * heads_local], jnp.zeros((width - 2 * heads_local,), f32)]
    )
    split_rows = jnp.concatenate(
        [
            rate_grads,
            filter_grads[:KW, : cuts[0]].reshape(-1, width),
            filter_grads[:KW, cuts[0] : cuts[1]].reshape(-1, width),
            filter_grads[:KW, cuts[1] : cuts[2]].reshape(-1, width),
            tail_row[None],
        ],
        axis=0,
    )
    totals = dp_total(jnp.concatenate([common, split_rows], axis=0))
    totals_other = swap_halves(totals)
    common = totals[:3] + totals_other[:3]
    lower = jnp.where(model_index == 0, totals, totals_other)[3:]
    upper = jnp.where(model_index == 0, totals_other, totals)[3:]

    def joined(start, rows, cols):
        return jnp.concatenate(
            [
                lower[start : start + rows].reshape(-1, cols),
                upper[start : start + rows].reshape(-1, cols),
            ],
            axis=1,
        )

    q_rows = KW * qk_cols // width
    v_rows = KW * v_cols // width
    at_q = 2 * heads_local
    at_k = at_q + q_rows
    at_v = at_k + q_rows
    at_tail = at_v + v_rows

    def rate_weight_grad(start):
        return jnp.concatenate(
            [lower[start : start + heads_local], upper[start : start + heads_local]], axis=0
        ).T

    def rate_grad(start):
        return jnp.concatenate(
            [
                lower[at_tail, start : start + heads_local],
                upper[at_tail, start : start + heads_local],
            ]
        )

    mix_shard = jnp.concatenate([mix_shards[0][:, v_cols:], mix_shards[1]], axis=1)
    ffn_shard = ffn_shard.astype(f32)
    return (
        block_output,
        input_grad,
        common[0],
        mix_shard[:, : cuts[0]],
        mix_shard[:, cuts[0] : cuts[1]],
        mix_shard[:, cuts[1] : cuts[2]],
        mix_shard[:, cuts[2] : cuts[3]],
        rate_weight_grad(0),
        rate_weight_grad(heads_local),
        joined(at_q, q_rows, qk_cols),
        joined(at_k, q_rows, qk_cols),
        joined(at_v, v_rows, v_cols),
        rate_grad(0),
        rate_grad(heads_local),
        common[2, :DV],
        mix_shards[0][:, :v_cols].T,
        common[1],
        ffn_shard[:, :ff_cols],
        ffn_shard[:, ff_cols : 2 * ff_cols],
        ffn_shard[:, 2 * ff_cols :].T,
    )


def solution(mesh):
    in_specs = (
        P(("dp", "mp"), None),
        P(),
        P(),
        P(),
        P("dp", "mp"),
        P("dp", "mp"),
        P("dp", "mp"),
        P("dp", "mp"),
        P(),
        P(),
        P(),
        P(),
        P(),
        P(),
        P(),
        P(),
        P("mp", "dp"),
        P(),
        P("dp", "mp"),
        P("dp", "mp"),
        P("mp", "dp"),
        P(("dp", "mp"), None),
    )
    out_specs = (
        P(("dp", "mp"), None),
        P(("dp", "mp"), None),
        P(),
        P("dp", "mp"),
        P("dp", "mp"),
        P("dp", "mp"),
        P("dp", "mp"),
        P(),
        P(),
        P(),
        P(),
        P(),
        P(),
        P(),
        P(),
        P("mp", "dp"),
        P(),
        P("dp", "mp"),
        P("dp", "mp"),
        P("mp", "dp"),
    )
    return jax.shard_map(
        on_device, mesh=mesh, in_specs=in_specs, out_specs=out_specs, check_vma=False
    )
```

```python
from functools import partial
import math

import jax
import jax.numpy as jnp
from jax import lax
from jax.experimental import pallas as pl
from jax.experimental.pallas import tpu as pltpu
from jax.sharding import PartitionSpec as P

DK = 128
DV = 256
KW = 4
SPAN = 64


EPS = 1e-06


def layout(seq_lengths, seq_owner, device, row_count):
    owned = seq_owner == device
    own_lengths = jnp.where(owned, seq_lengths, 0)
    offsets = jnp.cumsum(own_lengths) - own_lengths
    loaded = jnp.sum(own_lengths)
    span_starts = jnp.arange(row_count // SPAN, dtype=jnp.int32) * SPAN
    begins = jnp.any(
        (offsets[None, :] == span_starts[:, None]) & (own_lengths[None, :] > 0), axis=1
    )
    resets = begins | (span_starts == loaded)
    within = jnp.arange(SPAN, dtype=jnp.int32)
    keep_masks = jnp.stack(
        [
            jnp.logical_not(resets[:, None] & (within[None, :] < offset)).reshape(row_count)
            for offset in range(KW)
        ]
    ).astype(jnp.float32)
    valid_rows = (jnp.arange(row_count, dtype=jnp.int32) < loaded).astype(jnp.float32)
    return (keep_masks, resets, valid_rows)


def across_rows(left, right):
    return lax.dot_general(
        left, right, (((0,), (0,)), ((), ())), preferred_element_type=jnp.float32
    )


def against(left, right):
    return lax.dot_general(
        left, right, (((1,), (1,)), ((), ())), preferred_element_type=jnp.float32
    )


def rms_forward(values):
    inv_rms = lax.rsqrt(jnp.mean(values * values, -1, keepdims=True) + EPS)
    return (values * inv_rms, inv_rms)


def rms_backward(upstream, normed, inv_rms):
    return inv_rms * (upstream - normed * jnp.mean(upstream * normed, -1, keepdims=True))


ROWS = 128
NN = ((1,), (0,))
NT = ((1,), (1,))
TN = ((0,), (0,))
FINE_GRAM = True
FINE_INVERSE = True
FINE_MERGE = True
SUBS = 2
FINE_APPLY = True
FINE_STATE = True
FINE_BACK = True


def dot(left, right, dims):
    return lax.dot_general(left, right, (dims, ((), ())), preferred_element_type=jnp.float32)


def high_low(values):
    high = values.astype(jnp.bfloat16)
    return high, (values - high.astype(jnp.float32)).astype(jnp.bfloat16)


def product(left, right, dims, fine=False):
    if not fine:
        return dot(left.astype(jnp.bfloat16), right.astype(jnp.bfloat16), dims)
    left_high, left_low = high_low(left)
    right_high, right_low = high_low(right)
    return dot(left_high, right_high, dims) + (
        dot(left_high, right_low, dims) + dot(left_low, right_high, dims)
    )


def summed_by(mask, values, dims=NN):
    high, low = high_low(values)
    return dot(mask, high, dims) + dot(mask, low, dims)


def chunk_masks(resets_ref, chunk):
    first = 1.0 - resets_ref[2 * chunk].astype(jnp.float32)
    second = 1.0 - resets_ref[2 * chunk + 1].astype(jnp.float32)
    row = lax.broadcasted_iota(jnp.int32, (ROWS, ROWS), 0)
    col = lax.broadcasted_iota(jnp.int32, (ROWS, ROWS), 1)
    late = row >= SPAN
    reached = jnp.where(late, first * second, first)
    reaching = jnp.where(late, 1.0, second)
    joined = jnp.where(late & (col < SPAN), second, 1.0)
    return row, col, reached, reaching, joined, first * second


def unit_lower_inverses(couplings, row, col):
    eye = jnp.where(row == col, 1.0, 0.0)
    base = 16
    near = (row // base) == (col // base)
    powered = [jnp.where(near, coupling, 0.0) for coupling in couplings]
    inverses = [eye - power for power in powered]
    size = 2
    while size < base:
        powered = [product(power, power, NN, FINE_INVERSE) for power in powered]
        inverses = [
            inverse + product(inverse, power, NN, FINE_INVERSE)
            for inverse, power in zip(inverses, powered)
        ]
        size *= 2
    while base < ROWS:
        wide = 2 * base
        linked = ((row // wide) == (col // wide)) & ((row // base) != (col // base))
        steps = [
            product(jnp.where(linked, coupling, 0.0), inverse, NN, FINE_MERGE)
            for coupling, inverse in zip(couplings, inverses)
        ]
        inverses = [
            inverse - product(inverse, step, NN, FINE_MERGE)
            for inverse, step in zip(inverses, steps)
        ]
        base = wide
    return inverses


def sigmoid(values):
    return 1.0 / (1.0 + jnp.exp(-values))


def lane_sum(values):
    return jnp.sum(values, -1, keepdims=True)


def forward_kernel(
    heads,
    base,
    resets_ref,
    proj_ref,
    before_ref,
    state_in_ref,
    keep_ref,
    filter_ref,
    rates_ref,
    gain_ref,
    gated_ref,
    conv_ref,
    mixed_ref,
    state_ref,
    inverse_ref,
    parts_ref,
    written_ref,
    factor_ref,
    grams_ref,
    state_out_ref,
    rows_buf,
    state_buf,
):
    step = pl.program_id(0)
    qk = heads * DK
    conv_cols = 2 * qk + heads * DV
    proj_cols = conv_cols + heads * DV
    rows = SUBS * ROWS

    @pl.when(step == 0)
    def _():
        if base == 0:
            rows_buf[0:8, :] = jnp.zeros((8, conv_cols), jnp.float32)
        else:
            rows_buf[0:8, :] = before_ref[:, :conv_cols]
        state_buf[...] = state_in_ref[...]

    rows_buf[8 : 8 + rows, :] = proj_ref[:, :conv_cols]
    conv = rows_buf[8 : 8 + rows, :] * filter_ref[0:1, :]
    for offset in range(1, KW):
        conv = conv + rows_buf[8 - offset : 8 - offset + rows, :] * (
            filter_ref[offset : offset + 1, :] * keep_ref[:, offset : offset + 1]
        )
    rows_buf[0:8, :] = rows_buf[rows : rows + 8, :]
    conv_ref[...] = conv

    rate = proj_ref[:, proj_cols : proj_cols + 128]
    shifted = rate + rates_ref[0:1, :]
    decay_all = rates_ref[1:2, :] * (
        jnp.maximum(shifted, 0.0) + jnp.log1p(jnp.exp(-jnp.abs(shifted)))
    )
    beta_all = sigmoid(rate)
    units = [(sub, head) for sub in range(SUBS) for head in range(heads)]
    prepared = []
    for sub, head in units:
        row, col, reached, reaching, joined, passed = chunk_masks(
            resets_ref, base + step * SUBS + sub
        )
        lower = jnp.where(row >= col, 1.0, 0.0)
        at = slice(sub * ROWS, (sub + 1) * ROWS)
        decay = jnp.broadcast_to(decay_all[at, head : head + 1], (ROWS, ROWS))
        beta = beta_all[at, heads + head : heads + head + 1]
        sums = summed_by(
            lower.astype(jnp.bfloat16),
            jnp.concatenate([jnp.where(row > col, decay, 0.0), decay], axis=1),
        )
        factor = jnp.exp(sums[:, :ROWS]) * (lower * joined)
        total = sums[:, ROWS:]
        total_end = total[ROWS - 1 : ROWS, :]
        grown = jnp.exp(total) * reached
        tail = jnp.exp(total_end - total) * reaching
        end_decay = jnp.exp(total_end[:, :1]) * passed

        conv_q = conv[at, head * DK : (head + 1) * DK]
        conv_k = conv[at, qk + head * DK : qk + (head + 1) * DK]
        conv_v = conv[at, 2 * qk + head * DV : 2 * qk + (head + 1) * DV]
        query = conv_q * sigmoid(conv_q)
        query = query * (lax.rsqrt(lane_sum(query * query) + EPS) * (1.0 / math.sqrt(DK)))
        key = conv_k * sigmoid(conv_k)
        key = key * lax.rsqrt(lane_sum(key * key) + EPS)
        value = conv_v * sigmoid(conv_v)

        grams = product(jnp.concatenate([key, query], axis=0), key, NT, FINE_GRAM)
        coupling = jnp.where(row > col, factor * grams[:ROWS] * beta, 0.0)
        scaled = jnp.concatenate([beta * value, (beta * grown) * key], axis=1)
        factor_ref[sub, head] = factor
        grams_ref[sub, head] = grams
        prepared.append(
            (coupling, scaled, grown * query, factor * grams[ROWS:], tail * key, end_decay)
        )
    row = lax.broadcasted_iota(jnp.int32, (ROWS, ROWS), 0)
    col = lax.broadcasted_iota(jnp.int32, (ROWS, ROWS), 1)
    inverses = unit_lower_inverses([entry[0] for entry in prepared], row, col)
    for (sub, head), inverse, entry in zip(units, inverses, prepared):
        _, scaled, query_grown, mixing, key_tail, end_decay = entry
        at = slice(sub * ROWS, (sub + 1) * ROWS)
        parts = product(inverse, scaled, NN, FINE_APPLY)
        state = state_buf[head]
        from_state = product(
            jnp.concatenate([parts[:, DV:], query_grown], axis=0), state, NN, FINE_STATE
        )
        written = parts[:, :DV] - from_state[:ROWS]
        mixed = from_state[ROWS:] + product(mixing, written, NN, FINE_STATE)
        state_buf[head] = end_decay * state + product(key_tail, written, TN, FINE_STATE)

        gate = proj_ref[at, conv_cols + head * DV : conv_cols + (head + 1) * DV]
        normed = mixed * lax.rsqrt(lane_sum(mixed * mixed) * (1.0 / DV) + EPS)
        gated_ref[at, head * DV : (head + 1) * DV] = (
            normed * gain_ref[...] * (gate * sigmoid(gate))
        ).astype(jnp.bfloat16)
        mixed_ref[at, head * DV : (head + 1) * DV] = mixed
        state_ref[sub, head] = state
        inverse_ref[sub, head] = inverse
        parts_ref[sub, head] = parts
        written_ref[sub, head] = written

    @pl.when(step == pl.num_programs(0) - 1)
    def _():
        state_out_ref[...] = state_buf[...]


def backward_kernel(
    heads,
    base,
    chunks,
    resets_ref,
    own_ref,
    got_ref,
    resid_ref,
    cot_ref,
    ffn_gain_ref,
    out_weight_ref,
    dstate_in_ref,
    later_ref,
    proj_ref,
    keep_ref,
    filter_ref,
    rates_ref,
    gain_ref,
    conv_ref,
    mixed_ref,
    state_ref,
    inverse_ref,
    parts_ref,
    written_ref,
    factor_ref,
    grams_ref,
    *tail_refs,
):
    (
        dproj_ref,
        dfilter_ref,
        dsmall_ref,
        dmix_ref,
        dresid_ref,
        dffn_gain_ref,
        dstate_out_ref,
        first_ref,
        rows_buf,
        dstate_buf,
    ) = tail_refs[-10:]
    step = pl.program_id(0)
    chunk = base + chunks - 1 - step
    qk = heads * DK
    conv_cols = 2 * qk + heads * DV
    proj_cols = conv_cols + heads * DV

    @pl.when(step == 0)
    def _():
        rows_buf[ROWS : ROWS + 8, :] = later_ref[...]
        dstate_buf[...] = dstate_in_ref[...]
        dffn_gain_ref[...] = jnp.zeros_like(dffn_gain_ref)
        dfilter_ref[...] = jnp.zeros_like(dfilter_ref)
        dsmall_ref[...] = jnp.zeros_like(dsmall_ref)

    resid = resid_ref[...]
    inv_resid = lax.rsqrt(jnp.mean(resid * resid, -1, keepdims=True) + EPS)
    resid_normed = resid * inv_resid
    ffn_in_own = own_ref[...].astype(jnp.float32)
    dffn_gain_ref[0:1, :] += jnp.sum(ffn_in_own * resid_normed, 0, keepdims=True)
    scaled_up = (ffn_in_own + got_ref[...].astype(jnp.float32)) * ffn_gain_ref[...]
    dresid = cot_ref[...].astype(jnp.float32) + inv_resid * (
        scaled_up - resid_normed * jnp.mean(scaled_up * resid_normed, -1, keepdims=True)
    )
    dresid_ref[...] = dresid
    dmix = (dresid * keep_ref[:, 2 * KW : 2 * KW + 1]).astype(jnp.bfloat16)
    dmix_ref[...] = dmix
    dgated = dot(dmix, out_weight_ref[...], NN)
    row, col, reached, reaching, joined, passed = chunk_masks(resets_ref, chunk)
    lower = jnp.where(row >= col, 1.0, 0.0)
    lower_b = lower.astype(jnp.bfloat16)
    upper_b = jnp.where(row <= col, 1.0, 0.0).astype(jnp.bfloat16)
    rate = proj_ref[:, proj_cols : proj_cols + 128]
    shifted = rate + rates_ref[0:1, :]
    decay_all = rates_ref[1:2, :] * (
        jnp.maximum(shifted, 0.0) + jnp.log1p(jnp.exp(-jnp.abs(shifted)))
    )
    slope_all = rates_ref[1:2, :] * sigmoid(shifted)
    beta_all = sigmoid(rate)
    drate = jnp.zeros((ROWS, 128), jnp.float32)
    dsums = jnp.zeros((ROWS, 128), jnp.float32)
    lane = lax.broadcasted_iota(jnp.int32, (ROWS, 128), 1)
    dgain = jnp.zeros((1, DV), jnp.float32)
    for head in range(heads):
        decay = jnp.broadcast_to(decay_all[:, head : head + 1], (ROWS, ROWS))
        beta = beta_all[:, heads + head : heads + head + 1]
        total = summed_by(lower_b, decay)
        total_end = total[ROWS - 1 : ROWS, :]
        grown = jnp.exp(total) * reached
        tail = jnp.exp(total_end - total) * reaching
        end_decay = jnp.exp(total_end[:, :1]) * passed

        v_at = slice(head * DV, (head + 1) * DV)
        gate_at = slice(conv_cols + head * DV, conv_cols + (head + 1) * DV)
        q_at = slice(head * DK, (head + 1) * DK)
        k_at = slice(qk + head * DK, qk + (head + 1) * DK)
        value_at = slice(2 * qk + head * DV, 2 * qk + (head + 1) * DV)
        conv_q = conv_ref[:, q_at]
        conv_k = conv_ref[:, k_at]
        conv_v = conv_ref[:, value_at]
        sig_q = sigmoid(conv_q)
        sig_k = sigmoid(conv_k)
        sig_v = sigmoid(conv_v)
        query = conv_q * sig_q
        inv_q = lax.rsqrt(lane_sum(query * query) + EPS)
        query = query * (inv_q * (1.0 / math.sqrt(DK)))
        key = conv_k * sig_k
        inv_k = lax.rsqrt(lane_sum(key * key) + EPS)
        key = key * inv_k
        value = conv_v * sig_v

        mixed = mixed_ref[:, v_at]
        inv_o = lax.rsqrt(lane_sum(mixed * mixed) * (1.0 / DV) + EPS)
        normed = mixed * inv_o
        gate = proj_ref[:, gate_at]
        sig_g = sigmoid(gate)
        upstream = dgated[:, v_at]
        up_normed = upstream * normed
        dgain = dgain + jnp.sum(up_normed * (gate * sig_g), 0, keepdims=True)
        dproj_ref[:, gate_at] = (
            up_normed * gain_ref[...] * (sig_g * (1.0 + gate * (1.0 - sig_g)))
        ).astype(jnp.bfloat16)
        dnormed = upstream * gain_ref[...] * (gate * sig_g)
        dmixed = inv_o * (dnormed - normed * (lane_sum(dnormed * normed) * (1.0 / DV)))

        state = state_ref[0, head]
        dstate = dstate_buf[head]
        inverse = inverse_ref[0, head]
        parts = parts_ref[0, head]
        written = written_ref[0, head]
        factor = factor_ref[0, head]
        key_gram = grams_ref[0, head, :ROWS]
        query_key = grams_ref[0, head, ROWS:]
        mixing = factor * query_key
        query_grown = grown * query
        key_tail = tail * key

        dwritten = product(mixing, dmixed, TN, FINE_BACK) + product(
            key_tail, dstate, NN, FINE_BACK
        )
        stacked = jnp.concatenate([dmixed, -dwritten], axis=0)
        through = product(stacked, state, NT, FINE_BACK)
        dquery_grown = through[:ROWS]
        dprojected_key = through[ROWS:]
        dmixing = product(dmixed, written, NT, FINE_BACK)
        dkey_tail = product(written, dstate, NT, FINE_BACK)
        end_grad = end_decay * lane_sum(jnp.sum(state * dstate, 0, keepdims=True))
        dstate_buf[head] = end_decay * dstate + product(
            jnp.concatenate([query_grown, parts[:, DV:]], axis=0), stacked, TN, FINE_BACK
        )
        solved = product(
            inverse, jnp.concatenate([dwritten, dprojected_key], axis=1), TN, FINE_BACK
        )
        dcoupling = product(solved, parts, NT, FINE_BACK)
        dcoupling = jnp.where(row > col, -dcoupling * factor, 0.0)
        dcoupling_gram = dcoupling * key_gram
        dbeta = lane_sum(dcoupling_gram)
        dgap = beta * dcoupling_gram + dmixing * mixing
        dgrams = jnp.concatenate([beta * dcoupling, dmixing * factor], axis=0)
        by_key = product(dgrams, key, NN, FINE_BACK)
        dkey = by_key[:ROWS] + product(
            dgrams, jnp.concatenate([key, query], axis=0), TN, FINE_BACK
        )
        dquery = by_key[ROWS:] + grown * dquery_grown
        dvalue_scaled = solved[:, :DV]
        dkey_scaled = solved[:, DV:]
        scaled_rows = lane_sum(dkey_scaled * (grown * key))
        dbeta = dbeta + lane_sum(dvalue_scaled * value) + scaled_rows
        tail_rows = lane_sum(dkey_tail * key_tail)
        dkey = dkey + tail * dkey_tail + (beta * grown) * dkey_scaled
        dtotal = lane_sum(dquery_grown * query_grown) + beta * scaled_rows - tail_rows
        sums = summed_by(
            upper_b, jnp.concatenate([dgap, jnp.broadcast_to(dtotal, (ROWS, ROWS))], axis=1)
        )
        ddecay = (
            lane_sum(jnp.where(col < row, sums[:, :ROWS], 0.0))
            + sums[:, ROWS : ROWS + 1]
            + (end_grad + jnp.sum(tail_rows, 0, keepdims=True))
        )
        dshifted = ddecay * slope_all[:, head : head + 1]
        drate = drate + jnp.where(lane == head, dshifted, 0.0)
        drate = drate + jnp.where(lane == heads + head, dbeta * (beta * (1.0 - beta)), 0.0)
        dsums = dsums + jnp.where(lane == head, ddecay * decay, 0.0)
        dsums = dsums + jnp.where(lane == heads + head, dshifted, 0.0)

        unit = query * math.sqrt(DK)
        dunit = dquery * (1.0 / math.sqrt(DK))
        dsilu = inv_q * (dunit - unit * lane_sum(dunit * unit))
        rows_buf[0:ROWS, q_at] = dsilu * (sig_q * (1.0 + conv_q * (1.0 - sig_q)))
        dsilu = inv_k * (dkey - key * lane_sum(dkey * key))
        rows_buf[0:ROWS, k_at] = dsilu * (sig_k * (1.0 + conv_k * (1.0 - sig_k)))
        rows_buf[0:ROWS, value_at] = (beta * dvalue_scaled) * (
            sig_v * (1.0 + conv_v * (1.0 - sig_v))
        )

    signal = proj_ref[:, :conv_cols]
    shifted_grad = rows_buf[0:ROWS, :]
    dsignal = shifted_grad * filter_ref[0:1, :]
    dfilter_ref[0:1, :] += jnp.sum(signal * shifted_grad, 0, keepdims=True)
    for offset in range(1, KW):
        shifted_grad = (
            rows_buf[offset : offset + ROWS, :] * keep_ref[:, KW + offset : KW + offset + 1]
        )
        dsignal = dsignal + shifted_grad * filter_ref[offset : offset + 1, :]
        dfilter_ref[offset : offset + 1, :] += jnp.sum(signal * shifted_grad, 0, keepdims=True)
    rows_buf[ROWS : ROWS + 8, :] = rows_buf[0:8, :]
    dproj_ref[:, :conv_cols] = dsignal.astype(jnp.bfloat16)
    dproj_ref[:, proj_cols : proj_cols + 128] = drate.astype(jnp.bfloat16)
    dsmall_ref[0:1, :] += dgain
    dsmall_ref[1:2, 0:128] += jnp.sum(dsums, 0, keepdims=True)

    @pl.when(step == chunks - 1)
    def _():
        dstate_out_ref[...] = dstate_buf[...]
        first_ref[...] = rows_buf[0:8, :]


def ffn_kernel(
    mix_cols,
    ff_cols,
    own_ref,
    other_ref,
    inputs_ref,
    cot_ref,
    keep_ref,
    gain_ref,
    weight_ref,
    *tail_refs,
):
    resid_ref, dnormed_ref, summand_ref, normed_ref, acts_ref = tail_refs[-5:]
    f32 = jnp.float32
    bf16 = jnp.bfloat16
    gate_at = slice(mix_cols, mix_cols + ff_cols)
    up_at = slice(mix_cols + ff_cols, mix_cols + 2 * ff_cols)
    down_at = slice(mix_cols + 2 * ff_cols, mix_cols + 3 * ff_cols)
    gated = jnp.concatenate([own_ref[...], other_ref[...]], axis=1)
    resid = inputs_ref[...].astype(f32) + keep_ref[:, 2 * KW : 2 * KW + 1] * dot(
        gated, weight_ref[:, :mix_cols], NT
    )
    resid_ref[...] = resid
    inv_rms = lax.rsqrt(jnp.mean(resid * resid, -1, keepdims=True) + EPS)
    normed = (resid * inv_rms * gain_ref[...]).astype(bf16)
    normed_ref[...] = normed
    gate_pre = dot(normed, weight_ref[:, gate_at], NN)
    up_pre = dot(normed, weight_ref[:, up_at], NN)
    dhidden = dot(cot_ref[...], weight_ref[:, down_at], NN)
    sig = sigmoid(gate_pre)
    active = gate_pre * sig
    hidden = (active * up_pre).astype(bf16)
    dgate = (dhidden * up_pre * sig * (1.0 + gate_pre * (1.0 - sig))).astype(bf16)
    dup = (dhidden * active).astype(bf16)
    acts_ref[:, :ff_cols] = dgate
    acts_ref[:, ff_cols : 2 * ff_cols] = dup
    acts_ref[:, 2 * ff_cols :] = hidden
    dnormed_ref[...] = (
        dot(dgate, weight_ref[:, gate_at], NT) + dot(dup, weight_ref[:, up_at], NT)
    ).astype(bf16)
    summand_ref[...] = dot(hidden, weight_ref[:, down_at], NT).astype(bf16)


def kernel_cost(micros):
    return pl.CostEstimate(
        flops=int(micros * 4e9), bytes_accessed=int(micros * 8e6), transcendentals=0
    )


def whole(array):
    return pl.BlockSpec(array.shape, lambda c, r: (0,) * len(array.shape))


def mixer_forward(resets, proj, keep, filters, rates, head_gain, heads, start, stop, state):
    proj_width = proj.shape[1]
    row_count = stop - start
    chunks = row_count // ROWS
    rows = SUBS * ROWS
    first = start // rows
    conv_cols = 2 * heads * DK + heads * DV
    f32 = jnp.float32

    def rows_of(cols, dtype=f32):
        return jax.ShapeDtypeStruct((row_count, cols), dtype)

    def saved(rows, cols):
        return jax.ShapeDtypeStruct((chunks, heads, rows, cols), f32)

    def part_block(cols):
        return pl.BlockSpec((rows, cols), lambda c, r: (c + first, 0))

    def row_block(cols):
        return pl.BlockSpec((rows, cols), lambda c, r: (c, 0))

    def saved_block(rows, cols):
        return pl.BlockSpec((SUBS, heads, rows, cols), lambda c, r: (c, 0, 0, 0))

    before = max(start // 8 - 1, 0)
    return pl.pallas_call(
        partial(forward_kernel, heads, start // ROWS),
        grid_spec=pltpu.PrefetchScalarGridSpec(
            num_scalar_prefetch=1,
            grid=(chunks // SUBS,),
            in_specs=[
                part_block(proj_width),
                pl.BlockSpec((8, proj_width), lambda c, r: (before, 0)),
                whole(state),
                part_block(keep.shape[1]),
                whole(filters),
                whole(rates),
                whole(head_gain),
            ],
            out_specs=[
                row_block(heads * DV),
                row_block(conv_cols),
                row_block(heads * DV),
                saved_block(DK, DV),
                saved_block(ROWS, ROWS),
                saved_block(ROWS, DV + DK),
                saved_block(ROWS, DV),
                saved_block(ROWS, ROWS),
                saved_block(2 * ROWS, ROWS),
                whole(state),
            ],
            scratch_shapes=[
                pltpu.VMEM((rows + 8, conv_cols), f32),
                pltpu.VMEM((heads, DK, DV), f32),
            ],
        ),
        out_shape=[
            rows_of(heads * DV, jnp.bfloat16),
            rows_of(conv_cols),
            rows_of(heads * DV),
            saved(DK, DV),
            saved(ROWS, ROWS),
            saved(ROWS, DV + DK),
            saved(ROWS, DV),
            saved(ROWS, ROWS),
            saved(2 * ROWS, ROWS),
            jax.ShapeDtypeStruct(state.shape, f32),
        ],
        compiler_params=pltpu.CompilerParams(vmem_limit_bytes=60 << 20),
        cost_estimate=kernel_cost(24 * row_count / 1024),
        name="mixer_forward",
    )(resets, proj, proj, state, keep, filters, rates, head_gain)


def mixer_backward(
    resets,
    own,
    got,
    resid,
    cot,
    ffn_gain,
    out_weight,
    dstate,
    later,
    proj,
    keep,
    filters,
    rates,
    head_gain,
    saved,
    heads,
    start,
    filled,
):
    row_count = resid.shape[0]
    total_rows, proj_width = proj.shape
    chunks = row_count // ROWS
    first = start // ROWS
    conv_cols = 2 * heads * DK + heads * DV
    f32 = jnp.float32

    def row_block(array):
        return pl.BlockSpec((ROWS, array.shape[1]), lambda c, r: (chunks - 1 - c, 0))

    def part_block(array):
        return pl.BlockSpec((ROWS, array.shape[1]), lambda c, r: (first + chunks - 1 - c, 0))

    def saved_block(array):
        return pl.BlockSpec((1,) + array.shape[1:], lambda c, r: (chunks - 1 - c, 0, 0, 0))

    dproj = jax.ShapeDtypeStruct((total_rows, proj_width), jnp.bfloat16)
    dfilter = jax.ShapeDtypeStruct((8, conv_cols), f32)
    dsmall = jax.ShapeDtypeStruct((8, DV), f32)
    dmix = jax.ShapeDtypeStruct(resid.shape, jnp.bfloat16)
    dresid = jax.ShapeDtypeStruct(resid.shape, f32)
    dffn_gain = jax.ShapeDtypeStruct((8, resid.shape[1]), f32)
    args = [resets, own, got, resid, cot, ffn_gain, out_weight, dstate, later]
    args += [proj, keep, filters, rates, head_gain, *saved]
    specs = [row_block(own), row_block(got), row_block(resid), part_block(cot), whole(ffn_gain)]
    specs += [
        pl.BlockSpec(
            (resid.shape[1], heads * DV), lambda c, r: (0, 0), pipeline_mode=pl.Buffered(1)
        )
    ]
    specs += [whole(dstate), whole(later), part_block(proj), part_block(keep)]
    specs += [whole(filters), whole(rates), whole(head_gain)]
    specs += [row_block(saved[0]), row_block(saved[1])]
    specs += [saved_block(array) for array in saved[2:]]
    aliases = {}
    if filled is not None:
        aliases = {len(args): 0}
        args.append(filled)
        specs.append(pl.BlockSpec(memory_space=pl.ANY))
    return pl.pallas_call(
        partial(backward_kernel, heads, first, chunks),
        grid_spec=pltpu.PrefetchScalarGridSpec(
            num_scalar_prefetch=1,
            grid=(chunks,),
            in_specs=specs,
            out_specs=[
                part_block(dproj),
                whole(dfilter),
                whole(dsmall),
                row_block(dmix),
                row_block(dresid),
                whole(dffn_gain),
                whole(dstate),
                whole(later),
            ],
            scratch_shapes=[
                pltpu.VMEM((ROWS + 8, conv_cols), f32),
                pltpu.VMEM((heads, DK, DV), f32),
            ],
        ),
        out_shape=[
            dproj,
            dfilter,
            dsmall,
            dmix,
            dresid,
            dffn_gain,
            jax.ShapeDtypeStruct(dstate.shape, f32),
            jax.ShapeDtypeStruct(later.shape, f32),
        ],
        input_output_aliases=aliases,
        compiler_params=pltpu.CompilerParams(vmem_limit_bytes=60 << 20),
        cost_estimate=kernel_cost(30 * row_count / 1024),
        name="mixer_backward",
    )(*args)


def ffn_both_ways(own, other, inputs, cot_masked, keep, gain, weight, ff_cols, start, filled):
    row_count, own_cols = own.shape
    total_rows, width = inputs.shape
    rows = 256
    first = start // rows
    bf16 = jnp.bfloat16

    def whole(array, **mode):
        return pl.BlockSpec(array.shape, lambda c: (0, 0), **mode)

    def row_block(cols):
        return pl.BlockSpec((rows, cols), lambda c: (c, 0))

    def part_block(cols):
        return pl.BlockSpec((rows, cols), lambda c: (c + first, 0))

    args = [own, other, inputs, cot_masked, keep, gain, weight]
    specs = [row_block(own_cols), row_block(own_cols), part_block(width), part_block(width)]
    specs += [part_block(keep.shape[1]), whole(gain)]
    specs += [whole(weight, pipeline_mode=pl.Buffered(1))]
    aliases = {}
    if filled is not None:
        aliases = {len(args): 3, len(args) + 1: 4}
        args += list(filled)
        specs += [pl.BlockSpec(memory_space=pl.ANY)] * 2
    return pl.pallas_call(
        partial(ffn_kernel, 2 * own_cols, ff_cols),
        grid=(row_count // rows,),
        in_specs=specs,
        out_specs=[
            row_block(width),
            row_block(width),
            row_block(width),
            part_block(width),
            part_block(3 * ff_cols),
        ],
        out_shape=[
            jax.ShapeDtypeStruct((row_count, width), jnp.float32),
            jax.ShapeDtypeStruct((row_count, width), bf16),
            jax.ShapeDtypeStruct((row_count, width), bf16),
            jax.ShapeDtypeStruct((total_rows, width), bf16),
            jax.ShapeDtypeStruct((total_rows, 3 * ff_cols), bf16),
        ],
        input_output_aliases=aliases,
        compiler_params=pltpu.CompilerParams(vmem_limit_bytes=60 << 20),
        cost_estimate=kernel_cost(28 * row_count / 1024),
        name="ffn_both_ways",
    )(*args)


def grads_kernel(
    shard_rows,
    side_ref,
    normed_ref,
    dproj_ref,
    dmix_lo_ref,
    dmix_hi_ref,
    gated_lo_ref,
    gated_hi_ref,
    mine_a_ref,
    mine_b_ref,
    theirs_a_ref,
    theirs_b_ref,
    rate_ref,
):
    side = side_ref[0]
    normed = normed_ref[...]
    gate_cols = gated_lo_ref.shape[1]
    first_cols = mine_a_ref.shape[1]

    def put(grad, mine_ref, theirs_ref, cols):
        pairs = grad.reshape(-1, 2, shard_rows, grad.shape[-1])
        even = pairs[:, 0].reshape(-1, grad.shape[-1])
        odd = pairs[:, 1].reshape(-1, grad.shape[-1])
        mine_ref[:, cols] = jnp.where(side == 0, even, odd)
        theirs_ref[:, cols] = jnp.where(side == 0, odd, even).astype(jnp.bfloat16)

    put(dot(normed, dproj_ref[:, :first_cols], TN), mine_a_ref, theirs_a_ref, slice(None))
    put(
        dot(normed, dproj_ref[:, first_cols : first_cols + gate_cols], TN),
        mine_b_ref,
        theirs_b_ref,
        slice(0, gate_cols),
    )
    put(
        dot(dmix_lo_ref[...], gated_lo_ref[...], TN)
        + dot(dmix_hi_ref[...], gated_hi_ref[...], TN),
        mine_b_ref,
        theirs_b_ref,
        slice(gate_cols, 2 * gate_cols),
    )
    rate_ref[...] = dot(dproj_ref[:, first_cols + gate_cols :], normed, TN)[:8]


def mixer_weight_grads(side, normed, dproj, dmix_lo, dmix_hi, gated_lo, gated_hi, shard_rows):
    rows, width = normed.shape
    half_rows, v_cols = gated_lo.shape
    tile = 256
    first_cols = 2 * v_cols
    bf16 = jnp.bfloat16

    def column_block(array):
        return pl.BlockSpec((array.shape[0], tile), lambda c, r: (0, c))

    def row_block(cols):
        return pl.BlockSpec((tile // 2, cols), lambda c, r: (c, 0))

    return pl.pallas_call(
        partial(grads_kernel, shard_rows),
        grid_spec=pltpu.PrefetchScalarGridSpec(
            num_scalar_prefetch=1,
            grid=(width // tile,),
            in_specs=[
                column_block(normed),
                whole(dproj),
                column_block(dmix_lo),
                column_block(dmix_hi),
                whole(gated_lo),
                whole(gated_hi),
            ],
            out_specs=[
                row_block(first_cols),
                row_block(first_cols),
                row_block(first_cols),
                row_block(first_cols),
                pl.BlockSpec((8, tile), lambda c, r: (0, c)),
            ],
        ),
        out_shape=[
            jax.ShapeDtypeStruct((width // 2, first_cols), jnp.float32),
            jax.ShapeDtypeStruct((width // 2, first_cols), jnp.float32),
            jax.ShapeDtypeStruct((width // 2, first_cols), bf16),
            jax.ShapeDtypeStruct((width // 2, first_cols), bf16),
            jax.ShapeDtypeStruct((8, width), jnp.float32),
        ],
        compiler_params=pltpu.CompilerParams(vmem_limit_bytes=60 << 20),
        cost_estimate=kernel_cost(8),
        name="mixer_weight_grads",
    )(side, normed, dproj, dmix_lo, dmix_hi, gated_lo, gated_hi)


def swap_halves(array):
    return lax.ppermute(array, "mp", [(0, 1), (1, 0)])


def dp_total(array):
    count = lax.axis_size("dp")
    step = 1
    while step < count:
        array = array + lax.ppermute(array, "dp", [(i, i ^ step) for i in range(count)])
        step *= 2
    return array


def dp_swap(array, bit):
    count = lax.axis_size("dp")
    return lax.ppermute(array, "dp", [(i, i ^ bit) for i in range(count)])


def dp_gather(shard, cuts):
    index = lax.axis_index("dp")
    bits = [1 << i for i in reversed(range((lax.axis_size("dp") - 1).bit_length()))]
    pieces = [shard[None, :, start:stop] for start, stop in cuts]
    for bit in bits:
        others = [dp_swap(piece, bit) for piece in pieces]
        upper = (index & bit) != 0
        pieces = [
            jnp.stack(
                [jnp.where(upper, other, piece), jnp.where(upper, piece, other)], axis=1
            ).reshape((-1,) + piece.shape[1:])
            for piece, other in zip(pieces, others)
        ]
    return [piece.reshape(-1, piece.shape[-1]) for piece in pieces]


def dp_scatter(kept, sent):
    index = lax.axis_index("dp")
    count = lax.axis_size("dp")
    f32 = jnp.float32
    pieces = [mine + dp_swap(theirs, 1).astype(f32) for mine, theirs in zip(kept, sent)]
    bit = 2
    while bit < count:
        blocks = count // bit
        pieces = [piece.reshape(blocks, -1, piece.shape[-1]) for piece in pieces]
        side = (index & bit) // bit
        pairs = [piece.reshape((-1, 2) + piece.shape[1:]) for piece in pieces]
        others = [
            dp_swap(
                lax.dynamic_index_in_dim(pair, 1 - side, 1, False).astype(jnp.bfloat16), bit
            )
            for pair in pairs
        ]
        pieces = [
            lax.dynamic_index_in_dim(pair, side, 1, False) + other.astype(f32)
            for pair, other in zip(pairs, others)
        ]
        bit *= 2
    return [piece.reshape(-1, piece.shape[-1]) for piece in pieces]


def in_order(own, other, model_index, axis):
    first = jnp.where(model_index == 0, own, other)
    second = jnp.where(model_index == 0, other, own)
    return jnp.concatenate([first, second], axis=axis)


def on_device(
    block_input,
    seq_lengths,
    seq_owner,
    mix_gain,
    query_weight,
    key_weight,
    value_weight,
    gate_weight,
    decay_weight,
    beta_weight,
    query_filter,
    key_filter,
    value_filter,
    decay_log,
    decay_bias,
    head_gain,
    out_weight,
    ffn_gain,
    ffn_gate,
    ffn_up,
    ffn_down,
    cotangent,
):
    bf16 = jnp.bfloat16
    f32 = jnp.float32
    local_rows, width = block_input.shape
    dp_index = lax.axis_index("dp")
    model_count = lax.axis_size("mp")
    model_index = lax.axis_index("mp")
    row_count = local_rows * model_count
    keep_masks, resets, valid_rows = layout(seq_lengths, seq_owner, dp_index, row_count)
    valid_all = valid_rows[:, None]
    heads_local = decay_log.shape[0] // model_count
    qk_cols = heads_local * DK
    v_cols = heads_local * DV
    ff_cols = ffn_gate.shape[1]
    shard_rows = query_weight.shape[0]
    proj_cols = 2 * qk_cols + 2 * v_cols

    def own_columns(array, col_count):
        return lax.dynamic_slice_in_dim(array, model_index * col_count, col_count, array.ndim - 1)

    def own_shard(array):
        return lax.dynamic_slice_in_dim(array, dp_index * shard_rows, shard_rows, 0)

    small_weight = jnp.concatenate(
        [own_columns(decay_weight, heads_local), own_columns(beta_weight, heads_local)], axis=1
    )
    small_weight = jnp.pad(small_weight, ((0, 0), (0, 128 - 2 * heads_local)))
    shard_mix = jnp.concatenate(
        [query_weight, key_weight, value_weight, gate_weight, own_shard(small_weight)], axis=1
    )
    half = proj_cols // 256 * 128
    mix_weight = jnp.concatenate(
        dp_gather(shard_mix, ((0, half), (half, shard_mix.shape[1]))), axis=1
    )
    input_other = swap_halves(block_input)
    out_rows = out_weight.T
    out_other = swap_halves(out_rows)
    shard_rest = jnp.concatenate([out_rows, out_other, ffn_gate, ffn_up, ffn_down.T], axis=1)
    rest_weight = lax.all_gather(shard_rest, "dp", axis=0, tiled=True)
    cot_other = swap_halves(cotangent)

    filters = jnp.concatenate(
        [
            own_columns(query_filter, qk_cols),
            own_columns(key_filter, qk_cols),
            own_columns(value_filter, v_cols),
        ],
        axis=1,
    )
    filters = jnp.pad(filters, ((0, 8 - KW), (0, 0)))
    rates = jnp.stack(
        [own_columns(decay_bias, heads_local), -jnp.exp(own_columns(decay_log, heads_local))]
    )
    rates = jnp.pad(rates, ((0, 6), (0, 128 - heads_local)))
    gain_row = head_gain[None]
    restarts = resets.astype(jnp.int32)
    later_masks = [
        jnp.concatenate([keep_masks[offset, offset:], jnp.ones((offset,), f32)])
        for offset in range(KW)
    ]
    keep_cols = jnp.stack(
        [keep_masks[offset] for offset in range(KW)] + later_masks + [valid_rows] * 8, axis=1
    )
    inputs_b = in_order(block_input, input_other, model_index, 0)
    inputs_f = inputs_b.astype(f32)
    cot_all = in_order(cotangent, cot_other, model_index, 0)
    normed1, inv_rms1 = rms_forward(inputs_f)
    mixed_in = (normed1 * mix_gain).astype(bf16)
    proj = jnp.dot(mixed_in, mix_weight, preferred_element_type=f32)
    cuts = (qk_cols, 2 * qk_cols, 2 * qk_cols + v_cols, proj_cols)
    middle = row_count // 2
    zero_state = jnp.zeros((heads_local, DK, DV), f32)
    small_args = (keep_cols, filters, rates, gain_row)
    gated_lo, *saved_lo, carried = mixer_forward(
        restarts, proj, *small_args, heads_local, 0, middle, zero_state
    )
    cot_masked = cot_all * valid_all.astype(bf16)
    ffn_row = ffn_gain[None]
    carried, cot_all, cot_masked, inputs_b = lax.optimization_barrier(
        (carried, cot_all, cot_masked, inputs_b)
    )
    gated_hi, *saved_hi, _ = mixer_forward(
        restarts, proj, *small_args, heads_local, middle, row_count, carried
    )
    other_lo = swap_halves(gated_lo)
    gated_sent, other_lo = lax.optimization_barrier((gated_hi, other_lo))
    other_hi = swap_halves(gated_sent)
    ffn_args = (inputs_b, cot_masked, keep_cols, ffn_row, rest_weight, ff_cols)
    resid_hi, dnormed_hi, summand_hi, *filled = ffn_both_ways(
        gated_hi, other_hi, *ffn_args, middle, None
    )
    resid_lo, dnormed_lo, summand_lo, ffn_in, acts = ffn_both_ways(
        gated_lo, other_lo, *ffn_args, 0, filled
    )
    rest_grads = jnp.concatenate(
        [
            across_rows(ffn_in, acts[:, : 2 * ff_cols]).astype(bf16),
            across_rows(cot_masked, acts[:, 2 * ff_cols :]).astype(bf16),
        ],
        axis=1,
    )
    ffn_shard = lax.psum_scatter(rest_grads, "dp", scatter_dimension=0, tiled=True)
    got_hi, _ = lax.optimization_barrier((swap_halves(dnormed_hi), rest_grads))
    got_lo = swap_halves(dnormed_lo)

    def own_half(array):
        return lax.dynamic_slice_in_dim(array, model_index * local_rows, local_rows, 0)

    def other_half(array):
        return lax.dynamic_slice_in_dim(array, (1 - model_index) * local_rows, local_rows, 0)

    def own_of(low, high):
        return jnp.where(model_index == 0, low, high)

    zero_rows = jnp.zeros((8, proj_cols - v_cols), f32)
    proj_grad, filter_hi, small_hi, dmix_hi, dresid_hi, ffn_gain_hi, carried, later = (
        mixer_backward(
            restarts,
            dnormed_hi,
            got_hi,
            resid_hi,
            cot_all,
            ffn_row,
            rest_weight,
            zero_state,
            zero_rows,
            proj,
            *small_args,
            saved_hi,
            heads_local,
            middle,
            None,
        )
    )
    summand_sent, got_lo, proj_grad = lax.optimization_barrier(
        (own_of(summand_hi, summand_lo), got_lo, proj_grad)
    )
    proj_grad, filter_lo, small_lo, dmix_lo, dresid_lo, ffn_gain_lo, _, _ = mixer_backward(
        restarts,
        dnormed_lo,
        got_lo,
        resid_lo,
        cot_all,
        ffn_row,
        rest_weight,
        carried,
        later,
        proj,
        *small_args,
        saved_lo,
        heads_local,
        0,
        proj_grad,
    )
    summand_got, proj_grad, dmix_lo, filter_lo, small_lo, dresid_lo, ffn_gain_lo = (
        lax.optimization_barrier(
            (
                swap_halves(summand_sent),
                proj_grad,
                dmix_lo,
                filter_lo,
                small_lo,
                dresid_lo,
                ffn_gain_lo,
            )
        )
    )
    ffn_sum = own_of(summand_lo, summand_hi).astype(f32) + summand_got.astype(f32)
    block_output = (own_of(resid_lo, resid_hi) + own_half(valid_all) * ffn_sum).astype(bf16)
    filter_grads = filter_lo + filter_hi
    small_grads = small_lo + small_hi
    ffn_gain_part = ffn_gain_lo[0] + ffn_gain_hi[0]
    *grad_pieces, rate_grads = mixer_weight_grads(
        (dp_index & 1).reshape(1),
        mixed_in,
        proj_grad,
        dmix_lo,
        dmix_hi,
        gated_lo,
        gated_hi,
        shard_rows,
    )
    rate_grads = rate_grads[: 2 * heads_local]
    mix_shards = dp_scatter(grad_pieces[:2], grad_pieces[2:])
    proj_grad, _ = lax.optimization_barrier((proj_grad, rate_grads))
    mix_in_part = against(proj_grad, mix_weight)
    mix_in_got, _ = lax.optimization_barrier(
        (swap_halves(other_half(mix_in_part).astype(bf16)), mix_shards[0])
    )
    mix_in_sum = own_half(mix_in_part) + mix_in_got.astype(f32)
    mix_gain_part = jnp.sum(mix_in_part * normed1, 0)
    input_grad = own_of(dresid_lo, dresid_hi) + rms_backward(
        mix_in_sum * mix_gain, own_half(normed1), own_half(inv_rms1)
    )
    common = jnp.concatenate(
        [mix_gain_part, ffn_gain_part, small_grads[0], jnp.zeros((width - DV,), f32)]
    ).reshape(3, width)
    tail_row = jnp.concatenate(
        [small_grads[1, : 2 * heads_local], jnp.zeros((width - 2 * heads_local,), f32)]
    )
    split_rows = jnp.concatenate(
        [
            rate_grads,
            filter_grads[:KW, : cuts[0]].reshape(-1, width),
            filter_grads[:KW, cuts[0] : cuts[1]].reshape(-1, width),
            filter_grads[:KW, cuts[1] : cuts[2]].reshape(-1, width),
            tail_row[None],
        ],
        axis=0,
    )
    totals = dp_total(jnp.concatenate([common, split_rows], axis=0))
    totals_other, _ = lax.optimization_barrier((swap_halves(totals), mix_shards[1]))
    common = totals[:3] + totals_other[:3]
    lower = jnp.where(model_index == 0, totals, totals_other)[3:]
    upper = jnp.where(model_index == 0, totals_other, totals)[3:]

    def joined(start, rows, cols):
        return jnp.concatenate(
            [
                lower[start : start + rows].reshape(-1, cols),
                upper[start : start + rows].reshape(-1, cols),
            ],
            axis=1,
        )

    q_rows = KW * qk_cols // width
    v_rows = KW * v_cols // width
    at_q = 2 * heads_local
    at_k = at_q + q_rows
    at_v = at_k + q_rows
    at_tail = at_v + v_rows

    def rate_weight_grad(start):
        return jnp.concatenate(
            [lower[start : start + heads_local], upper[start : start + heads_local]], axis=0
        ).T

    def rate_grad(start):
        return jnp.concatenate(
            [
                lower[at_tail, start : start + heads_local],
                upper[at_tail, start : start + heads_local],
            ]
        )

    ffn_shard = ffn_shard.astype(f32)
    return (
        block_output,
        input_grad,
        common[0],
        mix_shards[0][:, : cuts[0]],
        mix_shards[0][:, cuts[0] : cuts[1]],
        mix_shards[0][:, cuts[1] :],
        mix_shards[1][:, :v_cols],
        rate_weight_grad(0),
        rate_weight_grad(heads_local),
        joined(at_q, q_rows, qk_cols),
        joined(at_k, q_rows, qk_cols),
        joined(at_v, v_rows, v_cols),
        rate_grad(0),
        rate_grad(heads_local),
        common[2, :DV],
        mix_shards[1][:, v_cols:].T,
        common[1],
        ffn_shard[:, :ff_cols],
        ffn_shard[:, ff_cols : 2 * ff_cols],
        ffn_shard[:, 2 * ff_cols :].T,
    )


def solution(mesh):
    in_specs = (
        P(("dp", "mp"), None),
        P(),
        P(),
        P(),
        P("dp", "mp"),
        P("dp", "mp"),
        P("dp", "mp"),
        P("dp", "mp"),
        P(),
        P(),
        P(),
        P(),
        P(),
        P(),
        P(),
        P(),
        P("mp", "dp"),
        P(),
        P("dp", "mp"),
        P("dp", "mp"),
        P("mp", "dp"),
        P(("dp", "mp"), None),
    )
    out_specs = (
        P(("dp", "mp"), None),
        P(("dp", "mp"), None),
        P(),
        P("dp", "mp"),
        P("dp", "mp"),
        P("dp", "mp"),
        P("dp", "mp"),
        P(),
        P(),
        P(),
        P(),
        P(),
        P(),
        P(),
        P(),
        P("mp", "dp"),
        P(),
        P("dp", "mp"),
        P("dp", "mp"),
        P("mp", "dp"),
    )
    return jax.shard_map(
        on_device, mesh=mesh, in_specs=in_specs, out_specs=out_specs, check_vma=False
    )
```

```python
from functools import partial
import math

import jax
import jax.numpy as jnp
from jax import lax
from jax.experimental import pallas as pl
from jax.experimental.pallas import tpu as pltpu
from jax.sharding import PartitionSpec as P

DK = 128
DV = 256
KW = 4
SPAN = 64


EPS = 1e-06


def layout(seq_lengths, seq_owner, device, row_count):
    owned = seq_owner == device
    own_lengths = jnp.where(owned, seq_lengths, 0)
    offsets = jnp.cumsum(own_lengths) - own_lengths
    loaded = jnp.sum(own_lengths)
    span_starts = jnp.arange(row_count // SPAN, dtype=jnp.int32) * SPAN
    begins = jnp.any(
        (offsets[None, :] == span_starts[:, None]) & (own_lengths[None, :] > 0), axis=1
    )
    resets = begins | (span_starts == loaded)
    within = jnp.arange(SPAN, dtype=jnp.int32)
    keep_masks = jnp.stack(
        [
            jnp.logical_not(resets[:, None] & (within[None, :] < offset)).reshape(row_count)
            for offset in range(KW)
        ]
    ).astype(jnp.float32)
    valid_rows = (jnp.arange(row_count, dtype=jnp.int32) < loaded).astype(jnp.float32)
    return (keep_masks, resets, valid_rows)


def across_rows(left, right):
    return lax.dot_general(
        left, right, (((0,), (0,)), ((), ())), preferred_element_type=jnp.float32
    )


def against(left, right):
    return lax.dot_general(
        left, right, (((1,), (1,)), ((), ())), preferred_element_type=jnp.float32
    )


def rms_forward(values):
    inv_rms = lax.rsqrt(jnp.mean(values * values, -1, keepdims=True) + EPS)
    return (values * inv_rms, inv_rms)


def rms_backward(upstream, normed, inv_rms):
    return inv_rms * (upstream - normed * jnp.mean(upstream * normed, -1, keepdims=True))


ROWS = 128
NN = ((1,), (0,))
NT = ((1,), (1,))
TN = ((0,), (0,))
FINE_GRAM = True
FINE_INVERSE = True
FINE_MERGE = True
SUBS = 2
FFN_ROWS = 256
FINE_APPLY = True
FINE_STATE = True
FINE_BACK = (True,) * 10
BACK_SUBS = 2


def dot(left, right, dims):
    return lax.dot_general(left, right, (dims, ((), ())), preferred_element_type=jnp.float32)


def high_low(values):
    high = values.astype(jnp.bfloat16)
    return high, (values - high.astype(jnp.float32)).astype(jnp.bfloat16)


def product(left, right, dims, fine=False):
    if not fine:
        return dot(left.astype(jnp.bfloat16), right.astype(jnp.bfloat16), dims)
    left_high, left_low = high_low(left)
    right_high, right_low = high_low(right)
    return dot(left_high, right_high, dims) + (
        dot(left_high, right_low, dims) + dot(left_low, right_high, dims)
    )


def summed_by(mask, values, dims=NN):
    high, low = high_low(values)
    return dot(mask, high, dims) + dot(mask, low, dims)


def chunk_masks(resets_ref, chunk):
    first = 1.0 - resets_ref[2 * chunk].astype(jnp.float32)
    second = 1.0 - resets_ref[2 * chunk + 1].astype(jnp.float32)
    row = lax.broadcasted_iota(jnp.int32, (ROWS, ROWS), 0)
    col = lax.broadcasted_iota(jnp.int32, (ROWS, ROWS), 1)
    late = row >= SPAN
    reached = jnp.where(late, first * second, first)
    reaching = jnp.where(late, 1.0, second)
    joined = jnp.where(late & (col < SPAN), second, 1.0)
    return row, col, reached, reaching, joined, first * second


def unit_lower_inverses(couplings, row, col):
    eye = jnp.where(row == col, 1.0, 0.0)
    base = 16
    near = (row // base) == (col // base)
    powered = [jnp.where(near, coupling, 0.0) for coupling in couplings]
    inverses = [eye - power for power in powered]
    size = 2
    while size < base:
        powered = [product(power, power, NN, FINE_INVERSE) for power in powered]
        inverses = [
            inverse + product(inverse, power, NN, FINE_INVERSE)
            for inverse, power in zip(inverses, powered)
        ]
        size *= 2
    while base < ROWS:
        wide = 2 * base
        linked = ((row // wide) == (col // wide)) & ((row // base) != (col // base))
        steps = [
            product(jnp.where(linked, coupling, 0.0), inverse, NN, FINE_MERGE)
            for coupling, inverse in zip(couplings, inverses)
        ]
        inverses = [
            inverse - product(inverse, step, NN, FINE_MERGE)
            for inverse, step in zip(inverses, steps)
        ]
        base = wide
    return inverses


def sigmoid(values):
    return 1.0 / (1.0 + jnp.exp(-values))


def lane_sum(values):
    return jnp.sum(values, -1, keepdims=True)


def forward_kernel(
    heads,
    base,
    resets_ref,
    proj_ref,
    before_ref,
    state_in_ref,
    keep_ref,
    filter_ref,
    rates_ref,
    gain_ref,
    gated_ref,
    conv_ref,
    mixed_ref,
    state_ref,
    inverse_ref,
    parts_ref,
    written_ref,
    factor_ref,
    grams_ref,
    state_out_ref,
    rows_buf,
    state_buf,
):
    step = pl.program_id(0)
    qk = heads * DK
    conv_cols = 2 * qk + heads * DV
    proj_cols = conv_cols + heads * DV
    rows = SUBS * ROWS

    @pl.when(step == 0)
    def _():
        if base == 0:
            rows_buf[0:8, :] = jnp.zeros((8, conv_cols), jnp.float32)
        else:
            rows_buf[0:8, :] = before_ref[:, :conv_cols]
        state_buf[...] = state_in_ref[...]

    rows_buf[8 : 8 + rows, :] = proj_ref[:, :conv_cols]
    conv = rows_buf[8 : 8 + rows, :] * filter_ref[0:1, :]
    for offset in range(1, KW):
        conv = conv + rows_buf[8 - offset : 8 - offset + rows, :] * (
            filter_ref[offset : offset + 1, :] * keep_ref[:, offset : offset + 1]
        )
    rows_buf[0:8, :] = rows_buf[rows : rows + 8, :]
    conv_ref[...] = conv

    rate = proj_ref[:, proj_cols : proj_cols + 128]
    shifted = rate + rates_ref[0:1, :]
    decay_all = rates_ref[1:2, :] * (
        jnp.maximum(shifted, 0.0) + jnp.log1p(jnp.exp(-jnp.abs(shifted)))
    )
    beta_all = sigmoid(rate)
    units = [(sub, head) for sub in range(SUBS) for head in range(heads)]
    prepared = []
    for sub, head in units:
        row, col, reached, reaching, joined, passed = chunk_masks(
            resets_ref, base + step * SUBS + sub
        )
        lower = jnp.where(row >= col, 1.0, 0.0)
        at = slice(sub * ROWS, (sub + 1) * ROWS)
        decay = jnp.broadcast_to(decay_all[at, head : head + 1], (ROWS, ROWS))
        beta = beta_all[at, heads + head : heads + head + 1]
        sums = summed_by(
            lower.astype(jnp.bfloat16),
            jnp.concatenate([jnp.where(row > col, decay, 0.0), decay], axis=1),
        )
        factor = jnp.exp(sums[:, :ROWS]) * (lower * joined)
        total = sums[:, ROWS:]
        total_end = total[ROWS - 1 : ROWS, :]
        grown = jnp.exp(total) * reached
        tail = jnp.exp(total_end - total) * reaching
        end_decay = jnp.exp(total_end[:, :1]) * passed

        conv_q = conv[at, head * DK : (head + 1) * DK]
        conv_k = conv[at, qk + head * DK : qk + (head + 1) * DK]
        conv_v = conv[at, 2 * qk + head * DV : 2 * qk + (head + 1) * DV]
        query = conv_q * sigmoid(conv_q)
        query = query * (lax.rsqrt(lane_sum(query * query) + EPS) * (1.0 / math.sqrt(DK)))
        key = conv_k * sigmoid(conv_k)
        key = key * lax.rsqrt(lane_sum(key * key) + EPS)
        value = conv_v * sigmoid(conv_v)

        grams = product(jnp.concatenate([key, query], axis=0), key, NT, FINE_GRAM)
        coupling = jnp.where(row > col, factor * grams[:ROWS] * beta, 0.0)
        scaled = jnp.concatenate([beta * value, (beta * grown) * key], axis=1)
        factor_ref[sub, head] = factor
        grams_ref[sub, head] = grams
        prepared.append(
            (coupling, scaled, grown * query, factor * grams[ROWS:], tail * key, end_decay)
        )
    row = lax.broadcasted_iota(jnp.int32, (ROWS, ROWS), 0)
    col = lax.broadcasted_iota(jnp.int32, (ROWS, ROWS), 1)
    inverses = unit_lower_inverses([entry[0] for entry in prepared], row, col)
    for (sub, head), inverse, entry in zip(units, inverses, prepared):
        _, scaled, query_grown, mixing, key_tail, end_decay = entry
        at = slice(sub * ROWS, (sub + 1) * ROWS)
        parts = product(inverse, scaled, NN, FINE_APPLY)
        state = state_buf[head]
        from_state = product(
            jnp.concatenate([parts[:, DV:], query_grown], axis=0), state, NN, FINE_STATE
        )
        written = parts[:, :DV] - from_state[:ROWS]
        mixed = from_state[ROWS:] + product(mixing, written, NN, FINE_STATE)
        state_buf[head] = end_decay * state + product(key_tail, written, TN, FINE_STATE)

        gate = proj_ref[at, conv_cols + head * DV : conv_cols + (head + 1) * DV]
        normed = mixed * lax.rsqrt(lane_sum(mixed * mixed) * (1.0 / DV) + EPS)
        gated_ref[at, head * DV : (head + 1) * DV] = (
            normed * gain_ref[...] * (gate * sigmoid(gate))
        ).astype(jnp.bfloat16)
        mixed_ref[at, head * DV : (head + 1) * DV] = mixed
        state_ref[sub, head] = state
        inverse_ref[sub, head] = inverse
        parts_ref[sub, head] = parts
        written_ref[sub, head] = written

    @pl.when(step == pl.num_programs(0) - 1)
    def _():
        state_out_ref[...] = state_buf[...]


def backward_kernel(
    heads,
    base,
    chunks,
    resets_ref,
    own_ref,
    got_ref,
    resid_ref,
    cot_ref,
    ffn_gain_ref,
    out_weight_ref,
    dstate_in_ref,
    later_ref,
    proj_ref,
    keep_ref,
    filter_ref,
    rates_ref,
    gain_ref,
    conv_ref,
    mixed_ref,
    state_ref,
    inverse_ref,
    parts_ref,
    written_ref,
    factor_ref,
    grams_ref,
    *tail_refs,
):
    (
        dproj_ref,
        dfilter_ref,
        dsmall_ref,
        dmix_ref,
        dresid_ref,
        dffn_gain_ref,
        dstate_out_ref,
        first_ref,
        rows_buf,
        dstate_buf,
    ) = tail_refs[-10:]
    step = pl.program_id(0)
    last_step = pl.num_programs(0) - 1
    rows = BACK_SUBS * ROWS
    qk = heads * DK
    conv_cols = 2 * qk + heads * DV
    proj_cols = conv_cols + heads * DV

    @pl.when(step == 0)
    def _():
        rows_buf[rows : rows + 8, :] = later_ref[...]
        dstate_buf[...] = dstate_in_ref[...]
        dffn_gain_ref[...] = jnp.zeros_like(dffn_gain_ref)
        dfilter_ref[...] = jnp.zeros_like(dfilter_ref)
        dsmall_ref[...] = jnp.zeros_like(dsmall_ref)

    resid = resid_ref[...]
    inv_resid = lax.rsqrt(jnp.mean(resid * resid, -1, keepdims=True) + EPS)
    resid_normed = resid * inv_resid
    ffn_in_own = own_ref[...].astype(jnp.float32)
    dffn_gain_ref[0:1, :] += jnp.sum(ffn_in_own * resid_normed, 0, keepdims=True)
    scaled_up = (ffn_in_own + got_ref[...].astype(jnp.float32)) * ffn_gain_ref[...]
    dresid = cot_ref[...].astype(jnp.float32) + inv_resid * (
        scaled_up - resid_normed * jnp.mean(scaled_up * resid_normed, -1, keepdims=True)
    )
    dresid_ref[...] = dresid
    dmix = (dresid * keep_ref[:, 2 * KW : 2 * KW + 1]).astype(jnp.bfloat16)
    dmix_ref[...] = dmix
    dgated = dot(dmix, out_weight_ref[...], NN)
    rate = proj_ref[:, proj_cols : proj_cols + 128]
    shifted = rate + rates_ref[0:1, :]
    decay_all = rates_ref[1:2, :] * (
        jnp.maximum(shifted, 0.0) + jnp.log1p(jnp.exp(-jnp.abs(shifted)))
    )
    slope_all = rates_ref[1:2, :] * sigmoid(shifted)
    beta_all = sigmoid(rate)
    row = lax.broadcasted_iota(jnp.int32, (ROWS, ROWS), 0)
    col = lax.broadcasted_iota(jnp.int32, (ROWS, ROWS), 1)
    lower_b = jnp.where(row >= col, 1.0, 0.0).astype(jnp.bfloat16)
    upper_b = jnp.where(row <= col, 1.0, 0.0).astype(jnp.bfloat16)
    lane = lax.broadcasted_iota(jnp.int32, (ROWS, 128), 1)
    dgain = jnp.zeros((1, DV), jnp.float32)
    units = [(sub, head) for sub in reversed(range(BACK_SUBS)) for head in range(heads)]
    prepared = []
    for sub, head in units:
        at = slice(sub * ROWS, (sub + 1) * ROWS)
        chunk = base + chunks - BACK_SUBS * (step + 1) + sub
        _, _, reached, reaching, _, passed = chunk_masks(resets_ref, chunk)
        decay = jnp.broadcast_to(decay_all[at, head : head + 1], (ROWS, ROWS))
        total = summed_by(lower_b, decay)
        total_end = total[ROWS - 1 : ROWS, :]
        grown = jnp.exp(total) * reached
        tail = jnp.exp(total_end - total) * reaching
        end_decay = jnp.exp(total_end[:, :1]) * passed

        v_at = slice(head * DV, (head + 1) * DV)
        gate_at = slice(conv_cols + head * DV, conv_cols + (head + 1) * DV)
        conv_q = conv_ref[at, head * DK : (head + 1) * DK]
        conv_k = conv_ref[at, qk + head * DK : qk + (head + 1) * DK]
        query = conv_q * sigmoid(conv_q)
        inv_q = lax.rsqrt(lane_sum(query * query) + EPS)
        query = query * (inv_q * (1.0 / math.sqrt(DK)))
        key = conv_k * sigmoid(conv_k)
        inv_k = lax.rsqrt(lane_sum(key * key) + EPS)
        key = key * inv_k

        mixed = mixed_ref[at, v_at]
        inv_o = lax.rsqrt(lane_sum(mixed * mixed) * (1.0 / DV) + EPS)
        normed = mixed * inv_o
        gate = proj_ref[at, gate_at]
        sig_g = sigmoid(gate)
        upstream = dgated[at, v_at]
        up_normed = upstream * normed
        dgain = dgain + jnp.sum(up_normed * (gate * sig_g), 0, keepdims=True)
        dproj_ref[at, gate_at] = (
            up_normed * gain_ref[...] * (sig_g * (1.0 + gate * (1.0 - sig_g)))
        ).astype(jnp.bfloat16)
        dnormed = upstream * gain_ref[...] * (gate * sig_g)
        dmixed = inv_o * (dnormed - normed * (lane_sum(dnormed * normed) * (1.0 / DV)))
        mixing = factor_ref[sub, head] * grams_ref[sub, head, ROWS:]
        within = product(mixing, dmixed, TN, FINE_BACK[0])
        dmixing = product(dmixed, written_ref[sub, head], NT, FINE_BACK[3])
        prepared.append(
            (decay, grown, tail, end_decay, query, inv_q, key, inv_k, dmixed, within, dmixing)
        )
    stepped = []
    for (sub, head), entry in zip(units, prepared):
        decay, grown, tail, end_decay, query, inv_q, key, inv_k, dmixed, within, dmixing = entry
        state = state_ref[sub, head]
        dstate = dstate_buf[head]
        dwritten = within + product(tail * key, dstate, NN, FINE_BACK[1])
        dkey_tail = product(written_ref[sub, head], dstate, NT, FINE_BACK[4])
        end_grad = end_decay * lane_sum(jnp.sum(state * dstate, 0, keepdims=True))
        stacked = jnp.concatenate([dmixed, -dwritten], axis=0)
        dstate_buf[head] = end_decay * dstate + product(
            jnp.concatenate([grown * query, parts_ref[sub, head, :, DV:]], axis=0),
            stacked,
            TN,
            FINE_BACK[5],
        )
        stepped.append((dwritten, dkey_tail, end_grad, stacked))
    drates = {sub: jnp.zeros((ROWS, 128), jnp.float32) for sub in range(BACK_SUBS)}
    dsums = jnp.zeros((ROWS, 128), jnp.float32)
    throughs = [
        product(entry[3], state_ref[sub, head], NT, FINE_BACK[2])
        for (sub, head), entry in zip(units, stepped)
    ]
    solveds = [
        product(
            inverse_ref[sub, head],
            jnp.concatenate([entry[0], through[ROWS:]], axis=1),
            TN,
            FINE_BACK[6],
        )
        for (sub, head), entry, through in zip(units, stepped, throughs)
    ]
    dcouplings = [
        product(solved, parts_ref[sub, head], NT, FINE_BACK[7])
        for (sub, head), solved in zip(units, solveds)
    ]
    for at_unit, (sub, head) in enumerate(units):
        decay, grown, tail, _, query, inv_q, key, inv_k, _, _, dmixing = prepared[at_unit]
        _, dkey_tail, end_grad, _ = stepped[at_unit]
        solved = solveds[at_unit]
        at = slice(sub * ROWS, (sub + 1) * ROWS)
        q_at = slice(head * DK, (head + 1) * DK)
        k_at = slice(qk + head * DK, qk + (head + 1) * DK)
        value_at = slice(2 * qk + head * DV, 2 * qk + (head + 1) * DV)
        beta = beta_all[at, heads + head : heads + head + 1]
        factor = factor_ref[sub, head]
        conv_q = conv_ref[at, q_at]
        conv_k = conv_ref[at, k_at]
        conv_v = conv_ref[at, value_at]
        sig_q = sigmoid(conv_q)
        sig_k = sigmoid(conv_k)
        sig_v = sigmoid(conv_v)
        value = conv_v * sig_v
        query_grown = grown * query
        key_tail = tail * key
        dquery_grown = throughs[at_unit][:ROWS]
        dcoupling = jnp.where(row > col, -dcouplings[at_unit] * factor, 0.0)
        dcoupling_gram = dcoupling * grams_ref[sub, head, :ROWS]
        dbeta = lane_sum(dcoupling_gram)
        dgap = beta * dcoupling_gram + dmixing * (factor * grams_ref[sub, head, ROWS:])
        dgrams = jnp.concatenate([beta * dcoupling, dmixing * factor], axis=0)
        by_key = product(dgrams, key, NN, FINE_BACK[8])
        dkey = by_key[:ROWS] + product(
            dgrams, jnp.concatenate([key, query], axis=0), TN, FINE_BACK[9]
        )
        dquery = by_key[ROWS:] + grown * dquery_grown
        dvalue_scaled = solved[:, :DV]
        dkey_scaled = solved[:, DV:]
        scaled_rows = lane_sum(dkey_scaled * (grown * key))
        dbeta = dbeta + lane_sum(dvalue_scaled * value) + scaled_rows
        tail_rows = lane_sum(dkey_tail * key_tail)
        dkey = dkey + tail * dkey_tail + (beta * grown) * dkey_scaled
        dtotal = lane_sum(dquery_grown * query_grown) + beta * scaled_rows - tail_rows
        sums = summed_by(
            upper_b, jnp.concatenate([dgap, jnp.broadcast_to(dtotal, (ROWS, ROWS))], axis=1)
        )
        ddecay = (
            lane_sum(jnp.where(col < row, sums[:, :ROWS], 0.0))
            + sums[:, ROWS : ROWS + 1]
            + (end_grad + jnp.sum(tail_rows, 0, keepdims=True))
        )
        dshifted = ddecay * slope_all[at, head : head + 1]
        drates[sub] = (
            drates[sub]
            + jnp.where(lane == head, dshifted, 0.0)
            + jnp.where(lane == heads + head, dbeta * (beta * (1.0 - beta)), 0.0)
        )
        dsums = dsums + jnp.where(lane == head, ddecay * decay, 0.0)
        dsums = dsums + jnp.where(lane == heads + head, dshifted, 0.0)

        unit = query * math.sqrt(DK)
        dunit = dquery * (1.0 / math.sqrt(DK))
        dsilu = inv_q * (dunit - unit * lane_sum(dunit * unit))
        rows_buf[at, q_at] = dsilu * (sig_q * (1.0 + conv_q * (1.0 - sig_q)))
        dsilu = inv_k * (dkey - key * lane_sum(dkey * key))
        rows_buf[at, k_at] = dsilu * (sig_k * (1.0 + conv_k * (1.0 - sig_k)))
        rows_buf[at, value_at] = (beta * dvalue_scaled) * (
            sig_v * (1.0 + conv_v * (1.0 - sig_v))
        )

    signal = proj_ref[:, :conv_cols]
    shifted_grad = rows_buf[0:rows, :]
    dsignal = shifted_grad * filter_ref[0:1, :]
    dfilter_ref[0:1, :] += jnp.sum(signal * shifted_grad, 0, keepdims=True)
    for offset in range(1, KW):
        shifted_grad = (
            rows_buf[offset : offset + rows, :] * keep_ref[:, KW + offset : KW + offset + 1]
        )
        dsignal = dsignal + shifted_grad * filter_ref[offset : offset + 1, :]
        dfilter_ref[offset : offset + 1, :] += jnp.sum(signal * shifted_grad, 0, keepdims=True)
    rows_buf[rows : rows + 8, :] = rows_buf[0:8, :]
    dproj_ref[:, :conv_cols] = dsignal.astype(jnp.bfloat16)
    for sub in range(BACK_SUBS):
        dproj_ref[sub * ROWS : (sub + 1) * ROWS, proj_cols : proj_cols + 128] = drates[
            sub
        ].astype(jnp.bfloat16)
    dsmall_ref[0:1, :] += dgain
    dsmall_ref[1:2, 0:128] += jnp.sum(dsums, 0, keepdims=True)

    @pl.when(step == last_step)
    def _():
        dstate_out_ref[...] = dstate_buf[...]
        first_ref[...] = rows_buf[0:8, :]


def ffn_kernel(
    mix_cols,
    ff_cols,
    own_ref,
    other_ref,
    inputs_ref,
    cot_ref,
    keep_ref,
    gain_ref,
    weight_hbm,
    *tail_refs,
):
    resid_ref, dnormed_ref, summand_ref, normed_ref, acts_ref, weight_ref, copy_sems = tail_refs[
        -7:
    ]
    f32 = jnp.float32
    bf16 = jnp.bfloat16
    edges = [0] + [mix_cols + part * ff_cols for part in range(4)]

    def copy(part):
        at = pl.ds(edges[part], edges[part + 1] - edges[part])
        return pltpu.make_async_copy(
            weight_hbm.at[:, at], weight_ref.at[:, at], copy_sems.at[part]
        )

    def arrived(part):
        @pl.when(pl.program_id(0) == 0)
        def _():
            copy(part).wait()

    @pl.when(pl.program_id(0) == 0)
    def _():
        for part in range(4):
            copy(part).start()

    arrived(0)
    gated = jnp.concatenate([own_ref[...], other_ref[...]], axis=1)
    resid = inputs_ref[...].astype(f32) + keep_ref[:, 2 * KW : 2 * KW + 1] * dot(
        gated, weight_ref[:, :mix_cols], NT
    )
    resid_ref[...] = resid
    inv_rms = lax.rsqrt(jnp.mean(resid * resid, -1, keepdims=True) + EPS)
    normed = (resid * inv_rms * gain_ref[...]).astype(bf16)
    normed_ref[...] = normed
    gate_at = slice(edges[1], edges[2])
    up_at = slice(edges[2], edges[3])
    down_at = slice(edges[3], edges[4])
    arrived(1)
    gate_pre = dot(normed, weight_ref[:, gate_at], NN)
    arrived(2)
    up_pre = dot(normed, weight_ref[:, up_at], NN)
    arrived(3)
    dhidden = dot(cot_ref[...], weight_ref[:, down_at], NN)
    sig = sigmoid(gate_pre)
    active = gate_pre * sig
    hidden = (active * up_pre).astype(bf16)
    dgate = (dhidden * up_pre * sig * (1.0 + gate_pre * (1.0 - sig))).astype(bf16)
    dup = (dhidden * active).astype(bf16)
    acts_ref[:, :ff_cols] = dgate
    acts_ref[:, ff_cols : 2 * ff_cols] = dup
    acts_ref[:, 2 * ff_cols :] = hidden
    dnormed_ref[...] = (
        dot(dgate, weight_ref[:, gate_at], NT) + dot(dup, weight_ref[:, up_at], NT)
    ).astype(bf16)
    summand_ref[...] = dot(hidden, weight_ref[:, down_at], NT).astype(bf16)


def kernel_cost(micros):
    return pl.CostEstimate(
        flops=int(micros * 4e9), bytes_accessed=int(micros * 8e6), transcendentals=0
    )


def whole(array):
    return pl.BlockSpec(array.shape, lambda c, r: (0,) * len(array.shape))


def mixer_forward(resets, proj, keep, filters, rates, head_gain, heads, start, stop, state):
    proj_width = proj.shape[1]
    row_count = stop - start
    chunks = row_count // ROWS
    rows = SUBS * ROWS
    first = start // rows
    conv_cols = 2 * heads * DK + heads * DV
    f32 = jnp.float32

    def rows_of(cols, dtype=f32):
        return jax.ShapeDtypeStruct((row_count, cols), dtype)

    def saved(rows, cols):
        return jax.ShapeDtypeStruct((chunks, heads, rows, cols), f32)

    def part_block(cols):
        return pl.BlockSpec((rows, cols), lambda c, r: (c + first, 0))

    def row_block(cols):
        return pl.BlockSpec((rows, cols), lambda c, r: (c, 0))

    def saved_block(rows, cols):
        return pl.BlockSpec((SUBS, heads, rows, cols), lambda c, r: (c, 0, 0, 0))

    before = max(start // 8 - 1, 0)
    return pl.pallas_call(
        partial(forward_kernel, heads, start // ROWS),
        grid_spec=pltpu.PrefetchScalarGridSpec(
            num_scalar_prefetch=1,
            grid=(chunks // SUBS,),
            in_specs=[
                part_block(proj_width),
                pl.BlockSpec((8, proj_width), lambda c, r: (before, 0)),
                whole(state),
                part_block(keep.shape[1]),
                whole(filters),
                whole(rates),
                whole(head_gain),
            ],
            out_specs=[
                row_block(heads * DV),
                row_block(conv_cols),
                row_block(heads * DV),
                saved_block(DK, DV),
                saved_block(ROWS, ROWS),
                saved_block(ROWS, DV + DK),
                saved_block(ROWS, DV),
                saved_block(ROWS, ROWS),
                saved_block(2 * ROWS, ROWS),
                whole(state),
            ],
            scratch_shapes=[
                pltpu.VMEM((rows + 8, conv_cols), f32),
                pltpu.VMEM((heads, DK, DV), f32),
            ],
        ),
        out_shape=[
            rows_of(heads * DV, jnp.bfloat16),
            rows_of(conv_cols),
            rows_of(heads * DV),
            saved(DK, DV),
            saved(ROWS, ROWS),
            saved(ROWS, DV + DK),
            saved(ROWS, DV),
            saved(ROWS, ROWS),
            saved(2 * ROWS, ROWS),
            jax.ShapeDtypeStruct(state.shape, f32),
        ],
        compiler_params=pltpu.CompilerParams(vmem_limit_bytes=60 << 20),
        cost_estimate=kernel_cost(24 * row_count / 1024),
        name="mixer_forward",
    )(resets, proj, proj, state, keep, filters, rates, head_gain)


def mixer_backward(
    resets,
    own,
    got,
    resid,
    cot,
    ffn_gain,
    out_weight,
    dstate,
    later,
    proj,
    keep,
    filters,
    rates,
    head_gain,
    saved,
    heads,
    start,
    filled,
):
    row_count = resid.shape[0]
    total_rows, proj_width = proj.shape
    chunks = row_count // ROWS
    first = start // ROWS
    conv_cols = 2 * heads * DK + heads * DV
    f32 = jnp.float32

    rows = BACK_SUBS * ROWS
    steps = row_count // rows
    first_block = start // rows

    def row_block(array):
        return pl.BlockSpec((rows, array.shape[1]), lambda c, r: (steps - 1 - c, 0))

    def part_block(array):
        return pl.BlockSpec(
            (rows, array.shape[1]), lambda c, r: (first_block + steps - 1 - c, 0)
        )

    def saved_block(array):
        return pl.BlockSpec(
            (BACK_SUBS,) + array.shape[1:], lambda c, r: (steps - 1 - c, 0, 0, 0)
        )

    dproj = jax.ShapeDtypeStruct((total_rows, proj_width), jnp.bfloat16)
    dfilter = jax.ShapeDtypeStruct((8, conv_cols), f32)
    dsmall = jax.ShapeDtypeStruct((8, DV), f32)
    dmix = jax.ShapeDtypeStruct(resid.shape, jnp.bfloat16)
    dresid = jax.ShapeDtypeStruct(resid.shape, f32)
    dffn_gain = jax.ShapeDtypeStruct((8, resid.shape[1]), f32)
    args = [resets, own, got, resid, cot, ffn_gain, out_weight, dstate, later]
    args += [proj, keep, filters, rates, head_gain, *saved]
    specs = [row_block(own), row_block(got), row_block(resid), part_block(cot), whole(ffn_gain)]
    specs += [
        pl.BlockSpec(
            (resid.shape[1], heads * DV), lambda c, r: (0, 0), pipeline_mode=pl.Buffered(1)
        )
    ]
    specs += [whole(dstate), whole(later), part_block(proj), part_block(keep)]
    specs += [whole(filters), whole(rates), whole(head_gain)]
    specs += [row_block(saved[0]), row_block(saved[1])]
    specs += [saved_block(array) for array in saved[2:]]
    aliases = {}
    if filled is not None:
        aliases = {len(args): 0}
        args.append(filled)
        specs.append(pl.BlockSpec(memory_space=pl.ANY))
    return pl.pallas_call(
        partial(backward_kernel, heads, first, chunks),
        grid_spec=pltpu.PrefetchScalarGridSpec(
            num_scalar_prefetch=1,
            grid=(steps,),
            in_specs=specs,
            out_specs=[
                part_block(dproj),
                whole(dfilter),
                whole(dsmall),
                row_block(dmix),
                row_block(dresid),
                whole(dffn_gain),
                whole(dstate),
                whole(later),
            ],
            scratch_shapes=[
                pltpu.VMEM((rows + 8, conv_cols), f32),
                pltpu.VMEM((heads, DK, DV), f32),
            ],
        ),
        out_shape=[
            dproj,
            dfilter,
            dsmall,
            dmix,
            dresid,
            dffn_gain,
            jax.ShapeDtypeStruct(dstate.shape, f32),
            jax.ShapeDtypeStruct(later.shape, f32),
        ],
        input_output_aliases=aliases,
        compiler_params=pltpu.CompilerParams(vmem_limit_bytes=60 << 20),
        cost_estimate=kernel_cost(30 * row_count / 1024),
        name="mixer_backward",
    )(*args)


def ffn_both_ways(own, other, inputs, cot_masked, keep, gain, weight, ff_cols, start, filled):
    row_count, own_cols = own.shape
    total_rows, width = inputs.shape
    rows = FFN_ROWS
    first = start // rows
    bf16 = jnp.bfloat16

    def whole(array):
        return pl.BlockSpec(array.shape, lambda c: (0, 0))

    def row_block(cols):
        return pl.BlockSpec((rows, cols), lambda c: (c, 0))

    def part_block(cols):
        return pl.BlockSpec((rows, cols), lambda c: (c + first, 0))

    args = [own, other, inputs, cot_masked, keep, gain, weight]
    specs = [row_block(own_cols), row_block(own_cols), part_block(width), part_block(width)]
    specs += [part_block(keep.shape[1]), whole(gain)]
    specs += [pl.BlockSpec(memory_space=pl.ANY)]
    aliases = {}
    if filled is not None:
        aliases = {len(args): 3, len(args) + 1: 4}
        args += list(filled)
        specs += [pl.BlockSpec(memory_space=pl.ANY)] * 2
    return pl.pallas_call(
        partial(ffn_kernel, 2 * own_cols, ff_cols),
        grid=(row_count // rows,),
        in_specs=specs,
        out_specs=[
            row_block(width),
            row_block(width),
            row_block(width),
            part_block(width),
            part_block(3 * ff_cols),
        ],
        out_shape=[
            jax.ShapeDtypeStruct((row_count, width), jnp.float32),
            jax.ShapeDtypeStruct((row_count, width), bf16),
            jax.ShapeDtypeStruct((row_count, width), bf16),
            jax.ShapeDtypeStruct((total_rows, width), bf16),
            jax.ShapeDtypeStruct((total_rows, 3 * ff_cols), bf16),
        ],
        scratch_shapes=[pltpu.VMEM(weight.shape, bf16), pltpu.SemaphoreType.DMA((4,))],
        input_output_aliases=aliases,
        compiler_params=pltpu.CompilerParams(vmem_limit_bytes=60 << 20),
        cost_estimate=kernel_cost(28 * row_count / 1024),
        name="ffn_both_ways",
    )(*args)


def grads_kernel(
    shard_rows,
    side_ref,
    normed_ref,
    dproj_ref,
    dmix_lo_ref,
    dmix_hi_ref,
    gated_lo_ref,
    gated_hi_ref,
    mine_a_ref,
    mine_b_ref,
    theirs_a_ref,
    theirs_b_ref,
    rate_ref,
):
    side = side_ref[0]
    normed = normed_ref[...]
    gate_cols = gated_lo_ref.shape[1]
    first_cols = mine_a_ref.shape[1]

    def put(grad, mine_ref, theirs_ref, cols):
        pairs = grad.reshape(-1, 2, shard_rows, grad.shape[-1])
        even = pairs[:, 0].reshape(-1, grad.shape[-1])
        odd = pairs[:, 1].reshape(-1, grad.shape[-1])
        mine_ref[:, cols] = jnp.where(side == 0, even, odd)
        theirs_ref[:, cols] = jnp.where(side == 0, odd, even).astype(jnp.bfloat16)

    put(dot(normed, dproj_ref[:, :first_cols], TN), mine_a_ref, theirs_a_ref, slice(None))
    put(
        dot(normed, dproj_ref[:, first_cols : first_cols + gate_cols], TN),
        mine_b_ref,
        theirs_b_ref,
        slice(0, gate_cols),
    )
    put(
        dot(dmix_lo_ref[...], gated_lo_ref[...], TN)
        + dot(dmix_hi_ref[...], gated_hi_ref[...], TN),
        mine_b_ref,
        theirs_b_ref,
        slice(gate_cols, 2 * gate_cols),
    )
    rate_ref[...] = dot(dproj_ref[:, first_cols + gate_cols :], normed, TN)[:8]


def mixer_weight_grads(side, normed, dproj, dmix_lo, dmix_hi, gated_lo, gated_hi, shard_rows):
    rows, width = normed.shape
    half_rows, v_cols = gated_lo.shape
    tile = 256
    first_cols = 2 * v_cols
    bf16 = jnp.bfloat16

    def column_block(array):
        return pl.BlockSpec((array.shape[0], tile), lambda c, r: (0, c))

    def row_block(cols):
        return pl.BlockSpec((tile // 2, cols), lambda c, r: (c, 0))

    return pl.pallas_call(
        partial(grads_kernel, shard_rows),
        grid_spec=pltpu.PrefetchScalarGridSpec(
            num_scalar_prefetch=1,
            grid=(width // tile,),
            in_specs=[
                column_block(normed),
                whole(dproj),
                column_block(dmix_lo),
                column_block(dmix_hi),
                whole(gated_lo),
                whole(gated_hi),
            ],
            out_specs=[
                row_block(first_cols),
                row_block(first_cols),
                row_block(first_cols),
                row_block(first_cols),
                pl.BlockSpec((8, tile), lambda c, r: (0, c)),
            ],
        ),
        out_shape=[
            jax.ShapeDtypeStruct((width // 2, first_cols), jnp.float32),
            jax.ShapeDtypeStruct((width // 2, first_cols), jnp.float32),
            jax.ShapeDtypeStruct((width // 2, first_cols), bf16),
            jax.ShapeDtypeStruct((width // 2, first_cols), bf16),
            jax.ShapeDtypeStruct((8, width), jnp.float32),
        ],
        compiler_params=pltpu.CompilerParams(vmem_limit_bytes=60 << 20),
        cost_estimate=kernel_cost(8),
        name="mixer_weight_grads",
    )(side, normed, dproj, dmix_lo, dmix_hi, gated_lo, gated_hi)


def ffn_grads_kernel(normed_ref, cot_ref, acts_ref, grads_ref):
    part = pl.program_id(0)

    @pl.when(part < 2)
    def _():
        grads_ref[...] = dot(normed_ref[...], acts_ref[...], TN).astype(jnp.bfloat16)

    @pl.when(part == 2)
    def _():
        grads_ref[...] = dot(cot_ref[...], acts_ref[...], TN).astype(jnp.bfloat16)


def ffn_weight_grads(normed, cot_masked, acts, ff_cols):
    rows, width = normed.shape

    def fixed(array):
        return pl.BlockSpec(array.shape, lambda c: (0, 0), pipeline_mode=pl.Buffered(1))

    return pl.pallas_call(
        ffn_grads_kernel,
        grid=(3,),
        in_specs=[
            fixed(normed),
            fixed(cot_masked),
            pl.BlockSpec((rows, ff_cols), lambda c: (0, c)),
        ],
        out_specs=pl.BlockSpec((width, ff_cols), lambda c: (0, c)),
        out_shape=jax.ShapeDtypeStruct((width, 3 * ff_cols), jnp.bfloat16),
        compiler_params=pltpu.CompilerParams(vmem_limit_bytes=60 << 20),
        cost_estimate=kernel_cost(0.1),
        name="ffn_weight_grads",
    )(normed, cot_masked, acts)


def swap_halves(array):
    return lax.ppermute(array, "mp", [(0, 1), (1, 0)])


def dp_total(array):
    count = lax.axis_size("dp")
    step = 1
    while step < count:
        array = array + lax.ppermute(array, "dp", [(i, i ^ step) for i in range(count)])
        step *= 2
    return array


def dp_swap(array, bit):
    count = lax.axis_size("dp")
    return lax.ppermute(array, "dp", [(i, i ^ bit) for i in range(count)])


def dp_gather(shard, cuts, first_held, then):
    index = lax.axis_index("dp")
    bits = [1 << i for i in reversed(range((lax.axis_size("dp") - 1).bit_length()))]
    pieces = [shard[None, :, start:stop] for start, stop in cuts]
    for at, bit in enumerate(bits):
        if at == 1:
            pieces, first_held = lax.optimization_barrier((pieces, first_held))
            then_held = then(first_held)
        if at == 3:
            pieces, then_held = lax.optimization_barrier((pieces, then_held))
        others = [dp_swap(piece, bit) for piece in pieces]
        upper = (index & bit) != 0
        pieces = [
            jnp.stack(
                [jnp.where(upper, other, piece), jnp.where(upper, piece, other)], axis=1
            ).reshape((-1,) + piece.shape[1:])
            for piece, other in zip(pieces, others)
        ]
    return [piece.reshape(-1, piece.shape[-1]) for piece in pieces], first_held, then_held


def scatter_first(kept, sent):
    return [
        (mine.astype(jnp.float32) + dp_swap(theirs, 1).astype(jnp.float32)).astype(mine.dtype)
        for mine, theirs in zip(kept, sent)
    ]


def scatter_step(pieces, at):
    index = lax.axis_index("dp")
    bits = [1 << i for i in range(1, (lax.axis_size("dp") - 1).bit_length())]
    orders = [bits, bits[1:2] + bits[:1] + bits[2:]]
    sums = []
    for piece, order in zip(pieces, orders):
        left = sorted(order[at:], reverse=True)
        bit = order[at]
        axis = left.index(bit)
        side = (index & bit) // bit
        cut = piece.reshape((2,) * len(left) + (-1, piece.shape[-1]))
        sent = lax.dynamic_index_in_dim(cut, 1 - side, axis, False).astype(jnp.bfloat16)
        mine = lax.dynamic_index_in_dim(cut, side, axis, False)
        total = mine.astype(jnp.float32) + dp_swap(sent, bit).astype(jnp.float32)
        sums.append(total.astype(piece.dtype).reshape(-1, piece.shape[-1]))
    return sums


def scatter_steps():
    return (lax.axis_size("dp") - 1).bit_length() - 1


def in_order(own, other, model_index, axis):
    first = jnp.where(model_index == 0, own, other)
    second = jnp.where(model_index == 0, other, own)
    return jnp.concatenate([first, second], axis=axis)


def on_device(
    block_input,
    seq_lengths,
    seq_owner,
    mix_gain,
    query_weight,
    key_weight,
    value_weight,
    gate_weight,
    decay_weight,
    beta_weight,
    query_filter,
    key_filter,
    value_filter,
    decay_log,
    decay_bias,
    head_gain,
    out_weight,
    ffn_gain,
    ffn_gate,
    ffn_up,
    ffn_down,
    cotangent,
):
    bf16 = jnp.bfloat16
    f32 = jnp.float32
    local_rows, width = block_input.shape
    dp_index = lax.axis_index("dp")
    model_count = lax.axis_size("mp")
    model_index = lax.axis_index("mp")
    row_count = local_rows * model_count
    keep_masks, resets, valid_rows = layout(seq_lengths, seq_owner, dp_index, row_count)
    valid_all = valid_rows[:, None]
    heads_local = decay_log.shape[0] // model_count
    qk_cols = heads_local * DK
    v_cols = heads_local * DV
    ff_cols = ffn_gate.shape[1]
    shard_rows = query_weight.shape[0]
    proj_cols = 2 * qk_cols + 2 * v_cols

    def own_columns(array, col_count):
        return lax.dynamic_slice_in_dim(array, model_index * col_count, col_count, array.ndim - 1)

    def own_shard(array):
        return lax.dynamic_slice_in_dim(array, dp_index * shard_rows, shard_rows, 0)

    small_weight = jnp.concatenate(
        [own_columns(decay_weight, heads_local), own_columns(beta_weight, heads_local)], axis=1
    )
    small_weight = jnp.pad(small_weight, ((0, 0), (0, 128 - 2 * heads_local)))
    shard_mix = jnp.concatenate(
        [query_weight, key_weight, value_weight, gate_weight, own_shard(small_weight)], axis=1
    )
    half = proj_cols // 256 * 128
    out_rows = out_weight.T
    shard_ffn = jnp.concatenate([ffn_gate, ffn_up, ffn_down.T], axis=1)
    out_other = swap_halves(out_rows)
    input_other = swap_halves(block_input)
    mix_pieces, (out_other, out_rows, shard_ffn), (input_other, cot_held) = dp_gather(
        shard_mix,
        ((0, half), (half, shard_mix.shape[1])),
        (out_other, out_rows, shard_ffn),
        lambda held: (input_other, cotangent),
    )
    mix_weight = jnp.concatenate(mix_pieces, axis=1)
    shard_rest = jnp.concatenate([out_rows, out_other, shard_ffn], axis=1)
    rest_weight = lax.all_gather(shard_rest, "dp", axis=0, tiled=True)
    cot_other = swap_halves(cot_held)

    filters = jnp.concatenate(
        [
            own_columns(query_filter, qk_cols),
            own_columns(key_filter, qk_cols),
            own_columns(value_filter, v_cols),
        ],
        axis=1,
    )
    filters = jnp.pad(filters, ((0, 8 - KW), (0, 0)))
    rates = jnp.stack(
        [own_columns(decay_bias, heads_local), -jnp.exp(own_columns(decay_log, heads_local))]
    )
    rates = jnp.pad(rates, ((0, 6), (0, 128 - heads_local)))
    gain_row = head_gain[None]
    restarts = resets.astype(jnp.int32)
    later_masks = [
        jnp.concatenate([keep_masks[offset, offset:], jnp.ones((offset,), f32)])
        for offset in range(KW)
    ]
    keep_cols = jnp.stack(
        [keep_masks[offset] for offset in range(KW)] + later_masks + [valid_rows] * 8, axis=1
    )
    inputs_b = in_order(block_input, input_other, model_index, 0)
    inputs_f = inputs_b.astype(f32)
    cot_all = in_order(cotangent, cot_other, model_index, 0)
    normed1, inv_rms1 = rms_forward(inputs_f)
    mixed_in = (normed1 * mix_gain).astype(bf16)
    proj = jnp.dot(mixed_in, mix_weight, preferred_element_type=f32)
    cuts = (qk_cols, 2 * qk_cols, 2 * qk_cols + v_cols, proj_cols)
    middle = row_count // 2
    zero_state = jnp.zeros((heads_local, DK, DV), f32)
    small_args = (keep_cols, filters, rates, gain_row)
    gated_lo, *saved_lo, carried = mixer_forward(
        restarts, proj, *small_args, heads_local, 0, middle, zero_state
    )
    cot_masked = cot_all * valid_all.astype(bf16)
    ffn_row = ffn_gain[None]
    carried, cot_all, cot_masked, inputs_b = lax.optimization_barrier(
        (carried, cot_all, cot_masked, inputs_b)
    )
    gated_hi, *saved_hi, _ = mixer_forward(
        restarts, proj, *small_args, heads_local, middle, row_count, carried
    )
    other_lo = swap_halves(gated_lo)
    gated_sent, other_lo = lax.optimization_barrier((gated_hi, other_lo))
    other_hi = swap_halves(gated_sent)
    ffn_args = (inputs_b, cot_masked, keep_cols, ffn_row, rest_weight, ff_cols)
    resid_hi, dnormed_hi, summand_hi, *filled = ffn_both_ways(
        gated_hi, other_hi, *ffn_args, middle, None
    )
    resid_lo, dnormed_lo, summand_lo, ffn_in, acts = ffn_both_ways(
        gated_lo, other_lo, *ffn_args, 0, filled
    )
    got_hi, dnormed_lo = lax.optimization_barrier((swap_halves(dnormed_hi), dnormed_lo))
    got_lo = swap_halves(dnormed_lo)
    core_side = (dp_index & 1).reshape(1)
    rest_grads = ffn_weight_grads(ffn_in, cot_masked, acts, ff_cols)
    got_hi, _ = lax.optimization_barrier((got_hi, rest_grads))
    ffn_shard = lax.psum_scatter(rest_grads, "dp", scatter_dimension=0, tiled=True)

    def own_half(array):
        return lax.dynamic_slice_in_dim(array, model_index * local_rows, local_rows, 0)

    def other_half(array):
        return lax.dynamic_slice_in_dim(array, (1 - model_index) * local_rows, local_rows, 0)

    def own_of(low, high):
        return jnp.where(model_index == 0, low, high)

    zero_rows = jnp.zeros((8, proj_cols - v_cols), f32)
    proj_grad, filter_hi, small_hi, dmix_hi, dresid_hi, ffn_gain_hi, carried, later = (
        mixer_backward(
            restarts,
            dnormed_hi,
            got_hi,
            resid_hi,
            cot_all,
            ffn_row,
            rest_weight,
            zero_state,
            zero_rows,
            proj,
            *small_args,
            saved_hi,
            heads_local,
            middle,
            None,
        )
    )
    summand_sent, got_lo, proj_grad = lax.optimization_barrier(
        (own_of(summand_hi, summand_lo), got_lo, proj_grad)
    )
    proj_grad, filter_lo, small_lo, dmix_lo, dresid_lo, ffn_gain_lo, _, _ = mixer_backward(
        restarts,
        dnormed_lo,
        got_lo,
        resid_lo,
        cot_all,
        ffn_row,
        rest_weight,
        carried,
        later,
        proj,
        *small_args,
        saved_lo,
        heads_local,
        0,
        proj_grad,
    )
    summand_got, proj_grad, dmix_lo, filter_lo, small_lo, dresid_lo, ffn_gain_lo = (
        lax.optimization_barrier(
            (
                swap_halves(summand_sent),
                proj_grad,
                dmix_lo,
                filter_lo,
                small_lo,
                dresid_lo,
                ffn_gain_lo,
            )
        )
    )
    ffn_sum = own_of(summand_lo, summand_hi).astype(f32) + summand_got.astype(f32)
    block_output = (own_of(resid_lo, resid_hi) + own_half(valid_all) * ffn_sum).astype(bf16)
    filter_grads = filter_lo + filter_hi
    small_grads = small_lo + small_hi
    ffn_gain_part = ffn_gain_lo[0] + ffn_gain_hi[0]
    *grad_pieces, rate_grads = mixer_weight_grads(
        core_side,
        mixed_in,
        proj_grad,
        dmix_lo,
        dmix_hi,
        gated_lo,
        gated_hi,
        shard_rows,
    )
    rate_grads = rate_grads[: 2 * heads_local]
    mix_sums = scatter_first(grad_pieces[:2], grad_pieces[2:])
    proj_grad, mix_sums, rate_grads = lax.optimization_barrier(
        (proj_grad, mix_sums, rate_grads)
    )
    mix_sums = scatter_step(mix_sums, 0)
    mix_in_part = against(proj_grad, mix_weight)
    mix_gain_part = jnp.sum(mix_in_part * normed1, 0)
    common = jnp.concatenate(
        [mix_gain_part, ffn_gain_part, small_grads[0], jnp.zeros((width - DV,), f32)]
    ).reshape(3, width)
    tail_row = jnp.concatenate(
        [small_grads[1, : 2 * heads_local], jnp.zeros((width - 2 * heads_local,), f32)]
    )
    split_rows = jnp.concatenate(
        [
            rate_grads,
            filter_grads[:KW, : cuts[0]].reshape(-1, width),
            filter_grads[:KW, cuts[0] : cuts[1]].reshape(-1, width),
            filter_grads[:KW, cuts[1] : cuts[2]].reshape(-1, width),
            tail_row[None],
        ],
        axis=0,
    )
    mix_in_sent = other_half(mix_in_part).astype(bf16)

    mix_in_got = swap_halves(mix_in_sent)
    mix_sums, small_sums = lax.optimization_barrier(
        (mix_sums, jnp.concatenate([common, split_rows], axis=0))
    )
    totals = dp_total(small_sums)
    totals, mix_in_got = lax.optimization_barrier((totals, mix_in_got))
    totals_other = swap_halves(totals)
    for step in range(1, scatter_steps()):
        if step == 2:
            mix_sums, totals, totals_other, mix_in_got = lax.optimization_barrier(
                (mix_sums, totals, totals_other, mix_in_got)
            )
        mix_sums = scatter_step(mix_sums, step)
    mix_shards = mix_sums
    mix_in_sum = own_half(mix_in_part) + mix_in_got.astype(f32)
    input_grad = own_of(dresid_lo, dresid_hi) + rms_backward(
        mix_in_sum * mix_gain, own_half(normed1), own_half(inv_rms1)
    )
    common = totals[:3] + totals_other[:3]
    lower = jnp.where(model_index == 0, totals, totals_other)[3:]
    upper = jnp.where(model_index == 0, totals_other, totals)[3:]

    def joined(start, rows, cols):
        return jnp.concatenate(
            [
                lower[start : start + rows].reshape(-1, cols),
                upper[start : start + rows].reshape(-1, cols),
            ],
            axis=1,
        )

    q_rows = KW * qk_cols // width
    v_rows = KW * v_cols // width
    at_q = 2 * heads_local
    at_k = at_q + q_rows
    at_v = at_k + q_rows
    at_tail = at_v + v_rows

    def rate_weight_grad(start):
        return jnp.concatenate(
            [lower[start : start + heads_local], upper[start : start + heads_local]], axis=0
        ).T

    def rate_grad(start):
        return jnp.concatenate(
            [
                lower[at_tail, start : start + heads_local],
                upper[at_tail, start : start + heads_local],
            ]
        )

    ffn_shard = ffn_shard.astype(f32)
    return (
        block_output,
        input_grad,
        common[0],
        mix_shards[0][:, : cuts[0]],
        mix_shards[0][:, cuts[0] : cuts[1]],
        mix_shards[0][:, cuts[1] :],
        mix_shards[1][:, :v_cols],
        rate_weight_grad(0),
        rate_weight_grad(heads_local),
        joined(at_q, q_rows, qk_cols),
        joined(at_k, q_rows, qk_cols),
        joined(at_v, v_rows, v_cols),
        rate_grad(0),
        rate_grad(heads_local),
        common[2, :DV],
        mix_shards[1][:, v_cols:].T,
        common[1],
        ffn_shard[:, :ff_cols],
        ffn_shard[:, ff_cols : 2 * ff_cols],
        ffn_shard[:, 2 * ff_cols :].T,
    )


def solution(mesh):
    in_specs = (
        P(("dp", "mp"), None),
        P(),
        P(),
        P(),
        P("dp", "mp"),
        P("dp", "mp"),
        P("dp", "mp"),
        P("dp", "mp"),
        P(),
        P(),
        P(),
        P(),
        P(),
        P(),
        P(),
        P(),
        P("mp", "dp"),
        P(),
        P("dp", "mp"),
        P("dp", "mp"),
        P("mp", "dp"),
        P(("dp", "mp"), None),
    )
    out_specs = (
        P(("dp", "mp"), None),
        P(("dp", "mp"), None),
        P(),
        P("dp", "mp"),
        P("dp", "mp"),
        P("dp", "mp"),
        P("dp", "mp"),
        P(),
        P(),
        P(),
        P(),
        P(),
        P(),
        P(),
        P(),
        P("mp", "dp"),
        P(),
        P("dp", "mp"),
        P("dp", "mp"),
        P("mp", "dp"),
    )
    return jax.shard_map(
        on_device, mesh=mesh, in_specs=in_specs, out_specs=out_specs, check_vma=False
    )
```

```python
from functools import partial
import math

import jax
import jax.numpy as jnp
from jax import lax
from jax.experimental import pallas as pl
from jax.experimental.pallas import tpu as pltpu
from jax.sharding import PartitionSpec as P

DK = 128
DV = 256
KW = 4
SPAN = 64


EPS = 1e-06


def layout(seq_lengths, seq_owner, device, row_count):
    owned = seq_owner == device
    own_lengths = jnp.where(owned, seq_lengths, 0)
    offsets = jnp.cumsum(own_lengths) - own_lengths
    loaded = jnp.sum(own_lengths)
    span_starts = jnp.arange(row_count // SPAN, dtype=jnp.int32) * SPAN
    begins = jnp.any(
        (offsets[None, :] == span_starts[:, None]) & (own_lengths[None, :] > 0), axis=1
    )
    resets = begins | (span_starts == loaded)
    within = jnp.arange(SPAN, dtype=jnp.int32)
    keep_masks = jnp.stack(
        [
            jnp.logical_not(resets[:, None] & (within[None, :] < offset)).reshape(row_count)
            for offset in range(KW)
        ]
    ).astype(jnp.float32)
    valid_rows = (jnp.arange(row_count, dtype=jnp.int32) < loaded).astype(jnp.float32)
    return (keep_masks, resets, valid_rows)


def across_rows(left, right):
    return lax.dot_general(
        left, right, (((0,), (0,)), ((), ())), preferred_element_type=jnp.float32
    )


def against(left, right):
    return lax.dot_general(
        left, right, (((1,), (1,)), ((), ())), preferred_element_type=jnp.float32
    )


def rms_forward(values):
    inv_rms = lax.rsqrt(jnp.mean(values * values, -1, keepdims=True) + EPS)
    return (values * inv_rms, inv_rms)


def rms_backward(upstream, normed, inv_rms):
    return inv_rms * (upstream - normed * jnp.mean(upstream * normed, -1, keepdims=True))


ROWS = 128
NN = ((1,), (0,))
NT = ((1,), (1,))
TN = ((0,), (0,))
FINE_GRAM = True
FINE_INVERSE = True
FINE_MERGE = True
SUBS = 2
FFN_ROWS = 256
FINE_APPLY = True
FINE_STATE = True
FINE_BACK = (True,) * 10
BACK_SUBS = 2


def dot(left, right, dims):
    return lax.dot_general(left, right, (dims, ((), ())), preferred_element_type=jnp.float32)


def high_low(values):
    high = values.astype(jnp.bfloat16)
    return high, (values - high.astype(jnp.float32)).astype(jnp.bfloat16)


def product(left, right, dims, fine=False):
    if not fine:
        return dot(left.astype(jnp.bfloat16), right.astype(jnp.bfloat16), dims)
    left_high, left_low = high_low(left)
    right_high, right_low = high_low(right)
    (left_axis,), (right_axis,) = dims
    depth = right.shape[right_axis]
    count = right.shape[1 - right_axis]
    if depth <= 128:
        both = jnp.concatenate([left_high, left_low], axis=left_axis)
        if count <= 128:
            wide = jnp.concatenate([right_high, right_low], axis=1 - right_axis)
            part = jnp.concatenate([right_high, jnp.zeros_like(right_low)], axis=1 - right_axis)
            result = dot(both, jnp.concatenate([wide, part], axis=right_axis), dims)
            return result[:, :count] + result[:, count:]
        return dot(both, jnp.concatenate([right_high, right_high], axis=right_axis), dims) + dot(
            left_high, right_low, dims
        )
    if count <= 128:
        wide = jnp.concatenate([right_high, right_low], axis=1 - right_axis)
        result = dot(left_high, wide, dims)
        return result[:, :count] + (result[:, count:] + dot(left_low, right_high, dims))
    return dot(left_high, right_high, dims) + (
        dot(left_high, right_low, dims) + dot(left_low, right_high, dims)
    )


def summed_by(mask, values, dims=NN):
    high, low = high_low(values)
    return dot(mask, high, dims) + dot(mask, low, dims)


def chunk_masks(resets_ref, chunk):
    first = 1.0 - resets_ref[2 * chunk].astype(jnp.float32)
    second = 1.0 - resets_ref[2 * chunk + 1].astype(jnp.float32)
    row = lax.broadcasted_iota(jnp.int32, (ROWS, ROWS), 0)
    col = lax.broadcasted_iota(jnp.int32, (ROWS, ROWS), 1)
    late = row >= SPAN
    reached = jnp.where(late, first * second, first)
    reaching = jnp.where(late, 1.0, second)
    joined = jnp.where(late & (col < SPAN), second, 1.0)
    return row, col, reached, reaching, joined, first * second


def unit_lower_inverses(couplings, row, col):
    eye = jnp.where(row == col, 1.0, 0.0)
    base = 16
    near = (row // base) == (col // base)
    powered = [jnp.where(near, coupling, 0.0) for coupling in couplings]
    inverses = [eye - power for power in powered]
    size = 2
    while size < base:
        powered = [product(power, power, NN, FINE_INVERSE) for power in powered]
        inverses = [
            inverse + product(inverse, power, NN, FINE_INVERSE)
            for inverse, power in zip(inverses, powered)
        ]
        size *= 2
    while base < ROWS:
        wide = 2 * base
        linked = ((row // wide) == (col // wide)) & ((row // base) != (col // base))
        steps = [
            product(jnp.where(linked, coupling, 0.0), inverse, NN, FINE_MERGE)
            for coupling, inverse in zip(couplings, inverses)
        ]
        inverses = [
            inverse - product(inverse, step, NN, FINE_MERGE)
            for inverse, step in zip(inverses, steps)
        ]
        base = wide
    return inverses


def sigmoid(values):
    return 1.0 / (1.0 + jnp.exp(-values))


def lane_sum(values):
    return jnp.sum(values, -1, keepdims=True)


def forward_kernel(
    heads,
    base,
    resets_ref,
    proj_ref,
    before_ref,
    state_in_ref,
    keep_ref,
    filter_ref,
    rates_ref,
    gain_ref,
    gated_ref,
    conv_ref,
    mixed_ref,
    state_ref,
    inverse_ref,
    parts_ref,
    written_ref,
    factor_ref,
    grams_ref,
    state_out_ref,
    rows_buf,
    state_buf,
):
    step = pl.program_id(0)
    qk = heads * DK
    conv_cols = 2 * qk + heads * DV
    proj_cols = conv_cols + heads * DV
    rows = SUBS * ROWS

    @pl.when(step == 0)
    def _():
        if base == 0:
            rows_buf[0:8, :] = jnp.zeros((8, conv_cols), jnp.float32)
        else:
            rows_buf[0:8, :] = before_ref[:, :conv_cols]
        state_buf[...] = state_in_ref[...]

    rows_buf[8 : 8 + rows, :] = proj_ref[:, :conv_cols]
    conv = rows_buf[8 : 8 + rows, :] * filter_ref[0:1, :]
    for offset in range(1, KW):
        conv = conv + rows_buf[8 - offset : 8 - offset + rows, :] * (
            filter_ref[offset : offset + 1, :] * keep_ref[:, offset : offset + 1]
        )
    rows_buf[0:8, :] = rows_buf[rows : rows + 8, :]
    conv_ref[...] = conv

    rate = proj_ref[:, proj_cols : proj_cols + 128]
    shifted = rate + rates_ref[0:1, :]
    decay_all = rates_ref[1:2, :] * (
        jnp.maximum(shifted, 0.0) + jnp.log1p(jnp.exp(-jnp.abs(shifted)))
    )
    beta_all = sigmoid(rate)
    units = [(sub, head) for sub in range(SUBS) for head in range(heads)]
    prepared = []
    for sub, head in units:
        row, col, reached, reaching, joined, passed = chunk_masks(
            resets_ref, base + step * SUBS + sub
        )
        lower = jnp.where(row >= col, 1.0, 0.0)
        at = slice(sub * ROWS, (sub + 1) * ROWS)
        decay = jnp.broadcast_to(decay_all[at, head : head + 1], (ROWS, ROWS))
        beta = beta_all[at, heads + head : heads + head + 1]
        sums = summed_by(
            lower.astype(jnp.bfloat16),
            jnp.concatenate([jnp.where(row > col, decay, 0.0), decay], axis=1),
        )
        factor = jnp.exp(sums[:, :ROWS]) * (lower * joined)
        total = sums[:, ROWS:]
        total_end = total[ROWS - 1 : ROWS, :]
        grown = jnp.exp(total) * reached
        tail = jnp.exp(total_end - total) * reaching
        end_decay = jnp.exp(total_end[:, :1]) * passed

        conv_q = conv[at, head * DK : (head + 1) * DK]
        conv_k = conv[at, qk + head * DK : qk + (head + 1) * DK]
        conv_v = conv[at, 2 * qk + head * DV : 2 * qk + (head + 1) * DV]
        query = conv_q * sigmoid(conv_q)
        query = query * (lax.rsqrt(lane_sum(query * query) + EPS) * (1.0 / math.sqrt(DK)))
        key = conv_k * sigmoid(conv_k)
        key = key * lax.rsqrt(lane_sum(key * key) + EPS)
        value = conv_v * sigmoid(conv_v)

        grams = product(jnp.concatenate([key, query], axis=0), key, NT, FINE_GRAM)
        coupling = jnp.where(row > col, factor * grams[:ROWS] * beta, 0.0)
        scaled = jnp.concatenate([beta * value, (beta * grown) * key], axis=1)
        factor_ref[sub, head] = factor
        grams_ref[sub, head] = grams
        prepared.append(
            (coupling, scaled, grown * query, factor * grams[ROWS:], tail * key, end_decay)
        )
    row = lax.broadcasted_iota(jnp.int32, (ROWS, ROWS), 0)
    col = lax.broadcasted_iota(jnp.int32, (ROWS, ROWS), 1)
    inverses = unit_lower_inverses([entry[0] for entry in prepared], row, col)
    for (sub, head), inverse, entry in zip(units, inverses, prepared):
        _, scaled, query_grown, mixing, key_tail, end_decay = entry
        at = slice(sub * ROWS, (sub + 1) * ROWS)
        parts = product(inverse, scaled, NN, FINE_APPLY)
        state = state_buf[head]
        from_state = product(
            jnp.concatenate([parts[:, DV:], query_grown], axis=0), state, NN, FINE_STATE
        )
        written = parts[:, :DV] - from_state[:ROWS]
        mixed = from_state[ROWS:] + product(mixing, written, NN, FINE_STATE)
        state_buf[head] = end_decay * state + product(key_tail, written, TN, FINE_STATE)

        gate = proj_ref[at, conv_cols + head * DV : conv_cols + (head + 1) * DV]
        normed = mixed * lax.rsqrt(lane_sum(mixed * mixed) * (1.0 / DV) + EPS)
        gated_ref[at, head * DV : (head + 1) * DV] = (
            normed * gain_ref[...] * (gate * sigmoid(gate))
        ).astype(jnp.bfloat16)
        mixed_ref[at, head * DV : (head + 1) * DV] = mixed
        state_ref[sub, head] = state
        inverse_ref[sub, head] = inverse
        parts_ref[sub, head] = parts
        written_ref[sub, head] = written

    @pl.when(step == pl.num_programs(0) - 1)
    def _():
        state_out_ref[...] = state_buf[...]


def backward_kernel(
    heads,
    base,
    chunks,
    resets_ref,
    own_ref,
    got_ref,
    resid_ref,
    cot_ref,
    ffn_gain_ref,
    out_weight_ref,
    dstate_in_ref,
    later_ref,
    proj_ref,
    keep_ref,
    filter_ref,
    rates_ref,
    gain_ref,
    conv_ref,
    mixed_ref,
    state_ref,
    inverse_ref,
    parts_ref,
    written_ref,
    factor_ref,
    grams_ref,
    *tail_refs,
):
    (
        dproj_ref,
        dfilter_ref,
        dsmall_ref,
        dmix_ref,
        dresid_ref,
        dffn_gain_ref,
        dstate_out_ref,
        first_ref,
        rows_buf,
        dstate_buf,
    ) = tail_refs[-10:]
    step = pl.program_id(0)
    last_step = pl.num_programs(0) - 1
    rows = BACK_SUBS * ROWS
    qk = heads * DK
    conv_cols = 2 * qk + heads * DV
    proj_cols = conv_cols + heads * DV

    @pl.when(step == 0)
    def _():
        rows_buf[rows : rows + 8, :] = later_ref[...]
        dstate_buf[...] = dstate_in_ref[...]
        dffn_gain_ref[...] = jnp.zeros_like(dffn_gain_ref)
        dfilter_ref[...] = jnp.zeros_like(dfilter_ref)
        dsmall_ref[...] = jnp.zeros_like(dsmall_ref)

    resid = resid_ref[...]
    inv_resid = lax.rsqrt(jnp.mean(resid * resid, -1, keepdims=True) + EPS)
    resid_normed = resid * inv_resid
    ffn_in_own = own_ref[...].astype(jnp.float32)
    dffn_gain_ref[0:1, :] += jnp.sum(ffn_in_own * resid_normed, 0, keepdims=True)
    scaled_up = (ffn_in_own + got_ref[...].astype(jnp.float32)) * ffn_gain_ref[...]
    dresid = cot_ref[...].astype(jnp.float32) + inv_resid * (
        scaled_up - resid_normed * jnp.mean(scaled_up * resid_normed, -1, keepdims=True)
    )
    dresid_ref[...] = dresid
    dmix = (dresid * keep_ref[:, 2 * KW : 2 * KW + 1]).astype(jnp.bfloat16)
    dmix_ref[...] = dmix
    dgated = dot(dmix, out_weight_ref[...], NN)
    rate = proj_ref[:, proj_cols : proj_cols + 128]
    shifted = rate + rates_ref[0:1, :]
    decay_all = rates_ref[1:2, :] * (
        jnp.maximum(shifted, 0.0) + jnp.log1p(jnp.exp(-jnp.abs(shifted)))
    )
    slope_all = rates_ref[1:2, :] * sigmoid(shifted)
    beta_all = sigmoid(rate)
    row = lax.broadcasted_iota(jnp.int32, (ROWS, ROWS), 0)
    col = lax.broadcasted_iota(jnp.int32, (ROWS, ROWS), 1)
    lower_b = jnp.where(row >= col, 1.0, 0.0).astype(jnp.bfloat16)
    upper_b = jnp.where(row <= col, 1.0, 0.0).astype(jnp.bfloat16)
    lane = lax.broadcasted_iota(jnp.int32, (ROWS, 128), 1)
    dgain = jnp.zeros((1, DV), jnp.float32)
    units = [(sub, head) for sub in reversed(range(BACK_SUBS)) for head in range(heads)]
    prepared = []
    for sub, head in units:
        at = slice(sub * ROWS, (sub + 1) * ROWS)
        chunk = base + chunks - BACK_SUBS * (step + 1) + sub
        _, _, reached, reaching, _, passed = chunk_masks(resets_ref, chunk)
        decay = jnp.broadcast_to(decay_all[at, head : head + 1], (ROWS, ROWS))
        total = summed_by(lower_b, decay)
        total_end = total[ROWS - 1 : ROWS, :]
        grown = jnp.exp(total) * reached
        tail = jnp.exp(total_end - total) * reaching
        end_decay = jnp.exp(total_end[:, :1]) * passed

        v_at = slice(head * DV, (head + 1) * DV)
        gate_at = slice(conv_cols + head * DV, conv_cols + (head + 1) * DV)
        conv_q = conv_ref[at, head * DK : (head + 1) * DK]
        conv_k = conv_ref[at, qk + head * DK : qk + (head + 1) * DK]
        query = conv_q * sigmoid(conv_q)
        inv_q = lax.rsqrt(lane_sum(query * query) + EPS)
        query = query * (inv_q * (1.0 / math.sqrt(DK)))
        key = conv_k * sigmoid(conv_k)
        inv_k = lax.rsqrt(lane_sum(key * key) + EPS)
        key = key * inv_k

        mixed = mixed_ref[at, v_at]
        inv_o = lax.rsqrt(lane_sum(mixed * mixed) * (1.0 / DV) + EPS)
        normed = mixed * inv_o
        gate = proj_ref[at, gate_at]
        sig_g = sigmoid(gate)
        upstream = dgated[at, v_at]
        up_normed = upstream * normed
        dgain = dgain + jnp.sum(up_normed * (gate * sig_g), 0, keepdims=True)
        dproj_ref[at, gate_at] = (
            up_normed * gain_ref[...] * (sig_g * (1.0 + gate * (1.0 - sig_g)))
        ).astype(jnp.bfloat16)
        dnormed = upstream * gain_ref[...] * (gate * sig_g)
        dmixed = inv_o * (dnormed - normed * (lane_sum(dnormed * normed) * (1.0 / DV)))
        mixing = factor_ref[sub, head] * grams_ref[sub, head, ROWS:]
        within = product(mixing, dmixed, TN, FINE_BACK[0])
        dmixing = product(dmixed, written_ref[sub, head], NT, FINE_BACK[3])
        prepared.append(
            (decay, grown, tail, end_decay, query, inv_q, key, inv_k, dmixed, within, dmixing)
        )
    stepped = []
    for (sub, head), entry in zip(units, prepared):
        decay, grown, tail, end_decay, query, inv_q, key, inv_k, dmixed, within, dmixing = entry
        state = state_ref[sub, head]
        dstate = dstate_buf[head]
        dwritten = within + product(tail * key, dstate, NN, FINE_BACK[1])
        dkey_tail = product(written_ref[sub, head], dstate, NT, FINE_BACK[4])
        end_grad = end_decay * lane_sum(jnp.sum(state * dstate, 0, keepdims=True))
        stacked = jnp.concatenate([dmixed, -dwritten], axis=0)
        dstate_buf[head] = end_decay * dstate + product(
            jnp.concatenate([grown * query, parts_ref[sub, head, :, DV:]], axis=0),
            stacked,
            TN,
            FINE_BACK[5],
        )
        stepped.append((dwritten, dkey_tail, end_grad, stacked))
    drates = {sub: jnp.zeros((ROWS, 128), jnp.float32) for sub in range(BACK_SUBS)}
    dsums = jnp.zeros((ROWS, 128), jnp.float32)
    throughs = [
        product(entry[3], state_ref[sub, head], NT, FINE_BACK[2])
        for (sub, head), entry in zip(units, stepped)
    ]
    solveds = [
        product(
            inverse_ref[sub, head],
            jnp.concatenate([entry[0], through[ROWS:]], axis=1),
            TN,
            FINE_BACK[6],
        )
        for (sub, head), entry, through in zip(units, stepped, throughs)
    ]
    dcouplings = [
        product(solved, parts_ref[sub, head], NT, FINE_BACK[7])
        for (sub, head), solved in zip(units, solveds)
    ]
    for at_unit, (sub, head) in enumerate(units):
        decay, grown, tail, _, query, inv_q, key, inv_k, _, _, dmixing = prepared[at_unit]
        _, dkey_tail, end_grad, _ = stepped[at_unit]
        solved = solveds[at_unit]
        at = slice(sub * ROWS, (sub + 1) * ROWS)
        q_at = slice(head * DK, (head + 1) * DK)
        k_at = slice(qk + head * DK, qk + (head + 1) * DK)
        value_at = slice(2 * qk + head * DV, 2 * qk + (head + 1) * DV)
        beta = beta_all[at, heads + head : heads + head + 1]
        factor = factor_ref[sub, head]
        conv_q = conv_ref[at, q_at]
        conv_k = conv_ref[at, k_at]
        conv_v = conv_ref[at, value_at]
        sig_q = sigmoid(conv_q)
        sig_k = sigmoid(conv_k)
        sig_v = sigmoid(conv_v)
        value = conv_v * sig_v
        query_grown = grown * query
        key_tail = tail * key
        dquery_grown = throughs[at_unit][:ROWS]
        dcoupling = jnp.where(row > col, -dcouplings[at_unit] * factor, 0.0)
        dcoupling_gram = dcoupling * grams_ref[sub, head, :ROWS]
        dbeta = lane_sum(dcoupling_gram)
        dgap = beta * dcoupling_gram + dmixing * (factor * grams_ref[sub, head, ROWS:])
        dgrams = jnp.concatenate([beta * dcoupling, dmixing * factor], axis=0)
        by_key = product(dgrams, key, NN, FINE_BACK[8])
        dkey = by_key[:ROWS] + product(
            dgrams, jnp.concatenate([key, query], axis=0), TN, FINE_BACK[9]
        )
        dquery = by_key[ROWS:] + grown * dquery_grown
        dvalue_scaled = solved[:, :DV]
        dkey_scaled = solved[:, DV:]
        scaled_rows = lane_sum(dkey_scaled * (grown * key))
        dbeta = dbeta + lane_sum(dvalue_scaled * value) + scaled_rows
        tail_rows = lane_sum(dkey_tail * key_tail)
        dkey = dkey + tail * dkey_tail + (beta * grown) * dkey_scaled
        dtotal = lane_sum(dquery_grown * query_grown) + beta * scaled_rows - tail_rows
        sums = summed_by(
            upper_b, jnp.concatenate([dgap, jnp.broadcast_to(dtotal, (ROWS, ROWS))], axis=1)
        )
        ddecay = (
            lane_sum(jnp.where(col < row, sums[:, :ROWS], 0.0))
            + sums[:, ROWS : ROWS + 1]
            + (end_grad + jnp.sum(tail_rows, 0, keepdims=True))
        )
        dshifted = ddecay * slope_all[at, head : head + 1]
        drates[sub] = (
            drates[sub]
            + jnp.where(lane == head, dshifted, 0.0)
            + jnp.where(lane == heads + head, dbeta * (beta * (1.0 - beta)), 0.0)
        )
        dsums = dsums + jnp.where(lane == head, ddecay * decay, 0.0)
        dsums = dsums + jnp.where(lane == heads + head, dshifted, 0.0)

        unit = query * math.sqrt(DK)
        dunit = dquery * (1.0 / math.sqrt(DK))
        dsilu = inv_q * (dunit - unit * lane_sum(dunit * unit))
        rows_buf[at, q_at] = dsilu * (sig_q * (1.0 + conv_q * (1.0 - sig_q)))
        dsilu = inv_k * (dkey - key * lane_sum(dkey * key))
        rows_buf[at, k_at] = dsilu * (sig_k * (1.0 + conv_k * (1.0 - sig_k)))
        rows_buf[at, value_at] = (beta * dvalue_scaled) * (
            sig_v * (1.0 + conv_v * (1.0 - sig_v))
        )

    signal = proj_ref[:, :conv_cols]
    shifted_grad = rows_buf[0:rows, :]
    dsignal = shifted_grad * filter_ref[0:1, :]
    dfilter_ref[0:1, :] += jnp.sum(signal * shifted_grad, 0, keepdims=True)
    for offset in range(1, KW):
        shifted_grad = (
            rows_buf[offset : offset + rows, :] * keep_ref[:, KW + offset : KW + offset + 1]
        )
        dsignal = dsignal + shifted_grad * filter_ref[offset : offset + 1, :]
        dfilter_ref[offset : offset + 1, :] += jnp.sum(signal * shifted_grad, 0, keepdims=True)
    rows_buf[rows : rows + 8, :] = rows_buf[0:8, :]
    dproj_ref[:, :conv_cols] = dsignal.astype(jnp.bfloat16)
    for sub in range(BACK_SUBS):
        dproj_ref[sub * ROWS : (sub + 1) * ROWS, proj_cols : proj_cols + 128] = drates[
            sub
        ].astype(jnp.bfloat16)
    dsmall_ref[0:1, :] += dgain
    dsmall_ref[1:2, 0:128] += jnp.sum(dsums, 0, keepdims=True)

    @pl.when(step == last_step)
    def _():
        dstate_out_ref[...] = dstate_buf[...]
        first_ref[...] = rows_buf[0:8, :]


def ffn_kernel(
    mix_cols,
    ff_cols,
    own_ref,
    other_ref,
    inputs_ref,
    cot_ref,
    keep_ref,
    gain_ref,
    weight_hbm,
    *tail_refs,
):
    resid_ref, dnormed_ref, summand_ref, normed_ref, acts_ref, weight_ref, copy_sems = tail_refs[
        -7:
    ]
    f32 = jnp.float32
    bf16 = jnp.bfloat16
    edges = [0] + [mix_cols + part * ff_cols for part in range(4)]

    def copy(part):
        at = pl.ds(edges[part], edges[part + 1] - edges[part])
        return pltpu.make_async_copy(
            weight_hbm.at[:, at], weight_ref.at[:, at], copy_sems.at[part]
        )

    def arrived(part):
        @pl.when(pl.program_id(0) == 0)
        def _():
            copy(part).wait()

    @pl.when(pl.program_id(0) == 0)
    def _():
        for part in range(4):
            copy(part).start()

    arrived(0)
    gated = jnp.concatenate([own_ref[...], other_ref[...]], axis=1)
    resid = inputs_ref[...].astype(f32) + keep_ref[:, 2 * KW : 2 * KW + 1] * dot(
        gated, weight_ref[:, :mix_cols], NT
    )
    resid_ref[...] = resid
    inv_rms = lax.rsqrt(jnp.mean(resid * resid, -1, keepdims=True) + EPS)
    normed = (resid * inv_rms * gain_ref[...]).astype(bf16)
    normed_ref[...] = normed
    gate_at = slice(edges[1], edges[2])
    up_at = slice(edges[2], edges[3])
    down_at = slice(edges[3], edges[4])
    arrived(1)
    gate_pre = dot(normed, weight_ref[:, gate_at], NN)
    arrived(2)
    up_pre = dot(normed, weight_ref[:, up_at], NN)
    arrived(3)
    dhidden = dot(cot_ref[...], weight_ref[:, down_at], NN)
    sig = sigmoid(gate_pre)
    active = gate_pre * sig
    hidden = (active * up_pre).astype(bf16)
    dgate = (dhidden * up_pre * sig * (1.0 + gate_pre * (1.0 - sig))).astype(bf16)
    dup = (dhidden * active).astype(bf16)
    acts_ref[:, :ff_cols] = dgate
    acts_ref[:, ff_cols : 2 * ff_cols] = dup
    acts_ref[:, 2 * ff_cols :] = hidden
    dnormed_ref[...] = (
        dot(dgate, weight_ref[:, gate_at], NT) + dot(dup, weight_ref[:, up_at], NT)
    ).astype(bf16)
    summand_ref[...] = dot(hidden, weight_ref[:, down_at], NT).astype(bf16)


def kernel_cost(micros):
    return pl.CostEstimate(
        flops=int(micros * 4e9), bytes_accessed=int(micros * 8e6), transcendentals=0
    )


def whole(array):
    return pl.BlockSpec(array.shape, lambda c, r: (0,) * len(array.shape))


def mixer_forward(resets, proj, keep, filters, rates, head_gain, heads, start, stop, state):
    proj_width = proj.shape[1]
    row_count = stop - start
    chunks = row_count // ROWS
    rows = SUBS * ROWS
    first = start // rows
    conv_cols = 2 * heads * DK + heads * DV
    f32 = jnp.float32

    def rows_of(cols, dtype=f32):
        return jax.ShapeDtypeStruct((row_count, cols), dtype)

    def saved(rows, cols):
        return jax.ShapeDtypeStruct((chunks, heads, rows, cols), f32)

    def part_block(cols):
        return pl.BlockSpec((rows, cols), lambda c, r: (c + first, 0))

    def row_block(cols):
        return pl.BlockSpec((rows, cols), lambda c, r: (c, 0))

    def saved_block(rows, cols):
        return pl.BlockSpec((SUBS, heads, rows, cols), lambda c, r: (c, 0, 0, 0))

    before = max(start // 8 - 1, 0)
    return pl.pallas_call(
        partial(forward_kernel, heads, start // ROWS),
        grid_spec=pltpu.PrefetchScalarGridSpec(
            num_scalar_prefetch=1,
            grid=(chunks // SUBS,),
            in_specs=[
                part_block(proj_width),
                pl.BlockSpec((8, proj_width), lambda c, r: (before, 0)),
                whole(state),
                part_block(keep.shape[1]),
                whole(filters),
                whole(rates),
                whole(head_gain),
            ],
            out_specs=[
                row_block(heads * DV),
                row_block(conv_cols),
                row_block(heads * DV),
                saved_block(DK, DV),
                saved_block(ROWS, ROWS),
                saved_block(ROWS, DV + DK),
                saved_block(ROWS, DV),
                saved_block(ROWS, ROWS),
                saved_block(2 * ROWS, ROWS),
                whole(state),
            ],
            scratch_shapes=[
                pltpu.VMEM((rows + 8, conv_cols), f32),
                pltpu.VMEM((heads, DK, DV), f32),
            ],
        ),
        out_shape=[
            rows_of(heads * DV, jnp.bfloat16),
            rows_of(conv_cols),
            rows_of(heads * DV),
            saved(DK, DV),
            saved(ROWS, ROWS),
            saved(ROWS, DV + DK),
            saved(ROWS, DV),
            saved(ROWS, ROWS),
            saved(2 * ROWS, ROWS),
            jax.ShapeDtypeStruct(state.shape, f32),
        ],
        compiler_params=pltpu.CompilerParams(vmem_limit_bytes=60 << 20),
        cost_estimate=kernel_cost(24 * row_count / 1024),
        name="mixer_forward",
    )(resets, proj, proj, state, keep, filters, rates, head_gain)


def mixer_backward(
    resets,
    own,
    got,
    resid,
    cot,
    ffn_gain,
    out_weight,
    dstate,
    later,
    proj,
    keep,
    filters,
    rates,
    head_gain,
    saved,
    heads,
    start,
    filled,
):
    row_count = resid.shape[0]
    total_rows, proj_width = proj.shape
    chunks = row_count // ROWS
    first = start // ROWS
    conv_cols = 2 * heads * DK + heads * DV
    f32 = jnp.float32

    rows = BACK_SUBS * ROWS
    steps = row_count // rows
    first_block = start // rows

    def row_block(array):
        return pl.BlockSpec((rows, array.shape[1]), lambda c, r: (steps - 1 - c, 0))

    def part_block(array):
        return pl.BlockSpec(
            (rows, array.shape[1]), lambda c, r: (first_block + steps - 1 - c, 0)
        )

    def saved_block(array):
        return pl.BlockSpec(
            (BACK_SUBS,) + array.shape[1:], lambda c, r: (steps - 1 - c, 0, 0, 0)
        )

    dproj = jax.ShapeDtypeStruct((total_rows, proj_width), jnp.bfloat16)
    dfilter = jax.ShapeDtypeStruct((8, conv_cols), f32)
    dsmall = jax.ShapeDtypeStruct((8, DV), f32)
    dmix = jax.ShapeDtypeStruct(resid.shape, jnp.bfloat16)
    dresid = jax.ShapeDtypeStruct(resid.shape, f32)
    dffn_gain = jax.ShapeDtypeStruct((8, resid.shape[1]), f32)
    args = [resets, own, got, resid, cot, ffn_gain, out_weight, dstate, later]
    args += [proj, keep, filters, rates, head_gain, *saved]
    specs = [row_block(own), row_block(got), row_block(resid), part_block(cot), whole(ffn_gain)]
    specs += [
        pl.BlockSpec(
            (resid.shape[1], heads * DV), lambda c, r: (0, 0), pipeline_mode=pl.Buffered(1)
        )
    ]
    specs += [whole(dstate), whole(later), part_block(proj), part_block(keep)]
    specs += [whole(filters), whole(rates), whole(head_gain)]
    specs += [row_block(saved[0]), row_block(saved[1])]
    specs += [saved_block(array) for array in saved[2:]]
    aliases = {}
    if filled is not None:
        aliases = {len(args): 0}
        args.append(filled)
        specs.append(pl.BlockSpec(memory_space=pl.ANY))
    return pl.pallas_call(
        partial(backward_kernel, heads, first, chunks),
        grid_spec=pltpu.PrefetchScalarGridSpec(
            num_scalar_prefetch=1,
            grid=(steps,),
            in_specs=specs,
            out_specs=[
                part_block(dproj),
                whole(dfilter),
                whole(dsmall),
                row_block(dmix),
                row_block(dresid),
                whole(dffn_gain),
                whole(dstate),
                whole(later),
            ],
            scratch_shapes=[
                pltpu.VMEM((rows + 8, conv_cols), f32),
                pltpu.VMEM((heads, DK, DV), f32),
            ],
        ),
        out_shape=[
            dproj,
            dfilter,
            dsmall,
            dmix,
            dresid,
            dffn_gain,
            jax.ShapeDtypeStruct(dstate.shape, f32),
            jax.ShapeDtypeStruct(later.shape, f32),
        ],
        input_output_aliases=aliases,
        compiler_params=pltpu.CompilerParams(vmem_limit_bytes=60 << 20),
        cost_estimate=kernel_cost(30 * row_count / 1024),
        name="mixer_backward",
    )(*args)


def ffn_both_ways(own, other, inputs, cot_masked, keep, gain, weight, ff_cols, start, filled):
    row_count, own_cols = own.shape
    total_rows, width = inputs.shape
    rows = FFN_ROWS
    first = start // rows
    bf16 = jnp.bfloat16

    def whole(array):
        return pl.BlockSpec(array.shape, lambda c: (0, 0))

    def row_block(cols):
        return pl.BlockSpec((rows, cols), lambda c: (c, 0))

    def part_block(cols):
        return pl.BlockSpec((rows, cols), lambda c: (c + first, 0))

    args = [own, other, inputs, cot_masked, keep, gain, weight]
    specs = [row_block(own_cols), row_block(own_cols), part_block(width), part_block(width)]
    specs += [part_block(keep.shape[1]), whole(gain)]
    specs += [pl.BlockSpec(memory_space=pl.ANY)]
    aliases = {}
    if filled is not None:
        aliases = {len(args): 3, len(args) + 1: 4}
        args += list(filled)
        specs += [pl.BlockSpec(memory_space=pl.ANY)] * 2
    return pl.pallas_call(
        partial(ffn_kernel, 2 * own_cols, ff_cols),
        grid=(row_count // rows,),
        in_specs=specs,
        out_specs=[
            row_block(width),
            row_block(width),
            row_block(width),
            part_block(width),
            part_block(3 * ff_cols),
        ],
        out_shape=[
            jax.ShapeDtypeStruct((row_count, width), jnp.float32),
            jax.ShapeDtypeStruct((row_count, width), bf16),
            jax.ShapeDtypeStruct((row_count, width), bf16),
            jax.ShapeDtypeStruct((total_rows, width), bf16),
            jax.ShapeDtypeStruct((total_rows, 3 * ff_cols), bf16),
        ],
        scratch_shapes=[pltpu.VMEM(weight.shape, bf16), pltpu.SemaphoreType.DMA((4,))],
        input_output_aliases=aliases,
        compiler_params=pltpu.CompilerParams(vmem_limit_bytes=60 << 20),
        cost_estimate=kernel_cost(28 * row_count / 1024),
        name="ffn_both_ways",
    )(*args)


def grads_kernel(
    shard_rows,
    side_ref,
    normed_ref,
    dproj_ref,
    dmix_lo_ref,
    dmix_hi_ref,
    gated_lo_ref,
    gated_hi_ref,
    mine_a_ref,
    mine_b_ref,
    theirs_a_ref,
    theirs_b_ref,
    rate_ref,
):
    side = side_ref[0]
    normed = normed_ref[...]
    gate_cols = gated_lo_ref.shape[1]
    first_cols = mine_a_ref.shape[1]

    def put(grad, mine_ref, theirs_ref, cols):
        pairs = grad.reshape(-1, 2, shard_rows, grad.shape[-1])
        even = pairs[:, 0].reshape(-1, grad.shape[-1])
        odd = pairs[:, 1].reshape(-1, grad.shape[-1])
        mine_ref[:, cols] = jnp.where(side == 0, even, odd)
        theirs_ref[:, cols] = jnp.where(side == 0, odd, even).astype(jnp.bfloat16)

    put(dot(normed, dproj_ref[:, :first_cols], TN), mine_a_ref, theirs_a_ref, slice(None))
    put(
        dot(normed, dproj_ref[:, first_cols : first_cols + gate_cols], TN),
        mine_b_ref,
        theirs_b_ref,
        slice(0, gate_cols),
    )
    put(
        dot(dmix_lo_ref[...], gated_lo_ref[...], TN)
        + dot(dmix_hi_ref[...], gated_hi_ref[...], TN),
        mine_b_ref,
        theirs_b_ref,
        slice(gate_cols, 2 * gate_cols),
    )
    rate_ref[...] = dot(dproj_ref[:, first_cols + gate_cols :], normed, TN)[:8]


def mixer_weight_grads(side, normed, dproj, dmix_lo, dmix_hi, gated_lo, gated_hi, shard_rows):
    rows, width = normed.shape
    half_rows, v_cols = gated_lo.shape
    tile = 256
    first_cols = 2 * v_cols
    bf16 = jnp.bfloat16

    def column_block(array):
        return pl.BlockSpec((array.shape[0], tile), lambda c, r: (0, c))

    def row_block(cols):
        return pl.BlockSpec((tile // 2, cols), lambda c, r: (c, 0))

    return pl.pallas_call(
        partial(grads_kernel, shard_rows),
        grid_spec=pltpu.PrefetchScalarGridSpec(
            num_scalar_prefetch=1,
            grid=(width // tile,),
            in_specs=[
                column_block(normed),
                whole(dproj),
                column_block(dmix_lo),
                column_block(dmix_hi),
                whole(gated_lo),
                whole(gated_hi),
            ],
            out_specs=[
                row_block(first_cols),
                row_block(first_cols),
                row_block(first_cols),
                row_block(first_cols),
                pl.BlockSpec((8, tile), lambda c, r: (0, c)),
            ],
        ),
        out_shape=[
            jax.ShapeDtypeStruct((width // 2, first_cols), jnp.float32),
            jax.ShapeDtypeStruct((width // 2, first_cols), jnp.float32),
            jax.ShapeDtypeStruct((width // 2, first_cols), bf16),
            jax.ShapeDtypeStruct((width // 2, first_cols), bf16),
            jax.ShapeDtypeStruct((8, width), jnp.float32),
        ],
        compiler_params=pltpu.CompilerParams(vmem_limit_bytes=60 << 20),
        cost_estimate=kernel_cost(8),
        name="mixer_weight_grads",
    )(side, normed, dproj, dmix_lo, dmix_hi, gated_lo, gated_hi)


def ffn_grads_kernel(normed_ref, cot_ref, acts_ref, grads_ref):
    part = pl.program_id(0)

    @pl.when(part < 2)
    def _():
        grads_ref[...] = dot(normed_ref[...], acts_ref[...], TN).astype(jnp.bfloat16)

    @pl.when(part == 2)
    def _():
        grads_ref[...] = dot(cot_ref[...], acts_ref[...], TN).astype(jnp.bfloat16)


def ffn_weight_grads(normed, cot_masked, acts, ff_cols):
    rows, width = normed.shape

    def fixed(array):
        return pl.BlockSpec(array.shape, lambda c: (0, 0), pipeline_mode=pl.Buffered(1))

    return pl.pallas_call(
        ffn_grads_kernel,
        grid=(3,),
        in_specs=[
            fixed(normed),
            fixed(cot_masked),
            pl.BlockSpec((rows, ff_cols), lambda c: (0, c)),
        ],
        out_specs=pl.BlockSpec((width, ff_cols), lambda c: (0, c)),
        out_shape=jax.ShapeDtypeStruct((width, 3 * ff_cols), jnp.bfloat16),
        compiler_params=pltpu.CompilerParams(vmem_limit_bytes=60 << 20),
        cost_estimate=kernel_cost(0.1),
        name="ffn_weight_grads",
    )(normed, cot_masked, acts)


def swap_halves(array):
    return lax.ppermute(array, "mp", [(0, 1), (1, 0)])


def dp_total(array):
    count = lax.axis_size("dp")
    step = 1
    while step < count:
        array = array + lax.ppermute(array, "dp", [(i, i ^ step) for i in range(count)])
        step *= 2
    return array


def dp_swap(array, bit):
    count = lax.axis_size("dp")
    return lax.ppermute(array, "dp", [(i, i ^ bit) for i in range(count)])


def dp_gather(shard, cuts, first_held, then):
    index = lax.axis_index("dp")
    bits = [1 << i for i in reversed(range((lax.axis_size("dp") - 1).bit_length()))]
    pieces = [shard[None, :, start:stop] for start, stop in cuts]
    for at, bit in enumerate(bits):
        if at == 1:
            pieces, first_held = lax.optimization_barrier((pieces, first_held))
            then_held = then(first_held)
        if at == 3:
            pieces, then_held = lax.optimization_barrier((pieces, then_held))
        others = [dp_swap(piece, bit) for piece in pieces]
        upper = (index & bit) != 0
        pieces = [
            jnp.stack(
                [jnp.where(upper, other, piece), jnp.where(upper, piece, other)], axis=1
            ).reshape((-1,) + piece.shape[1:])
            for piece, other in zip(pieces, others)
        ]
    return [piece.reshape(-1, piece.shape[-1]) for piece in pieces], first_held, then_held


def scatter_first(kept, sent):
    return [
        (mine.astype(jnp.float32) + dp_swap(theirs, 1).astype(jnp.float32)).astype(mine.dtype)
        for mine, theirs in zip(kept, sent)
    ]


def scatter_step(pieces, at):
    index = lax.axis_index("dp")
    bits = [1 << i for i in range(1, (lax.axis_size("dp") - 1).bit_length())]
    orders = [bits, bits[1:2] + bits[:1] + bits[2:]]
    sums = []
    for piece, order in zip(pieces, orders):
        left = sorted(order[at:], reverse=True)
        bit = order[at]
        axis = left.index(bit)
        side = (index & bit) // bit
        cut = piece.reshape((2,) * len(left) + (-1, piece.shape[-1]))
        sent = lax.dynamic_index_in_dim(cut, 1 - side, axis, False).astype(jnp.bfloat16)
        mine = lax.dynamic_index_in_dim(cut, side, axis, False)
        total = mine.astype(jnp.float32) + dp_swap(sent, bit).astype(jnp.float32)
        sums.append(total.astype(piece.dtype).reshape(-1, piece.shape[-1]))
    return sums


def scatter_steps():
    return (lax.axis_size("dp") - 1).bit_length() - 1


def in_order(own, other, model_index, axis):
    first = jnp.where(model_index == 0, own, other)
    second = jnp.where(model_index == 0, other, own)
    return jnp.concatenate([first, second], axis=axis)


def on_device(
    block_input,
    seq_lengths,
    seq_owner,
    mix_gain,
    query_weight,
    key_weight,
    value_weight,
    gate_weight,
    decay_weight,
    beta_weight,
    query_filter,
    key_filter,
    value_filter,
    decay_log,
    decay_bias,
    head_gain,
    out_weight,
    ffn_gain,
    ffn_gate,
    ffn_up,
    ffn_down,
    cotangent,
):
    bf16 = jnp.bfloat16
    f32 = jnp.float32
    local_rows, width = block_input.shape
    dp_index = lax.axis_index("dp")
    model_count = lax.axis_size("mp")
    model_index = lax.axis_index("mp")
    row_count = local_rows * model_count
    keep_masks, resets, valid_rows = layout(seq_lengths, seq_owner, dp_index, row_count)
    valid_all = valid_rows[:, None]
    heads_local = decay_log.shape[0] // model_count
    qk_cols = heads_local * DK
    v_cols = heads_local * DV
    ff_cols = ffn_gate.shape[1]
    shard_rows = query_weight.shape[0]
    proj_cols = 2 * qk_cols + 2 * v_cols

    def own_columns(array, col_count):
        return lax.dynamic_slice_in_dim(array, model_index * col_count, col_count, array.ndim - 1)

    def own_shard(array):
        return lax.dynamic_slice_in_dim(array, dp_index * shard_rows, shard_rows, 0)

    small_weight = jnp.concatenate(
        [own_columns(decay_weight, heads_local), own_columns(beta_weight, heads_local)], axis=1
    )
    small_weight = jnp.pad(small_weight, ((0, 0), (0, 128 - 2 * heads_local)))
    shard_mix = jnp.concatenate(
        [query_weight, key_weight, value_weight, gate_weight, own_shard(small_weight)], axis=1
    )
    half = proj_cols // 256 * 128
    out_rows = out_weight.T
    shard_ffn = jnp.concatenate([ffn_gate, ffn_up, ffn_down.T], axis=1)
    out_other = swap_halves(out_rows)
    input_other = swap_halves(block_input)
    mix_pieces, (out_other, out_rows, shard_ffn), (input_other, cot_held) = dp_gather(
        shard_mix,
        ((0, half), (half, shard_mix.shape[1])),
        (out_other, out_rows, shard_ffn),
        lambda held: (input_other, cotangent),
    )
    mix_weight = jnp.concatenate(mix_pieces, axis=1)
    shard_rest = jnp.concatenate([out_rows, out_other, shard_ffn], axis=1)
    rest_weight = lax.all_gather(shard_rest, "dp", axis=0, tiled=True)
    cot_other = swap_halves(cot_held)

    filters = jnp.concatenate(
        [
            own_columns(query_filter, qk_cols),
            own_columns(key_filter, qk_cols),
            own_columns(value_filter, v_cols),
        ],
        axis=1,
    )
    filters = jnp.pad(filters, ((0, 8 - KW), (0, 0)))
    rates = jnp.stack(
        [own_columns(decay_bias, heads_local), -jnp.exp(own_columns(decay_log, heads_local))]
    )
    rates = jnp.pad(rates, ((0, 6), (0, 128 - heads_local)))
    gain_row = head_gain[None]
    restarts = resets.astype(jnp.int32)
    later_masks = [
        jnp.concatenate([keep_masks[offset, offset:], jnp.ones((offset,), f32)])
        for offset in range(KW)
    ]
    keep_cols = jnp.stack(
        [keep_masks[offset] for offset in range(KW)] + later_masks + [valid_rows] * 8, axis=1
    )
    inputs_b = in_order(block_input, input_other, model_index, 0)
    inputs_f = inputs_b.astype(f32)
    cot_all = in_order(cotangent, cot_other, model_index, 0)
    normed1, inv_rms1 = rms_forward(inputs_f)
    mixed_in = (normed1 * mix_gain).astype(bf16)
    proj = jnp.dot(mixed_in, mix_weight, preferred_element_type=f32)
    cuts = (qk_cols, 2 * qk_cols, 2 * qk_cols + v_cols, proj_cols)
    middle = row_count // 2
    zero_state = jnp.zeros((heads_local, DK, DV), f32)
    small_args = (keep_cols, filters, rates, gain_row)
    gated_lo, *saved_lo, carried = mixer_forward(
        restarts, proj, *small_args, heads_local, 0, middle, zero_state
    )
    cot_masked = cot_all * valid_all.astype(bf16)
    ffn_row = ffn_gain[None]
    carried, cot_all, cot_masked, inputs_b = lax.optimization_barrier(
        (carried, cot_all, cot_masked, inputs_b)
    )
    gated_hi, *saved_hi, _ = mixer_forward(
        restarts, proj, *small_args, heads_local, middle, row_count, carried
    )
    other_lo = swap_halves(gated_lo)
    gated_sent, other_lo = lax.optimization_barrier((gated_hi, other_lo))
    other_hi = swap_halves(gated_sent)
    ffn_args = (inputs_b, cot_masked, keep_cols, ffn_row, rest_weight, ff_cols)
    resid_lo, dnormed_lo, summand_lo, *filled = ffn_both_ways(
        gated_lo, other_lo, *ffn_args, 0, None
    )
    resid_hi, dnormed_hi, summand_hi, ffn_in, acts = ffn_both_ways(
        gated_hi, other_hi, *ffn_args, middle, filled
    )
    got_hi, dnormed_lo = lax.optimization_barrier((swap_halves(dnormed_hi), dnormed_lo))
    got_lo = swap_halves(dnormed_lo)
    core_side = (dp_index & 1).reshape(1)
    rest_grads = ffn_weight_grads(ffn_in, cot_masked, acts, ff_cols)
    got_hi, _ = lax.optimization_barrier((got_hi, rest_grads))
    ffn_shard = lax.psum_scatter(rest_grads, "dp", scatter_dimension=0, tiled=True)

    def own_half(array):
        return lax.dynamic_slice_in_dim(array, model_index * local_rows, local_rows, 0)

    def other_half(array):
        return lax.dynamic_slice_in_dim(array, (1 - model_index) * local_rows, local_rows, 0)

    def own_of(low, high):
        return jnp.where(model_index == 0, low, high)

    zero_rows = jnp.zeros((8, proj_cols - v_cols), f32)
    proj_grad, filter_hi, small_hi, dmix_hi, dresid_hi, ffn_gain_hi, carried, later = (
        mixer_backward(
            restarts,
            dnormed_hi,
            got_hi,
            resid_hi,
            cot_all,
            ffn_row,
            rest_weight,
            zero_state,
            zero_rows,
            proj,
            *small_args,
            saved_hi,
            heads_local,
            middle,
            None,
        )
    )
    summand_sent, got_lo, proj_grad = lax.optimization_barrier(
        (own_of(summand_hi, summand_lo), got_lo, proj_grad)
    )
    proj_grad, filter_lo, small_lo, dmix_lo, dresid_lo, ffn_gain_lo, _, _ = mixer_backward(
        restarts,
        dnormed_lo,
        got_lo,
        resid_lo,
        cot_all,
        ffn_row,
        rest_weight,
        carried,
        later,
        proj,
        *small_args,
        saved_lo,
        heads_local,
        0,
        proj_grad,
    )
    summand_got, proj_grad, dmix_lo, filter_lo, small_lo, dresid_lo, ffn_gain_lo = (
        lax.optimization_barrier(
            (
                swap_halves(summand_sent),
                proj_grad,
                dmix_lo,
                filter_lo,
                small_lo,
                dresid_lo,
                ffn_gain_lo,
            )
        )
    )
    ffn_sum = own_of(summand_lo, summand_hi).astype(f32) + summand_got.astype(f32)
    block_output = (own_of(resid_lo, resid_hi) + own_half(valid_all) * ffn_sum).astype(bf16)
    filter_grads = filter_lo + filter_hi
    small_grads = small_lo + small_hi
    ffn_gain_part = ffn_gain_lo[0] + ffn_gain_hi[0]
    *grad_pieces, rate_grads = mixer_weight_grads(
        core_side,
        mixed_in,
        proj_grad,
        dmix_lo,
        dmix_hi,
        gated_lo,
        gated_hi,
        shard_rows,
    )
    rate_grads = rate_grads[: 2 * heads_local]
    mix_sums = scatter_first(grad_pieces[:2], grad_pieces[2:])
    proj_grad, mix_sums, rate_grads = lax.optimization_barrier(
        (proj_grad, mix_sums, rate_grads)
    )
    mix_sums = scatter_step(mix_sums, 0)
    mix_in_part = against(proj_grad, mix_weight)
    mix_gain_part = jnp.sum(mix_in_part * normed1, 0)
    common = jnp.concatenate(
        [mix_gain_part, ffn_gain_part, small_grads[0], jnp.zeros((width - DV,), f32)]
    ).reshape(3, width)
    tail_row = jnp.concatenate(
        [small_grads[1, : 2 * heads_local], jnp.zeros((width - 2 * heads_local,), f32)]
    )
    split_rows = jnp.concatenate(
        [
            rate_grads,
            filter_grads[:KW, : cuts[0]].reshape(-1, width),
            filter_grads[:KW, cuts[0] : cuts[1]].reshape(-1, width),
            filter_grads[:KW, cuts[1] : cuts[2]].reshape(-1, width),
            tail_row[None],
        ],
        axis=0,
    )
    mix_in_sent = other_half(mix_in_part).astype(bf16)

    mix_in_got = swap_halves(mix_in_sent)
    mix_sums, small_sums = lax.optimization_barrier(
        (mix_sums, jnp.concatenate([common, split_rows], axis=0))
    )
    totals = dp_total(small_sums)
    totals, mix_in_got = lax.optimization_barrier((totals, mix_in_got))
    totals_other = swap_halves(totals)
    for step in range(1, scatter_steps()):
        if step == 2:
            mix_sums, totals, totals_other, mix_in_got = lax.optimization_barrier(
                (mix_sums, totals, totals_other, mix_in_got)
            )
        mix_sums = scatter_step(mix_sums, step)
    mix_shards = mix_sums
    mix_in_sum = own_half(mix_in_part) + mix_in_got.astype(f32)
    input_grad = own_of(dresid_lo, dresid_hi) + rms_backward(
        mix_in_sum * mix_gain, own_half(normed1), own_half(inv_rms1)
    )
    common = totals[:3] + totals_other[:3]
    lower = jnp.where(model_index == 0, totals, totals_other)[3:]
    upper = jnp.where(model_index == 0, totals_other, totals)[3:]

    def joined(start, rows, cols):
        return jnp.concatenate(
            [
                lower[start : start + rows].reshape(-1, cols),
                upper[start : start + rows].reshape(-1, cols),
            ],
            axis=1,
        )

    q_rows = KW * qk_cols // width
    v_rows = KW * v_cols // width
    at_q = 2 * heads_local
    at_k = at_q + q_rows
    at_v = at_k + q_rows
    at_tail = at_v + v_rows

    def rate_weight_grad(start):
        return jnp.concatenate(
            [lower[start : start + heads_local], upper[start : start + heads_local]], axis=0
        ).T

    def rate_grad(start):
        return jnp.concatenate(
            [
                lower[at_tail, start : start + heads_local],
                upper[at_tail, start : start + heads_local],
            ]
        )

    ffn_shard = ffn_shard.astype(f32)
    return (
        block_output,
        input_grad,
        common[0],
        mix_shards[0][:, : cuts[0]],
        mix_shards[0][:, cuts[0] : cuts[1]],
        mix_shards[0][:, cuts[1] :],
        mix_shards[1][:, :v_cols],
        rate_weight_grad(0),
        rate_weight_grad(heads_local),
        joined(at_q, q_rows, qk_cols),
        joined(at_k, q_rows, qk_cols),
        joined(at_v, v_rows, v_cols),
        rate_grad(0),
        rate_grad(heads_local),
        common[2, :DV],
        mix_shards[1][:, v_cols:].T,
        common[1],
        ffn_shard[:, :ff_cols],
        ffn_shard[:, ff_cols : 2 * ff_cols],
        ffn_shard[:, 2 * ff_cols :].T,
    )


def solution(mesh):
    in_specs = (
        P(("dp", "mp"), None),
        P(),
        P(),
        P(),
        P("dp", "mp"),
        P("dp", "mp"),
        P("dp", "mp"),
        P("dp", "mp"),
        P(),
        P(),
        P(),
        P(),
        P(),
        P(),
        P(),
        P(),
        P("mp", "dp"),
        P(),
        P("dp", "mp"),
        P("dp", "mp"),
        P("mp", "dp"),
        P(("dp", "mp"), None),
    )
    out_specs = (
        P(("dp", "mp"), None),
        P(("dp", "mp"), None),
        P(),
        P("dp", "mp"),
        P("dp", "mp"),
        P("dp", "mp"),
        P("dp", "mp"),
        P(),
        P(),
        P(),
        P(),
        P(),
        P(),
        P(),
        P(),
        P("mp", "dp"),
        P(),
        P("dp", "mp"),
        P("dp", "mp"),
        P("mp", "dp"),
    )
    return jax.shard_map(
        on_device, mesh=mesh, in_specs=in_specs, out_specs=out_specs, check_vma=False
    )
```

```python
from functools import partial
import math

import jax
import jax.numpy as jnp
from jax import lax
from jax.experimental import pallas as pl
from jax.experimental.pallas import tpu as pltpu
from jax.sharding import PartitionSpec as P

DK = 128
DV = 256
KW = 4
SPAN = 64


EPS = 1e-06


def layout(seq_lengths, seq_owner, device, row_count):
    owned = seq_owner == device
    own_lengths = jnp.where(owned, seq_lengths, 0)
    offsets = jnp.cumsum(own_lengths) - own_lengths
    loaded = jnp.sum(own_lengths)
    span_starts = jnp.arange(row_count // SPAN, dtype=jnp.int32) * SPAN
    begins = jnp.any(
        (offsets[None, :] == span_starts[:, None]) & (own_lengths[None, :] > 0), axis=1
    )
    resets = begins | (span_starts == loaded)
    within = jnp.arange(SPAN, dtype=jnp.int32)
    keep_masks = jnp.stack(
        [
            jnp.logical_not(resets[:, None] & (within[None, :] < offset)).reshape(row_count)
            for offset in range(KW)
        ]
    ).astype(jnp.float32)
    valid_rows = (jnp.arange(row_count, dtype=jnp.int32) < loaded).astype(jnp.float32)
    return (keep_masks, resets, valid_rows)


def across_rows(left, right):
    return lax.dot_general(
        left, right, (((0,), (0,)), ((), ())), preferred_element_type=jnp.float32
    )


def against(left, right):
    return lax.dot_general(
        left, right, (((1,), (1,)), ((), ())), preferred_element_type=jnp.float32
    )


def rms_forward(values):
    inv_rms = lax.rsqrt(jnp.mean(values * values, -1, keepdims=True) + EPS)
    return (values * inv_rms, inv_rms)


def rms_backward(upstream, normed, inv_rms):
    return inv_rms * (upstream - normed * jnp.mean(upstream * normed, -1, keepdims=True))


ROWS = 128
NN = ((1,), (0,))
NT = ((1,), (1,))
TN = ((0,), (0,))
FINE_GRAM = True
FINE_INVERSE = True
FINE_MERGE = True
SUBS = 2
FFN_ROWS = 256
FINE_APPLY = True
FINE_STATE = True
FINE_BACK = (True,) * 10
BACK_SUBS = 2


def dot(left, right, dims):
    return lax.dot_general(left, right, (dims, ((), ())), preferred_element_type=jnp.float32)


def high_low(values):
    high = values.astype(jnp.bfloat16)
    return high, (values - high.astype(jnp.float32)).astype(jnp.bfloat16)


def product(left, right, dims, fine=False):
    if not fine:
        return dot(left.astype(jnp.bfloat16), right.astype(jnp.bfloat16), dims)
    left_high, left_low = high_low(left)
    right_high, right_low = high_low(right)
    (left_axis,), (right_axis,) = dims
    depth = right.shape[right_axis]
    count = right.shape[1 - right_axis]
    if depth <= 128:
        both = jnp.concatenate([left_high, left_low], axis=left_axis)
        if count <= 128:
            wide = jnp.concatenate([right_high, right_low], axis=1 - right_axis)
            part = jnp.concatenate([right_high, jnp.zeros_like(right_low)], axis=1 - right_axis)
            result = dot(both, jnp.concatenate([wide, part], axis=right_axis), dims)
            return result[:, :count] + result[:, count:]
        return dot(both, jnp.concatenate([right_high, right_high], axis=right_axis), dims) + dot(
            left_high, right_low, dims
        )
    if count <= 128:
        wide = jnp.concatenate([right_high, right_low], axis=1 - right_axis)
        result = dot(left_high, wide, dims)
        return result[:, :count] + (result[:, count:] + dot(left_low, right_high, dims))
    return dot(left_high, right_high, dims) + (
        dot(left_high, right_low, dims) + dot(left_low, right_high, dims)
    )


def summed_by(mask, values, dims=NN):
    high, low = high_low(values)
    return dot(mask, high, dims) + dot(mask, low, dims)


def chunk_masks(resets_ref, chunk):
    first = 1.0 - resets_ref[2 * chunk].astype(jnp.float32)
    second = 1.0 - resets_ref[2 * chunk + 1].astype(jnp.float32)
    row = lax.broadcasted_iota(jnp.int32, (ROWS, ROWS), 0)
    col = lax.broadcasted_iota(jnp.int32, (ROWS, ROWS), 1)
    late = row >= SPAN
    reached = jnp.where(late, first * second, first)
    reaching = jnp.where(late, 1.0, second)
    joined = jnp.where(late & (col < SPAN), second, 1.0)
    return row, col, reached, reaching, joined, first * second


def unit_lower_inverses(couplings, row, col):
    eye = jnp.where(row == col, 1.0, 0.0)
    base = 16
    near = (row // base) == (col // base)
    powered = [jnp.where(near, coupling, 0.0) for coupling in couplings]
    inverses = [eye - power for power in powered]
    size = 2
    while size < base:
        powered = [product(power, power, NN, FINE_INVERSE) for power in powered]
        inverses = [
            inverse + product(inverse, power, NN, FINE_INVERSE)
            for inverse, power in zip(inverses, powered)
        ]
        size *= 2
    while base < ROWS:
        wide = 2 * base
        linked = ((row // wide) == (col // wide)) & ((row // base) != (col // base))
        steps = [
            product(jnp.where(linked, coupling, 0.0), inverse, NN, FINE_MERGE)
            for coupling, inverse in zip(couplings, inverses)
        ]
        inverses = [
            inverse - product(inverse, step, NN, FINE_MERGE)
            for inverse, step in zip(inverses, steps)
        ]
        base = wide
    return inverses


def sigmoid(values):
    return 1.0 / (1.0 + jnp.exp(-values))


def lane_sum(values):
    return jnp.sum(values, -1, keepdims=True)


def forward_kernel(
    heads,
    base,
    resets_ref,
    proj_ref,
    before_ref,
    state_in_ref,
    keep_ref,
    filter_ref,
    rates_ref,
    gain_ref,
    gated_ref,
    conv_ref,
    mixed_ref,
    state_ref,
    inverse_ref,
    parts_ref,
    written_ref,
    factor_ref,
    grams_ref,
    state_out_ref,
    rows_buf,
    state_buf,
):
    step = pl.program_id(0)
    qk = heads * DK
    conv_cols = 2 * qk + heads * DV
    proj_cols = conv_cols + heads * DV
    rows = SUBS * ROWS

    @pl.when(step == 0)
    def _():
        if base == 0:
            rows_buf[0:8, :] = jnp.zeros((8, conv_cols), jnp.float32)
        else:
            rows_buf[0:8, :] = before_ref[:, :conv_cols]
        state_buf[...] = state_in_ref[...]

    rows_buf[8 : 8 + rows, :] = proj_ref[:, :conv_cols]
    conv = rows_buf[8 : 8 + rows, :] * filter_ref[0:1, :]
    for offset in range(1, KW):
        conv = conv + rows_buf[8 - offset : 8 - offset + rows, :] * (
            filter_ref[offset : offset + 1, :] * keep_ref[:, offset : offset + 1]
        )
    rows_buf[0:8, :] = rows_buf[rows : rows + 8, :]
    conv_ref[...] = conv

    rate = proj_ref[:, proj_cols : proj_cols + 128]
    shifted = rate + rates_ref[0:1, :]
    decay_all = rates_ref[1:2, :] * (
        jnp.maximum(shifted, 0.0) + jnp.log1p(jnp.exp(-jnp.abs(shifted)))
    )
    beta_all = sigmoid(rate)
    units = [(sub, head) for sub in range(SUBS) for head in range(heads)]
    prepared = []
    for sub, head in units:
        row, col, reached, reaching, joined, passed = chunk_masks(
            resets_ref, base + step * SUBS + sub
        )
        lower = jnp.where(row >= col, 1.0, 0.0)
        at = slice(sub * ROWS, (sub + 1) * ROWS)
        decay = jnp.broadcast_to(decay_all[at, head : head + 1], (ROWS, ROWS))
        beta = beta_all[at, heads + head : heads + head + 1]
        sums = summed_by(
            lower.astype(jnp.bfloat16),
            jnp.concatenate([jnp.where(row > col, decay, 0.0), decay], axis=1),
        )
        factor = jnp.exp(sums[:, :ROWS]) * (lower * joined)
        total = sums[:, ROWS:]
        total_end = total[ROWS - 1 : ROWS, :]
        grown = jnp.exp(total) * reached
        tail = jnp.exp(total_end - total) * reaching
        end_decay = jnp.exp(total_end[:, :1]) * passed

        conv_q = conv[at, head * DK : (head + 1) * DK]
        conv_k = conv[at, qk + head * DK : qk + (head + 1) * DK]
        conv_v = conv[at, 2 * qk + head * DV : 2 * qk + (head + 1) * DV]
        query = conv_q * sigmoid(conv_q)
        query = query * (lax.rsqrt(lane_sum(query * query) + EPS) * (1.0 / math.sqrt(DK)))
        key = conv_k * sigmoid(conv_k)
        key = key * lax.rsqrt(lane_sum(key * key) + EPS)
        value = conv_v * sigmoid(conv_v)

        grams = product(jnp.concatenate([key, query], axis=0), key, NT, FINE_GRAM)
        coupling = jnp.where(row > col, factor * grams[:ROWS] * beta, 0.0)
        scaled = jnp.concatenate([beta * value, (beta * grown) * key], axis=1)
        factor_ref[sub, head] = factor
        grams_ref[sub, head] = grams
        prepared.append(
            (coupling, scaled, grown * query, factor * grams[ROWS:], tail * key, end_decay)
        )
    row = lax.broadcasted_iota(jnp.int32, (ROWS, ROWS), 0)
    col = lax.broadcasted_iota(jnp.int32, (ROWS, ROWS), 1)
    inverses = unit_lower_inverses([entry[0] for entry in prepared], row, col)
    for (sub, head), inverse, entry in zip(units, inverses, prepared):
        _, scaled, query_grown, mixing, key_tail, end_decay = entry
        at = slice(sub * ROWS, (sub + 1) * ROWS)
        parts = product(inverse, scaled, NN, FINE_APPLY)
        state = state_buf[head]
        from_state = product(
            jnp.concatenate([parts[:, DV:], query_grown], axis=0), state, NN, FINE_STATE
        )
        written = parts[:, :DV] - from_state[:ROWS]
        mixed = from_state[ROWS:] + product(mixing, written, NN, FINE_STATE)
        state_buf[head] = end_decay * state + product(key_tail, written, TN, FINE_STATE)

        gate = proj_ref[at, conv_cols + head * DV : conv_cols + (head + 1) * DV]
        normed = mixed * lax.rsqrt(lane_sum(mixed * mixed) * (1.0 / DV) + EPS)
        gated_ref[at, head * DV : (head + 1) * DV] = (
            normed * gain_ref[...] * (gate * sigmoid(gate))
        ).astype(jnp.bfloat16)
        mixed_ref[at, head * DV : (head + 1) * DV] = mixed
        state_ref[sub, head] = state
        inverse_ref[sub, head] = inverse
        parts_ref[sub, head] = parts
        written_ref[sub, head] = written

    @pl.when(step == pl.num_programs(0) - 1)
    def _():
        state_out_ref[...] = state_buf[...]


def backward_kernel(
    heads,
    base,
    chunks,
    resets_ref,
    own_ref,
    got_ref,
    resid_ref,
    cot_ref,
    ffn_gain_ref,
    out_weight_ref,
    dstate_in_ref,
    later_ref,
    proj_ref,
    keep_ref,
    filter_ref,
    rates_ref,
    gain_ref,
    conv_ref,
    mixed_ref,
    state_ref,
    inverse_ref,
    parts_ref,
    written_ref,
    factor_ref,
    grams_ref,
    *tail_refs,
):
    (
        dproj_ref,
        dfilter_ref,
        dsmall_ref,
        dmix_ref,
        dresid_ref,
        dffn_gain_ref,
        dstate_out_ref,
        first_ref,
        rows_buf,
        dstate_buf,
    ) = tail_refs[-10:]
    step = pl.program_id(0)
    last_step = pl.num_programs(0) - 1
    rows = BACK_SUBS * ROWS
    qk = heads * DK
    conv_cols = 2 * qk + heads * DV
    proj_cols = conv_cols + heads * DV

    @pl.when(step == 0)
    def _():
        rows_buf[rows : rows + 8, :] = later_ref[...]
        dstate_buf[...] = dstate_in_ref[...]
        dffn_gain_ref[...] = jnp.zeros_like(dffn_gain_ref)
        dfilter_ref[...] = jnp.zeros_like(dfilter_ref)
        dsmall_ref[...] = jnp.zeros_like(dsmall_ref)

    resid = resid_ref[...]
    inv_resid = lax.rsqrt(jnp.mean(resid * resid, -1, keepdims=True) + EPS)
    resid_normed = resid * inv_resid
    ffn_in_own = own_ref[...].astype(jnp.float32)
    dffn_gain_ref[0:1, :] += jnp.sum(ffn_in_own * resid_normed, 0, keepdims=True)
    scaled_up = (ffn_in_own + got_ref[...].astype(jnp.float32)) * ffn_gain_ref[...]
    dresid = cot_ref[...].astype(jnp.float32) + inv_resid * (
        scaled_up - resid_normed * jnp.mean(scaled_up * resid_normed, -1, keepdims=True)
    )
    dresid_ref[...] = dresid
    dmix = (dresid * keep_ref[:, 2 * KW : 2 * KW + 1]).astype(jnp.bfloat16)
    dmix_ref[...] = dmix
    dgated = dot(dmix, out_weight_ref[...], NN)
    rate = proj_ref[:, proj_cols : proj_cols + 128]
    shifted = rate + rates_ref[0:1, :]
    decay_all = rates_ref[1:2, :] * (
        jnp.maximum(shifted, 0.0) + jnp.log1p(jnp.exp(-jnp.abs(shifted)))
    )
    slope_all = rates_ref[1:2, :] * sigmoid(shifted)
    beta_all = sigmoid(rate)
    row = lax.broadcasted_iota(jnp.int32, (ROWS, ROWS), 0)
    col = lax.broadcasted_iota(jnp.int32, (ROWS, ROWS), 1)
    lower_b = jnp.where(row >= col, 1.0, 0.0).astype(jnp.bfloat16)
    upper_b = jnp.where(row <= col, 1.0, 0.0).astype(jnp.bfloat16)
    lane = lax.broadcasted_iota(jnp.int32, (ROWS, 128), 1)
    dgain = jnp.zeros((1, DV), jnp.float32)
    units = [(sub, head) for sub in reversed(range(BACK_SUBS)) for head in range(heads)]
    prepared = []
    for sub, head in units:
        at = slice(sub * ROWS, (sub + 1) * ROWS)
        chunk = base + chunks - BACK_SUBS * (step + 1) + sub
        _, _, reached, reaching, _, passed = chunk_masks(resets_ref, chunk)
        decay = jnp.broadcast_to(decay_all[at, head : head + 1], (ROWS, ROWS))
        total = summed_by(lower_b, decay)
        total_end = total[ROWS - 1 : ROWS, :]
        grown = jnp.exp(total) * reached
        tail = jnp.exp(total_end - total) * reaching
        end_decay = jnp.exp(total_end[:, :1]) * passed

        v_at = slice(head * DV, (head + 1) * DV)
        gate_at = slice(conv_cols + head * DV, conv_cols + (head + 1) * DV)
        conv_q = conv_ref[at, head * DK : (head + 1) * DK]
        conv_k = conv_ref[at, qk + head * DK : qk + (head + 1) * DK]
        query = conv_q * sigmoid(conv_q)
        inv_q = lax.rsqrt(lane_sum(query * query) + EPS)
        query = query * (inv_q * (1.0 / math.sqrt(DK)))
        key = conv_k * sigmoid(conv_k)
        inv_k = lax.rsqrt(lane_sum(key * key) + EPS)
        key = key * inv_k

        mixed = mixed_ref[at, v_at]
        inv_o = lax.rsqrt(lane_sum(mixed * mixed) * (1.0 / DV) + EPS)
        normed = mixed * inv_o
        gate = proj_ref[at, gate_at]
        sig_g = sigmoid(gate)
        upstream = dgated[at, v_at]
        up_normed = upstream * normed
        dgain = dgain + jnp.sum(up_normed * (gate * sig_g), 0, keepdims=True)
        dproj_ref[at, gate_at] = (
            up_normed * gain_ref[...] * (sig_g * (1.0 + gate * (1.0 - sig_g)))
        ).astype(jnp.bfloat16)
        dnormed = upstream * gain_ref[...] * (gate * sig_g)
        dmixed = inv_o * (dnormed - normed * (lane_sum(dnormed * normed) * (1.0 / DV)))
        mixing = factor_ref[sub, head] * grams_ref[sub, head, ROWS:]
        within = product(mixing, dmixed, TN, FINE_BACK[0])
        dmixing = product(dmixed, written_ref[sub, head], NT, FINE_BACK[3])
        prepared.append(
            (decay, grown, tail, end_decay, query, inv_q, key, inv_k, dmixed, within, dmixing)
        )
    stepped = []
    for (sub, head), entry in zip(units, prepared):
        decay, grown, tail, end_decay, query, inv_q, key, inv_k, dmixed, within, dmixing = entry
        state = state_ref[sub, head]
        dstate = dstate_buf[head]
        dwritten = within + product(tail * key, dstate, NN, FINE_BACK[1])
        dkey_tail = product(written_ref[sub, head], dstate, NT, FINE_BACK[4])
        end_grad = end_decay * lane_sum(jnp.sum(state * dstate, 0, keepdims=True))
        stacked = jnp.concatenate([dmixed, -dwritten], axis=0)
        dstate_buf[head] = end_decay * dstate + product(
            jnp.concatenate([grown * query, parts_ref[sub, head, :, DV:]], axis=0),
            stacked,
            TN,
            FINE_BACK[5],
        )
        stepped.append((dwritten, dkey_tail, end_grad, stacked))
    drates = {sub: jnp.zeros((ROWS, 128), jnp.float32) for sub in range(BACK_SUBS)}
    dsums = jnp.zeros((ROWS, 128), jnp.float32)
    throughs = [
        product(entry[3], state_ref[sub, head], NT, FINE_BACK[2])
        for (sub, head), entry in zip(units, stepped)
    ]
    solveds = [
        product(
            inverse_ref[sub, head],
            jnp.concatenate([entry[0], through[ROWS:]], axis=1),
            TN,
            FINE_BACK[6],
        )
        for (sub, head), entry, through in zip(units, stepped, throughs)
    ]
    dcouplings = [
        product(solved, parts_ref[sub, head], NT, FINE_BACK[7])
        for (sub, head), solved in zip(units, solveds)
    ]
    for at_unit, (sub, head) in enumerate(units):
        decay, grown, tail, _, query, inv_q, key, inv_k, _, _, dmixing = prepared[at_unit]
        _, dkey_tail, end_grad, _ = stepped[at_unit]
        solved = solveds[at_unit]
        at = slice(sub * ROWS, (sub + 1) * ROWS)
        q_at = slice(head * DK, (head + 1) * DK)
        k_at = slice(qk + head * DK, qk + (head + 1) * DK)
        value_at = slice(2 * qk + head * DV, 2 * qk + (head + 1) * DV)
        beta = beta_all[at, heads + head : heads + head + 1]
        factor = factor_ref[sub, head]
        conv_q = conv_ref[at, q_at]
        conv_k = conv_ref[at, k_at]
        conv_v = conv_ref[at, value_at]
        sig_q = sigmoid(conv_q)
        sig_k = sigmoid(conv_k)
        sig_v = sigmoid(conv_v)
        value = conv_v * sig_v
        query_grown = grown * query
        key_tail = tail * key
        dquery_grown = throughs[at_unit][:ROWS]
        dcoupling = jnp.where(row > col, -dcouplings[at_unit] * factor, 0.0)
        dcoupling_gram = dcoupling * grams_ref[sub, head, :ROWS]
        dbeta = lane_sum(dcoupling_gram)
        dgap = beta * dcoupling_gram + dmixing * (factor * grams_ref[sub, head, ROWS:])
        dgrams = jnp.concatenate([beta * dcoupling, dmixing * factor], axis=0)
        by_key = product(dgrams, key, NN, FINE_BACK[8])
        dkey = by_key[:ROWS] + product(
            dgrams, jnp.concatenate([key, query], axis=0), TN, FINE_BACK[9]
        )
        dquery = by_key[ROWS:] + grown * dquery_grown
        dvalue_scaled = solved[:, :DV]
        dkey_scaled = solved[:, DV:]
        scaled_rows = lane_sum(dkey_scaled * (grown * key))
        dbeta = dbeta + lane_sum(dvalue_scaled * value) + scaled_rows
        tail_rows = lane_sum(dkey_tail * key_tail)
        dkey = dkey + tail * dkey_tail + (beta * grown) * dkey_scaled
        dtotal = lane_sum(dquery_grown * query_grown) + beta * scaled_rows - tail_rows
        sums = summed_by(
            upper_b, jnp.concatenate([dgap, jnp.broadcast_to(dtotal, (ROWS, ROWS))], axis=1)
        )
        ddecay = (
            lane_sum(jnp.where(col < row, sums[:, :ROWS], 0.0))
            + sums[:, ROWS : ROWS + 1]
            + (end_grad + jnp.sum(tail_rows, 0, keepdims=True))
        )
        dshifted = ddecay * slope_all[at, head : head + 1]
        drates[sub] = (
            drates[sub]
            + jnp.where(lane == head, dshifted, 0.0)
            + jnp.where(lane == heads + head, dbeta * (beta * (1.0 - beta)), 0.0)
        )
        dsums = dsums + jnp.where(lane == head, ddecay * decay, 0.0)
        dsums = dsums + jnp.where(lane == heads + head, dshifted, 0.0)

        unit = query * math.sqrt(DK)
        dunit = dquery * (1.0 / math.sqrt(DK))
        dsilu = inv_q * (dunit - unit * lane_sum(dunit * unit))
        rows_buf[at, q_at] = dsilu * (sig_q * (1.0 + conv_q * (1.0 - sig_q)))
        dsilu = inv_k * (dkey - key * lane_sum(dkey * key))
        rows_buf[at, k_at] = dsilu * (sig_k * (1.0 + conv_k * (1.0 - sig_k)))
        rows_buf[at, value_at] = (beta * dvalue_scaled) * (
            sig_v * (1.0 + conv_v * (1.0 - sig_v))
        )

    signal = proj_ref[:, :conv_cols]
    shifted_grad = rows_buf[0:rows, :]
    dsignal = shifted_grad * filter_ref[0:1, :]
    dfilter_ref[0:1, :] += jnp.sum(signal * shifted_grad, 0, keepdims=True)
    for offset in range(1, KW):
        shifted_grad = (
            rows_buf[offset : offset + rows, :] * keep_ref[:, KW + offset : KW + offset + 1]
        )
        dsignal = dsignal + shifted_grad * filter_ref[offset : offset + 1, :]
        dfilter_ref[offset : offset + 1, :] += jnp.sum(signal * shifted_grad, 0, keepdims=True)
    rows_buf[rows : rows + 8, :] = rows_buf[0:8, :]
    dproj_ref[:, :conv_cols] = dsignal.astype(jnp.bfloat16)
    for sub in range(BACK_SUBS):
        dproj_ref[sub * ROWS : (sub + 1) * ROWS, proj_cols : proj_cols + 128] = drates[
            sub
        ].astype(jnp.bfloat16)
    dsmall_ref[0:1, :] += dgain
    dsmall_ref[1:2, 0:128] += jnp.sum(dsums, 0, keepdims=True)

    @pl.when(step == last_step)
    def _():
        dstate_out_ref[...] = dstate_buf[...]
        first_ref[...] = rows_buf[0:8, :]


def ffn_kernel(
    mix_cols,
    ff_cols,
    own_ref,
    other_ref,
    inputs_ref,
    cot_ref,
    keep_ref,
    gain_ref,
    weight_hbm,
    *tail_refs,
):
    resid_ref, dnormed_ref, normed_ref, acts_ref, weight_ref, copy_sems = tail_refs[-6:]
    f32 = jnp.float32
    bf16 = jnp.bfloat16
    edges = [0] + [mix_cols + part * ff_cols for part in range(4)]

    def copy(part):
        at = pl.ds(edges[part], edges[part + 1] - edges[part])
        return pltpu.make_async_copy(
            weight_hbm.at[:, at], weight_ref.at[:, at], copy_sems.at[part]
        )

    def arrived(part):
        @pl.when(pl.program_id(0) == 0)
        def _():
            copy(part).wait()

    @pl.when(pl.program_id(0) == 0)
    def _():
        for part in range(4):
            copy(part).start()

    arrived(0)
    gated = jnp.concatenate([own_ref[...], other_ref[...]], axis=1)
    resid = inputs_ref[...].astype(f32) + keep_ref[:, 2 * KW : 2 * KW + 1] * dot(
        gated, weight_ref[:, :mix_cols], NT
    )
    resid_ref[...] = resid
    inv_rms = lax.rsqrt(jnp.mean(resid * resid, -1, keepdims=True) + EPS)
    normed = (resid * inv_rms * gain_ref[...]).astype(bf16)
    normed_ref[...] = normed
    gate_at = slice(edges[1], edges[2])
    up_at = slice(edges[2], edges[3])
    down_at = slice(edges[3], edges[4])
    arrived(1)
    gate_pre = dot(normed, weight_ref[:, gate_at], NN)
    arrived(2)
    up_pre = dot(normed, weight_ref[:, up_at], NN)
    arrived(3)
    dhidden = dot(cot_ref[...], weight_ref[:, down_at], NN)
    sig = sigmoid(gate_pre)
    active = gate_pre * sig
    hidden = (active * up_pre).astype(bf16)
    dgate = (dhidden * up_pre * sig * (1.0 + gate_pre * (1.0 - sig))).astype(bf16)
    dup = (dhidden * active).astype(bf16)
    acts_ref[:, :ff_cols] = dgate
    acts_ref[:, ff_cols : 2 * ff_cols] = dup
    acts_ref[:, 2 * ff_cols :] = hidden
    dnormed_ref[...] = (
        dot(dgate, weight_ref[:, gate_at], NT) + dot(dup, weight_ref[:, up_at], NT)
    ).astype(bf16)


def ffn_out_kernel(down_start, hidden_ref, weight_hbm, summand_ref, weight_ref, copy_sem):
    @pl.when(pl.program_id(0) == 0)
    def _():
        at = pl.ds(down_start, weight_ref.shape[1])
        copy = pltpu.make_async_copy(weight_hbm.at[:, at], weight_ref, copy_sem)
        copy.start()
        copy.wait()

    summand_ref[...] = dot(hidden_ref[...], weight_ref[...], NT).astype(jnp.bfloat16)


def kernel_cost(micros):
    return pl.CostEstimate(
        flops=int(micros * 4e9), bytes_accessed=int(micros * 8e6), transcendentals=0
    )


def whole(array):
    return pl.BlockSpec(array.shape, lambda c, r: (0,) * len(array.shape))


def mixer_forward(resets, proj, keep, filters, rates, head_gain, heads, start, stop, state):
    proj_width = proj.shape[1]
    row_count = stop - start
    chunks = row_count // ROWS
    rows = SUBS * ROWS
    first = start // rows
    conv_cols = 2 * heads * DK + heads * DV
    f32 = jnp.float32

    def rows_of(cols, dtype=f32):
        return jax.ShapeDtypeStruct((row_count, cols), dtype)

    def saved(rows, cols):
        return jax.ShapeDtypeStruct((chunks, heads, rows, cols), f32)

    def part_block(cols):
        return pl.BlockSpec((rows, cols), lambda c, r: (c + first, 0))

    def row_block(cols):
        return pl.BlockSpec((rows, cols), lambda c, r: (c, 0))

    def saved_block(rows, cols):
        return pl.BlockSpec((SUBS, heads, rows, cols), lambda c, r: (c, 0, 0, 0))

    before = max(start // 8 - 1, 0)
    return pl.pallas_call(
        partial(forward_kernel, heads, start // ROWS),
        grid_spec=pltpu.PrefetchScalarGridSpec(
            num_scalar_prefetch=1,
            grid=(chunks // SUBS,),
            in_specs=[
                part_block(proj_width),
                pl.BlockSpec((8, proj_width), lambda c, r: (before, 0)),
                whole(state),
                part_block(keep.shape[1]),
                whole(filters),
                whole(rates),
                whole(head_gain),
            ],
            out_specs=[
                row_block(heads * DV),
                row_block(conv_cols),
                row_block(heads * DV),
                saved_block(DK, DV),
                saved_block(ROWS, ROWS),
                saved_block(ROWS, DV + DK),
                saved_block(ROWS, DV),
                saved_block(ROWS, ROWS),
                saved_block(2 * ROWS, ROWS),
                whole(state),
            ],
            scratch_shapes=[
                pltpu.VMEM((rows + 8, conv_cols), f32),
                pltpu.VMEM((heads, DK, DV), f32),
            ],
        ),
        out_shape=[
            rows_of(heads * DV, jnp.bfloat16),
            rows_of(conv_cols),
            rows_of(heads * DV),
            saved(DK, DV),
            saved(ROWS, ROWS),
            saved(ROWS, DV + DK),
            saved(ROWS, DV),
            saved(ROWS, ROWS),
            saved(2 * ROWS, ROWS),
            jax.ShapeDtypeStruct(state.shape, f32),
        ],
        compiler_params=pltpu.CompilerParams(vmem_limit_bytes=60 << 20),
        cost_estimate=kernel_cost(24 * row_count / 1024),
        name="mixer_forward",
    )(resets, proj, proj, state, keep, filters, rates, head_gain)


def mixer_backward(
    resets,
    own,
    got,
    resid,
    cot,
    ffn_gain,
    out_weight,
    dstate,
    later,
    proj,
    keep,
    filters,
    rates,
    head_gain,
    saved,
    heads,
    start,
    filled,
):
    row_count = resid.shape[0]
    total_rows, proj_width = proj.shape
    chunks = row_count // ROWS
    first = start // ROWS
    conv_cols = 2 * heads * DK + heads * DV
    f32 = jnp.float32

    rows = BACK_SUBS * ROWS
    steps = row_count // rows
    first_block = start // rows

    def row_block(array):
        return pl.BlockSpec((rows, array.shape[1]), lambda c, r: (steps - 1 - c, 0))

    def part_block(array):
        return pl.BlockSpec(
            (rows, array.shape[1]), lambda c, r: (first_block + steps - 1 - c, 0)
        )

    def saved_block(array):
        return pl.BlockSpec(
            (BACK_SUBS,) + array.shape[1:], lambda c, r: (steps - 1 - c, 0, 0, 0)
        )

    dproj = jax.ShapeDtypeStruct((total_rows, proj_width), jnp.bfloat16)
    dfilter = jax.ShapeDtypeStruct((8, conv_cols), f32)
    dsmall = jax.ShapeDtypeStruct((8, DV), f32)
    dmix = jax.ShapeDtypeStruct(resid.shape, jnp.bfloat16)
    dresid = jax.ShapeDtypeStruct(resid.shape, f32)
    dffn_gain = jax.ShapeDtypeStruct((8, resid.shape[1]), f32)
    args = [resets, own, got, resid, cot, ffn_gain, out_weight, dstate, later]
    args += [proj, keep, filters, rates, head_gain, *saved]
    specs = [row_block(own), row_block(got), row_block(resid), part_block(cot), whole(ffn_gain)]
    specs += [
        pl.BlockSpec(
            (resid.shape[1], heads * DV), lambda c, r: (0, 0), pipeline_mode=pl.Buffered(1)
        )
    ]
    specs += [whole(dstate), whole(later), part_block(proj), part_block(keep)]
    specs += [whole(filters), whole(rates), whole(head_gain)]
    specs += [row_block(saved[0]), row_block(saved[1])]
    specs += [saved_block(array) for array in saved[2:]]
    aliases = {}
    if filled is not None:
        aliases = {len(args): 0}
        args.append(filled)
        specs.append(pl.BlockSpec(memory_space=pl.ANY))
    return pl.pallas_call(
        partial(backward_kernel, heads, first, chunks),
        grid_spec=pltpu.PrefetchScalarGridSpec(
            num_scalar_prefetch=1,
            grid=(steps,),
            in_specs=specs,
            out_specs=[
                part_block(dproj),
                whole(dfilter),
                whole(dsmall),
                row_block(dmix),
                row_block(dresid),
                whole(dffn_gain),
                whole(dstate),
                whole(later),
            ],
            scratch_shapes=[
                pltpu.VMEM((rows + 8, conv_cols), f32),
                pltpu.VMEM((heads, DK, DV), f32),
            ],
        ),
        out_shape=[
            dproj,
            dfilter,
            dsmall,
            dmix,
            dresid,
            dffn_gain,
            jax.ShapeDtypeStruct(dstate.shape, f32),
            jax.ShapeDtypeStruct(later.shape, f32),
        ],
        input_output_aliases=aliases,
        compiler_params=pltpu.CompilerParams(vmem_limit_bytes=60 << 20),
        cost_estimate=kernel_cost(30 * row_count / 1024),
        name="mixer_backward",
    )(*args)


def ffn_both_ways(own, other, inputs, cot_masked, keep, gain, weight, ff_cols, start, filled):
    row_count, own_cols = own.shape
    total_rows, width = inputs.shape
    rows = FFN_ROWS
    first = start // rows
    bf16 = jnp.bfloat16

    def whole(array):
        return pl.BlockSpec(array.shape, lambda c: (0, 0))

    def row_block(cols):
        return pl.BlockSpec((rows, cols), lambda c: (c, 0))

    def part_block(cols):
        return pl.BlockSpec((rows, cols), lambda c: (c + first, 0))

    args = [own, other, inputs, cot_masked, keep, gain, weight]
    specs = [row_block(own_cols), row_block(own_cols), part_block(width), part_block(width)]
    specs += [part_block(keep.shape[1]), whole(gain)]
    specs += [pl.BlockSpec(memory_space=pl.ANY)]
    aliases = {}
    if filled is not None:
        aliases = {len(args): 2, len(args) + 1: 3}
        args += list(filled)
        specs += [pl.BlockSpec(memory_space=pl.ANY)] * 2
    return pl.pallas_call(
        partial(ffn_kernel, 2 * own_cols, ff_cols),
        grid=(row_count // rows,),
        in_specs=specs,
        out_specs=[
            row_block(width),
            row_block(width),
            part_block(width),
            part_block(3 * ff_cols),
        ],
        out_shape=[
            jax.ShapeDtypeStruct((row_count, width), jnp.float32),
            jax.ShapeDtypeStruct((row_count, width), bf16),
            jax.ShapeDtypeStruct((total_rows, width), bf16),
            jax.ShapeDtypeStruct((total_rows, 3 * ff_cols), bf16),
        ],
        scratch_shapes=[pltpu.VMEM(weight.shape, bf16), pltpu.SemaphoreType.DMA((4,))],
        input_output_aliases=aliases,
        compiler_params=pltpu.CompilerParams(vmem_limit_bytes=60 << 20),
        cost_estimate=kernel_cost(28 * row_count / 1024),
        name="ffn_both_ways",
    )(*args)


def ffn_outputs(acts, weight, ff_cols):
    row_count = acts.shape[0]
    width = weight.shape[0]
    rows = 256
    bf16 = jnp.bfloat16
    return pl.pallas_call(
        partial(ffn_out_kernel, weight.shape[1] - ff_cols),
        grid=(row_count // rows,),
        in_specs=[
            pl.BlockSpec((rows, ff_cols), lambda c: (c, 2)),
            pl.BlockSpec(memory_space=pl.ANY),
        ],
        out_specs=pl.BlockSpec((rows, width), lambda c: (c, 0)),
        out_shape=jax.ShapeDtypeStruct((row_count, width), bf16),
        scratch_shapes=[pltpu.VMEM((width, ff_cols), bf16), pltpu.SemaphoreType.DMA],
        compiler_params=pltpu.CompilerParams(vmem_limit_bytes=60 << 20),
        cost_estimate=kernel_cost(0.1),
        name="ffn_outputs",
    )(acts, weight)


def grads_kernel(
    shard_rows,
    side_ref,
    normed_ref,
    dproj_ref,
    dmix_lo_ref,
    dmix_hi_ref,
    gated_lo_ref,
    gated_hi_ref,
    mine_a_ref,
    mine_b_ref,
    theirs_a_ref,
    theirs_b_ref,
    rate_ref,
):
    side = side_ref[0]
    normed = normed_ref[...]
    gate_cols = gated_lo_ref.shape[1]
    first_cols = mine_a_ref.shape[1]

    def put(grad, mine_ref, theirs_ref, cols):
        pairs = grad.reshape(-1, 2, shard_rows, grad.shape[-1])
        even = pairs[:, 0].reshape(-1, grad.shape[-1])
        odd = pairs[:, 1].reshape(-1, grad.shape[-1])
        mine_ref[:, cols] = jnp.where(side == 0, even, odd).astype(jnp.bfloat16)
        theirs_ref[:, cols] = jnp.where(side == 0, odd, even).astype(jnp.bfloat16)

    put(dot(normed, dproj_ref[:, :first_cols], TN), mine_a_ref, theirs_a_ref, slice(None))
    put(
        dot(normed, dproj_ref[:, first_cols : first_cols + gate_cols], TN),
        mine_b_ref,
        theirs_b_ref,
        slice(0, gate_cols),
    )
    put(
        dot(dmix_lo_ref[...], gated_lo_ref[...], TN)
        + dot(dmix_hi_ref[...], gated_hi_ref[...], TN),
        mine_b_ref,
        theirs_b_ref,
        slice(gate_cols, 2 * gate_cols),
    )
    rate_ref[...] = dot(dproj_ref[:, first_cols + gate_cols :], normed, TN)[:8]


def mixer_weight_grads(side, normed, dproj, dmix_lo, dmix_hi, gated_lo, gated_hi, shard_rows):
    rows, width = normed.shape
    half_rows, v_cols = gated_lo.shape
    tile = 256
    first_cols = 2 * v_cols
    bf16 = jnp.bfloat16

    def column_block(array):
        return pl.BlockSpec((array.shape[0], tile), lambda c, r: (0, c))

    def row_block(cols):
        return pl.BlockSpec((tile // 2, cols), lambda c, r: (c, 0))

    return pl.pallas_call(
        partial(grads_kernel, shard_rows),
        grid_spec=pltpu.PrefetchScalarGridSpec(
            num_scalar_prefetch=1,
            grid=(width // tile,),
            in_specs=[
                column_block(normed),
                whole(dproj),
                column_block(dmix_lo),
                column_block(dmix_hi),
                whole(gated_lo),
                whole(gated_hi),
            ],
            out_specs=[
                row_block(first_cols),
                row_block(first_cols),
                row_block(first_cols),
                row_block(first_cols),
                pl.BlockSpec((8, tile), lambda c, r: (0, c)),
            ],
        ),
        out_shape=[
            jax.ShapeDtypeStruct((width // 2, first_cols), bf16),
            jax.ShapeDtypeStruct((width // 2, first_cols), bf16),
            jax.ShapeDtypeStruct((width // 2, first_cols), bf16),
            jax.ShapeDtypeStruct((width // 2, first_cols), bf16),
            jax.ShapeDtypeStruct((8, width), jnp.float32),
        ],
        compiler_params=pltpu.CompilerParams(vmem_limit_bytes=60 << 20),
        cost_estimate=kernel_cost(8),
        name="mixer_weight_grads",
    )(side, normed, dproj, dmix_lo, dmix_hi, gated_lo, gated_hi)


def ffn_grads_kernel(normed_ref, cot_ref, acts_ref, grads_ref):
    part = pl.program_id(0)

    @pl.when(part < 2)
    def _():
        grads_ref[...] = dot(normed_ref[...], acts_ref[...], TN).astype(jnp.bfloat16)

    @pl.when(part == 2)
    def _():
        grads_ref[...] = dot(cot_ref[...], acts_ref[...], TN).astype(jnp.bfloat16)


def ffn_weight_grads(normed, cot_masked, acts, ff_cols):
    rows, width = normed.shape

    def fixed(array):
        return pl.BlockSpec(array.shape, lambda c: (0, 0), pipeline_mode=pl.Buffered(1))

    return pl.pallas_call(
        ffn_grads_kernel,
        grid=(3,),
        in_specs=[
            fixed(normed),
            fixed(cot_masked),
            pl.BlockSpec((rows, ff_cols), lambda c: (0, c)),
        ],
        out_specs=pl.BlockSpec((width, ff_cols), lambda c: (0, c)),
        out_shape=jax.ShapeDtypeStruct((width, 3 * ff_cols), jnp.bfloat16),
        compiler_params=pltpu.CompilerParams(vmem_limit_bytes=60 << 20),
        cost_estimate=kernel_cost(0.1),
        name="ffn_weight_grads",
    )(normed, cot_masked, acts)


def swap_halves(array):
    return lax.ppermute(array, "mp", [(0, 1), (1, 0)])


def dp_total(array):
    count = lax.axis_size("dp")
    step = 1
    while step < count:
        array = array + lax.ppermute(array, "dp", [(i, i ^ step) for i in range(count)])
        step *= 2
    return array


def dp_swap(array, bit):
    count = lax.axis_size("dp")
    return lax.ppermute(array, "dp", [(i, i ^ bit) for i in range(count)])


def dp_gather(shard, cuts, first_held, then):
    index = lax.axis_index("dp")
    bits = [1 << i for i in reversed(range((lax.axis_size("dp") - 1).bit_length()))]
    pieces = [shard[None, :, start:stop] for start, stop in cuts]
    for at, bit in enumerate(bits):
        if at == 1:
            pieces, first_held = lax.optimization_barrier((pieces, first_held))
            then_held = then(first_held)
        if at == 3:
            pieces, then_held = lax.optimization_barrier((pieces, then_held))
        others = [dp_swap(piece, bit) for piece in pieces]
        upper = (index & bit) != 0
        pieces = [
            jnp.stack(
                [jnp.where(upper, other, piece), jnp.where(upper, piece, other)], axis=1
            ).reshape((-1,) + piece.shape[1:])
            for piece, other in zip(pieces, others)
        ]
    return [piece.reshape(-1, piece.shape[-1]) for piece in pieces], first_held, then_held


def scatter_first(kept, sent):
    return [
        (mine.astype(jnp.float32) + dp_swap(theirs, 1).astype(jnp.float32)).astype(mine.dtype)
        for mine, theirs in zip(kept, sent)
    ]


def scatter_step(pieces, at):
    index = lax.axis_index("dp")
    bits = [1 << i for i in range(1, (lax.axis_size("dp") - 1).bit_length())]
    orders = [bits, bits[1:2] + bits[:1] + bits[2:]]
    sums = []
    for piece, order in zip(pieces, orders):
        left = sorted(order[at:], reverse=True)
        bit = order[at]
        axis = left.index(bit)
        side = (index & bit) // bit
        cut = piece.reshape((2,) * len(left) + (-1, piece.shape[-1]))
        sent = lax.dynamic_index_in_dim(cut, 1 - side, axis, False).astype(jnp.bfloat16)
        mine = lax.dynamic_index_in_dim(cut, side, axis, False)
        total = mine.astype(jnp.float32) + dp_swap(sent, bit).astype(jnp.float32)
        sums.append(total.astype(piece.dtype).reshape(-1, piece.shape[-1]))
    return sums


def scatter_steps():
    return (lax.axis_size("dp") - 1).bit_length() - 1


def in_order(own, other, model_index, axis):
    first = jnp.where(model_index == 0, own, other)
    second = jnp.where(model_index == 0, other, own)
    return jnp.concatenate([first, second], axis=axis)


def on_device(
    block_input,
    seq_lengths,
    seq_owner,
    mix_gain,
    query_weight,
    key_weight,
    value_weight,
    gate_weight,
    decay_weight,
    beta_weight,
    query_filter,
    key_filter,
    value_filter,
    decay_log,
    decay_bias,
    head_gain,
    out_weight,
    ffn_gain,
    ffn_gate,
    ffn_up,
    ffn_down,
    cotangent,
):
    bf16 = jnp.bfloat16
    f32 = jnp.float32
    local_rows, width = block_input.shape
    dp_index = lax.axis_index("dp")
    model_count = lax.axis_size("mp")
    model_index = lax.axis_index("mp")
    row_count = local_rows * model_count
    keep_masks, resets, valid_rows = layout(seq_lengths, seq_owner, dp_index, row_count)
    valid_all = valid_rows[:, None]
    heads_local = decay_log.shape[0] // model_count
    qk_cols = heads_local * DK
    v_cols = heads_local * DV
    ff_cols = ffn_gate.shape[1]
    shard_rows = query_weight.shape[0]
    proj_cols = 2 * qk_cols + 2 * v_cols

    def own_columns(array, col_count):
        return lax.dynamic_slice_in_dim(array, model_index * col_count, col_count, array.ndim - 1)

    def own_shard(array):
        return lax.dynamic_slice_in_dim(array, dp_index * shard_rows, shard_rows, 0)

    small_weight = jnp.concatenate(
        [own_columns(decay_weight, heads_local), own_columns(beta_weight, heads_local)], axis=1
    )
    small_weight = jnp.pad(small_weight, ((0, 0), (0, 128 - 2 * heads_local)))
    shard_mix = jnp.concatenate(
        [query_weight, key_weight, value_weight, gate_weight, own_shard(small_weight)], axis=1
    )
    half = proj_cols // 256 * 128
    out_rows = out_weight.T
    shard_ffn = jnp.concatenate([ffn_gate, ffn_up, ffn_down.T], axis=1)
    out_other = swap_halves(out_rows)
    input_other = swap_halves(block_input)
    mix_pieces, (out_other, out_rows, shard_ffn), (input_other, cot_held) = dp_gather(
        shard_mix,
        ((0, half), (half, shard_mix.shape[1])),
        (out_other, out_rows, shard_ffn),
        lambda held: (input_other, cotangent),
    )
    mix_weight = jnp.concatenate(mix_pieces, axis=1)
    shard_rest = jnp.concatenate([out_rows, out_other, shard_ffn], axis=1)
    rest_weight = lax.all_gather(shard_rest, "dp", axis=0, tiled=True)
    cot_other = swap_halves(cot_held)

    filters = jnp.concatenate(
        [
            own_columns(query_filter, qk_cols),
            own_columns(key_filter, qk_cols),
            own_columns(value_filter, v_cols),
        ],
        axis=1,
    )
    filters = jnp.pad(filters, ((0, 8 - KW), (0, 0)))
    rates = jnp.stack(
        [own_columns(decay_bias, heads_local), -jnp.exp(own_columns(decay_log, heads_local))]
    )
    rates = jnp.pad(rates, ((0, 6), (0, 128 - heads_local)))
    gain_row = head_gain[None]
    restarts = resets.astype(jnp.int32)
    later_masks = [
        jnp.concatenate([keep_masks[offset, offset:], jnp.ones((offset,), f32)])
        for offset in range(KW)
    ]
    keep_cols = jnp.stack(
        [keep_masks[offset] for offset in range(KW)] + later_masks + [valid_rows] * 8, axis=1
    )
    inputs_b = in_order(block_input, input_other, model_index, 0)
    inputs_f = inputs_b.astype(f32)
    cot_all = in_order(cotangent, cot_other, model_index, 0)
    normed1, inv_rms1 = rms_forward(inputs_f)
    mixed_in = (normed1 * mix_gain).astype(bf16)
    proj = jnp.dot(mixed_in, mix_weight, preferred_element_type=f32)
    cuts = (qk_cols, 2 * qk_cols, 2 * qk_cols + v_cols, proj_cols)
    middle = row_count // 2
    zero_state = jnp.zeros((heads_local, DK, DV), f32)
    small_args = (keep_cols, filters, rates, gain_row)
    gated_lo, *saved_lo, carried = mixer_forward(
        restarts, proj, *small_args, heads_local, 0, middle, zero_state
    )
    cot_masked = cot_all * valid_all.astype(bf16)
    ffn_row = ffn_gain[None]
    carried, cot_all, cot_masked, inputs_b = lax.optimization_barrier(
        (carried, cot_all, cot_masked, inputs_b)
    )
    gated_hi, *saved_hi, _ = mixer_forward(
        restarts, proj, *small_args, heads_local, middle, row_count, carried
    )
    other_lo = swap_halves(gated_lo)
    gated_sent, other_lo = lax.optimization_barrier((gated_hi, other_lo))
    other_hi = swap_halves(gated_sent)
    ffn_args = (inputs_b, cot_masked, keep_cols, ffn_row, rest_weight, ff_cols)
    resid_lo, dnormed_lo, *filled = ffn_both_ways(
        gated_lo, other_lo, *ffn_args, 0, None
    )
    resid_hi, dnormed_hi, ffn_in, acts = ffn_both_ways(
        gated_hi, other_hi, *ffn_args, middle, filled
    )
    got_hi, dnormed_lo = lax.optimization_barrier((swap_halves(dnormed_hi), dnormed_lo))
    got_lo = swap_halves(dnormed_lo)
    core_side = (dp_index & 1).reshape(1)
    rest_grads = ffn_weight_grads(ffn_in, cot_masked, acts, ff_cols)
    acts_later, _ = lax.optimization_barrier((acts, rest_grads))
    summand = ffn_outputs(acts_later, rest_weight, ff_cols)
    got_hi, summand = lax.optimization_barrier((got_hi, summand))
    ffn_shard = lax.psum_scatter(rest_grads, "dp", scatter_dimension=0, tiled=True)

    def own_half(array):
        return lax.dynamic_slice_in_dim(array, model_index * local_rows, local_rows, 0)

    def other_half(array):
        return lax.dynamic_slice_in_dim(array, (1 - model_index) * local_rows, local_rows, 0)

    def own_of(low, high):
        return jnp.where(model_index == 0, low, high)

    zero_rows = jnp.zeros((8, proj_cols - v_cols), f32)
    proj_grad, filter_hi, small_hi, dmix_hi, dresid_hi, ffn_gain_hi, carried, later = (
        mixer_backward(
            restarts,
            dnormed_hi,
            got_hi,
            resid_hi,
            cot_all,
            ffn_row,
            rest_weight,
            zero_state,
            zero_rows,
            proj,
            *small_args,
            saved_hi,
            heads_local,
            middle,
            None,
        )
    )
    summand_sent, got_lo, proj_grad = lax.optimization_barrier(
        (other_half(summand), got_lo, proj_grad)
    )
    proj_grad, filter_lo, small_lo, dmix_lo, dresid_lo, ffn_gain_lo, _, _ = mixer_backward(
        restarts,
        dnormed_lo,
        got_lo,
        resid_lo,
        cot_all,
        ffn_row,
        rest_weight,
        carried,
        later,
        proj,
        *small_args,
        saved_lo,
        heads_local,
        0,
        proj_grad,
    )
    summand_got, proj_grad, dmix_lo, filter_lo, small_lo, dresid_lo, ffn_gain_lo = (
        lax.optimization_barrier(
            (
                swap_halves(summand_sent),
                proj_grad,
                dmix_lo,
                filter_lo,
                small_lo,
                dresid_lo,
                ffn_gain_lo,
            )
        )
    )
    ffn_sum = own_half(summand).astype(f32) + summand_got.astype(f32)
    block_output = (own_of(resid_lo, resid_hi) + own_half(valid_all) * ffn_sum).astype(bf16)
    filter_grads = filter_lo + filter_hi
    small_grads = small_lo + small_hi
    ffn_gain_part = ffn_gain_lo[0] + ffn_gain_hi[0]
    *grad_pieces, rate_grads = mixer_weight_grads(
        core_side,
        mixed_in,
        proj_grad,
        dmix_lo,
        dmix_hi,
        gated_lo,
        gated_hi,
        shard_rows,
    )
    rate_grads = rate_grads[: 2 * heads_local]
    mix_sums = scatter_first(grad_pieces[:2], grad_pieces[2:])
    proj_grad, mix_sums, rate_grads = lax.optimization_barrier(
        (proj_grad, mix_sums, rate_grads)
    )
    mix_sums = scatter_step(mix_sums, 0)
    mix_in_part = against(proj_grad, mix_weight)
    mix_gain_part = jnp.sum(mix_in_part * normed1, 0)
    common = jnp.concatenate(
        [mix_gain_part, ffn_gain_part, small_grads[0], jnp.zeros((width - DV,), f32)]
    ).reshape(3, width)
    tail_row = jnp.concatenate(
        [small_grads[1, : 2 * heads_local], jnp.zeros((width - 2 * heads_local,), f32)]
    )
    split_rows = jnp.concatenate(
        [
            rate_grads,
            filter_grads[:KW, : cuts[0]].reshape(-1, width),
            filter_grads[:KW, cuts[0] : cuts[1]].reshape(-1, width),
            filter_grads[:KW, cuts[1] : cuts[2]].reshape(-1, width),
            tail_row[None],
        ],
        axis=0,
    )
    mix_in_sent = other_half(mix_in_part).astype(bf16)
    mix_in_got = swap_halves(mix_in_sent)
    mix_sums, small_sums, _ = lax.optimization_barrier(
        (mix_sums, jnp.concatenate([common, split_rows], axis=0), mix_in_sent)
    )
    totals = dp_total(small_sums)
    for step in range(1, scatter_steps()):
        if step == 2:
            mix_sums, totals, mix_in_got = lax.optimization_barrier(
                (mix_sums, totals, mix_in_got)
            )
            totals_other = swap_halves(totals)
        mix_sums = scatter_step(mix_sums, step)
    mix_shards = [piece.astype(f32) for piece in mix_sums]
    mix_in_sum = own_half(mix_in_part) + mix_in_got.astype(f32)
    input_grad = own_of(dresid_lo, dresid_hi) + rms_backward(
        mix_in_sum * mix_gain, own_half(normed1), own_half(inv_rms1)
    )
    common = totals[:3] + totals_other[:3]
    lower = jnp.where(model_index == 0, totals, totals_other)[3:]
    upper = jnp.where(model_index == 0, totals_other, totals)[3:]

    def joined(start, rows, cols):
        return jnp.concatenate(
            [
                lower[start : start + rows].reshape(-1, cols),
                upper[start : start + rows].reshape(-1, cols),
            ],
            axis=1,
        )

    q_rows = KW * qk_cols // width
    v_rows = KW * v_cols // width
    at_q = 2 * heads_local
    at_k = at_q + q_rows
    at_v = at_k + q_rows
    at_tail = at_v + v_rows

    def rate_weight_grad(start):
        return jnp.concatenate(
            [lower[start : start + heads_local], upper[start : start + heads_local]], axis=0
        ).T

    def rate_grad(start):
        return jnp.concatenate(
            [
                lower[at_tail, start : start + heads_local],
                upper[at_tail, start : start + heads_local],
            ]
        )

    ffn_shard = ffn_shard.astype(f32)
    return (
        block_output,
        input_grad,
        common[0],
        mix_shards[0][:, : cuts[0]],
        mix_shards[0][:, cuts[0] : cuts[1]],
        mix_shards[0][:, cuts[1] :],
        mix_shards[1][:, :v_cols],
        rate_weight_grad(0),
        rate_weight_grad(heads_local),
        joined(at_q, q_rows, qk_cols),
        joined(at_k, q_rows, qk_cols),
        joined(at_v, v_rows, v_cols),
        rate_grad(0),
        rate_grad(heads_local),
        common[2, :DV],
        mix_shards[1][:, v_cols:].T,
        common[1],
        ffn_shard[:, :ff_cols],
        ffn_shard[:, ff_cols : 2 * ff_cols],
        ffn_shard[:, 2 * ff_cols :].T,
    )


def solution(mesh):
    in_specs = (
        P(("dp", "mp"), None),
        P(),
        P(),
        P(),
        P("dp", "mp"),
        P("dp", "mp"),
        P("dp", "mp"),
        P("dp", "mp"),
        P(),
        P(),
        P(),
        P(),
        P(),
        P(),
        P(),
        P(),
        P("mp", "dp"),
        P(),
        P("dp", "mp"),
        P("dp", "mp"),
        P("mp", "dp"),
        P(("dp", "mp"), None),
    )
    out_specs = (
        P(("dp", "mp"), None),
        P(("dp", "mp"), None),
        P(),
        P("dp", "mp"),
        P("dp", "mp"),
        P("dp", "mp"),
        P("dp", "mp"),
        P(),
        P(),
        P(),
        P(),
        P(),
        P(),
        P(),
        P(),
        P("mp", "dp"),
        P(),
        P("dp", "mp"),
        P("dp", "mp"),
        P("mp", "dp"),
    )
    return jax.shard_map(
        on_device, mesh=mesh, in_specs=in_specs, out_specs=out_specs, check_vma=False
    )
```

```python
from functools import partial
import math

import jax
import jax.numpy as jnp
from jax import lax
from jax.experimental import pallas as pl
from jax.experimental.pallas import tpu as pltpu
from jax.sharding import PartitionSpec as P

DK = 128
DV = 256
KW = 4
SPAN = 64


EPS = 1e-06


def layout(seq_lengths, seq_owner, device, row_count):
    owned = seq_owner == device
    own_lengths = jnp.where(owned, seq_lengths, 0)
    offsets = jnp.cumsum(own_lengths) - own_lengths
    loaded = jnp.sum(own_lengths)
    span_starts = jnp.arange(row_count // SPAN, dtype=jnp.int32) * SPAN
    begins = jnp.any(
        (offsets[None, :] == span_starts[:, None]) & (own_lengths[None, :] > 0), axis=1
    )
    resets = begins | (span_starts == loaded)
    within = jnp.arange(SPAN, dtype=jnp.int32)
    keep_masks = jnp.stack(
        [
            jnp.logical_not(resets[:, None] & (within[None, :] < offset)).reshape(row_count)
            for offset in range(KW)
        ]
    ).astype(jnp.float32)
    valid_rows = (jnp.arange(row_count, dtype=jnp.int32) < loaded).astype(jnp.float32)
    return (keep_masks, resets, valid_rows)


def across_rows(left, right):
    return lax.dot_general(
        left, right, (((0,), (0,)), ((), ())), preferred_element_type=jnp.float32
    )


def against(left, right):
    return lax.dot_general(
        left, right, (((1,), (1,)), ((), ())), preferred_element_type=jnp.float32
    )


def rms_forward(values):
    inv_rms = lax.rsqrt(jnp.mean(values * values, -1, keepdims=True) + EPS)
    return (values * inv_rms, inv_rms)


def rms_backward(upstream, normed, inv_rms):
    return inv_rms * (upstream - normed * jnp.mean(upstream * normed, -1, keepdims=True))


ROWS = 128
NN = ((1,), (0,))
NT = ((1,), (1,))
TN = ((0,), (0,))
FINE_GRAM = True
FINE_INVERSE = True
FINE_MERGE = True
SUBS = 2
FFN_ROWS = 256
FINE_APPLY = True
FINE_STATE = True
FINE_BACK = (True,) * 10
BACK_SUBS = 2


def dot(left, right, dims):
    return lax.dot_general(left, right, (dims, ((), ())), preferred_element_type=jnp.float32)


def high_low(values):
    high = values.astype(jnp.bfloat16)
    return high, (values - high.astype(jnp.float32)).astype(jnp.bfloat16)


def product(left, right, dims, fine=False):
    if not fine:
        return dot(left.astype(jnp.bfloat16), right.astype(jnp.bfloat16), dims)
    left_high, left_low = high_low(left)
    right_high, right_low = high_low(right)
    (left_axis,), (right_axis,) = dims
    depth = right.shape[right_axis]
    count = right.shape[1 - right_axis]
    if depth <= 128:
        both = jnp.concatenate([left_high, left_low], axis=left_axis)
        if count <= 128:
            wide = jnp.concatenate([right_high, right_low], axis=1 - right_axis)
            part = jnp.concatenate([right_high, jnp.zeros_like(right_low)], axis=1 - right_axis)
            result = dot(both, jnp.concatenate([wide, part], axis=right_axis), dims)
            return result[:, :count] + result[:, count:]
        return dot(both, jnp.concatenate([right_high, right_high], axis=right_axis), dims) + dot(
            left_high, right_low, dims
        )
    if count <= 128:
        wide = jnp.concatenate([right_high, right_low], axis=1 - right_axis)
        result = dot(left_high, wide, dims)
        return result[:, :count] + (result[:, count:] + dot(left_low, right_high, dims))
    return dot(left_high, right_high, dims) + (
        dot(left_high, right_low, dims) + dot(left_low, right_high, dims)
    )


def summed_by(mask, values, dims=NN):
    high, low = high_low(values)
    return dot(mask, high, dims) + dot(mask, low, dims)


def chunk_masks(resets_ref, chunk):
    first = 1.0 - resets_ref[2 * chunk].astype(jnp.float32)
    second = 1.0 - resets_ref[2 * chunk + 1].astype(jnp.float32)
    row = lax.broadcasted_iota(jnp.int32, (ROWS, ROWS), 0)
    col = lax.broadcasted_iota(jnp.int32, (ROWS, ROWS), 1)
    late = row >= SPAN
    reached = jnp.where(late, first * second, first)
    reaching = jnp.where(late, 1.0, second)
    joined = jnp.where(late & (col < SPAN), second, 1.0)
    return row, col, reached, reaching, joined, first * second


def unit_lower_inverses(couplings, row, col):
    eye = jnp.where(row == col, 1.0, 0.0)
    base = 16
    near = (row // base) == (col // base)
    powered = [jnp.where(near, coupling, 0.0) for coupling in couplings]
    inverses = [eye - power for power in powered]
    size = 2
    while size < base:
        powered = [product(power, power, NN, FINE_INVERSE) for power in powered]
        inverses = [
            inverse + product(inverse, power, NN, FINE_INVERSE)
            for inverse, power in zip(inverses, powered)
        ]
        size *= 2
    while base < ROWS:
        wide = 2 * base
        linked = ((row // wide) == (col // wide)) & ((row // base) != (col // base))
        steps = [
            product(jnp.where(linked, coupling, 0.0), inverse, NN, FINE_MERGE)
            for coupling, inverse in zip(couplings, inverses)
        ]
        inverses = [
            inverse - product(inverse, step, NN, FINE_MERGE)
            for inverse, step in zip(inverses, steps)
        ]
        base = wide
    return inverses


def sigmoid(values):
    return 1.0 / (1.0 + jnp.exp(-values))


def lane_sum(values):
    return jnp.sum(values, -1, keepdims=True)


def forward_kernel(
    heads,
    base,
    resets_ref,
    proj_ref,
    before_ref,
    state_in_ref,
    keep_ref,
    filter_ref,
    rates_ref,
    gain_ref,
    gated_ref,
    conv_ref,
    mixed_ref,
    state_ref,
    inverse_ref,
    parts_ref,
    written_ref,
    factor_ref,
    grams_ref,
    state_out_ref,
    rows_buf,
    state_buf,
):
    step = pl.program_id(0)
    qk = heads * DK
    conv_cols = 2 * qk + heads * DV
    proj_cols = conv_cols + heads * DV
    rows = SUBS * ROWS

    @pl.when(step == 0)
    def _():
        if base == 0:
            rows_buf[0:8, :] = jnp.zeros((8, conv_cols), jnp.float32)
        else:
            rows_buf[0:8, :] = before_ref[:, :conv_cols]
        state_buf[...] = state_in_ref[...]

    rows_buf[8 : 8 + rows, :] = proj_ref[:, :conv_cols]
    conv = rows_buf[8 : 8 + rows, :] * filter_ref[0:1, :]
    for offset in range(1, KW):
        conv = conv + rows_buf[8 - offset : 8 - offset + rows, :] * (
            filter_ref[offset : offset + 1, :] * keep_ref[:, offset : offset + 1]
        )
    rows_buf[0:8, :] = rows_buf[rows : rows + 8, :]
    conv_ref[...] = conv

    rate = proj_ref[:, proj_cols : proj_cols + 128]
    shifted = rate + rates_ref[0:1, :]
    decay_all = rates_ref[1:2, :] * (
        jnp.maximum(shifted, 0.0) + jnp.log1p(jnp.exp(-jnp.abs(shifted)))
    )
    beta_all = sigmoid(rate)
    units = [(sub, head) for sub in range(SUBS) for head in range(heads)]
    prepared = []
    for sub, head in units:
        row, col, reached, reaching, joined, passed = chunk_masks(
            resets_ref, base + step * SUBS + sub
        )
        lower = jnp.where(row >= col, 1.0, 0.0)
        at = slice(sub * ROWS, (sub + 1) * ROWS)
        decay = jnp.broadcast_to(decay_all[at, head : head + 1], (ROWS, ROWS))
        beta = beta_all[at, heads + head : heads + head + 1]
        sums = summed_by(
            lower.astype(jnp.bfloat16),
            jnp.concatenate([jnp.where(row > col, decay, 0.0), decay], axis=1),
        )
        factor = jnp.exp(sums[:, :ROWS]) * (lower * joined)
        total = sums[:, ROWS:]
        total_end = total[ROWS - 1 : ROWS, :]
        grown = jnp.exp(total) * reached
        tail = jnp.exp(total_end - total) * reaching
        end_decay = jnp.exp(total_end[:, :1]) * passed

        conv_q = conv[at, head * DK : (head + 1) * DK]
        conv_k = conv[at, qk + head * DK : qk + (head + 1) * DK]
        conv_v = conv[at, 2 * qk + head * DV : 2 * qk + (head + 1) * DV]
        query = conv_q * sigmoid(conv_q)
        query = query * (lax.rsqrt(lane_sum(query * query) + EPS) * (1.0 / math.sqrt(DK)))
        key = conv_k * sigmoid(conv_k)
        key = key * lax.rsqrt(lane_sum(key * key) + EPS)
        value = conv_v * sigmoid(conv_v)

        grams = product(jnp.concatenate([key, query], axis=0), key, NT, FINE_GRAM)
        coupling = jnp.where(row > col, factor * grams[:ROWS] * beta, 0.0)
        scaled = jnp.concatenate([beta * value, (beta * grown) * key], axis=1)
        factor_ref[sub, head] = factor
        grams_ref[sub, head] = grams
        prepared.append(
            (coupling, scaled, grown * query, factor * grams[ROWS:], tail * key, end_decay)
        )
    row = lax.broadcasted_iota(jnp.int32, (ROWS, ROWS), 0)
    col = lax.broadcasted_iota(jnp.int32, (ROWS, ROWS), 1)
    inverses = unit_lower_inverses([entry[0] for entry in prepared], row, col)
    for (sub, head), inverse, entry in zip(units, inverses, prepared):
        _, scaled, query_grown, mixing, key_tail, end_decay = entry
        at = slice(sub * ROWS, (sub + 1) * ROWS)
        parts = product(inverse, scaled, NN, FINE_APPLY)
        state = state_buf[head]
        from_state = product(
            jnp.concatenate([parts[:, DV:], query_grown], axis=0), state, NN, FINE_STATE
        )
        written = parts[:, :DV] - from_state[:ROWS]
        mixed = from_state[ROWS:] + product(mixing, written, NN, FINE_STATE)
        state_buf[head] = end_decay * state + product(key_tail, written, TN, FINE_STATE)

        gate = proj_ref[at, conv_cols + head * DV : conv_cols + (head + 1) * DV]
        normed = mixed * lax.rsqrt(lane_sum(mixed * mixed) * (1.0 / DV) + EPS)
        gated_ref[at, head * DV : (head + 1) * DV] = (
            normed * gain_ref[...] * (gate * sigmoid(gate))
        ).astype(jnp.bfloat16)
        mixed_ref[at, head * DV : (head + 1) * DV] = mixed
        state_ref[sub, head] = state
        inverse_ref[sub, head] = inverse
        parts_ref[sub, head] = parts
        written_ref[sub, head] = written

    @pl.when(step == pl.num_programs(0) - 1)
    def _():
        state_out_ref[...] = state_buf[...]


def backward_kernel(
    heads,
    base,
    chunks,
    resets_ref,
    own_ref,
    got_ref,
    resid_ref,
    cot_ref,
    ffn_gain_ref,
    out_weight_ref,
    dstate_in_ref,
    later_ref,
    proj_ref,
    keep_ref,
    filter_ref,
    rates_ref,
    gain_ref,
    conv_ref,
    mixed_ref,
    state_ref,
    inverse_ref,
    parts_ref,
    written_ref,
    factor_ref,
    grams_ref,
    *tail_refs,
):
    (
        dproj_ref,
        dfilter_ref,
        dsmall_ref,
        dmix_ref,
        dresid_ref,
        dffn_gain_ref,
        dstate_out_ref,
        first_ref,
        rows_buf,
        dstate_buf,
    ) = tail_refs[-10:]
    step = pl.program_id(0)
    last_step = pl.num_programs(0) - 1
    rows = BACK_SUBS * ROWS
    qk = heads * DK
    conv_cols = 2 * qk + heads * DV
    proj_cols = conv_cols + heads * DV

    @pl.when(step == 0)
    def _():
        rows_buf[rows : rows + 8, :] = later_ref[...]
        dstate_buf[...] = dstate_in_ref[...]
        dffn_gain_ref[...] = jnp.zeros_like(dffn_gain_ref)
        dfilter_ref[...] = jnp.zeros_like(dfilter_ref)
        dsmall_ref[...] = jnp.zeros_like(dsmall_ref)

    resid = resid_ref[...]
    inv_resid = lax.rsqrt(jnp.mean(resid * resid, -1, keepdims=True) + EPS)
    resid_normed = resid * inv_resid
    ffn_in_own = own_ref[...].astype(jnp.float32)
    dffn_gain_ref[0:1, :] += jnp.sum(ffn_in_own * resid_normed, 0, keepdims=True)
    scaled_up = (ffn_in_own + got_ref[...].astype(jnp.float32)) * ffn_gain_ref[...]
    dresid = cot_ref[...].astype(jnp.float32) + inv_resid * (
        scaled_up - resid_normed * jnp.mean(scaled_up * resid_normed, -1, keepdims=True)
    )
    dresid_ref[...] = dresid
    dmix = (dresid * keep_ref[:, 2 * KW : 2 * KW + 1]).astype(jnp.bfloat16)
    dmix_ref[...] = dmix
    dgated = dot(dmix, out_weight_ref[...], NN)
    rate = proj_ref[:, proj_cols : proj_cols + 128]
    shifted = rate + rates_ref[0:1, :]
    decay_all = rates_ref[1:2, :] * (
        jnp.maximum(shifted, 0.0) + jnp.log1p(jnp.exp(-jnp.abs(shifted)))
    )
    slope_all = rates_ref[1:2, :] * sigmoid(shifted)
    beta_all = sigmoid(rate)
    row = lax.broadcasted_iota(jnp.int32, (ROWS, ROWS), 0)
    col = lax.broadcasted_iota(jnp.int32, (ROWS, ROWS), 1)
    lower_b = jnp.where(row >= col, 1.0, 0.0).astype(jnp.bfloat16)
    upper_b = jnp.where(row <= col, 1.0, 0.0).astype(jnp.bfloat16)
    lane = lax.broadcasted_iota(jnp.int32, (ROWS, 128), 1)
    dgain = jnp.zeros((1, DV), jnp.float32)
    units = [(sub, head) for sub in reversed(range(BACK_SUBS)) for head in range(heads)]
    prepared = []
    for sub, head in units:
        at = slice(sub * ROWS, (sub + 1) * ROWS)
        chunk = base + chunks - BACK_SUBS * (step + 1) + sub
        _, _, reached, reaching, _, passed = chunk_masks(resets_ref, chunk)
        decay = jnp.broadcast_to(decay_all[at, head : head + 1], (ROWS, ROWS))
        total = summed_by(lower_b, decay)
        total_end = total[ROWS - 1 : ROWS, :]
        grown = jnp.exp(total) * reached
        tail = jnp.exp(total_end - total) * reaching
        end_decay = jnp.exp(total_end[:, :1]) * passed

        v_at = slice(head * DV, (head + 1) * DV)
        gate_at = slice(conv_cols + head * DV, conv_cols + (head + 1) * DV)
        conv_q = conv_ref[at, head * DK : (head + 1) * DK]
        conv_k = conv_ref[at, qk + head * DK : qk + (head + 1) * DK]
        query = conv_q * sigmoid(conv_q)
        inv_q = lax.rsqrt(lane_sum(query * query) + EPS)
        query = query * (inv_q * (1.0 / math.sqrt(DK)))
        key = conv_k * sigmoid(conv_k)
        inv_k = lax.rsqrt(lane_sum(key * key) + EPS)
        key = key * inv_k

        mixed = mixed_ref[at, v_at]
        inv_o = lax.rsqrt(lane_sum(mixed * mixed) * (1.0 / DV) + EPS)
        normed = mixed * inv_o
        gate = proj_ref[at, gate_at]
        sig_g = sigmoid(gate)
        upstream = dgated[at, v_at]
        up_normed = upstream * normed
        dgain = dgain + jnp.sum(up_normed * (gate * sig_g), 0, keepdims=True)
        dproj_ref[at, gate_at] = (
            up_normed * gain_ref[...] * (sig_g * (1.0 + gate * (1.0 - sig_g)))
        ).astype(jnp.bfloat16)
        dnormed = upstream * gain_ref[...] * (gate * sig_g)
        dmixed = inv_o * (dnormed - normed * (lane_sum(dnormed * normed) * (1.0 / DV)))
        mixing = factor_ref[sub, head] * grams_ref[sub, head, ROWS:]
        within = product(mixing, dmixed, TN, FINE_BACK[0])
        dmixing = product(dmixed, written_ref[sub, head], NT, FINE_BACK[3])
        prepared.append(
            (decay, grown, tail, end_decay, query, inv_q, key, inv_k, dmixed, within, dmixing)
        )
    stepped = []
    for (sub, head), entry in zip(units, prepared):
        decay, grown, tail, end_decay, query, inv_q, key, inv_k, dmixed, within, dmixing = entry
        state = state_ref[sub, head]
        dstate = dstate_buf[head]
        dwritten = within + product(tail * key, dstate, NN, FINE_BACK[1])
        dkey_tail = product(written_ref[sub, head], dstate, NT, FINE_BACK[4])
        end_grad = end_decay * lane_sum(jnp.sum(state * dstate, 0, keepdims=True))
        stacked = jnp.concatenate([dmixed, -dwritten], axis=0)
        dstate_buf[head] = end_decay * dstate + product(
            jnp.concatenate([grown * query, parts_ref[sub, head, :, DV:]], axis=0),
            stacked,
            TN,
            FINE_BACK[5],
        )
        stepped.append((dwritten, dkey_tail, end_grad, stacked))
    drates = {sub: jnp.zeros((ROWS, 128), jnp.float32) for sub in range(BACK_SUBS)}
    dsums = jnp.zeros((ROWS, 128), jnp.float32)
    throughs = [
        product(entry[3], state_ref[sub, head], NT, FINE_BACK[2])
        for (sub, head), entry in zip(units, stepped)
    ]
    solveds = [
        product(
            inverse_ref[sub, head],
            jnp.concatenate([entry[0], through[ROWS:]], axis=1),
            TN,
            FINE_BACK[6],
        )
        for (sub, head), entry, through in zip(units, stepped, throughs)
    ]
    dcouplings = [
        product(solved, parts_ref[sub, head], NT, FINE_BACK[7])
        for (sub, head), solved in zip(units, solveds)
    ]
    for at_unit, (sub, head) in enumerate(units):
        decay, grown, tail, _, query, inv_q, key, inv_k, _, _, dmixing = prepared[at_unit]
        _, dkey_tail, end_grad, _ = stepped[at_unit]
        solved = solveds[at_unit]
        at = slice(sub * ROWS, (sub + 1) * ROWS)
        q_at = slice(head * DK, (head + 1) * DK)
        k_at = slice(qk + head * DK, qk + (head + 1) * DK)
        value_at = slice(2 * qk + head * DV, 2 * qk + (head + 1) * DV)
        beta = beta_all[at, heads + head : heads + head + 1]
        factor = factor_ref[sub, head]
        conv_q = conv_ref[at, q_at]
        conv_k = conv_ref[at, k_at]
        conv_v = conv_ref[at, value_at]
        sig_q = sigmoid(conv_q)
        sig_k = sigmoid(conv_k)
        sig_v = sigmoid(conv_v)
        value = conv_v * sig_v
        query_grown = grown * query
        key_tail = tail * key
        dquery_grown = throughs[at_unit][:ROWS]
        dcoupling = jnp.where(row > col, -dcouplings[at_unit] * factor, 0.0)
        dcoupling_gram = dcoupling * grams_ref[sub, head, :ROWS]
        dbeta = lane_sum(dcoupling_gram)
        dgap = beta * dcoupling_gram + dmixing * (factor * grams_ref[sub, head, ROWS:])
        dgrams = jnp.concatenate([beta * dcoupling, dmixing * factor], axis=0)
        by_key = product(dgrams, key, NN, FINE_BACK[8])
        dkey = by_key[:ROWS] + product(
            dgrams, jnp.concatenate([key, query], axis=0), TN, FINE_BACK[9]
        )
        dquery = by_key[ROWS:] + grown * dquery_grown
        dvalue_scaled = solved[:, :DV]
        dkey_scaled = solved[:, DV:]
        scaled_rows = lane_sum(dkey_scaled * (grown * key))
        dbeta = dbeta + lane_sum(dvalue_scaled * value) + scaled_rows
        tail_rows = lane_sum(dkey_tail * key_tail)
        dkey = dkey + tail * dkey_tail + (beta * grown) * dkey_scaled
        dtotal = lane_sum(dquery_grown * query_grown) + beta * scaled_rows - tail_rows
        sums = summed_by(
            upper_b, jnp.concatenate([dgap, jnp.broadcast_to(dtotal, (ROWS, ROWS))], axis=1)
        )
        ddecay = (
            lane_sum(jnp.where(col < row, sums[:, :ROWS], 0.0))
            + sums[:, ROWS : ROWS + 1]
            + (end_grad + jnp.sum(tail_rows, 0, keepdims=True))
        )
        dshifted = ddecay * slope_all[at, head : head + 1]
        drates[sub] = (
            drates[sub]
            + jnp.where(lane == head, dshifted, 0.0)
            + jnp.where(lane == heads + head, dbeta * (beta * (1.0 - beta)), 0.0)
        )
        dsums = dsums + jnp.where(lane == head, ddecay * decay, 0.0)
        dsums = dsums + jnp.where(lane == heads + head, dshifted, 0.0)

        unit = query * math.sqrt(DK)
        dunit = dquery * (1.0 / math.sqrt(DK))
        dsilu = inv_q * (dunit - unit * lane_sum(dunit * unit))
        rows_buf[at, q_at] = dsilu * (sig_q * (1.0 + conv_q * (1.0 - sig_q)))
        dsilu = inv_k * (dkey - key * lane_sum(dkey * key))
        rows_buf[at, k_at] = dsilu * (sig_k * (1.0 + conv_k * (1.0 - sig_k)))
        rows_buf[at, value_at] = (beta * dvalue_scaled) * (
            sig_v * (1.0 + conv_v * (1.0 - sig_v))
        )

    signal = proj_ref[:, :conv_cols]
    shifted_grad = rows_buf[0:rows, :]
    dsignal = shifted_grad * filter_ref[0:1, :]
    dfilter_ref[0:1, :] += jnp.sum(signal * shifted_grad, 0, keepdims=True)
    for offset in range(1, KW):
        shifted_grad = (
            rows_buf[offset : offset + rows, :] * keep_ref[:, KW + offset : KW + offset + 1]
        )
        dsignal = dsignal + shifted_grad * filter_ref[offset : offset + 1, :]
        dfilter_ref[offset : offset + 1, :] += jnp.sum(signal * shifted_grad, 0, keepdims=True)
    rows_buf[rows : rows + 8, :] = rows_buf[0:8, :]
    dproj_ref[:, :conv_cols] = dsignal.astype(jnp.bfloat16)
    for sub in range(BACK_SUBS):
        dproj_ref[sub * ROWS : (sub + 1) * ROWS, proj_cols : proj_cols + 128] = drates[
            sub
        ].astype(jnp.bfloat16)
    dsmall_ref[0:1, :] += dgain
    dsmall_ref[1:2, 0:128] += jnp.sum(dsums, 0, keepdims=True)

    @pl.when(step == last_step)
    def _():
        dstate_out_ref[...] = dstate_buf[...]
        first_ref[...] = rows_buf[0:8, :]


def ffn_kernel(
    mix_cols,
    ff_cols,
    own_ref,
    other_ref,
    inputs_ref,
    cot_ref,
    keep_ref,
    gain_ref,
    weight_hbm,
    *tail_refs,
):
    resid_ref, dnormed_ref, normed_ref, acts_ref, weight_ref, copy_sems = tail_refs[-6:]
    f32 = jnp.float32
    bf16 = jnp.bfloat16
    edges = [0] + [mix_cols + part * ff_cols for part in range(4)]

    def copy(part):
        at = pl.ds(edges[part], edges[part + 1] - edges[part])
        return pltpu.make_async_copy(
            weight_hbm.at[:, at], weight_ref.at[:, at], copy_sems.at[part]
        )

    def arrived(part):
        @pl.when(pl.program_id(0) == 0)
        def _():
            copy(part).wait()

    @pl.when(pl.program_id(0) == 0)
    def _():
        for part in range(4):
            copy(part).start()

    arrived(0)
    gated = jnp.concatenate([own_ref[...], other_ref[...]], axis=1)
    resid = inputs_ref[...].astype(f32) + keep_ref[:, 2 * KW : 2 * KW + 1] * dot(
        gated, weight_ref[:, :mix_cols], NT
    )
    resid_ref[...] = resid
    inv_rms = lax.rsqrt(jnp.mean(resid * resid, -1, keepdims=True) + EPS)
    normed = (resid * inv_rms * gain_ref[...]).astype(bf16)
    normed_ref[...] = normed
    gate_at = slice(edges[1], edges[2])
    up_at = slice(edges[2], edges[3])
    down_at = slice(edges[3], edges[4])
    arrived(1)
    gate_pre = dot(normed, weight_ref[:, gate_at], NN)
    arrived(2)
    up_pre = dot(normed, weight_ref[:, up_at], NN)
    arrived(3)
    dhidden = dot(cot_ref[...], weight_ref[:, down_at], NN)
    sig = sigmoid(gate_pre)
    active = gate_pre * sig
    hidden = (active * up_pre).astype(bf16)
    dgate = (dhidden * up_pre * sig * (1.0 + gate_pre * (1.0 - sig))).astype(bf16)
    dup = (dhidden * active).astype(bf16)
    acts_ref[:, :ff_cols] = dgate
    acts_ref[:, ff_cols : 2 * ff_cols] = dup
    acts_ref[:, 2 * ff_cols :] = hidden
    dnormed_ref[...] = (
        dot(dgate, weight_ref[:, gate_at], NT) + dot(dup, weight_ref[:, up_at], NT)
    ).astype(bf16)


def ffn_out_kernel(down_start, hidden_ref, weight_hbm, summand_ref, weight_ref, copy_sem):
    @pl.when(pl.program_id(0) == 0)
    def _():
        at = pl.ds(down_start, weight_ref.shape[1])
        copy = pltpu.make_async_copy(weight_hbm.at[:, at], weight_ref, copy_sem)
        copy.start()
        copy.wait()

    summand_ref[...] = dot(hidden_ref[...], weight_ref[...], NT).astype(jnp.bfloat16)


def kernel_cost(micros):
    return pl.CostEstimate(
        flops=int(micros * 4e9), bytes_accessed=int(micros * 8e6), transcendentals=0
    )


def whole(array):
    return pl.BlockSpec(array.shape, lambda c, r: (0,) * len(array.shape))


def mixer_forward(resets, proj, keep, filters, rates, head_gain, heads, start, stop, state):
    proj_width = proj.shape[1]
    row_count = stop - start
    chunks = row_count // ROWS
    rows = SUBS * ROWS
    first = start // rows
    conv_cols = 2 * heads * DK + heads * DV
    f32 = jnp.float32

    def rows_of(cols, dtype=f32):
        return jax.ShapeDtypeStruct((row_count, cols), dtype)

    def saved(rows, cols):
        return jax.ShapeDtypeStruct((chunks, heads, rows, cols), f32)

    def part_block(cols):
        return pl.BlockSpec((rows, cols), lambda c, r: (c + first, 0))

    def row_block(cols):
        return pl.BlockSpec((rows, cols), lambda c, r: (c, 0))

    def saved_block(rows, cols):
        return pl.BlockSpec((SUBS, heads, rows, cols), lambda c, r: (c, 0, 0, 0))

    before = max(start // 8 - 1, 0)
    return pl.pallas_call(
        partial(forward_kernel, heads, start // ROWS),
        grid_spec=pltpu.PrefetchScalarGridSpec(
            num_scalar_prefetch=1,
            grid=(chunks // SUBS,),
            in_specs=[
                part_block(proj_width),
                pl.BlockSpec((8, proj_width), lambda c, r: (before, 0)),
                whole(state),
                part_block(keep.shape[1]),
                whole(filters),
                whole(rates),
                whole(head_gain),
            ],
            out_specs=[
                row_block(heads * DV),
                row_block(conv_cols),
                row_block(heads * DV),
                saved_block(DK, DV),
                saved_block(ROWS, ROWS),
                saved_block(ROWS, DV + DK),
                saved_block(ROWS, DV),
                saved_block(ROWS, ROWS),
                saved_block(2 * ROWS, ROWS),
                whole(state),
            ],
            scratch_shapes=[
                pltpu.VMEM((rows + 8, conv_cols), f32),
                pltpu.VMEM((heads, DK, DV), f32),
            ],
        ),
        out_shape=[
            rows_of(heads * DV, jnp.bfloat16),
            rows_of(conv_cols),
            rows_of(heads * DV),
            saved(DK, DV),
            saved(ROWS, ROWS),
            saved(ROWS, DV + DK),
            saved(ROWS, DV),
            saved(ROWS, ROWS),
            saved(2 * ROWS, ROWS),
            jax.ShapeDtypeStruct(state.shape, f32),
        ],
        compiler_params=pltpu.CompilerParams(vmem_limit_bytes=60 << 20),
        cost_estimate=kernel_cost(24 * row_count / 1024),
        name="mixer_forward",
    )(resets, proj, proj, state, keep, filters, rates, head_gain)


def mixer_backward(
    resets,
    own,
    got,
    resid,
    cot,
    ffn_gain,
    out_weight,
    dstate,
    later,
    proj,
    keep,
    filters,
    rates,
    head_gain,
    saved,
    heads,
    start,
    filled,
):
    row_count = resid.shape[0]
    total_rows, proj_width = proj.shape
    chunks = row_count // ROWS
    first = start // ROWS
    conv_cols = 2 * heads * DK + heads * DV
    f32 = jnp.float32

    rows = BACK_SUBS * ROWS
    steps = row_count // rows
    first_block = start // rows

    def row_block(array):
        return pl.BlockSpec((rows, array.shape[1]), lambda c, r: (steps - 1 - c, 0))

    def part_block(array):
        return pl.BlockSpec(
            (rows, array.shape[1]), lambda c, r: (first_block + steps - 1 - c, 0)
        )

    def saved_block(array):
        return pl.BlockSpec(
            (BACK_SUBS,) + array.shape[1:], lambda c, r: (steps - 1 - c, 0, 0, 0)
        )

    dproj = jax.ShapeDtypeStruct((total_rows, proj_width), jnp.bfloat16)
    dfilter = jax.ShapeDtypeStruct((8, conv_cols), f32)
    dsmall = jax.ShapeDtypeStruct((8, DV), f32)
    dmix = jax.ShapeDtypeStruct(resid.shape, jnp.bfloat16)
    dresid = jax.ShapeDtypeStruct(resid.shape, f32)
    dffn_gain = jax.ShapeDtypeStruct((8, resid.shape[1]), f32)
    args = [resets, own, got, resid, cot, ffn_gain, out_weight, dstate, later]
    args += [proj, keep, filters, rates, head_gain, *saved]
    specs = [row_block(own), row_block(got), row_block(resid), part_block(cot), whole(ffn_gain)]
    specs += [
        pl.BlockSpec(
            (resid.shape[1], heads * DV), lambda c, r: (0, 0), pipeline_mode=pl.Buffered(1)
        )
    ]
    specs += [whole(dstate), whole(later), part_block(proj), part_block(keep)]
    specs += [whole(filters), whole(rates), whole(head_gain)]
    specs += [row_block(saved[0]), row_block(saved[1])]
    specs += [saved_block(array) for array in saved[2:]]
    aliases = {}
    if filled is not None:
        aliases = {len(args): 0}
        args.append(filled)
        specs.append(pl.BlockSpec(memory_space=pl.ANY))
    return pl.pallas_call(
        partial(backward_kernel, heads, first, chunks),
        grid_spec=pltpu.PrefetchScalarGridSpec(
            num_scalar_prefetch=1,
            grid=(steps,),
            in_specs=specs,
            out_specs=[
                part_block(dproj),
                whole(dfilter),
                whole(dsmall),
                row_block(dmix),
                row_block(dresid),
                whole(dffn_gain),
                whole(dstate),
                whole(later),
            ],
            scratch_shapes=[
                pltpu.VMEM((rows + 8, conv_cols), f32),
                pltpu.VMEM((heads, DK, DV), f32),
            ],
        ),
        out_shape=[
            dproj,
            dfilter,
            dsmall,
            dmix,
            dresid,
            dffn_gain,
            jax.ShapeDtypeStruct(dstate.shape, f32),
            jax.ShapeDtypeStruct(later.shape, f32),
        ],
        input_output_aliases=aliases,
        compiler_params=pltpu.CompilerParams(vmem_limit_bytes=60 << 20),
        cost_estimate=kernel_cost(30 * row_count / 1024),
        name="mixer_backward",
    )(*args)


def ffn_both_ways(own, other, inputs, cot_masked, keep, gain, weight, ff_cols, start, filled):
    row_count, own_cols = own.shape
    total_rows, width = inputs.shape
    rows = FFN_ROWS
    first = start // rows
    bf16 = jnp.bfloat16

    def whole(array):
        return pl.BlockSpec(array.shape, lambda c: (0, 0))

    def row_block(cols):
        return pl.BlockSpec((rows, cols), lambda c: (c, 0))

    def part_block(cols):
        return pl.BlockSpec((rows, cols), lambda c: (c + first, 0))

    args = [own, other, inputs, cot_masked, keep, gain, weight]
    specs = [row_block(own_cols), row_block(own_cols), part_block(width), part_block(width)]
    specs += [part_block(keep.shape[1]), whole(gain)]
    specs += [pl.BlockSpec(memory_space=pl.ANY)]
    aliases = {}
    if filled is not None:
        aliases = {len(args): 2, len(args) + 1: 3}
        args += list(filled)
        specs += [pl.BlockSpec(memory_space=pl.ANY)] * 2
    return pl.pallas_call(
        partial(ffn_kernel, 2 * own_cols, ff_cols),
        grid=(row_count // rows,),
        in_specs=specs,
        out_specs=[
            row_block(width),
            row_block(width),
            part_block(width),
            part_block(3 * ff_cols),
        ],
        out_shape=[
            jax.ShapeDtypeStruct((row_count, width), jnp.float32),
            jax.ShapeDtypeStruct((row_count, width), bf16),
            jax.ShapeDtypeStruct((total_rows, width), bf16),
            jax.ShapeDtypeStruct((total_rows, 3 * ff_cols), bf16),
        ],
        scratch_shapes=[pltpu.VMEM(weight.shape, bf16), pltpu.SemaphoreType.DMA((4,))],
        input_output_aliases=aliases,
        compiler_params=pltpu.CompilerParams(vmem_limit_bytes=60 << 20),
        cost_estimate=kernel_cost(28 * row_count / 1024),
        name="ffn_both_ways",
    )(*args)


def ffn_outputs(acts, weight, ff_cols):
    row_count = acts.shape[0]
    width = weight.shape[0]
    rows = 256
    bf16 = jnp.bfloat16
    return pl.pallas_call(
        partial(ffn_out_kernel, weight.shape[1] - ff_cols),
        grid=(row_count // rows,),
        in_specs=[
            pl.BlockSpec((rows, ff_cols), lambda c: (c, 2)),
            pl.BlockSpec(memory_space=pl.ANY),
        ],
        out_specs=pl.BlockSpec((rows, width), lambda c: (c, 0)),
        out_shape=jax.ShapeDtypeStruct((row_count, width), bf16),
        scratch_shapes=[pltpu.VMEM((width, ff_cols), bf16), pltpu.SemaphoreType.DMA],
        compiler_params=pltpu.CompilerParams(vmem_limit_bytes=60 << 20),
        cost_estimate=kernel_cost(0.1),
        name="ffn_outputs",
    )(acts, weight)


def grads_kernel(
    shard_rows,
    side_ref,
    normed_ref,
    dproj_ref,
    dmix_lo_ref,
    dmix_hi_ref,
    gated_lo_ref,
    gated_hi_ref,
    mine_a_ref,
    mine_b_ref,
    theirs_a_ref,
    theirs_b_ref,
    rate_ref,
):
    side = side_ref[0]
    normed = normed_ref[...]
    gate_cols = gated_lo_ref.shape[1]
    first_cols = mine_a_ref.shape[1]

    def put(grad, mine_ref, theirs_ref, cols):
        pairs = grad.reshape(-1, 2, shard_rows, grad.shape[-1])
        even = pairs[:, 0].reshape(-1, grad.shape[-1])
        odd = pairs[:, 1].reshape(-1, grad.shape[-1])
        mine_ref[:, cols] = jnp.where(side == 0, even, odd).astype(jnp.bfloat16)
        theirs_ref[:, cols] = jnp.where(side == 0, odd, even).astype(jnp.bfloat16)

    put(dot(normed, dproj_ref[:, :first_cols], TN), mine_a_ref, theirs_a_ref, slice(None))
    put(
        dot(normed, dproj_ref[:, first_cols : first_cols + gate_cols], TN),
        mine_b_ref,
        theirs_b_ref,
        slice(0, gate_cols),
    )
    put(
        dot(dmix_lo_ref[...], gated_lo_ref[...], TN)
        + dot(dmix_hi_ref[...], gated_hi_ref[...], TN),
        mine_b_ref,
        theirs_b_ref,
        slice(gate_cols, 2 * gate_cols),
    )
    rate_ref[...] = dot(dproj_ref[:, first_cols + gate_cols :], normed, TN)[:8]


def mixer_weight_grads(side, normed, dproj, dmix_lo, dmix_hi, gated_lo, gated_hi, shard_rows):
    rows, width = normed.shape
    half_rows, v_cols = gated_lo.shape
    tile = 256
    first_cols = 2 * v_cols
    bf16 = jnp.bfloat16

    def column_block(array):
        return pl.BlockSpec((array.shape[0], tile), lambda c, r: (0, c))

    def row_block(cols):
        return pl.BlockSpec((tile // 2, cols), lambda c, r: (c, 0))

    return pl.pallas_call(
        partial(grads_kernel, shard_rows),
        grid_spec=pltpu.PrefetchScalarGridSpec(
            num_scalar_prefetch=1,
            grid=(width // tile,),
            in_specs=[
                column_block(normed),
                whole(dproj),
                column_block(dmix_lo),
                column_block(dmix_hi),
                whole(gated_lo),
                whole(gated_hi),
            ],
            out_specs=[
                row_block(first_cols),
                row_block(first_cols),
                row_block(first_cols),
                row_block(first_cols),
                pl.BlockSpec((8, tile), lambda c, r: (0, c)),
            ],
        ),
        out_shape=[
            jax.ShapeDtypeStruct((width // 2, first_cols), bf16),
            jax.ShapeDtypeStruct((width // 2, first_cols), bf16),
            jax.ShapeDtypeStruct((width // 2, first_cols), bf16),
            jax.ShapeDtypeStruct((width // 2, first_cols), bf16),
            jax.ShapeDtypeStruct((8, width), jnp.float32),
        ],
        compiler_params=pltpu.CompilerParams(vmem_limit_bytes=60 << 20),
        cost_estimate=kernel_cost(8),
        name="mixer_weight_grads",
    )(side, normed, dproj, dmix_lo, dmix_hi, gated_lo, gated_hi)


def ffn_grads_kernel(normed_ref, cot_ref, acts_ref, grads_ref):
    part = pl.program_id(0)

    @pl.when(part < 2)
    def _():
        grads_ref[...] = dot(normed_ref[...], acts_ref[...], TN).astype(jnp.bfloat16)

    @pl.when(part == 2)
    def _():
        grads_ref[...] = dot(cot_ref[...], acts_ref[...], TN).astype(jnp.bfloat16)


def ffn_weight_grads(normed, cot_masked, acts, ff_cols):
    rows, width = normed.shape

    def fixed(array):
        return pl.BlockSpec(array.shape, lambda c: (0, 0), pipeline_mode=pl.Buffered(1))

    return pl.pallas_call(
        ffn_grads_kernel,
        grid=(3,),
        in_specs=[
            fixed(normed),
            fixed(cot_masked),
            pl.BlockSpec((rows, ff_cols), lambda c: (0, c)),
        ],
        out_specs=pl.BlockSpec((width, ff_cols), lambda c: (0, c)),
        out_shape=jax.ShapeDtypeStruct((width, 3 * ff_cols), jnp.bfloat16),
        compiler_params=pltpu.CompilerParams(vmem_limit_bytes=60 << 20),
        cost_estimate=kernel_cost(0.1),
        name="ffn_weight_grads",
    )(normed, cot_masked, acts)


def swap_halves(array):
    return lax.ppermute(array, "mp", [(0, 1), (1, 0)])


def dp_total(array):
    count = lax.axis_size("dp")
    step = 1
    while step < count:
        array = array + lax.ppermute(array, "dp", [(i, i ^ step) for i in range(count)])
        step *= 2
    return array


def dp_swap(array, bit):
    count = lax.axis_size("dp")
    return lax.ppermute(array, "dp", [(i, i ^ bit) for i in range(count)])


def dp_gather(shard, cuts, first_held, then):
    index = lax.axis_index("dp")
    bits = [1 << i for i in reversed(range((lax.axis_size("dp") - 1).bit_length()))]
    pieces = [shard[None, :, start:stop] for start, stop in cuts]
    for at, bit in enumerate(bits):
        if at == 1:
            pieces, first_held = lax.optimization_barrier((pieces, first_held))
            then_held = then(first_held)
        if at == 3:
            pieces, then_held = lax.optimization_barrier((pieces, then_held))
        others = [dp_swap(piece, bit) for piece in pieces]
        upper = (index & bit) != 0
        pieces = [
            jnp.stack(
                [jnp.where(upper, other, piece), jnp.where(upper, piece, other)], axis=1
            ).reshape((-1,) + piece.shape[1:])
            for piece, other in zip(pieces, others)
        ]
    return [piece.reshape(-1, piece.shape[-1]) for piece in pieces], first_held, then_held


def scatter_first(kept, sent):
    return [
        (mine.astype(jnp.float32) + dp_swap(theirs, 1).astype(jnp.float32)).astype(mine.dtype)
        for mine, theirs in zip(kept, sent)
    ]


def scatter_step(pieces, at):
    index = lax.axis_index("dp")
    bits = [1 << i for i in range(1, (lax.axis_size("dp") - 1).bit_length())]
    orders = [bits, bits[1:2] + bits[:1] + bits[2:]]
    sums = []
    for piece, order in zip(pieces, orders):
        left = sorted(order[at:], reverse=True)
        bit = order[at]
        axis = left.index(bit)
        side = (index & bit) // bit
        cut = piece.reshape((2,) * len(left) + (-1, piece.shape[-1]))
        sent = lax.dynamic_index_in_dim(cut, 1 - side, axis, False).astype(jnp.bfloat16)
        mine = lax.dynamic_index_in_dim(cut, side, axis, False)
        total = mine.astype(jnp.float32) + dp_swap(sent, bit).astype(jnp.float32)
        sums.append(total.astype(piece.dtype).reshape(-1, piece.shape[-1]))
    return sums


def scatter_steps():
    return (lax.axis_size("dp") - 1).bit_length() - 1


def in_order(own, other, model_index, axis):
    first = jnp.where(model_index == 0, own, other)
    second = jnp.where(model_index == 0, other, own)
    return jnp.concatenate([first, second], axis=axis)


def on_device(
    block_input,
    seq_lengths,
    seq_owner,
    mix_gain,
    query_weight,
    key_weight,
    value_weight,
    gate_weight,
    decay_weight,
    beta_weight,
    query_filter,
    key_filter,
    value_filter,
    decay_log,
    decay_bias,
    head_gain,
    out_weight,
    ffn_gain,
    ffn_gate,
    ffn_up,
    ffn_down,
    cotangent,
):
    bf16 = jnp.bfloat16
    f32 = jnp.float32
    local_rows, width = block_input.shape
    dp_index = lax.axis_index("dp")
    model_count = lax.axis_size("mp")
    model_index = lax.axis_index("mp")
    row_count = local_rows * model_count
    keep_masks, resets, valid_rows = layout(seq_lengths, seq_owner, dp_index, row_count)
    valid_all = valid_rows[:, None]
    heads_local = decay_log.shape[0] // model_count
    qk_cols = heads_local * DK
    v_cols = heads_local * DV
    ff_cols = ffn_gate.shape[1]
    shard_rows = query_weight.shape[0]
    proj_cols = 2 * qk_cols + 2 * v_cols

    def own_columns(array, col_count):
        return lax.dynamic_slice_in_dim(array, model_index * col_count, col_count, array.ndim - 1)

    def own_shard(array):
        return lax.dynamic_slice_in_dim(array, dp_index * shard_rows, shard_rows, 0)

    small_weight = jnp.concatenate(
        [own_columns(decay_weight, heads_local), own_columns(beta_weight, heads_local)], axis=1
    )
    small_weight = jnp.pad(small_weight, ((0, 0), (0, 128 - 2 * heads_local)))
    shard_mix = jnp.concatenate(
        [query_weight, key_weight, value_weight, gate_weight, own_shard(small_weight)], axis=1
    )
    half = proj_cols // 256 * 128
    out_rows = out_weight.T
    shard_ffn = jnp.concatenate([ffn_gate, ffn_up, ffn_down.T], axis=1)
    out_other = swap_halves(out_rows)
    input_other = swap_halves(block_input)
    mix_pieces, (out_other, out_rows, shard_ffn), (input_other, cot_held) = dp_gather(
        shard_mix,
        ((0, half), (half, shard_mix.shape[1])),
        (out_other, out_rows, shard_ffn),
        lambda held: (input_other, cotangent),
    )
    mix_weight = jnp.concatenate(mix_pieces, axis=1)
    shard_rest = jnp.concatenate([out_rows, out_other, shard_ffn], axis=1)
    rest_weight = lax.all_gather(shard_rest, "dp", axis=0, tiled=True)
    cot_other = swap_halves(cot_held)

    filters = jnp.concatenate(
        [
            own_columns(query_filter, qk_cols),
            own_columns(key_filter, qk_cols),
            own_columns(value_filter, v_cols),
        ],
        axis=1,
    )
    filters = jnp.pad(filters, ((0, 8 - KW), (0, 0)))
    rates = jnp.stack(
        [own_columns(decay_bias, heads_local), -jnp.exp(own_columns(decay_log, heads_local))]
    )
    rates = jnp.pad(rates, ((0, 6), (0, 128 - heads_local)))
    gain_row = head_gain[None]
    restarts = resets.astype(jnp.int32)
    later_masks = [
        jnp.concatenate([keep_masks[offset, offset:], jnp.ones((offset,), f32)])
        for offset in range(KW)
    ]
    keep_cols = jnp.stack(
        [keep_masks[offset] for offset in range(KW)] + later_masks + [valid_rows] * 8, axis=1
    )
    inputs_b = in_order(block_input, input_other, model_index, 0)
    inputs_f = inputs_b.astype(f32)
    cot_all = in_order(cotangent, cot_other, model_index, 0)
    normed1, inv_rms1 = rms_forward(inputs_f)
    mixed_in = (normed1 * mix_gain).astype(bf16)
    proj = jnp.dot(mixed_in, mix_weight, preferred_element_type=f32)
    cuts = (qk_cols, 2 * qk_cols, 2 * qk_cols + v_cols, proj_cols)
    middle = row_count // 2
    zero_state = jnp.zeros((heads_local, DK, DV), f32)
    small_args = (keep_cols, filters, rates, gain_row)
    gated_lo, *saved_lo, carried = mixer_forward(
        restarts, proj, *small_args, heads_local, 0, middle, zero_state
    )
    cot_masked = cot_all * valid_all.astype(bf16)
    ffn_row = ffn_gain[None]
    carried, cot_all, cot_masked, inputs_b = lax.optimization_barrier(
        (carried, cot_all, cot_masked, inputs_b)
    )
    gated_hi, *saved_hi, _ = mixer_forward(
        restarts, proj, *small_args, heads_local, middle, row_count, carried
    )
    other_lo = swap_halves(gated_lo)
    gated_sent, other_lo = lax.optimization_barrier((gated_hi, other_lo))
    other_hi = swap_halves(gated_sent)
    ffn_args = (inputs_b, cot_masked, keep_cols, ffn_row, rest_weight, ff_cols)
    resid_lo, dnormed_lo, *filled = ffn_both_ways(
        gated_lo, other_lo, *ffn_args, 0, None
    )
    resid_hi, dnormed_hi, ffn_in, acts = ffn_both_ways(
        gated_hi, other_hi, *ffn_args, middle, filled
    )
    got_hi, dnormed_lo = lax.optimization_barrier((swap_halves(dnormed_hi), dnormed_lo))
    got_lo = swap_halves(dnormed_lo)
    core_side = (dp_index & 1).reshape(1)
    rest_grads = ffn_weight_grads(ffn_in, cot_masked, acts, ff_cols)
    acts_later, _ = lax.optimization_barrier((acts, rest_grads))
    summand = ffn_outputs(acts_later, rest_weight, ff_cols)
    got_hi, summand = lax.optimization_barrier((got_hi, summand))
    ffn_shard = lax.psum_scatter(rest_grads, "dp", scatter_dimension=0, tiled=True)

    def own_half(array):
        return lax.dynamic_slice_in_dim(array, model_index * local_rows, local_rows, 0)

    def other_half(array):
        return lax.dynamic_slice_in_dim(array, (1 - model_index) * local_rows, local_rows, 0)

    def own_of(low, high):
        return jnp.where(model_index == 0, low, high)

    zero_rows = jnp.zeros((8, proj_cols - v_cols), f32)
    proj_grad, filter_hi, small_hi, dmix_hi, dresid_hi, ffn_gain_hi, carried, later = (
        mixer_backward(
            restarts,
            dnormed_hi,
            got_hi,
            resid_hi,
            cot_all,
            ffn_row,
            rest_weight,
            zero_state,
            zero_rows,
            proj,
            *small_args,
            saved_hi,
            heads_local,
            middle,
            None,
        )
    )
    summand_sent, got_lo, proj_grad = lax.optimization_barrier(
        (other_half(summand), got_lo, proj_grad)
    )
    proj_grad, filter_lo, small_lo, dmix_lo, dresid_lo, ffn_gain_lo, _, _ = mixer_backward(
        restarts,
        dnormed_lo,
        got_lo,
        resid_lo,
        cot_all,
        ffn_row,
        rest_weight,
        carried,
        later,
        proj,
        *small_args,
        saved_lo,
        heads_local,
        0,
        proj_grad,
    )
    summand_got, proj_grad, dmix_lo, filter_lo, small_lo, dresid_lo, ffn_gain_lo = (
        lax.optimization_barrier(
            (
                swap_halves(summand_sent),
                proj_grad,
                dmix_lo,
                filter_lo,
                small_lo,
                dresid_lo,
                ffn_gain_lo,
            )
        )
    )
    ffn_sum = own_half(summand).astype(f32) + summand_got.astype(f32)
    block_output = (own_of(resid_lo, resid_hi) + own_half(valid_all) * ffn_sum).astype(bf16)
    filter_grads = filter_lo + filter_hi
    small_grads = small_lo + small_hi
    ffn_gain_part = ffn_gain_lo[0] + ffn_gain_hi[0]
    *grad_pieces, rate_grads = mixer_weight_grads(
        core_side,
        mixed_in,
        proj_grad,
        dmix_lo,
        dmix_hi,
        gated_lo,
        gated_hi,
        shard_rows,
    )
    rate_grads = rate_grads[: 2 * heads_local]
    mix_sums = scatter_first(grad_pieces[:2], grad_pieces[2:])
    proj_grad, mix_sums, rate_grads = lax.optimization_barrier(
        (proj_grad, mix_sums, rate_grads)
    )
    mix_sums = scatter_step(mix_sums, 0)
    mix_in_part = against(proj_grad, mix_weight)
    mix_gain_part = jnp.sum(mix_in_part * normed1, 0)
    common = jnp.concatenate(
        [mix_gain_part, ffn_gain_part, small_grads[0], jnp.zeros((width - DV,), f32)]
    ).reshape(3, width)
    tail_row = jnp.concatenate(
        [small_grads[1, : 2 * heads_local], jnp.zeros((width - 2 * heads_local,), f32)]
    )
    split_rows = jnp.concatenate(
        [
            rate_grads,
            filter_grads[:KW, : cuts[0]].reshape(-1, width),
            filter_grads[:KW, cuts[0] : cuts[1]].reshape(-1, width),
            filter_grads[:KW, cuts[1] : cuts[2]].reshape(-1, width),
            tail_row[None],
        ],
        axis=0,
    )
    mix_in_rounded = mix_in_part.astype(bf16)
    mix_in_sent = other_half(mix_in_rounded)
    mix_in_got = swap_halves(mix_in_sent)
    mix_sums, small_sums, _ = lax.optimization_barrier(
        (mix_sums, jnp.concatenate([common, split_rows], axis=0), mix_in_sent)
    )
    totals = dp_total(small_sums)
    for step in range(1, scatter_steps()):
        if step == 2:
            mix_sums, totals, mix_in_got = lax.optimization_barrier(
                (mix_sums, totals, mix_in_got)
            )
            totals_other = swap_halves(totals)
        mix_sums = scatter_step(mix_sums, step)
    mix_shards = [piece.astype(f32) for piece in mix_sums]
    mix_in_sum = own_half(mix_in_rounded).astype(f32) + mix_in_got.astype(f32)
    input_grad = own_of(dresid_lo, dresid_hi) + rms_backward(
        mix_in_sum * mix_gain, own_half(normed1), own_half(inv_rms1)
    )
    common = totals[:3] + totals_other[:3]
    lower = jnp.where(model_index == 0, totals, totals_other)[3:]
    upper = jnp.where(model_index == 0, totals_other, totals)[3:]

    def joined(start, rows, cols):
        return jnp.concatenate(
            [
                lower[start : start + rows].reshape(-1, cols),
                upper[start : start + rows].reshape(-1, cols),
            ],
            axis=1,
        )

    q_rows = KW * qk_cols // width
    v_rows = KW * v_cols // width
    at_q = 2 * heads_local
    at_k = at_q + q_rows
    at_v = at_k + q_rows
    at_tail = at_v + v_rows

    def rate_weight_grad(start):
        return jnp.concatenate(
            [lower[start : start + heads_local], upper[start : start + heads_local]], axis=0
        ).T

    def rate_grad(start):
        return jnp.concatenate(
            [
                lower[at_tail, start : start + heads_local],
                upper[at_tail, start : start + heads_local],
            ]
        )

    ffn_shard = ffn_shard.astype(f32)
    return (
        block_output,
        input_grad,
        common[0],
        mix_shards[0][:, : cuts[0]],
        mix_shards[0][:, cuts[0] : cuts[1]],
        mix_shards[0][:, cuts[1] :],
        mix_shards[1][:, :v_cols],
        rate_weight_grad(0),
        rate_weight_grad(heads_local),
        joined(at_q, q_rows, qk_cols),
        joined(at_k, q_rows, qk_cols),
        joined(at_v, v_rows, v_cols),
        rate_grad(0),
        rate_grad(heads_local),
        common[2, :DV],
        mix_shards[1][:, v_cols:].T,
        common[1],
        ffn_shard[:, :ff_cols],
        ffn_shard[:, ff_cols : 2 * ff_cols],
        ffn_shard[:, 2 * ff_cols :].T,
    )


def solution(mesh):
    in_specs = (
        P(("dp", "mp"), None),
        P(),
        P(),
        P(),
        P("dp", "mp"),
        P("dp", "mp"),
        P("dp", "mp"),
        P("dp", "mp"),
        P(),
        P(),
        P(),
        P(),
        P(),
        P(),
        P(),
        P(),
        P("mp", "dp"),
        P(),
        P("dp", "mp"),
        P("dp", "mp"),
        P("mp", "dp"),
        P(("dp", "mp"), None),
    )
    out_specs = (
        P(("dp", "mp"), None),
        P(("dp", "mp"), None),
        P(),
        P("dp", "mp"),
        P("dp", "mp"),
        P("dp", "mp"),
        P("dp", "mp"),
        P(),
        P(),
        P(),
        P(),
        P(),
        P(),
        P(),
        P(),
        P("mp", "dp"),
        P(),
        P("dp", "mp"),
        P("dp", "mp"),
        P("mp", "dp"),
    )
    return jax.shard_map(
        on_device, mesh=mesh, in_specs=in_specs, out_specs=out_specs, check_vma=False
    )
```

```python
from functools import partial
import math

import jax
import jax.numpy as jnp
from jax import lax
from jax.experimental import pallas as pl
from jax.experimental.pallas import tpu as pltpu
from jax.sharding import PartitionSpec as P

DK = 128
DV = 256
KW = 4
SPAN = 64


EPS = 1e-06


def layout(seq_lengths, seq_owner, device, row_count):
    owned = seq_owner == device
    own_lengths = jnp.where(owned, seq_lengths, 0)
    offsets = jnp.cumsum(own_lengths) - own_lengths
    loaded = jnp.sum(own_lengths)
    span_starts = jnp.arange(row_count // SPAN, dtype=jnp.int32) * SPAN
    begins = jnp.any(
        (offsets[None, :] == span_starts[:, None]) & (own_lengths[None, :] > 0), axis=1
    )
    resets = begins | (span_starts == loaded)
    within = jnp.arange(SPAN, dtype=jnp.int32)
    keep_masks = jnp.stack(
        [
            jnp.logical_not(resets[:, None] & (within[None, :] < offset)).reshape(row_count)
            for offset in range(KW)
        ]
    ).astype(jnp.float32)
    valid_rows = (jnp.arange(row_count, dtype=jnp.int32) < loaded).astype(jnp.float32)
    return (keep_masks, resets, valid_rows)


def across_rows(left, right):
    return lax.dot_general(
        left, right, (((0,), (0,)), ((), ())), preferred_element_type=jnp.float32
    )


def against(left, right):
    return lax.dot_general(
        left, right, (((1,), (1,)), ((), ())), preferred_element_type=jnp.float32
    )


def rms_forward(values):
    inv_rms = lax.rsqrt(jnp.mean(values * values, -1, keepdims=True) + EPS)
    return (values * inv_rms, inv_rms)


def rms_backward(upstream, normed, inv_rms):
    return inv_rms * (upstream - normed * jnp.mean(upstream * normed, -1, keepdims=True))


ROWS = 128
NN = ((1,), (0,))
NT = ((1,), (1,))
TN = ((0,), (0,))
FINE_GRAM = True
FINE_INVERSE = True
FINE_MERGE = True
SUBS = 2
FFN_ROWS = 256
FINE_APPLY = True
FINE_STATE = True
FINE_BACK = (True,) * 10
BACK_SUBS = 2


def dot(left, right, dims):
    return lax.dot_general(left, right, (dims, ((), ())), preferred_element_type=jnp.float32)


def high_low(values):
    high = values.astype(jnp.bfloat16)
    return high, (values - high.astype(jnp.float32)).astype(jnp.bfloat16)


def product(left, right, dims, fine=False):
    if not fine:
        return dot(left.astype(jnp.bfloat16), right.astype(jnp.bfloat16), dims)
    left_high, left_low = high_low(left)
    right_high, right_low = high_low(right)
    (left_axis,), (right_axis,) = dims
    depth = right.shape[right_axis]
    count = right.shape[1 - right_axis]
    if depth <= 128:
        both = jnp.concatenate([left_high, left_low], axis=left_axis)
        if count <= 128:
            wide = jnp.concatenate([right_high, right_low], axis=1 - right_axis)
            part = jnp.concatenate([right_high, jnp.zeros_like(right_low)], axis=1 - right_axis)
            result = dot(both, jnp.concatenate([wide, part], axis=right_axis), dims)
            return result[:, :count] + result[:, count:]
        return dot(both, jnp.concatenate([right_high, right_high], axis=right_axis), dims) + dot(
            left_high, right_low, dims
        )
    if count <= 128:
        wide = jnp.concatenate([right_high, right_low], axis=1 - right_axis)
        result = dot(left_high, wide, dims)
        return result[:, :count] + (result[:, count:] + dot(left_low, right_high, dims))
    return dot(left_high, right_high, dims) + (
        dot(left_high, right_low, dims) + dot(left_low, right_high, dims)
    )


def summed_by(mask, values, dims=NN):
    high, low = high_low(values)
    return dot(mask, high, dims) + dot(mask, low, dims)


def chunk_masks(resets_ref, chunk):
    first = 1.0 - resets_ref[2 * chunk].astype(jnp.float32)
    second = 1.0 - resets_ref[2 * chunk + 1].astype(jnp.float32)
    row = lax.broadcasted_iota(jnp.int32, (ROWS, ROWS), 0)
    col = lax.broadcasted_iota(jnp.int32, (ROWS, ROWS), 1)
    late = row >= SPAN
    reached = jnp.where(late, first * second, first)
    reaching = jnp.where(late, 1.0, second)
    joined = jnp.where(late & (col < SPAN), second, 1.0)
    return row, col, reached, reaching, joined, first * second


def unit_lower_inverses(couplings, row, col):
    eye = jnp.where(row == col, 1.0, 0.0)
    base = 16
    near = (row // base) == (col // base)
    powered = [jnp.where(near, coupling, 0.0) for coupling in couplings]
    inverses = [eye - power for power in powered]
    size = 2
    while size < base:
        powered = [product(power, power, NN, FINE_INVERSE) for power in powered]
        inverses = [
            inverse + product(inverse, power, NN, FINE_INVERSE)
            for inverse, power in zip(inverses, powered)
        ]
        size *= 2
    while base < ROWS:
        wide = 2 * base
        linked = ((row // wide) == (col // wide)) & ((row // base) != (col // base))
        steps = [
            product(jnp.where(linked, coupling, 0.0), inverse, NN, FINE_MERGE)
            for coupling, inverse in zip(couplings, inverses)
        ]
        inverses = [
            inverse - product(inverse, step, NN, FINE_MERGE)
            for inverse, step in zip(inverses, steps)
        ]
        base = wide
    return inverses


def sigmoid(values):
    return 1.0 / (1.0 + jnp.exp(-values))


def lane_sum(values):
    return jnp.sum(values, -1, keepdims=True)


def forward_kernel(
    heads,
    base,
    resets_ref,
    proj_ref,
    before_ref,
    state_in_ref,
    keep_ref,
    filter_ref,
    rates_ref,
    gain_ref,
    gated_ref,
    conv_ref,
    mixed_ref,
    state_ref,
    inverse_ref,
    parts_ref,
    written_ref,
    factor_ref,
    grams_ref,
    state_out_ref,
    rows_buf,
    state_buf,
):
    step = pl.program_id(0)
    qk = heads * DK
    conv_cols = 2 * qk + heads * DV
    proj_cols = conv_cols + heads * DV
    rows = SUBS * ROWS

    @pl.when(step == 0)
    def _():
        if base == 0:
            rows_buf[0:8, :] = jnp.zeros((8, conv_cols), jnp.float32)
        else:
            rows_buf[0:8, :] = before_ref[:, :conv_cols]
        state_buf[...] = state_in_ref[...]

    rows_buf[8 : 8 + rows, :] = proj_ref[:, :conv_cols]
    conv = rows_buf[8 : 8 + rows, :] * filter_ref[0:1, :]
    for offset in range(1, KW):
        conv = conv + rows_buf[8 - offset : 8 - offset + rows, :] * (
            filter_ref[offset : offset + 1, :] * keep_ref[:, offset : offset + 1]
        )
    rows_buf[0:8, :] = rows_buf[rows : rows + 8, :]
    conv_ref[...] = conv

    rate = proj_ref[:, proj_cols : proj_cols + 128]
    shifted = rate + rates_ref[0:1, :]
    decay_all = rates_ref[1:2, :] * (
        jnp.maximum(shifted, 0.0) + jnp.log1p(jnp.exp(-jnp.abs(shifted)))
    )
    beta_all = sigmoid(rate)
    units = [(sub, head) for sub in range(SUBS) for head in range(heads)]
    prepared = []
    for sub, head in units:
        row, col, reached, reaching, joined, passed = chunk_masks(
            resets_ref, base + step * SUBS + sub
        )
        lower = jnp.where(row >= col, 1.0, 0.0)
        at = slice(sub * ROWS, (sub + 1) * ROWS)
        decay = jnp.broadcast_to(decay_all[at, head : head + 1], (ROWS, ROWS))
        beta = beta_all[at, heads + head : heads + head + 1]
        sums = summed_by(
            lower.astype(jnp.bfloat16),
            jnp.concatenate([jnp.where(row > col, decay, 0.0), decay], axis=1),
        )
        factor = jnp.exp(sums[:, :ROWS]) * (lower * joined)
        total = sums[:, ROWS:]
        total_end = total[ROWS - 1 : ROWS, :]
        grown = jnp.exp(total) * reached
        tail = jnp.exp(total_end - total) * reaching
        end_decay = jnp.exp(total_end[:, :1]) * passed

        conv_q = conv[at, head * DK : (head + 1) * DK]
        conv_k = conv[at, qk + head * DK : qk + (head + 1) * DK]
        conv_v = conv[at, 2 * qk + head * DV : 2 * qk + (head + 1) * DV]
        query = conv_q * sigmoid(conv_q)
        query = query * (lax.rsqrt(lane_sum(query * query) + EPS) * (1.0 / math.sqrt(DK)))
        key = conv_k * sigmoid(conv_k)
        key = key * lax.rsqrt(lane_sum(key * key) + EPS)
        value = conv_v * sigmoid(conv_v)

        grams = product(jnp.concatenate([key, query], axis=0), key, NT, FINE_GRAM)
        coupling = jnp.where(row > col, factor * grams[:ROWS] * beta, 0.0)
        scaled = jnp.concatenate([beta * value, (beta * grown) * key], axis=1)
        factor_ref[sub, head] = factor
        grams_ref[sub, head] = grams
        prepared.append(
            (coupling, scaled, grown * query, factor * grams[ROWS:], tail * key, end_decay)
        )
    row = lax.broadcasted_iota(jnp.int32, (ROWS, ROWS), 0)
    col = lax.broadcasted_iota(jnp.int32, (ROWS, ROWS), 1)
    inverses = unit_lower_inverses([entry[0] for entry in prepared], row, col)
    for (sub, head), inverse, entry in zip(units, inverses, prepared):
        _, scaled, query_grown, mixing, key_tail, end_decay = entry
        at = slice(sub * ROWS, (sub + 1) * ROWS)
        parts = product(inverse, scaled, NN, FINE_APPLY)
        state = state_buf[head]
        from_state = product(
            jnp.concatenate([parts[:, DV:], query_grown], axis=0), state, NN, FINE_STATE
        )
        written = parts[:, :DV] - from_state[:ROWS]
        mixed = from_state[ROWS:] + product(mixing, written, NN, FINE_STATE)
        state_buf[head] = end_decay * state + product(key_tail, written, TN, FINE_STATE)

        gate = proj_ref[at, conv_cols + head * DV : conv_cols + (head + 1) * DV]
        normed = mixed * lax.rsqrt(lane_sum(mixed * mixed) * (1.0 / DV) + EPS)
        gated_ref[at, head * DV : (head + 1) * DV] = (
            normed * gain_ref[...] * (gate * sigmoid(gate))
        ).astype(jnp.bfloat16)
        mixed_ref[at, head * DV : (head + 1) * DV] = mixed
        state_ref[sub, head] = state
        inverse_ref[sub, head] = inverse
        parts_ref[sub, head] = parts
        written_ref[sub, head] = written

    @pl.when(step == pl.num_programs(0) - 1)
    def _():
        state_out_ref[...] = state_buf[...]


def backward_kernel(
    heads,
    base,
    chunks,
    resets_ref,
    own_ref,
    got_ref,
    resid_ref,
    cot_ref,
    ffn_gain_ref,
    out_weight_ref,
    dstate_in_ref,
    later_ref,
    proj_ref,
    keep_ref,
    filter_ref,
    rates_ref,
    gain_ref,
    conv_ref,
    mixed_ref,
    state_ref,
    inverse_ref,
    parts_ref,
    written_ref,
    factor_ref,
    grams_ref,
    *tail_refs,
):
    (
        dproj_ref,
        dfilter_ref,
        dsmall_ref,
        dmix_ref,
        dresid_ref,
        dffn_gain_ref,
        dstate_out_ref,
        first_ref,
        rows_buf,
        dstate_buf,
    ) = tail_refs[-10:]
    step = pl.program_id(0)
    last_step = pl.num_programs(0) - 1
    rows = BACK_SUBS * ROWS
    qk = heads * DK
    conv_cols = 2 * qk + heads * DV
    proj_cols = conv_cols + heads * DV

    @pl.when(step == 0)
    def _():
        rows_buf[rows : rows + 8, :] = later_ref[...]
        dstate_buf[...] = dstate_in_ref[...]
        dffn_gain_ref[...] = jnp.zeros_like(dffn_gain_ref)
        dfilter_ref[...] = jnp.zeros_like(dfilter_ref)
        dsmall_ref[...] = jnp.zeros_like(dsmall_ref)

    resid = resid_ref[...]
    inv_resid = lax.rsqrt(jnp.mean(resid * resid, -1, keepdims=True) + EPS)
    resid_normed = resid * inv_resid
    ffn_in_own = own_ref[...].astype(jnp.float32)
    dffn_gain_ref[0:1, :] += jnp.sum(ffn_in_own * resid_normed, 0, keepdims=True)
    scaled_up = (ffn_in_own + got_ref[...].astype(jnp.float32)) * ffn_gain_ref[...]
    dresid = cot_ref[...].astype(jnp.float32) + inv_resid * (
        scaled_up - resid_normed * jnp.mean(scaled_up * resid_normed, -1, keepdims=True)
    )
    dresid_ref[...] = dresid
    dmix = (dresid * keep_ref[:, 2 * KW : 2 * KW + 1]).astype(jnp.bfloat16)
    dmix_ref[...] = dmix
    dgated = dot(dmix, out_weight_ref[...], NN)
    rate = proj_ref[:, proj_cols : proj_cols + 128]
    shifted = rate + rates_ref[0:1, :]
    decay_all = rates_ref[1:2, :] * (
        jnp.maximum(shifted, 0.0) + jnp.log1p(jnp.exp(-jnp.abs(shifted)))
    )
    slope_all = rates_ref[1:2, :] * sigmoid(shifted)
    beta_all = sigmoid(rate)
    row = lax.broadcasted_iota(jnp.int32, (ROWS, ROWS), 0)
    col = lax.broadcasted_iota(jnp.int32, (ROWS, ROWS), 1)
    lower_b = jnp.where(row >= col, 1.0, 0.0).astype(jnp.bfloat16)
    upper_b = jnp.where(row <= col, 1.0, 0.0).astype(jnp.bfloat16)
    lane = lax.broadcasted_iota(jnp.int32, (ROWS, 128), 1)
    dgain = jnp.zeros((1, DV), jnp.float32)
    units = [(sub, head) for sub in reversed(range(BACK_SUBS)) for head in range(heads)]
    prepared = []
    for sub, head in units:
        at = slice(sub * ROWS, (sub + 1) * ROWS)
        chunk = base + chunks - BACK_SUBS * (step + 1) + sub
        _, _, reached, reaching, _, passed = chunk_masks(resets_ref, chunk)
        decay = jnp.broadcast_to(decay_all[at, head : head + 1], (ROWS, ROWS))
        total = summed_by(lower_b, decay)
        total_end = total[ROWS - 1 : ROWS, :]
        grown = jnp.exp(total) * reached
        tail = jnp.exp(total_end - total) * reaching
        end_decay = jnp.exp(total_end[:, :1]) * passed

        v_at = slice(head * DV, (head + 1) * DV)
        gate_at = slice(conv_cols + head * DV, conv_cols + (head + 1) * DV)
        conv_q = conv_ref[at, head * DK : (head + 1) * DK]
        conv_k = conv_ref[at, qk + head * DK : qk + (head + 1) * DK]
        query = conv_q * sigmoid(conv_q)
        inv_q = lax.rsqrt(lane_sum(query * query) + EPS)
        query = query * (inv_q * (1.0 / math.sqrt(DK)))
        key = conv_k * sigmoid(conv_k)
        inv_k = lax.rsqrt(lane_sum(key * key) + EPS)
        key = key * inv_k

        mixed = mixed_ref[at, v_at]
        inv_o = lax.rsqrt(lane_sum(mixed * mixed) * (1.0 / DV) + EPS)
        normed = mixed * inv_o
        gate = proj_ref[at, gate_at]
        sig_g = sigmoid(gate)
        upstream = dgated[at, v_at]
        up_normed = upstream * normed
        dgain = dgain + jnp.sum(up_normed * (gate * sig_g), 0, keepdims=True)
        dproj_ref[at, gate_at] = (
            up_normed * gain_ref[...] * (sig_g * (1.0 + gate * (1.0 - sig_g)))
        ).astype(jnp.bfloat16)
        dnormed = upstream * gain_ref[...] * (gate * sig_g)
        dmixed = inv_o * (dnormed - normed * (lane_sum(dnormed * normed) * (1.0 / DV)))
        mixing = factor_ref[sub, head] * grams_ref[sub, head, ROWS:]
        within = product(mixing, dmixed, TN, FINE_BACK[0])
        dmixing = product(dmixed, written_ref[sub, head], NT, FINE_BACK[3])
        prepared.append(
            (decay, grown, tail, end_decay, query, inv_q, key, inv_k, dmixed, within, dmixing)
        )
    stepped = []
    for (sub, head), entry in zip(units, prepared):
        decay, grown, tail, end_decay, query, inv_q, key, inv_k, dmixed, within, dmixing = entry
        state = state_ref[sub, head]
        dstate = dstate_buf[head]
        dwritten = within + product(tail * key, dstate, NN, FINE_BACK[1])
        dkey_tail = product(written_ref[sub, head], dstate, NT, FINE_BACK[4])
        end_grad = end_decay * lane_sum(jnp.sum(state * dstate, 0, keepdims=True))
        stacked = jnp.concatenate([dmixed, -dwritten], axis=0)
        dstate_buf[head] = end_decay * dstate + product(
            jnp.concatenate([grown * query, parts_ref[sub, head, :, DV:]], axis=0),
            stacked,
            TN,
            FINE_BACK[5],
        )
        stepped.append((dwritten, dkey_tail, end_grad, stacked))
    drates = {sub: jnp.zeros((ROWS, 128), jnp.float32) for sub in range(BACK_SUBS)}
    dsums = jnp.zeros((ROWS, 128), jnp.float32)
    throughs = [
        product(entry[3], state_ref[sub, head], NT, FINE_BACK[2])
        for (sub, head), entry in zip(units, stepped)
    ]
    solveds = [
        product(
            inverse_ref[sub, head],
            jnp.concatenate([entry[0], through[ROWS:]], axis=1),
            TN,
            FINE_BACK[6],
        )
        for (sub, head), entry, through in zip(units, stepped, throughs)
    ]
    dcouplings = [
        product(solved, parts_ref[sub, head], NT, FINE_BACK[7])
        for (sub, head), solved in zip(units, solveds)
    ]
    for at_unit, (sub, head) in enumerate(units):
        decay, grown, tail, _, query, inv_q, key, inv_k, _, _, dmixing = prepared[at_unit]
        _, dkey_tail, end_grad, _ = stepped[at_unit]
        solved = solveds[at_unit]
        at = slice(sub * ROWS, (sub + 1) * ROWS)
        q_at = slice(head * DK, (head + 1) * DK)
        k_at = slice(qk + head * DK, qk + (head + 1) * DK)
        value_at = slice(2 * qk + head * DV, 2 * qk + (head + 1) * DV)
        beta = beta_all[at, heads + head : heads + head + 1]
        factor = factor_ref[sub, head]
        conv_q = conv_ref[at, q_at]
        conv_k = conv_ref[at, k_at]
        conv_v = conv_ref[at, value_at]
        sig_q = sigmoid(conv_q)
        sig_k = sigmoid(conv_k)
        sig_v = sigmoid(conv_v)
        value = conv_v * sig_v
        query_grown = grown * query
        key_tail = tail * key
        dquery_grown = throughs[at_unit][:ROWS]
        dcoupling = jnp.where(row > col, -dcouplings[at_unit] * factor, 0.0)
        dcoupling_gram = dcoupling * grams_ref[sub, head, :ROWS]
        dbeta = lane_sum(dcoupling_gram)
        dgap = beta * dcoupling_gram + dmixing * (factor * grams_ref[sub, head, ROWS:])
        dgrams = jnp.concatenate([beta * dcoupling, dmixing * factor], axis=0)
        by_key = product(dgrams, key, NN, FINE_BACK[8])
        dkey = by_key[:ROWS] + product(
            dgrams, jnp.concatenate([key, query], axis=0), TN, FINE_BACK[9]
        )
        dquery = by_key[ROWS:] + grown * dquery_grown
        dvalue_scaled = solved[:, :DV]
        dkey_scaled = solved[:, DV:]
        scaled_rows = lane_sum(dkey_scaled * (grown * key))
        dbeta = dbeta + lane_sum(dvalue_scaled * value) + scaled_rows
        tail_rows = lane_sum(dkey_tail * key_tail)
        dkey = dkey + tail * dkey_tail + (beta * grown) * dkey_scaled
        dtotal = lane_sum(dquery_grown * query_grown) + beta * scaled_rows - tail_rows
        sums = summed_by(
            upper_b, jnp.concatenate([dgap, jnp.broadcast_to(dtotal, (ROWS, ROWS))], axis=1)
        )
        ddecay = (
            lane_sum(jnp.where(col < row, sums[:, :ROWS], 0.0))
            + sums[:, ROWS : ROWS + 1]
            + (end_grad + jnp.sum(tail_rows, 0, keepdims=True))
        )
        dshifted = ddecay * slope_all[at, head : head + 1]
        drates[sub] = (
            drates[sub]
            + jnp.where(lane == head, dshifted, 0.0)
            + jnp.where(lane == heads + head, dbeta * (beta * (1.0 - beta)), 0.0)
        )
        dsums = dsums + jnp.where(lane == head, ddecay * decay, 0.0)
        dsums = dsums + jnp.where(lane == heads + head, dshifted, 0.0)

        unit = query * math.sqrt(DK)
        dunit = dquery * (1.0 / math.sqrt(DK))
        dsilu = inv_q * (dunit - unit * lane_sum(dunit * unit))
        rows_buf[at, q_at] = dsilu * (sig_q * (1.0 + conv_q * (1.0 - sig_q)))
        dsilu = inv_k * (dkey - key * lane_sum(dkey * key))
        rows_buf[at, k_at] = dsilu * (sig_k * (1.0 + conv_k * (1.0 - sig_k)))
        rows_buf[at, value_at] = (beta * dvalue_scaled) * (
            sig_v * (1.0 + conv_v * (1.0 - sig_v))
        )

    signal = proj_ref[:, :conv_cols]
    shifted_grad = rows_buf[0:rows, :]
    dsignal = shifted_grad * filter_ref[0:1, :]
    dfilter_ref[0:1, :] += jnp.sum(signal * shifted_grad, 0, keepdims=True)
    for offset in range(1, KW):
        shifted_grad = (
            rows_buf[offset : offset + rows, :] * keep_ref[:, KW + offset : KW + offset + 1]
        )
        dsignal = dsignal + shifted_grad * filter_ref[offset : offset + 1, :]
        dfilter_ref[offset : offset + 1, :] += jnp.sum(signal * shifted_grad, 0, keepdims=True)
    rows_buf[rows : rows + 8, :] = rows_buf[0:8, :]
    dproj_ref[:, :conv_cols] = dsignal.astype(jnp.bfloat16)
    for sub in range(BACK_SUBS):
        dproj_ref[sub * ROWS : (sub + 1) * ROWS, proj_cols : proj_cols + 128] = drates[
            sub
        ].astype(jnp.bfloat16)
    dsmall_ref[0:1, :] += dgain
    dsmall_ref[1:2, 0:128] += jnp.sum(dsums, 0, keepdims=True)

    @pl.when(step == last_step)
    def _():
        dstate_out_ref[...] = dstate_buf[...]
        first_ref[...] = rows_buf[0:8, :]


def ffn_kernel(
    mix_cols,
    ff_cols,
    own_ref,
    other_ref,
    inputs_ref,
    cot_ref,
    keep_ref,
    gain_ref,
    weight_hbm,
    *tail_refs,
):
    resid_ref, dnormed_ref, normed_ref, acts_ref, weight_ref, copy_sems = tail_refs[-6:]
    f32 = jnp.float32
    bf16 = jnp.bfloat16
    edges = [0] + [mix_cols + part * ff_cols for part in range(4)]

    def copy(part):
        at = pl.ds(edges[part], edges[part + 1] - edges[part])
        return pltpu.make_async_copy(
            weight_hbm.at[:, at], weight_ref.at[:, at], copy_sems.at[part]
        )

    def arrived(part):
        @pl.when(pl.program_id(0) == 0)
        def _():
            copy(part).wait()

    @pl.when(pl.program_id(0) == 0)
    def _():
        for part in range(4):
            copy(part).start()

    arrived(0)
    gated = jnp.concatenate([own_ref[...], other_ref[...]], axis=1)
    resid = inputs_ref[...].astype(f32) + keep_ref[:, 2 * KW : 2 * KW + 1] * dot(
        gated, weight_ref[:, :mix_cols], NT
    )
    resid_ref[...] = resid
    inv_rms = lax.rsqrt(jnp.mean(resid * resid, -1, keepdims=True) + EPS)
    normed = (resid * inv_rms * gain_ref[...]).astype(bf16)
    normed_ref[...] = normed
    gate_at = slice(edges[1], edges[2])
    up_at = slice(edges[2], edges[3])
    down_at = slice(edges[3], edges[4])
    arrived(1)
    gate_pre = dot(normed, weight_ref[:, gate_at], NN)
    arrived(2)
    up_pre = dot(normed, weight_ref[:, up_at], NN)
    arrived(3)
    dhidden = dot(cot_ref[...], weight_ref[:, down_at], NN)
    sig = sigmoid(gate_pre)
    active = gate_pre * sig
    hidden = (active * up_pre).astype(bf16)
    dgate = (dhidden * up_pre * sig * (1.0 + gate_pre * (1.0 - sig))).astype(bf16)
    dup = (dhidden * active).astype(bf16)
    acts_ref[:, :ff_cols] = dgate
    acts_ref[:, ff_cols : 2 * ff_cols] = dup
    acts_ref[:, 2 * ff_cols :] = hidden
    dnormed_ref[...] = (
        dot(dgate, weight_ref[:, gate_at], NT) + dot(dup, weight_ref[:, up_at], NT)
    ).astype(bf16)


def ffn_out_kernel(down_start, hidden_ref, weight_hbm, summand_ref, weight_ref, copy_sem):
    @pl.when(pl.program_id(0) == 0)
    def _():
        at = pl.ds(down_start, weight_ref.shape[1])
        copy = pltpu.make_async_copy(weight_hbm.at[:, at], weight_ref, copy_sem)
        copy.start()
        copy.wait()

    summand_ref[...] = dot(hidden_ref[...], weight_ref[...], NT).astype(jnp.bfloat16)


def kernel_cost(micros):
    return pl.CostEstimate(
        flops=int(micros * 4e9), bytes_accessed=int(micros * 8e6), transcendentals=0
    )


def whole(array):
    return pl.BlockSpec(array.shape, lambda c, r: (0,) * len(array.shape))


def mixer_forward(resets, proj, keep, filters, rates, head_gain, heads, start, stop, state):
    proj_width = proj.shape[1]
    row_count = stop - start
    chunks = row_count // ROWS
    rows = SUBS * ROWS
    first = start // rows
    conv_cols = 2 * heads * DK + heads * DV
    f32 = jnp.float32

    def rows_of(cols, dtype=f32):
        return jax.ShapeDtypeStruct((row_count, cols), dtype)

    def saved(rows, cols):
        return jax.ShapeDtypeStruct((chunks, heads, rows, cols), f32)

    def part_block(cols):
        return pl.BlockSpec((rows, cols), lambda c, r: (c + first, 0))

    def row_block(cols):
        return pl.BlockSpec((rows, cols), lambda c, r: (c, 0))

    def saved_block(rows, cols):
        return pl.BlockSpec((SUBS, heads, rows, cols), lambda c, r: (c, 0, 0, 0))

    before = max(start // 8 - 1, 0)
    return pl.pallas_call(
        partial(forward_kernel, heads, start // ROWS),
        grid_spec=pltpu.PrefetchScalarGridSpec(
            num_scalar_prefetch=1,
            grid=(chunks // SUBS,),
            in_specs=[
                part_block(proj_width),
                pl.BlockSpec((8, proj_width), lambda c, r: (before, 0)),
                whole(state),
                part_block(keep.shape[1]),
                whole(filters),
                whole(rates),
                whole(head_gain),
            ],
            out_specs=[
                row_block(heads * DV),
                row_block(conv_cols),
                row_block(heads * DV),
                saved_block(DK, DV),
                saved_block(ROWS, ROWS),
                saved_block(ROWS, DV + DK),
                saved_block(ROWS, DV),
                saved_block(ROWS, ROWS),
                saved_block(2 * ROWS, ROWS),
                whole(state),
            ],
            scratch_shapes=[
                pltpu.VMEM((rows + 8, conv_cols), f32),
                pltpu.VMEM((heads, DK, DV), f32),
            ],
        ),
        out_shape=[
            rows_of(heads * DV, jnp.bfloat16),
            rows_of(conv_cols),
            rows_of(heads * DV),
            saved(DK, DV),
            saved(ROWS, ROWS),
            saved(ROWS, DV + DK),
            saved(ROWS, DV),
            saved(ROWS, ROWS),
            saved(2 * ROWS, ROWS),
            jax.ShapeDtypeStruct(state.shape, f32),
        ],
        compiler_params=pltpu.CompilerParams(vmem_limit_bytes=60 << 20),
        cost_estimate=kernel_cost(24 * row_count / 1024),
        name="mixer_forward",
    )(resets, proj, proj, state, keep, filters, rates, head_gain)


def mixer_backward(
    resets,
    own,
    got,
    resid,
    cot,
    ffn_gain,
    out_weight,
    dstate,
    later,
    proj,
    keep,
    filters,
    rates,
    head_gain,
    saved,
    heads,
    start,
    filled,
):
    row_count = resid.shape[0]
    total_rows, proj_width = proj.shape
    chunks = row_count // ROWS
    first = start // ROWS
    conv_cols = 2 * heads * DK + heads * DV
    f32 = jnp.float32

    rows = BACK_SUBS * ROWS
    steps = row_count // rows
    first_block = start // rows

    def row_block(array):
        return pl.BlockSpec((rows, array.shape[1]), lambda c, r: (steps - 1 - c, 0))

    def part_block(array):
        return pl.BlockSpec(
            (rows, array.shape[1]), lambda c, r: (first_block + steps - 1 - c, 0)
        )

    def saved_block(array):
        return pl.BlockSpec(
            (BACK_SUBS,) + array.shape[1:], lambda c, r: (steps - 1 - c, 0, 0, 0)
        )

    dproj = jax.ShapeDtypeStruct((total_rows, proj_width), jnp.bfloat16)
    dfilter = jax.ShapeDtypeStruct((8, conv_cols), f32)
    dsmall = jax.ShapeDtypeStruct((8, DV), f32)
    dmix = jax.ShapeDtypeStruct(resid.shape, jnp.bfloat16)
    dresid = jax.ShapeDtypeStruct(resid.shape, f32)
    dffn_gain = jax.ShapeDtypeStruct((8, resid.shape[1]), f32)
    args = [resets, own, got, resid, cot, ffn_gain, out_weight, dstate, later]
    args += [proj, keep, filters, rates, head_gain, *saved]
    specs = [row_block(own), row_block(got), row_block(resid), part_block(cot), whole(ffn_gain)]
    specs += [
        pl.BlockSpec(
            (resid.shape[1], heads * DV), lambda c, r: (0, 0), pipeline_mode=pl.Buffered(1)
        )
    ]
    specs += [whole(dstate), whole(later), part_block(proj), part_block(keep)]
    specs += [whole(filters), whole(rates), whole(head_gain)]
    specs += [row_block(saved[0]), row_block(saved[1])]
    specs += [saved_block(array) for array in saved[2:]]
    aliases = {}
    if filled is not None:
        aliases = {len(args): 0}
        args.append(filled)
        specs.append(pl.BlockSpec(memory_space=pl.ANY))
    return pl.pallas_call(
        partial(backward_kernel, heads, first, chunks),
        grid_spec=pltpu.PrefetchScalarGridSpec(
            num_scalar_prefetch=1,
            grid=(steps,),
            in_specs=specs,
            out_specs=[
                part_block(dproj),
                whole(dfilter),
                whole(dsmall),
                row_block(dmix),
                row_block(dresid),
                whole(dffn_gain),
                whole(dstate),
                whole(later),
            ],
            scratch_shapes=[
                pltpu.VMEM((rows + 8, conv_cols), f32),
                pltpu.VMEM((heads, DK, DV), f32),
            ],
        ),
        out_shape=[
            dproj,
            dfilter,
            dsmall,
            dmix,
            dresid,
            dffn_gain,
            jax.ShapeDtypeStruct(dstate.shape, f32),
            jax.ShapeDtypeStruct(later.shape, f32),
        ],
        input_output_aliases=aliases,
        compiler_params=pltpu.CompilerParams(vmem_limit_bytes=60 << 20),
        cost_estimate=kernel_cost(30 * row_count / 1024),
        name="mixer_backward",
    )(*args)


def ffn_both_ways(own, other, inputs, cot_masked, keep, gain, weight, ff_cols, start, filled):
    row_count, own_cols = own.shape
    total_rows, width = inputs.shape
    rows = FFN_ROWS
    first = start // rows
    bf16 = jnp.bfloat16

    def whole(array):
        return pl.BlockSpec(array.shape, lambda c: (0, 0))

    def row_block(cols):
        return pl.BlockSpec((rows, cols), lambda c: (c, 0))

    def part_block(cols):
        return pl.BlockSpec((rows, cols), lambda c: (c + first, 0))

    args = [own, other, inputs, cot_masked, keep, gain, weight]
    specs = [row_block(own_cols), row_block(own_cols), part_block(width), part_block(width)]
    specs += [part_block(keep.shape[1]), whole(gain)]
    specs += [pl.BlockSpec(memory_space=pl.ANY)]
    aliases = {}
    if filled is not None:
        aliases = {len(args): 2, len(args) + 1: 3}
        args += list(filled)
        specs += [pl.BlockSpec(memory_space=pl.ANY)] * 2
    return pl.pallas_call(
        partial(ffn_kernel, 2 * own_cols, ff_cols),
        grid=(row_count // rows,),
        in_specs=specs,
        out_specs=[
            row_block(width),
            row_block(width),
            part_block(width),
            part_block(3 * ff_cols),
        ],
        out_shape=[
            jax.ShapeDtypeStruct((row_count, width), jnp.float32),
            jax.ShapeDtypeStruct((row_count, width), bf16),
            jax.ShapeDtypeStruct((total_rows, width), bf16),
            jax.ShapeDtypeStruct((total_rows, 3 * ff_cols), bf16),
        ],
        scratch_shapes=[pltpu.VMEM(weight.shape, bf16), pltpu.SemaphoreType.DMA((4,))],
        input_output_aliases=aliases,
        compiler_params=pltpu.CompilerParams(vmem_limit_bytes=60 << 20),
        cost_estimate=kernel_cost(28 * row_count / 1024),
        name="ffn_both_ways",
    )(*args)


def ffn_outputs(acts, weight, ff_cols):
    row_count = acts.shape[0]
    width = weight.shape[0]
    rows = 256
    bf16 = jnp.bfloat16
    return pl.pallas_call(
        partial(ffn_out_kernel, weight.shape[1] - ff_cols),
        grid=(row_count // rows,),
        in_specs=[
            pl.BlockSpec((rows, ff_cols), lambda c: (c, 2)),
            pl.BlockSpec(memory_space=pl.ANY),
        ],
        out_specs=pl.BlockSpec((rows, width), lambda c: (c, 0)),
        out_shape=jax.ShapeDtypeStruct((row_count, width), bf16),
        scratch_shapes=[pltpu.VMEM((width, ff_cols), bf16), pltpu.SemaphoreType.DMA],
        compiler_params=pltpu.CompilerParams(vmem_limit_bytes=60 << 20),
        cost_estimate=kernel_cost(0.1),
        name="ffn_outputs",
    )(acts, weight)


def grads_kernel(
    shard_rows,
    side_ref,
    normed_ref,
    dproj_ref,
    dmix_lo_ref,
    dmix_hi_ref,
    gated_lo_ref,
    gated_hi_ref,
    mine_a_ref,
    mine_b_ref,
    theirs_a_ref,
    theirs_b_ref,
    rate_ref,
):
    side = side_ref[0]
    normed = normed_ref[...]
    gate_cols = gated_lo_ref.shape[1]
    first_cols = mine_a_ref.shape[1]

    def put(grad, mine_ref, theirs_ref, cols):
        pairs = grad.reshape(-1, 2, shard_rows, grad.shape[-1])
        even = pairs[:, 0].reshape(-1, grad.shape[-1])
        odd = pairs[:, 1].reshape(-1, grad.shape[-1])
        mine_ref[:, cols] = jnp.where(side == 0, even, odd).astype(jnp.bfloat16)
        theirs_ref[:, cols] = jnp.where(side == 0, odd, even).astype(jnp.bfloat16)

    put(dot(normed, dproj_ref[:, :first_cols], TN), mine_a_ref, theirs_a_ref, slice(None))
    put(
        dot(normed, dproj_ref[:, first_cols : first_cols + gate_cols], TN),
        mine_b_ref,
        theirs_b_ref,
        slice(0, gate_cols),
    )
    put(
        dot(dmix_lo_ref[...], gated_lo_ref[...], TN)
        + dot(dmix_hi_ref[...], gated_hi_ref[...], TN),
        mine_b_ref,
        theirs_b_ref,
        slice(gate_cols, 2 * gate_cols),
    )
    rate_ref[...] = dot(dproj_ref[:, first_cols + gate_cols :], normed, TN)[:8]


def mixer_weight_grads(side, normed, dproj, dmix_lo, dmix_hi, gated_lo, gated_hi, shard_rows):
    rows, width = normed.shape
    half_rows, v_cols = gated_lo.shape
    tile = 256
    first_cols = 2 * v_cols
    bf16 = jnp.bfloat16

    def column_block(array):
        return pl.BlockSpec((array.shape[0], tile), lambda c, r: (0, c))

    def row_block(cols):
        return pl.BlockSpec((tile // 2, cols), lambda c, r: (c, 0))

    return pl.pallas_call(
        partial(grads_kernel, shard_rows),
        grid_spec=pltpu.PrefetchScalarGridSpec(
            num_scalar_prefetch=1,
            grid=(width // tile,),
            in_specs=[
                column_block(normed),
                whole(dproj),
                column_block(dmix_lo),
                column_block(dmix_hi),
                whole(gated_lo),
                whole(gated_hi),
            ],
            out_specs=[
                row_block(first_cols),
                row_block(first_cols),
                row_block(first_cols),
                row_block(first_cols),
                pl.BlockSpec((8, tile), lambda c, r: (0, c)),
            ],
        ),
        out_shape=[
            jax.ShapeDtypeStruct((width // 2, first_cols), bf16),
            jax.ShapeDtypeStruct((width // 2, first_cols), bf16),
            jax.ShapeDtypeStruct((width // 2, first_cols), bf16),
            jax.ShapeDtypeStruct((width // 2, first_cols), bf16),
            jax.ShapeDtypeStruct((8, width), jnp.float32),
        ],
        compiler_params=pltpu.CompilerParams(vmem_limit_bytes=60 << 20),
        cost_estimate=kernel_cost(8),
        name="mixer_weight_grads",
    )(side, normed, dproj, dmix_lo, dmix_hi, gated_lo, gated_hi)


def ffn_grads_kernel(normed_ref, cot_ref, acts_ref, grads_ref):
    part = pl.program_id(0)

    @pl.when(part < 2)
    def _():
        grads_ref[...] = dot(normed_ref[...], acts_ref[...], TN).astype(jnp.bfloat16)

    @pl.when(part == 2)
    def _():
        grads_ref[...] = dot(cot_ref[...], acts_ref[...], TN).astype(jnp.bfloat16)


def ffn_weight_grads(normed, cot_masked, acts, ff_cols):
    rows, width = normed.shape

    def fixed(array):
        return pl.BlockSpec(array.shape, lambda c: (0, 0), pipeline_mode=pl.Buffered(1))

    return pl.pallas_call(
        ffn_grads_kernel,
        grid=(3,),
        in_specs=[
            fixed(normed),
            fixed(cot_masked),
            pl.BlockSpec((rows, ff_cols), lambda c: (0, c)),
        ],
        out_specs=pl.BlockSpec((width, ff_cols), lambda c: (0, c)),
        out_shape=jax.ShapeDtypeStruct((width, 3 * ff_cols), jnp.bfloat16),
        compiler_params=pltpu.CompilerParams(vmem_limit_bytes=60 << 20),
        cost_estimate=kernel_cost(0.1),
        name="ffn_weight_grads",
    )(normed, cot_masked, acts)


def swap_halves(array):
    return lax.ppermute(array, "mp", [(0, 1), (1, 0)])


def dp_total(array):
    count = lax.axis_size("dp")
    step = 1
    while step < count:
        array = array + lax.ppermute(array, "dp", [(i, i ^ step) for i in range(count)])
        step *= 2
    return array


def dp_swap(array, bit):
    count = lax.axis_size("dp")
    return lax.ppermute(array, "dp", [(i, i ^ bit) for i in range(count)])


def dp_gather(shard, cuts, first_held, then):
    index = lax.axis_index("dp")
    bits = [1 << i for i in reversed(range((lax.axis_size("dp") - 1).bit_length()))]
    pieces = [shard[None, :, start:stop] for start, stop in cuts]
    for at, bit in enumerate(bits):
        if at == 1:
            pieces, first_held = lax.optimization_barrier((pieces, first_held))
            then_held = then(first_held)
        if at == 3:
            pieces, then_held = lax.optimization_barrier((pieces, then_held))
        others = [dp_swap(piece, bit) for piece in pieces]
        upper = (index & bit) != 0
        pieces = [
            jnp.stack(
                [jnp.where(upper, other, piece), jnp.where(upper, piece, other)], axis=1
            ).reshape((-1,) + piece.shape[1:])
            for piece, other in zip(pieces, others)
        ]
    return [piece.reshape(-1, piece.shape[-1]) for piece in pieces], first_held, then_held


def scatter_first(kept, sent):
    return [
        (mine.astype(jnp.float32) + dp_swap(theirs, 1).astype(jnp.float32)).astype(mine.dtype)
        for mine, theirs in zip(kept, sent)
    ]


def scatter_step(pieces, at):
    index = lax.axis_index("dp")
    bits = [1 << i for i in range(1, (lax.axis_size("dp") - 1).bit_length())]
    orders = [bits, bits[1:2] + bits[:1] + bits[2:]]
    sums = []
    for piece, order in zip(pieces, orders):
        left = sorted(order[at:], reverse=True)
        bit = order[at]
        axis = left.index(bit)
        side = (index & bit) // bit
        cut = piece.reshape((2,) * len(left) + (-1, piece.shape[-1]))
        sent = lax.dynamic_index_in_dim(cut, 1 - side, axis, False).astype(jnp.bfloat16)
        mine = lax.dynamic_index_in_dim(cut, side, axis, False)
        total = mine.astype(jnp.float32) + dp_swap(sent, bit).astype(jnp.float32)
        sums.append(total.astype(piece.dtype).reshape(-1, piece.shape[-1]))
    return sums


def scatter_steps():
    return (lax.axis_size("dp") - 1).bit_length() - 1


def in_order(own, other, model_index, axis):
    first = jnp.where(model_index == 0, own, other)
    second = jnp.where(model_index == 0, other, own)
    return jnp.concatenate([first, second], axis=axis)


def on_device(
    block_input,
    seq_lengths,
    seq_owner,
    mix_gain,
    query_weight,
    key_weight,
    value_weight,
    gate_weight,
    decay_weight,
    beta_weight,
    query_filter,
    key_filter,
    value_filter,
    decay_log,
    decay_bias,
    head_gain,
    out_weight,
    ffn_gain,
    ffn_gate,
    ffn_up,
    ffn_down,
    cotangent,
):
    bf16 = jnp.bfloat16
    f32 = jnp.float32
    local_rows, width = block_input.shape
    dp_index = lax.axis_index("dp")
    model_count = lax.axis_size("mp")
    model_index = lax.axis_index("mp")
    row_count = local_rows * model_count
    keep_masks, resets, valid_rows = layout(seq_lengths, seq_owner, dp_index, row_count)
    valid_all = valid_rows[:, None]
    heads_local = decay_log.shape[0] // model_count
    qk_cols = heads_local * DK
    v_cols = heads_local * DV
    ff_cols = ffn_gate.shape[1]
    shard_rows = query_weight.shape[0]
    proj_cols = 2 * qk_cols + 2 * v_cols

    def own_columns(array, col_count):
        return lax.dynamic_slice_in_dim(array, model_index * col_count, col_count, array.ndim - 1)

    def own_shard(array):
        return lax.dynamic_slice_in_dim(array, dp_index * shard_rows, shard_rows, 0)

    small_weight = jnp.concatenate(
        [own_columns(decay_weight, heads_local), own_columns(beta_weight, heads_local)], axis=1
    )
    small_weight = jnp.pad(small_weight, ((0, 0), (0, 128 - 2 * heads_local)))
    shard_mix = jnp.concatenate(
        [query_weight, key_weight, value_weight, gate_weight, own_shard(small_weight)], axis=1
    )
    half = proj_cols // 256 * 128
    out_rows = out_weight.T
    shard_ffn = jnp.concatenate([ffn_gate, ffn_up, ffn_down.T], axis=1)
    out_other = swap_halves(out_rows)
    input_other = swap_halves(block_input)
    mix_pieces, (out_other, out_rows, shard_ffn), (input_other, cot_held) = dp_gather(
        shard_mix,
        ((0, half), (half, shard_mix.shape[1])),
        (out_other, out_rows, shard_ffn),
        lambda held: (input_other, cotangent),
    )
    mix_weight = jnp.concatenate(mix_pieces, axis=1)
    shard_rest = jnp.concatenate([out_rows, out_other, shard_ffn], axis=1)
    rest_weight = lax.all_gather(shard_rest, "dp", axis=0, tiled=True)
    cot_other = swap_halves(cot_held)

    filters = jnp.concatenate(
        [
            own_columns(query_filter, qk_cols),
            own_columns(key_filter, qk_cols),
            own_columns(value_filter, v_cols),
        ],
        axis=1,
    )
    filters = jnp.pad(filters, ((0, 8 - KW), (0, 0)))
    rates = jnp.stack(
        [own_columns(decay_bias, heads_local), -jnp.exp(own_columns(decay_log, heads_local))]
    )
    rates = jnp.pad(rates, ((0, 6), (0, 128 - heads_local)))
    gain_row = head_gain[None]
    restarts = resets.astype(jnp.int32)
    later_masks = [
        jnp.concatenate([keep_masks[offset, offset:], jnp.ones((offset,), f32)])
        for offset in range(KW)
    ]
    keep_cols = jnp.stack(
        [keep_masks[offset] for offset in range(KW)] + later_masks + [valid_rows] * 8, axis=1
    )
    inputs_b = in_order(block_input, input_other, model_index, 0)
    inputs_f = inputs_b.astype(f32)
    cot_all = in_order(cotangent, cot_other, model_index, 0)
    normed1, inv_rms1 = rms_forward(inputs_f)
    mixed_in = (normed1 * mix_gain).astype(bf16)
    proj = jnp.dot(mixed_in, mix_weight, preferred_element_type=f32)
    cuts = (qk_cols, 2 * qk_cols, 2 * qk_cols + v_cols, proj_cols)
    middle = row_count // 2
    zero_state = jnp.zeros((heads_local, DK, DV), f32)
    small_args = (keep_cols, filters, rates, gain_row)
    gated_lo, *saved_lo, carried = mixer_forward(
        restarts, proj, *small_args, heads_local, 0, middle, zero_state
    )
    cot_masked = cot_all * valid_all.astype(bf16)
    ffn_row = ffn_gain[None]
    carried, cot_all, cot_masked, inputs_b = lax.optimization_barrier(
        (carried, cot_all, cot_masked, inputs_b)
    )
    gated_hi, *saved_hi, _ = mixer_forward(
        restarts, proj, *small_args, heads_local, middle, row_count, carried
    )
    other_lo = swap_halves(gated_lo)
    gated_sent, other_lo = lax.optimization_barrier((gated_hi, other_lo))
    other_hi = swap_halves(gated_sent)
    ffn_args = (inputs_b, cot_masked, keep_cols, ffn_row, rest_weight, ff_cols)
    resid_lo, dnormed_lo, *filled = ffn_both_ways(
        gated_lo, other_lo, *ffn_args, 0, None
    )
    resid_hi, dnormed_hi, ffn_in, acts = ffn_both_ways(
        gated_hi, other_hi, *ffn_args, middle, filled
    )
    got_hi, dnormed_lo = lax.optimization_barrier((swap_halves(dnormed_hi), dnormed_lo))
    got_lo = swap_halves(dnormed_lo)
    core_side = (dp_index & 1).reshape(1)
    rest_grads = ffn_weight_grads(ffn_in, cot_masked, acts, ff_cols)
    acts_later, _ = lax.optimization_barrier((acts, rest_grads))
    summand = ffn_outputs(acts_later, rest_weight, ff_cols)
    got_hi, summand = lax.optimization_barrier((got_hi, summand))
    ffn_shard = lax.psum_scatter(rest_grads, "dp", scatter_dimension=0, tiled=True)

    def own_half(array):
        return lax.dynamic_slice_in_dim(array, model_index * local_rows, local_rows, 0)

    def other_half(array):
        return lax.dynamic_slice_in_dim(array, (1 - model_index) * local_rows, local_rows, 0)

    def own_of(low, high):
        return jnp.where(model_index == 0, low, high)

    zero_rows = jnp.zeros((8, proj_cols - v_cols), f32)
    proj_grad, filter_hi, small_hi, dmix_hi, dresid_hi, ffn_gain_hi, carried, later = (
        mixer_backward(
            restarts,
            dnormed_hi,
            got_hi,
            resid_hi,
            cot_all,
            ffn_row,
            rest_weight,
            zero_state,
            zero_rows,
            proj,
            *small_args,
            saved_hi,
            heads_local,
            middle,
            None,
        )
    )
    summand_sent, got_lo, proj_grad = lax.optimization_barrier(
        (other_half(summand), got_lo, proj_grad)
    )
    proj_grad, filter_lo, small_lo, dmix_lo, dresid_lo, ffn_gain_lo, _, _ = mixer_backward(
        restarts,
        dnormed_lo,
        got_lo,
        resid_lo,
        cot_all,
        ffn_row,
        rest_weight,
        carried,
        later,
        proj,
        *small_args,
        saved_lo,
        heads_local,
        0,
        proj_grad,
    )
    summand_got, proj_grad, dmix_lo, filter_lo, small_lo, dresid_lo, ffn_gain_lo = (
        lax.optimization_barrier(
            (
                swap_halves(summand_sent),
                proj_grad,
                dmix_lo,
                filter_lo,
                small_lo,
                dresid_lo,
                ffn_gain_lo,
            )
        )
    )
    ffn_sum = own_half(summand).astype(f32) + summand_got.astype(f32)
    block_output = (own_of(resid_lo, resid_hi) + own_half(valid_all) * ffn_sum).astype(bf16)
    filter_grads = filter_lo + filter_hi
    small_grads = small_lo + small_hi
    ffn_gain_part = ffn_gain_lo[0] + ffn_gain_hi[0]
    *grad_pieces, rate_grads = mixer_weight_grads(
        core_side,
        mixed_in,
        proj_grad,
        dmix_lo,
        dmix_hi,
        gated_lo,
        gated_hi,
        shard_rows,
    )
    rate_grads = rate_grads[: 2 * heads_local]
    mix_sums = scatter_first(grad_pieces[:2], grad_pieces[2:])
    proj_grad, mix_sums, rate_grads = lax.optimization_barrier(
        (proj_grad, mix_sums, rate_grads)
    )
    mix_sums = scatter_step(mix_sums, 0)
    mix_in_part = against(proj_grad, mix_weight)
    mix_gain_part = jnp.sum(mix_in_part * normed1, 0)
    common = jnp.concatenate(
        [mix_gain_part, ffn_gain_part, small_grads[0], jnp.zeros((width - DV,), f32)]
    ).reshape(3, width)
    tail_row = jnp.concatenate(
        [small_grads[1, : 2 * heads_local], jnp.zeros((width - 2 * heads_local,), f32)]
    )
    split_rows = jnp.concatenate(
        [
            rate_grads,
            filter_grads[:KW, : cuts[0]].reshape(-1, width),
            filter_grads[:KW, cuts[0] : cuts[1]].reshape(-1, width),
            filter_grads[:KW, cuts[1] : cuts[2]].reshape(-1, width),
            tail_row[None],
        ],
        axis=0,
    )
    small_rows = jnp.concatenate([common, split_rows], axis=0)
    small_other = swap_halves(small_rows)
    lower = own_of(small_rows, small_other)[3:]
    upper = own_of(small_other, small_rows)[3:]
    small_sums = jnp.concatenate([small_rows[:3] + small_other[:3], lower, upper], axis=0)
    small_sums = jnp.pad(small_sums, ((0, -small_sums.shape[0] % 8), (0, 0)))
    small_sums, mix_in_sent = lax.optimization_barrier(
        (small_sums, other_half(mix_in_part).astype(bf16))
    )
    mix_in_got = swap_halves(mix_in_sent)
    mix_sums, small_sums = lax.optimization_barrier((mix_sums, small_sums))
    totals = dp_total(small_sums)
    for step in range(1, scatter_steps()):
        if step == 2:
            mix_sums, totals, mix_in_got = lax.optimization_barrier(
                (mix_sums, totals, mix_in_got)
            )
        mix_sums = scatter_step(mix_sums, step)
    mix_shards = [piece.astype(f32) for piece in mix_sums]
    mix_in_sum = own_half(mix_in_part) + mix_in_got.astype(f32)
    input_grad = own_of(dresid_lo, dresid_hi) + rms_backward(
        mix_in_sum * mix_gain, own_half(normed1), own_half(inv_rms1)
    )
    common = totals[:3]
    split_count = split_rows.shape[0]
    lower = totals[3 : 3 + split_count]
    upper = totals[3 + split_count : 3 + 2 * split_count]

    def joined(start, rows, cols):
        return jnp.concatenate(
            [
                lower[start : start + rows].reshape(-1, cols),
                upper[start : start + rows].reshape(-1, cols),
            ],
            axis=1,
        )

    q_rows = KW * qk_cols // width
    v_rows = KW * v_cols // width
    at_q = 2 * heads_local
    at_k = at_q + q_rows
    at_v = at_k + q_rows
    at_tail = at_v + v_rows

    def rate_weight_grad(start):
        return jnp.concatenate(
            [lower[start : start + heads_local], upper[start : start + heads_local]], axis=0
        ).T

    def rate_grad(start):
        return jnp.concatenate(
            [
                lower[at_tail, start : start + heads_local],
                upper[at_tail, start : start + heads_local],
            ]
        )

    ffn_shard = ffn_shard.astype(f32)
    return (
        block_output,
        input_grad,
        common[0],
        mix_shards[0][:, : cuts[0]],
        mix_shards[0][:, cuts[0] : cuts[1]],
        mix_shards[0][:, cuts[1] :],
        mix_shards[1][:, :v_cols],
        rate_weight_grad(0),
        rate_weight_grad(heads_local),
        joined(at_q, q_rows, qk_cols),
        joined(at_k, q_rows, qk_cols),
        joined(at_v, v_rows, v_cols),
        rate_grad(0),
        rate_grad(heads_local),
        common[2, :DV],
        mix_shards[1][:, v_cols:].T,
        common[1],
        ffn_shard[:, :ff_cols],
        ffn_shard[:, ff_cols : 2 * ff_cols],
        ffn_shard[:, 2 * ff_cols :].T,
    )


def solution(mesh):
    in_specs = (
        P(("dp", "mp"), None),
        P(),
        P(),
        P(),
        P("dp", "mp"),
        P("dp", "mp"),
        P("dp", "mp"),
        P("dp", "mp"),
        P(),
        P(),
        P(),
        P(),
        P(),
        P(),
        P(),
        P(),
        P("mp", "dp"),
        P(),
        P("dp", "mp"),
        P("dp", "mp"),
        P("mp", "dp"),
        P(("dp", "mp"), None),
    )
    out_specs = (
        P(("dp", "mp"), None),
        P(("dp", "mp"), None),
        P(),
        P("dp", "mp"),
        P("dp", "mp"),
        P("dp", "mp"),
        P("dp", "mp"),
        P(),
        P(),
        P(),
        P(),
        P(),
        P(),
        P(),
        P(),
        P("mp", "dp"),
        P(),
        P("dp", "mp"),
        P("dp", "mp"),
        P("mp", "dp"),
    )
    return jax.shard_map(
        on_device, mesh=mesh, in_specs=in_specs, out_specs=out_specs, check_vma=False
    )
```
